256 devices in a mesh: band: 32 (over x_hi, z, core), pencil: 8 (over x_lo, y).
Axes of the slice: x: 4 (x_hi: 2, x_lo: 2; x = x_hi * 2 + x_lo), y: 4, z: 8, core: 2. Of those that a mesh axis runs over, the one named last changes fastest.
Arguments:
- orbitals: float32 [64, 72, 5184], P('band', 'pencil'), may hold values from -6 to 6
- pair_mask: int32 [32, 2, 2, 2], P('band'), may hold values 0 or 1
Outputs:
- exchange_term: float32 [64, 72, 5184], P('band', 'pencil')
The draws below stay inside these ranges and needn't reach their ends.
All inputs are finite; a program needn't handle non-finite values. No bound on the sum of `pair_mask` on one device may be relied on, other than what follows from the above.
Results may differ from the reference program's by a relative error of at most 0.0001.
Values sent between devices are 32-bit elements; how exact they have to be, the bound alone decides.
A program may use at most 64 MiB of HBM per device.

```python
import jax
import jax.numpy as jnp
from jax import lax

NG = 72
BLOCK = 2
STEPS = 2
BANDS = 64
N_BAND = 32


def touch_ends(result, key, least, top_value):
    dims = result.shape
    index_at = [jax.random.randint(jax.random.fold_in(key, axis), (), 0, dims[axis]) for axis in range(len(dims))]
    result = result.at[tuple(index_at)].set(least)
    longest = dims.index(max(dims))
    index_at[longest] = (index_at[longest] + 1) % dims[longest]
    return result.at[tuple(index_at)].set(top_value)


def shard_levels(rng, extent, split, smallest, top_value):
    loudness, own = 1.0, jax.random.fold_in(rng, 6)
    for axis_at, blocks in split:
        steps = jnp.exp(jax.random.uniform(jax.random.fold_in(own, axis_at), (blocks,), jnp.float32, smallest / len(split), top_value / len(split)))
        loudness = loudness * jnp.repeat(steps, extent[axis_at] // blocks).reshape([-1 if axis == axis_at else 1 for axis in range(len(extent))])
    return loudness


def bell_draw(key, extent, deviation, most, shards=(), kind=jnp.bfloat16):
    drawn = jax.random.normal(key, extent, jnp.float32) * deviation
    if len(shards) > 0:
        drawn = shard_levels(key, extent, shards, -0.22, 0.18) * drawn
    return jnp.clip(drawn, min=-most, max=most).astype(kind)


def setup_inputs(seed: int = 0) -> dict:
    keys = jax.random.split(jax.random.key(seed), 3)
    return {
        "orbitals": bell_draw(keys[0], (BANDS, NG, NG * NG), 1.0, 6.0, ((0, 32), (1, 8)), jnp.float32),
        "pair_mask": touch_ends((jax.random.randint(keys[1], (N_BAND, STEPS, BLOCK, BLOCK), 0, 4) < 3).astype(jnp.int32), jax.random.fold_in(keys[1], 1), 0, 1),
    }


coulomb_scale = 20.0
screening = 0.25
highest = lax.Precision.HIGHEST


def kernel_table():
    frequency = jnp.fft.fftfreq(NG) * NG
    squared = frequency[:, None, None] * frequency[:, None, None] + frequency[None, :, None] * frequency[None, :, None] + frequency[None, None, :] * frequency[None, None, :]
    return coulomb_scale / (squared + screening)


def reference(orbitals, pair_mask):
    orbital_blocks = orbitals.reshape(N_BAND, BLOCK, NG, NG, NG)
    kernel = kernel_table()
    accumulated = jnp.zeros_like(orbital_blocks)
    for distance in range(1, STEPS + 1):
        visitors = jnp.roll(orbital_blocks, distance, axis=0)
        weights = pair_mask[:, distance - 1].astype(jnp.float32)

        def one_group(group_items):
            resident, visitor, weight = group_items
            density = resident[:, None] * visitor[None, :]
            spectrum = jnp.fft.fftn(density, axes=(-3, -2, -1))
            potential = jnp.real(jnp.fft.ifftn(spectrum * kernel, axes=(-3, -2, -1)))
            potential = potential.astype(resident.dtype) * weight[:, :, None, None, None]
            resident_add = jnp.einsum('acxyz,cxyz->axyz', potential, visitor, precision=highest)
            visitor_add = jnp.einsum('acxyz,axyz->cxyz', potential, resident, precision=highest)
            return resident_add, visitor_add

        resident_add, visitor_add = lax.map(one_group, (orbital_blocks, visitors, weights))
        accumulated = accumulated + resident_add + jnp.roll(visitor_add, -distance, axis=0)
    return (-accumulated).reshape(BANDS, NG, NG * NG)
```

```python
import functools
import math

import jax
import jax.numpy as jnp
import ml_dtypes
import numpy as np
from jax import lax
from jax.experimental import pallas as pl
from jax.experimental.pallas import tpu as pltpu
from jax.sharding import PartitionSpec as P

MESH = pl.DeviceIdType.MESH
NG = 72
PLANES = 9
PEERS = 8
FIELDS = 4
ROWS = 40
BLOCK = 184
LAST = 160
MERGED = NG * NG
WIDTH = 5248
OWN = 640
TAIL = PEERS * OWN
TAIL_OWNER = (0, 6)
FOLD = 11
MASKS = FOLD
QUARTERS = [(q * FOLD, min((q + 1) * FOLD, 41)) for q in range(4)]
TILES = WIDTH // 128
OWN_TILES = OWN // 128
TAIL_TILE = TILES - 1
coulomb_scale = 20.0
screening = 0.25
HALF = math.sqrt(0.5)


def dft8(x):
    a = [x[j] + x[j + 4] for j in range(4)]
    b = [x[j] - x[j + 4] for j in range(4)]
    e, o = a[0] + a[2], a[1] + a[3]
    u, v = HALF * (b[1] - b[3]), HALF * (b[1] + b[3])
    return [e + o, e - o, b[0] + u, v + b[2], a[0] - a[2], a[1] - a[3], b[0] - u, v - b[2]]


def dft8_adjoint(c):
    p, q = c[0] + c[1], c[0] - c[1]
    a = [p + c[4], q + c[5], p - c[4], q - c[5]]
    d, s = HALF * (c[2] - c[6]), HALF * (c[3] + c[7])
    b = [c[2] + c[6], d + s, c[3] - c[7], s - d]
    return [a[j] + b[j] for j in range(4)] + [a[j] - b[j] for j in range(4)]


def cos9(n):
    return math.cos(2.0 * math.pi * (n % 9) / 9)


def sin9(n):
    return math.sin(2.0 * math.pi * (n % 9) / 9)


def weighted(values, factors):
    total = values[0] * factors[0]
    for value, factor in zip(values[1:], factors[1:]):
        total = total + value * factor
    return total


def dft9(x):
    e = [x[n] + x[9 - n] for n in range(1, 5)]
    o = [x[n] - x[9 - n] for n in range(1, 5)]
    third = e[0] + e[1] + e[3]
    cosines = [x[0] + third + e[2]]
    sines = [None]
    for k in range(1, 5):
        if k == 3:
            cosines.append(x[0] + e[2] - 0.5 * third)
            sines.append(sin9(3) * (o[0] - o[1] + o[3]))
        else:
            cosines.append(x[0] + weighted(e, [cos9(k * n) for n in range(1, 5)]))
            sines.append(weighted(o, [sin9(k * n) for n in range(1, 5)]))
    return cosines, sines


def dft9_adjoint(cosines, sines):
    c, s = cosines, sines
    out = [None] * 9
    out[0] = c[0] + ((c[1] + c[2]) + (c[3] + c[4]))
    for n in range(1, 5):
        if n == 3:
            even = c[0] + c[3] - 0.5 * (c[1] + c[2] + c[4])
            odd = sin9(3) * (s[1] - s[2] + s[4])
        else:
            even = c[0] + weighted(c[1:], [cos9(k * n) for k in range(1, 5)])
            odd = weighted(s[1:], [sin9(k * n) for k in range(1, 5)])
        out[n] = even + odd
        out[9 - n] = even - odd
    return out


def finish72(load, save):
    for part in (0, 1):
        cosines, sines = dft9([load(part, b) for b in range(9)])
        base = part * 9
        save(base, cosines[0])
        for k in range(1, 5):
            save(base + 2 * k - 1, cosines[k])
            save(base + 2 * k, sines[k])
    for k8 in range(3):
        base = 18 + 18 * k8
        cc, cs = dft9([load(2 + 2 * k8, b) for b in range(9)])
        sc, ss = dft9([load(3 + 2 * k8, b) for b in range(9)])
        save(base, cc[0])
        save(base + 1, sc[0])
        for k in range(1, 5):
            at = base + 4 * k - 2
            save(at, cc[k] - ss[k])
            save(at + 1, cc[k] + ss[k])
            save(at + 2, sc[k] + cs[k])
            save(at + 3, sc[k] - cs[k])


def finish72_adjoint(load, save):
    for part in (0, 1):
        base = part * 9
        cosines = [load(base)] + [load(base + 2 * k - 1) for k in range(1, 5)]
        sines = [None] + [load(base + 2 * k) for k in range(1, 5)]
        for b, value in enumerate(dft9_adjoint(cosines, sines)):
            save(part, b, value)
    for k8 in range(3):
        base = 18 + 18 * k8
        cc, sc, cs, ss = [load(base)], [load(base + 1)], [None], [None]
        for k in range(1, 5):
            at = base + 4 * k - 2
            plus, minus, sine_plus, sine_minus = [load(at + i) for i in range(4)]
            cc.append(plus + minus)
            ss.append(minus - plus)
            sc.append(sine_plus + sine_minus)
            cs.append(sine_plus - sine_minus)
        for b, value in enumerate(dft9_adjoint(cc, cs)):
            save(2 + 2 * k8, b, value)
        for b, value in enumerate(dft9_adjoint(sc, ss)):
            save(3 + 2 * k8, b, value)


def point72(a, b):
    return (9 * a + 8 * b) % NG


def split(table):
    high = table.astype(ml_dtypes.bfloat16).astype(np.float64)
    return high, (table - high).astype(ml_dtypes.bfloat16).astype(np.float64)


def from_left(table):
    high, low = split(table)
    wide = np.zeros((80, 256))
    wide[:NG, : 3 * NG] = np.concatenate([high, high, low], axis=1)
    return wide


def from_right(table):
    high, low = split(table)
    return np.block([[high, low], [high, np.zeros_like(low)]])


@functools.cache
def tables():
    at = np.arange(NG)
    basis, freq = [np.full(NG, 1.0)], [0]
    for k in range(1, NG // 2):
        basis += [np.cos(2 * np.pi * k * at / NG), np.sin(2 * np.pi * k * at / NG)]
        freq += [k, k]
    basis.append(np.cos(np.pi * at))
    freq.append(NG // 2)
    basis = np.array(basis)
    basis /= np.sqrt((basis * basis).sum(1, keepdims=True))
    freq = np.array(freq, np.float64)
    eye = np.eye(NG)
    parts = [dft8([eye[point72(a, b)] for a in range(8)]) for b in range(9)]
    slots = [None] * NG
    finish72(lambda part, b: parts[b][part], slots.__setitem__)
    slots = np.array(slots)
    norm = (slots * slots).sum(1)
    spectrum = np.abs(np.fft.fft(slots, axis=1))[:, : NG // 2 + 1]
    freq_y = spectrum.argmax(1).astype(np.float64)
    along_z = np.zeros((128, 128))
    along_z[:NG, :NG] = basis.T
    along_x = basis.reshape(NG, PEERS, PLANES)
    along_x = np.concatenate([along_x[:, :, :8].reshape(NG, -1), along_x[:, :, 8]], axis=1)
    column = np.zeros((8, WIDTH), np.float32)
    column[0, :MERGED] = (freq_y[:, None] ** 2 + freq[None, :] ** 2).reshape(-1)
    column[1, :MERGED] = np.repeat(1.0 / norm, NG)
    freq_x = np.broadcast_to((freq**2)[:, None], (NG, 128)).astype(np.float32)
    wide = np.concatenate(
        [from_right(along_z), from_right(along_z.T), from_left(along_x), from_left(along_x.T)]
    )
    return wide.astype(ml_dtypes.bfloat16), column, freq_x


def take(load, start):
    tile, lane = divmod(start, 128)
    value = load(tile)
    if lane == 0:
        return value
    if lane + NG > 128:
        at = lax.broadcasted_iota(jnp.int32, value.shape, 1)
        value = jnp.where(at >= lane, value, load(tile + 1))
    return pltpu.roll(value, 128 - lane, 1)


def put(store, start, value):
    tile, lane = divmod(start, 128)
    if lane:
        value = pltpu.roll(value, lane, 1)
    end = min(lane + NG, 128)
    store(tile, slice(lane, end), value[:, lane:end])
    if lane + NG > 128:
        store(tile + 1, slice(0, lane + NG - 128), value[:, : lane + NG - 128])


def matmul(a, b):
    return jnp.dot(a, b, preferred_element_type=jnp.float32)


def halves(x):
    high = x.astype(jnp.bfloat16)
    return high, (x - high.astype(jnp.float32)).astype(jnp.bfloat16)


def left(table, x):
    high, low = [part.astype(jnp.float32) for part in halves(x)]
    zeros = jnp.zeros((8, x.shape[1]), jnp.float32)
    operand = jnp.concatenate([high, low, high, zeros], axis=0).astype(jnp.bfloat16)
    return matmul(table[:, 0 : operand.shape[0]], operand)[0:NG]


def kernel(
    bands,
    mask_ref,
    bands_hbm,
    wide_hbm,
    column_hbm,
    freq_hbm,
    out_ref,
    bands_ref,
    wide,
    column_ref,
    freq_ref,
    own,
    own_fold,
    visit,
    visit_fold,
    rho,
    work,
    work2,
    wave,
    wave_last,
    wave_tail,
    recv,
    recv_tail,
    back,
    back_tail,
    field,
    field_tail,
    relay,
    kernel_table,
    kernel_tail,
    total,
    total_fold,
    give,
    give_fold,
    given,
    given_fold,
    visit_send,
    visit_recv,
    give_send,
    give_recv,
    wave_send,
    wave_recv,
    tail_send,
    tail_recv,
    back_send,
    back_recv,
    back_tail_send,
    back_tail_recv,
    copy_sem,
    hop_send,
    hop_recv,
    forward_send,
    load_sem,
):
    me = lax.axis_index("pencil")
    group = lax.axis_index("band")
    me_x, me_y = lax.div(me, 4), lax.rem(me, 4)

    loads = [
        pltpu.make_async_copy(src, dst, load_sem.at[i])
        for i, (src, dst) in enumerate(
            [
                (bands_hbm, bands_ref),
                (wide_hbm, wide),
                (column_hbm, column_ref),
                (freq_hbm, freq_ref),
            ]
        )
    ]
    for load in loads:
        load.start()

    def peer(j):
        return lax.rem(me + j, PEERS)

    def at(dx, dy):
        return lax.rem(me_x + dx, 2) * 4 + lax.rem(me_y + dy + 4, 4)

    def group_at(j):
        return lax.rem(group + j + bands, bands)

    barrier = pltpu.get_barrier_semaphore()
    for j in range(1, PEERS):
        pl.semaphore_signal(barrier, inc=1, device_id={"pencil": peer(j)}, device_id_type=MESH)
    for j in (-2, -1, 1, 2):
        pl.semaphore_signal(barrier, inc=1, device_id={"band": group_at(j)}, device_id_type=MESH)
    loads[0].wait()
    for tile in range(TILES):
        lanes = slice(tile * 128, min(tile * 128 + 128, MERGED))
        live = slice(0, lanes.stop - lanes.start)
        if tile == TAIL_TILE:
            own[tile] = jnp.zeros((16, 128), jnp.float32)
            own_fold[tile % FOLD, 6:8, :] = jnp.zeros((2, 128), jnp.float32)
        for plane in range(PLANES - 1):
            own[tile, 2 * plane : 2 * plane + 2, live] = bands_ref[plane, :, lanes]
        row = tile // FOLD * 2
        own_fold[tile % FOLD, row : row + 2, live] = bands_ref[PLANES - 1, :, lanes]

    def own_mask(s, f):
        return mask_ref[0, s, f // 2, f % 2].astype(jnp.float32)

    for m in range(2 * FIELDS):
        value = own_mask(m // FIELDS, m % FIELDS)
        own_fold[MASKS, m : m + 1, :] = jnp.zeros((1, 128), jnp.float32) + value
    pl.semaphore_wait(barrier, PEERS - 1 + 4)

    def remote(src, dst, send, recv, **device):
        return pltpu.make_async_remote_copy(
            src_ref=src,
            dst_ref=dst,
            send_sem=send,
            recv_sem=recv,
            device_id=device,
            device_id_type=MESH,
        )

    odd = lax.rem(group, 2)
    even = odd == 0
    visitor_group = (
        jnp.where(even, group_at(2), group_at(1)),
        jnp.where(even, group_at(1), group_at(-2)),
    )

    def parts(main, fold):
        return [
            *(main.at[pl.ds(begin, end - begin)] for begin, end in QUARTERS),
            fold,
        ]

    def block_copies(src, dst, send, recv, to):
        return [
            remote(one, two, send.at[q], recv.at[q], band=to)
            for q, (one, two) in enumerate(zip(parts(*src), parts(*dst)))
        ]

    def visit_at(s):
        return visit.at[s], visit_fold.at[s]

    def visit_copies(s, src, send, to):
        return block_copies(src, visit_at(s), send, visit_recv.at[s], to)

    def lower_sends():
        return visit_copies(0, (own, own_fold), visit_send.at[0], group_at(-2))

    def lower_relays():
        return visit_copies(0, visit_at(0), visit_send.at[1], group_at(1))

    def upper_sends():
        return visit_copies(1, (own, own_fold), visit_send.at[0], group_at(2)) + visit_copies(
            1, (own, own_fold), visit_send.at[1], group_at(-1)
        )

    @pl.when(even)
    def _():
        for copy in lower_sends():
            copy.start()

    @pl.when(jnp.logical_not(even))
    def _():
        for copy in upper_sends():
            copy.start()

    def kernel_columns(start, width):
        squared = column_ref[0:1, pl.ds(start, width)]
        scale = column_ref[1:2, pl.ds(start, width)]
        return coulomb_scale / (freq_ref[:, 0:1] + squared + screening) * scale

    for load in loads[1:]:
        load.wait()
    kernel_table[...] = kernel_columns(pl.multiple_of(me * OWN, 128), OWN)
    kernel_tail[...] = kernel_columns(TAIL, 128)
    wave_tail[...] = jnp.zeros((2, ROWS, 128), jnp.float32)
    for s in range(2):
        for p in range(PEERS):
            back[s, (p + 1) * BLOCK - 8 : (p + 1) * BLOCK, :] = jnp.zeros((8, 128), jnp.float32)
            back_tail[s, (p + 1) * ROWS - 8 : (p + 1) * ROWS, :] = jnp.zeros((8, 128), jnp.float32)

    first_band = [pl.ds(band, 8, stride=2) for band in range(2)]
    field_rows = [pl.ds(f, 8, stride=FIELDS) for f in range(FIELDS)]
    row_at = lax.broadcasted_iota(jnp.int32, (8, 128), 0)
    resident_one = lax.rem(lax.div(row_at, 2), 2) == 1
    visitor_one = lax.rem(row_at, 2) == 1

    def last_planes(s, j, q):
        a = [own_fold[j, 2 * q + band : 2 * q + band + 1, :] for band in range(2)]
        c = [visit_fold[s, j, 2 * q + band : 2 * q + band + 1, :] for band in range(2)]
        wide_a = [jnp.broadcast_to(row, (8, 128)) for row in a]
        wide_c = [jnp.broadcast_to(row, (8, 128)) for row in c]
        return (
            jnp.where(resident_one, wide_a[1], wide_a[0]),
            jnp.where(visitor_one, wide_c[1], wide_c[0]),
        )

    def along_z(start):
        table = wide[start : start + 256, :]

        def step(i, carry):
            rows = pl.ds(pl.multiple_of(i * 720, 720), 720)
            both = matmul(jnp.concatenate(halves(work[rows, :]), axis=1), table)
            work2[rows, :] = both[:, :128] + both[:, 128:]
            return carry

        lax.fori_loop(0, NG * ROWS // 720, step, 0)

    def place(part, b, t):
        return pl.ds(pl.multiple_of((part * 9 + b) * ROWS + t * 8, 8), 8)

    def first(s):
        arriving = visit_copies(s, (own, own_fold), visit_send.at[0], group_at(1))
        arriving[4].wait_recv()
        relays = lower_relays()
        if s == 0:

            @pl.when(even)
            def _():
                relays[4].start()

        for q, (begin, end) in enumerate(QUARTERS):
            arriving[q].wait_recv()
            if s == 0:

                @pl.when(even)
                def _(q=q):
                    relays[q].start()

            def products(j, carry, q=q, begin=begin):
                tile = begin + j
                phi = [own[tile, rows, :] for rows in first_band]
                chi = [visit[s, tile, rows, :] for rows in first_band]
                for f in range(FIELDS):
                    rho[tile, field_rows[f], :] = phi[f // 2] * chi[f % 2]
                phi, chi = last_planes(s, j, q)
                rho[tile, 32:40, :] = phi * chi
                return carry

            lax.fori_loop(0, end - begin, products, 0, unroll=True)
        for b in range(9):
            starts = [point72(a, b) * NG for a in range(8)]
            parts = dft8([take(lambda i: rho[i], at) for at in starts])
            for part in range(8):
                base = (part * 9 + b) * ROWS
                work[base : base + ROWS, :] = parts[part]
        along_z(0)

        def finish(t, target):
            def load(part, b):
                return work2[place(part, b, t), :]

            def save(slot, value):
                put(target, slot * NG, value)

            finish72(load, save)

        def planes(t, carry):
            def target(tile, lanes, piece):
                if tile == TAIL_TILE:
                    wave_tail[s, pl.ds(pl.multiple_of(t * 8, 8), 8), lanes] = piece
                else:
                    start = tile // OWN_TILES * BLOCK + tile % OWN_TILES * 32
                    wave[s, pl.ds(pl.multiple_of(start + t * 8, 8), 8), lanes] = piece

            finish(t, target)
            return carry

        lax.fori_loop(0, 4, planes, 0)

        def last(tile, lanes, piece):
            if tile == TAIL_TILE:
                wave_tail[s, 32:40, lanes] = piece
            else:
                wave_last[tile * 8 : tile * 8 + 8, lanes] = piece

        finish(4, last)
        upper = lax.broadcasted_iota(jnp.int32, (8, 128), 0) < FIELDS
        for q in range(PEERS):
            for i in range(3):
                tile = (q * OWN_TILES + i) * 8
                piece = wave_last[tile : tile + 8, :]
                if i < 2:
                    piece = jnp.where(upper, piece, wave_last[tile + 24 : tile + 32, :])
                start = q * BLOCK + LAST + i * 8
                wave[s, start : start + 8, :] = piece

    def block_of(ref, s, index):
        return ref.at[s, pl.ds(pl.multiple_of(index * BLOCK, 8), BLOCK), :]

    def tail_of(ref, s, index):
        return ref.at[s, pl.ds(pl.multiple_of(index * ROWS, 8), ROWS), :]

    way = jnp.where(even, 1, -1)
    exchange_refs = ((wave, recv, wave_send, wave_recv), (back, field, back_send, back_recv))

    def hop(phase, s, dx):
        return remote(
            block_of(exchange_refs[phase][0], s, at(dx, 2)),
            relay.at[phase, s, dx],
            hop_send.at[phase, s, dx],
            hop_recv.at[phase, s, dx],
            pencil=at(dx, way),
        )

    def forward(phase, s, dx):
        return remote(
            relay.at[phase, s, dx],
            block_of(exchange_refs[phase][1], s, at(dx, -way)),
            forward_send.at[phase, s, dx],
            exchange_refs[phase][3].at[s, dx * 4 + 2],
            pencil=at(0, way),
        )

    def direct(phase, s, dx, dy):
        src, dst, send, recv_sem = exchange_refs[phase]
        return remote(
            block_of(src, s, at(dx, dy)),
            block_of(dst, s, me),
            send.at[s, dx * 4 + dy],
            recv_sem.at[s, dx * 4 + dy],
            pencil=at(dx, dy),
        )

    straight = [(1, 1), (1, 3), (0, 1), (0, 3), (1, 0)]

    def keep(phase, s):
        src, dst = exchange_refs[phase][:2]
        return pltpu.make_async_copy(
            block_of(src, s, me), block_of(dst, s, me), copy_sem.at[phase, s]
        )

    def send_blocks(phase, s):
        for dx in range(2):
            hop(phase, s, dx).start()
        for dx, dy in straight:
            direct(phase, s, dx, dy).start()
        keep(phase, s).start()

    def forward_blocks(phase, s):
        for dx in range(2):
            hop(phase, s, dx).wait_recv()
            forward(phase, s, dx).start()

    def wait_blocks(phase, s):
        keep(phase, s).wait()
        for dx, dy in straight:
            direct(phase, s, dx, dy).wait_recv()
        for dx in range(2):
            forward(phase, s, dx).wait_recv()

    def end_blocks(phase, s):
        for dx, dy in straight:
            direct(phase, s, dx, dy).wait_send()
        for dx in range(2):
            hop(phase, s, dx).wait_send()
            forward(phase, s, dx).wait_send()

    def tail_copy(s):
        owner = TAIL_OWNER[s]
        distance = lax.rem(owner - me + PEERS, PEERS)
        return remote(
            wave_tail.at[s],
            tail_of(recv_tail, s, me),
            tail_send.at[s],
            tail_recv.at[s, distance],
            pencil=jnp.int32(owner),
        )

    def lines(f, tile, block, last):
        first_rows = [
            pl.ds(p * block + tile * 32 + f, 8, stride=FIELDS) for p in range(PEERS)
        ]
        below = FIELDS * (tile // 3)
        return first_rows + [pl.ds(last + tile % 3 * 8 + below + f, PEERS, stride=block)]

    def spectrum_step(source, target, s, tiles, table, block, last):
        columns = slice(tiles[0] * 128, (tiles[-1] + 1) * 128)
        for f in range(FIELDS):
            rows = [lines(f, tile, block, last) for tile in tiles]
            loaded = [
                jnp.concatenate([source[s, part, :] for part in parts], axis=0) for parts in rows
            ]
            spectrum = left(wide[512:592, :], jnp.concatenate(loaded, axis=1))
            result = left(wide[592:672, :], spectrum * table[:, columns])
            for i, parts in enumerate(rows):
                for j, part in enumerate(parts):
                    target[s, part, :] = result[j * 8 : j * 8 + 8, i * 128 : (i + 1) * 128]

    def second(s):
        spectrum_step(recv, back, s, range(OWN_TILES), kernel_table, BLOCK, LAST)

    def give_copies(s):
        return block_copies(
            (give.at[s], give_fold.at[s]),
            (given.at[odd], given_fold.at[odd]),
            give_send.at[s],
            give_recv.at[odd],
            visitor_group[s],
        )

    def given_copies(source):
        return block_copies(
            (give.at[0], give_fold.at[0]),
            (given.at[source], given_fold.at[source]),
            give_send.at[0],
            give_recv.at[source],
            visitor_group[0],
        )

    def third(s):
        def start(t, source):
            def load(slot):
                return take(source, slot * NG)

            def save(part, b, value):
                work[place(part, b, t), :] = value

            finish72_adjoint(load, save)

        def planes(t, carry):
            def source(tile):
                if tile == TAIL_TILE:
                    return field_tail[s, pl.ds(pl.multiple_of(t * 8, 8), 8), :]
                first_row = tile // OWN_TILES * BLOCK + tile % OWN_TILES * 32
                return field[s, pl.ds(pl.multiple_of(first_row + t * 8, 8), 8), :]

            start(t, source)
            return carry

        lax.fori_loop(0, 4, planes, 0)

        def last(tile):
            if tile == TAIL_TILE:
                return field_tail[s, 32:40, :]
            which = tile % OWN_TILES
            first_row = tile // OWN_TILES * BLOCK + LAST + which % 3 * 8
            value = field[s, first_row : first_row + 8, :]
            return pltpu.roll(value, FIELDS, 0) if which > 2 else value

        start(4, last)
        along_z(256)
        for b in range(9):
            parts = []
            for part in range(8):
                base = (part * 9 + b) * ROWS
                parts.append(work2[base : base + ROWS, :])
            for a, value in enumerate(dft8_adjoint(parts)):


                def store(tile, lanes, piece):
                    rho[tile, :, lanes] = piece

                put(store, point72(a, b) * NG, value)
        weights = []
        for f in range(FIELDS):
            g = 2 * (f % 2) + f // 2
            if s == 0:
                row = jnp.where(
                    even,
                    visit_fold[s, MASKS, FIELDS + g : FIELDS + g + 1, :],
                    visit_fold[s, MASKS, g : g + 1, :],
                )
            else:
                row = jnp.where(
                    even,
                    visit_fold[s, MASKS, g : g + 1, :],
                    own_fold[MASKS, FIELDS + f : FIELDS + f + 1, :],
                )
            weights.append(jnp.broadcast_to(row, (8, 128)))
        last_weight = weights[3]
        for f in range(3):
            last_weight = jnp.where(row_at == f, weights[f], last_weight)

        leaving = give_copies(s)
        for q, (begin, end) in enumerate(QUARTERS):

            def gather(j, carry, q=q, begin=begin):
                tile = begin + j
                phi = [own[tile, rows, :] for rows in first_band]
                chi = [visit[s, tile, rows, :] for rows in first_band]
                value = [rho[tile, field_rows[f], :] * weights[f] for f in range(FIELDS)]
                for a in range(2):
                    stay = value[2 * a] * chi[0] + value[2 * a + 1] * chi[1]
                    if s > 0:
                        stay = stay + total[tile, first_band[a], :]
                    total[tile, first_band[a], :] = stay
                for c in range(2):
                    give[s, tile, first_band[c], :] = value[c] * phi[0] + value[2 + c] * phi[1]
                phi, chi = last_planes(s, j, q)
                value = rho[tile, 32:40, :] * last_weight
                stay, leave = value * chi, value * phi
                stay = stay + pltpu.roll(stay, 7, 0)
                leave = leave + pltpu.roll(leave, 6, 0)
                for band in range(2):
                    row = slice(2 * q + band, 2 * q + band + 1)
                    kept = stay[2 * band : 2 * band + 1]
                    if s > 0:
                        kept = kept + total_fold[j, row, :]
                    total_fold[j, row, :] = kept
                    give_fold[s, j, row, :] = leave[band : band + 1]
                return carry

            lax.fori_loop(0, end - begin, gather, 0, unroll=True)
            leaving[q].start()
        leaving[4].start()

    def tail_back(s, j):
        return remote(
            tail_of(back_tail, s, peer(j)),
            field_tail.at[s],
            back_tail_send.at[s, j],
            back_tail_recv.at[s],
            pencil=peer(j),
        )

    def send_tail(s):
        owner = TAIL_OWNER[s]

        @pl.when(me == owner)
        def _():
            recv_tail[s, owner * ROWS : (owner + 1) * ROWS, :] = wave_tail[s]

        @pl.when(me != owner)
        def _():
            tail_copy(s).start()

    def turn_tail(s):
        owner = TAIL_OWNER[s]

        @pl.when(me == owner)
        def _():
            for j in range(1, PEERS):
                remote(
                    wave_tail.at[s],
                    tail_of(recv_tail, s, me),
                    tail_send.at[s],
                    tail_recv.at[s, j],
                    pencil=peer(j),
                ).wait_recv()
            spectrum_step(recv_tail, back_tail, s, (0,), kernel_tail, ROWS, 32)
            for j in range(1, PEERS):
                tail_back(s, j).start()
            field_tail[s] = back_tail[s, owner * ROWS : (owner + 1) * ROWS, :]

    def end_tail(s):
        owner = TAIL_OWNER[s]

        @pl.when(me == owner)
        def _():
            for j in range(1, PEERS):
                tail_back(s, j).wait_send()

        @pl.when(me != owner)
        def _():
            tail_copy(s).wait_send()
            tail_back(s, 1).wait_recv()

    for s in range(2):
        first(s)
        if s == 1:
            forward_blocks(0, 0)
        send_blocks(0, s)
        send_tail(s)
    for s in range(2):
        wait_blocks(0, s)
        second(s)
        send_blocks(1, s)
        turn_tail(s)
        if s == 0:
            forward_blocks(0, 1)
            forward_blocks(1, 0)
    for s in range(2):
        wait_blocks(1, s)
        end_tail(s)
        third(s)
        if s == 0:
            forward_blocks(1, 1)
    for q, (begin, end) in enumerate(QUARTERS):
        for source in range(2):
            given_copies(source)[q].wait_recv()
        for tile in range(begin, end):
            lanes = slice(tile * 128, min(tile * 128 + 128, MERGED))
            term = -(total[tile] + given[0, tile] + given[1, tile])
            for plane in range(PLANES - 1):
                piece = term[2 * plane : 2 * plane + 2, 0 : lanes.stop - lanes.start]
                out_ref[plane, :, lanes] = piece
    for source in range(2):
        given_copies(source)[4].wait_recv()
    for q, (begin, end) in enumerate(QUARTERS):
        for tile in range(begin, end):
            lanes = slice(tile * 128, min(tile * 128 + 128, MERGED))
            j, rows = tile - begin, slice(2 * q, 2 * q + 2)
            term = total_fold[j, rows, :] + given_fold[0, j, rows, :] + given_fold[1, j, rows, :]
            out_ref[PLANES - 1, :, lanes] = -term[:, 0 : lanes.stop - lanes.start]

    @pl.when(even)
    def _():
        for copy in lower_sends() + lower_relays():
            copy.wait_send()

    @pl.when(jnp.logical_not(even))
    def _():
        for copy in upper_sends():
            copy.wait_send()

    for s in range(2):
        for copy in give_copies(s):
            copy.wait_send()
    for phase in range(2):
        for s in range(2):
            end_blocks(phase, s)


def body(bands, orbitals, pair_mask):
    hbm = pl.BlockSpec(memory_space=pltpu.HBM)
    smem = pl.BlockSpec(memory_space=pltpu.SMEM)
    consts = [jnp.asarray(table) for table in tables()]
    dma = pltpu.SemaphoreType.DMA

    def buffer(*shape):
        return pltpu.VMEM(shape, jnp.float32)

    out = pl.pallas_call(
        functools.partial(kernel, bands),
        out_shape=jax.ShapeDtypeStruct((PLANES, 2, MERGED), jnp.float32),
        in_specs=[smem] + [hbm] * (1 + len(consts)),
        out_specs=pl.BlockSpec(memory_space=pltpu.VMEM),
        scratch_shapes=[
            buffer(PLANES, 2, MERGED),
            pltpu.VMEM(consts[0].shape, jnp.bfloat16),
            buffer(*consts[1].shape),
            buffer(*consts[2].shape),
            buffer(TILES, 16, 128),
            buffer(FOLD + 1, 8, 128),
            buffer(2, TILES, 16, 128),
            buffer(2, FOLD + 1, 8, 128),
            buffer(TILES, ROWS, 128),
            buffer(NG * ROWS, 128),
            buffer(NG * ROWS, 128),
            buffer(2, PEERS * BLOCK, 128),
            buffer(TAIL_TILE * 8, 128),
            buffer(2, ROWS, 128),
            buffer(2, PEERS * BLOCK, 128),
            buffer(2, PEERS * ROWS, 128),
            buffer(2, PEERS * BLOCK, 128),
            buffer(2, PEERS * ROWS, 128),
            buffer(2, PEERS * BLOCK, 128),
            buffer(2, ROWS, 128),
            buffer(2, 2, 2, BLOCK, 128),
            buffer(NG, OWN),
            buffer(NG, 128),
            buffer(TILES, 16, 128),
            buffer(FOLD + 1, 8, 128),
            buffer(2, TILES, 16, 128),
            buffer(2, FOLD + 1, 8, 128),
            buffer(2, TILES, 16, 128),
            buffer(2, FOLD + 1, 8, 128),
            dma((2, 5)),
            dma((2, 5)),
            dma((2, 5)),
            dma((2, 5)),
            dma((2, PEERS)),
            dma((2, PEERS)),
            dma((2,)),
            dma((2, PEERS)),
            dma((2, PEERS)),
            dma((2, PEERS)),
            dma((2, PEERS)),
            dma((2,)),
            dma((2, 2)),
            dma((2, 2, 2)),
            dma((2, 2, 2)),
            dma((2, 2, 2)),
            dma((4,)),
        ],
        compiler_params=pltpu.CompilerParams(
            collective_id=0, has_side_effects=True, vmem_limit_bytes=64 * 1024 * 1024 - 65536
        ),
    )(pair_mask, orbitals.transpose(1, 0, 2), *consts)
    return out.transpose(1, 0, 2)


def solution(mesh):
    return jax.shard_map(
        functools.partial(body, mesh.shape["band"]),
        mesh=mesh,
        in_specs=(P("band", "pencil", None), P("band", None, None, None)),
        out_specs=P("band", "pencil", None),
        check_vma=False,
    )
```

```python
import functools
import math

import jax
import jax.numpy as jnp
import ml_dtypes
import numpy as np
from jax import lax
from jax.experimental import pallas as pl
from jax.experimental.pallas import tpu as pltpu
from jax.sharding import PartitionSpec as P

MESH = pl.DeviceIdType.MESH
NG = 72
PLANES = 9
PEERS = 8
FIELDS = 4
ROWS = 40
BLOCK = 184
LAST = 160
MERGED = NG * NG
WIDTH = 5248
OWN = 640
TAIL = PEERS * OWN
PIECE = 16
FOLD = 11
MASKS = FOLD
QUARTERS = [(q * FOLD, min((q + 1) * FOLD, 41)) for q in range(4)]
TILES = WIDTH // 128
OWN_TILES = OWN // 128
TAIL_TILE = TILES - 1
coulomb_scale = 20.0
screening = 0.25
HALF = math.sqrt(0.5)


def dft8(x):
    a = [x[j] + x[j + 4] for j in range(4)]
    b = [x[j] - x[j + 4] for j in range(4)]
    e, o = a[0] + a[2], a[1] + a[3]
    u, v = HALF * (b[1] - b[3]), HALF * (b[1] + b[3])
    return [e + o, e - o, b[0] + u, v + b[2], a[0] - a[2], a[1] - a[3], b[0] - u, v - b[2]]


def dft8_adjoint(c):
    p, q = c[0] + c[1], c[0] - c[1]
    a = [p + c[4], q + c[5], p - c[4], q - c[5]]
    d, s = HALF * (c[2] - c[6]), HALF * (c[3] + c[7])
    b = [c[2] + c[6], d + s, c[3] - c[7], s - d]
    return [a[j] + b[j] for j in range(4)] + [a[j] - b[j] for j in range(4)]


def cos9(n):
    return math.cos(2.0 * math.pi * (n % 9) / 9)


def sin9(n):
    return math.sin(2.0 * math.pi * (n % 9) / 9)


def weighted(values, factors):
    total = values[0] * factors[0]
    for value, factor in zip(values[1:], factors[1:]):
        total = total + value * factor
    return total


def dft9(x):
    e = [x[n] + x[9 - n] for n in range(1, 5)]
    o = [x[n] - x[9 - n] for n in range(1, 5)]
    third = e[0] + e[1] + e[3]
    cosines = [x[0] + third + e[2]]
    sines = [None]
    for k in range(1, 5):
        if k == 3:
            cosines.append(x[0] + e[2] - 0.5 * third)
            sines.append(sin9(3) * (o[0] - o[1] + o[3]))
        else:
            cosines.append(x[0] + weighted(e, [cos9(k * n) for n in range(1, 5)]))
            sines.append(weighted(o, [sin9(k * n) for n in range(1, 5)]))
    return cosines, sines


def dft9_adjoint(cosines, sines):
    c, s = cosines, sines
    out = [None] * 9
    out[0] = c[0] + ((c[1] + c[2]) + (c[3] + c[4]))
    for n in range(1, 5):
        if n == 3:
            even = c[0] + c[3] - 0.5 * (c[1] + c[2] + c[4])
            odd = sin9(3) * (s[1] - s[2] + s[4])
        else:
            even = c[0] + weighted(c[1:], [cos9(k * n) for k in range(1, 5)])
            odd = weighted(s[1:], [sin9(k * n) for k in range(1, 5)])
        out[n] = even + odd
        out[9 - n] = even - odd
    return out


def finish72(load, save):
    for part in (0, 1):
        cosines, sines = dft9([load(part, b) for b in range(9)])
        base = part * 9
        save(base, cosines[0])
        for k in range(1, 5):
            save(base + 2 * k - 1, cosines[k])
            save(base + 2 * k, sines[k])
    for k8 in range(3):
        base = 18 + 18 * k8
        cc, cs = dft9([load(2 + 2 * k8, b) for b in range(9)])
        sc, ss = dft9([load(3 + 2 * k8, b) for b in range(9)])
        save(base, cc[0])
        save(base + 1, sc[0])
        for k in range(1, 5):
            at = base + 4 * k - 2
            save(at, cc[k] - ss[k])
            save(at + 1, cc[k] + ss[k])
            save(at + 2, sc[k] + cs[k])
            save(at + 3, sc[k] - cs[k])


def finish72_adjoint(load, save):
    for part in (0, 1):
        base = part * 9
        cosines = [load(base)] + [load(base + 2 * k - 1) for k in range(1, 5)]
        sines = [None] + [load(base + 2 * k) for k in range(1, 5)]
        for b, value in enumerate(dft9_adjoint(cosines, sines)):
            save(part, b, value)
    for k8 in range(3):
        base = 18 + 18 * k8
        cc, sc, cs, ss = [load(base)], [load(base + 1)], [None], [None]
        for k in range(1, 5):
            at = base + 4 * k - 2
            plus, minus, sine_plus, sine_minus = [load(at + i) for i in range(4)]
            cc.append(plus + minus)
            ss.append(minus - plus)
            sc.append(sine_plus + sine_minus)
            cs.append(sine_plus - sine_minus)
        for b, value in enumerate(dft9_adjoint(cc, cs)):
            save(2 + 2 * k8, b, value)
        for b, value in enumerate(dft9_adjoint(sc, ss)):
            save(3 + 2 * k8, b, value)


def point72(a, b):
    return (9 * a + 8 * b) % NG


def split(table):
    high = table.astype(ml_dtypes.bfloat16).astype(np.float64)
    return high, (table - high).astype(ml_dtypes.bfloat16).astype(np.float64)


def from_left(table):
    high, low = split(table)
    wide = np.zeros((80, 256))
    wide[:NG, : 3 * NG] = np.concatenate([high, high, low], axis=1)
    return wide


def from_right(table):
    high, low = split(table)
    return np.block([[high, low], [high, np.zeros_like(low)]])


@functools.cache
def tables():
    at = np.arange(NG)
    basis, freq = [np.full(NG, 1.0)], [0]
    for k in range(1, NG // 2):
        basis += [np.cos(2 * np.pi * k * at / NG), np.sin(2 * np.pi * k * at / NG)]
        freq += [k, k]
    basis.append(np.cos(np.pi * at))
    freq.append(NG // 2)
    basis = np.array(basis)
    basis /= np.sqrt((basis * basis).sum(1, keepdims=True))
    freq = np.array(freq, np.float64)
    eye = np.eye(NG)
    parts = [dft8([eye[point72(a, b)] for a in range(8)]) for b in range(9)]
    slots = [None] * NG
    finish72(lambda part, b: parts[b][part], slots.__setitem__)
    slots = np.array(slots)
    norm = (slots * slots).sum(1)
    spectrum = np.abs(np.fft.fft(slots, axis=1))[:, : NG // 2 + 1]
    freq_y = spectrum.argmax(1).astype(np.float64)
    along_z = np.zeros((128, 128))
    along_z[:NG, :NG] = basis.T
    along_x = basis.reshape(NG, PEERS, PLANES)
    along_x = np.concatenate([along_x[:, :, :8].reshape(NG, -1), along_x[:, :, 8]], axis=1)
    column = np.zeros((8, WIDTH), np.float32)
    column[0, :MERGED] = (freq_y[:, None] ** 2 + freq[None, :] ** 2).reshape(-1)
    column[1, :MERGED] = np.repeat(1.0 / norm, NG)
    freq_x = np.broadcast_to((freq**2)[:, None], (NG, 128)).astype(np.float32)
    wide = np.concatenate(
        [from_right(along_z), from_right(along_z.T), from_left(along_x), from_left(along_x.T)]
    )
    return wide.astype(ml_dtypes.bfloat16), column, freq_x


def take(load, start):
    tile, lane = divmod(start, 128)
    value = load(tile)
    if lane == 0:
        return value
    if lane + NG > 128:
        at = lax.broadcasted_iota(jnp.int32, value.shape, 1)
        value = jnp.where(at >= lane, value, load(tile + 1))
    return pltpu.roll(value, 128 - lane, 1)


def put(store, start, value):
    tile, lane = divmod(start, 128)
    if lane:
        value = pltpu.roll(value, lane, 1)
    end = min(lane + NG, 128)
    store(tile, slice(lane, end), value[:, lane:end])
    if lane + NG > 128:
        store(tile + 1, slice(0, lane + NG - 128), value[:, : lane + NG - 128])


def matmul(a, b):
    return jnp.dot(a, b, preferred_element_type=jnp.float32)


def halves(x):
    high = x.astype(jnp.bfloat16)
    return high, (x - high.astype(jnp.float32)).astype(jnp.bfloat16)


def left(table, x):
    high, low = [part.astype(jnp.float32) for part in halves(x)]
    zeros = jnp.zeros((8, x.shape[1]), jnp.float32)
    operand = jnp.concatenate([high, low, high, zeros], axis=0).astype(jnp.bfloat16)
    return matmul(table[:, 0 : operand.shape[0]], operand)[0:NG]


def kernel(
    bands,
    mask_ref,
    bands_hbm,
    wide_hbm,
    column_hbm,
    freq_hbm,
    out_ref,
    bands_ref,
    wide,
    column_ref,
    freq_ref,
    mixed,
    own,
    own_fold,
    visit,
    visit_fold,
    rho,
    work,
    work2,
    wave,
    wave_last,
    wave_tail,
    wave_piece,
    recv,
    recv_tail,
    back,
    back_tail,
    field,
    field_tail,
    field_piece,
    relay,
    kernel_table,
    kernel_tail,
    total,
    total_fold,
    give,
    give_fold,
    given,
    given_fold,
    visit_send,
    visit_recv,
    give_send,
    give_recv,
    wave_send,
    wave_recv,
    tail_send,
    tail_recv,
    back_send,
    back_recv,
    back_tail_send,
    back_tail_recv,
    copy_sem,
    hop_send,
    hop_recv,
    forward_send,
    load_sem,
):
    me = lax.axis_index("pencil")
    group = lax.axis_index("band")
    me_x, me_y = lax.div(me, 4), lax.rem(me, 4)

    loads = [
        pltpu.make_async_copy(src, dst, load_sem.at[i])
        for i, (src, dst) in enumerate(
            [
                (bands_hbm, bands_ref),
                (wide_hbm, wide),
                (column_hbm, column_ref),
                (freq_hbm, freq_ref),
            ]
        )
    ]
    for load in loads:
        load.start()

    def peer(j):
        return lax.rem(me + j, PEERS)

    def at(dx, dy):
        return lax.rem(me_x + dx, 2) * 4 + lax.rem(me_y + dy + 4, 4)

    def group_at(j):
        return lax.rem(group + j + bands, bands)

    barrier = pltpu.get_barrier_semaphore()
    for j in range(1, PEERS):
        pl.semaphore_signal(barrier, inc=1, device_id={"pencil": peer(j)}, device_id_type=MESH)
    for j in (-2, -1, 1, 2):
        pl.semaphore_signal(barrier, inc=1, device_id={"band": group_at(j)}, device_id_type=MESH)
    loads[0].wait()
    for tile in range(TILES):
        lanes = slice(tile * 128, min(tile * 128 + 128, MERGED))
        live = slice(0, lanes.stop - lanes.start)
        if tile == TAIL_TILE:
            mixed[tile] = jnp.zeros((16, 128), jnp.float32)
            own_fold[tile % FOLD, 6:8, :] = jnp.zeros((2, 128), jnp.float32)
        for plane in range(PLANES - 1):
            mixed[tile, 2 * plane : 2 * plane + 2, live] = bands_ref[plane, :, lanes]
        for band in range(2):
            own[tile, band * 8 : band * 8 + 8, :] = mixed[tile, pl.ds(band, 8, stride=2), :]
        row = tile // FOLD * 2
        own_fold[tile % FOLD, row : row + 2, live] = bands_ref[PLANES - 1, :, lanes]

    def own_mask(s, f):
        return mask_ref[0, s, f // 2, f % 2].astype(jnp.float32)

    for m in range(2 * FIELDS):
        value = own_mask(m // FIELDS, m % FIELDS)
        own_fold[MASKS, m : m + 1, :] = jnp.zeros((1, 128), jnp.float32) + value
    pl.semaphore_wait(barrier, PEERS - 1 + 4)

    def remote(src, dst, send, recv, **device):
        return pltpu.make_async_remote_copy(
            src_ref=src,
            dst_ref=dst,
            send_sem=send,
            recv_sem=recv,
            device_id=device,
            device_id_type=MESH,
        )

    odd = lax.rem(group, 2)
    even = odd == 0
    visitor_group = (
        jnp.where(even, group_at(2), group_at(1)),
        jnp.where(even, group_at(1), group_at(-2)),
    )

    def parts(main, fold):
        return [
            *(main.at[pl.ds(begin, end - begin)] for begin, end in QUARTERS),
            fold,
        ]

    def block_copies(src, dst, send, recv, to):
        return [
            remote(one, two, send.at[q], recv.at[q], band=to)
            for q, (one, two) in enumerate(zip(parts(*src), parts(*dst)))
        ]

    def visit_at(s):
        return visit.at[s], visit_fold.at[s]

    def visit_copies(s, src, send, to):
        return block_copies(src, visit_at(s), send, visit_recv.at[s], to)

    def lower_sends():
        return visit_copies(0, (own, own_fold), visit_send.at[0], group_at(-2))

    def lower_relays():
        return visit_copies(0, visit_at(0), visit_send.at[1], group_at(1))

    def upper_sends():
        return visit_copies(1, (own, own_fold), visit_send.at[0], group_at(2)) + visit_copies(
            1, (own, own_fold), visit_send.at[1], group_at(-1)
        )

    @pl.when(even)
    def _():
        for copy in lower_sends():
            copy.start()

    @pl.when(jnp.logical_not(even))
    def _():
        for copy in upper_sends():
            copy.start()

    def kernel_columns(start, width):
        squared = column_ref[0:1, pl.ds(start, width)]
        scale = column_ref[1:2, pl.ds(start, width)]
        return coulomb_scale / (freq_ref[:, 0:1] + squared + screening) * scale

    for load in loads[1:]:
        load.wait()
    kernel_table[...] = kernel_columns(pl.multiple_of(me * OWN, 128), OWN)
    kernel_tail[...] = kernel_columns(TAIL, 128)
    wave_tail[...] = jnp.zeros((2, ROWS, 128), jnp.float32)
    for s in range(2):
        for p in range(PEERS):
            back[s, (p + 1) * BLOCK - 8 : (p + 1) * BLOCK, :] = jnp.zeros((8, 128), jnp.float32)
            back_tail[s, (p + 1) * PIECE - 8 : (p + 1) * PIECE, :] = jnp.zeros((8, 128), jnp.float32)
        field_tail[s, 32:40, :] = jnp.zeros((8, 128), jnp.float32)
        for f in range(FIELDS):
            wave_piece[s, f, 8:16, :] = jnp.zeros((8, 128), jnp.float32)

    first_band = [slice(band * 8, band * 8 + 8) for band in range(2)]
    field_rows = [slice(f * 8, f * 8 + 8) for f in range(FIELDS)]
    row_at = lax.broadcasted_iota(jnp.int32, (8, 128), 0)
    resident_one = lax.rem(lax.div(row_at, 2), 2) == 1
    visitor_one = lax.rem(row_at, 2) == 1

    def last_planes(s, j, q):
        a = [own_fold[j, 2 * q + band : 2 * q + band + 1, :] for band in range(2)]
        c = [visit_fold[s, j, 2 * q + band : 2 * q + band + 1, :] for band in range(2)]
        wide_a = [jnp.broadcast_to(row, (8, 128)) for row in a]
        wide_c = [jnp.broadcast_to(row, (8, 128)) for row in c]
        return (
            jnp.where(resident_one, wide_a[1], wide_a[0]),
            jnp.where(visitor_one, wide_c[1], wide_c[0]),
        )

    def along_z(start):
        table = wide[start : start + 256, :]

        def step(i, carry):
            rows = pl.ds(pl.multiple_of(i * 720, 720), 720)
            both = matmul(jnp.concatenate(halves(work[rows, :]), axis=1), table)
            work2[rows, :] = both[:, :128] + both[:, 128:]
            return carry

        lax.fori_loop(0, NG * ROWS // 720, step, 0)

    def place(part, b, t):
        return pl.ds(pl.multiple_of((part * 9 + b) * ROWS + t * 8, 8), 8)

    def first(s, between):
        arriving = visit_copies(s, (own, own_fold), visit_send.at[0], group_at(1))
        arriving[4].wait_recv()
        relays = lower_relays()
        if s == 0:

            @pl.when(even)
            def _():
                relays[4].start()

        for q, (begin, end) in enumerate(QUARTERS):
            arriving[q].wait_recv()
            if s == 0:

                @pl.when(even)
                def _(q=q):
                    relays[q].start()

            def products(j, carry, q=q, begin=begin):
                tile = begin + j
                phi = [own[tile, rows, :] for rows in first_band]
                chi = [visit[s, tile, rows, :] for rows in first_band]
                for f in range(FIELDS):
                    rho[tile, field_rows[f], :] = phi[f // 2] * chi[f % 2]
                phi, chi = last_planes(s, j, q)
                rho[tile, 32:40, :] = phi * chi
                return carry

            lax.fori_loop(0, end - begin, products, 0, unroll=True)
        for b in range(9):
            starts = [point72(a, b) * NG for a in range(8)]
            parts = dft8([take(lambda i: rho[i], at) for at in starts])
            for part in range(8):
                base = (part * 9 + b) * ROWS
                work[base : base + ROWS, :] = parts[part]
        along_z(0)
        between()

        def finish(t, target):
            def load(part, b):
                return work2[place(part, b, t), :]

            def save(slot, value):
                put(target, slot * NG, value)

            finish72(load, save)

        def planes(t, carry):
            def target(tile, lanes, piece):
                if tile == TAIL_TILE:
                    wave_tail[s, pl.ds(pl.multiple_of(t * 8, 8), 8), lanes] = piece
                else:
                    start = tile // OWN_TILES * BLOCK + tile % OWN_TILES * 32
                    wave[s, pl.ds(pl.multiple_of(start + t * 8, 8), 8), lanes] = piece

            finish(t, target)
            return carry

        lax.fori_loop(0, 4, planes, 0)

        def last(tile, lanes, piece):
            if tile == TAIL_TILE:
                wave_tail[s, 32:40, lanes] = piece
            else:
                wave_last[tile * 8 : tile * 8 + 8, lanes] = piece

        finish(4, last)
        for f in range(FIELDS):
            wave_piece[s, f, 0:8, :] = wave_tail[s, field_rows[f], :]
            wave_piece[s, f, 8:9, :] = wave_tail[s, 32 + f : 33 + f, :]
        upper = lax.broadcasted_iota(jnp.int32, (8, 128), 0) < FIELDS
        for q in range(PEERS):
            for i in range(3):
                tile = (q * OWN_TILES + i) * 8
                piece = wave_last[tile : tile + 8, :]
                if i < 2:
                    piece = jnp.where(upper, piece, wave_last[tile + 24 : tile + 32, :])
                start = q * BLOCK + LAST + i * 8
                wave[s, start : start + 8, :] = piece

    def block_of(ref, s, index):
        return ref.at[s, pl.ds(pl.multiple_of(index * BLOCK, 8), BLOCK), :]

    def tail_of(ref, s, index):
        return ref.at[s, pl.ds(pl.multiple_of(index * ROWS, 8), ROWS), :]

    way = jnp.where(even, 1, -1)
    exchange_refs = ((wave, recv, wave_send, wave_recv), (back, field, back_send, back_recv))

    def hop(phase, s, dx):
        return remote(
            block_of(exchange_refs[phase][0], s, at(dx, 2)),
            relay.at[phase, s, dx],
            hop_send.at[phase, s, dx],
            hop_recv.at[phase, s, dx],
            pencil=at(dx, way),
        )

    def forward(phase, s, dx):
        return remote(
            relay.at[phase, s, dx],
            block_of(exchange_refs[phase][1], s, at(dx, -way)),
            forward_send.at[phase, s, dx],
            exchange_refs[phase][3].at[s, dx * 4 + 2],
            pencil=at(0, way),
        )

    def direct(phase, s, dx, dy):
        src, dst, send, recv_sem = exchange_refs[phase]
        return remote(
            block_of(src, s, at(dx, dy)),
            block_of(dst, s, me),
            send.at[s, dx * 4 + dy],
            recv_sem.at[s, dx * 4 + dy],
            pencil=at(dx, dy),
        )

    straight = [(1, 1), (1, 3), (0, 1), (0, 3), (1, 0)]

    def keep(phase, s):
        src, dst = exchange_refs[phase][:2]
        return pltpu.make_async_copy(
            block_of(src, s, me), block_of(dst, s, me), copy_sem.at[phase, s]
        )

    def send_blocks(phase, s):
        for dx in range(2):
            hop(phase, s, dx).start()
        for dx, dy in straight:
            direct(phase, s, dx, dy).start()
        keep(phase, s).start()

    def forward_blocks(phase, s):
        for dx in range(2):
            hop(phase, s, dx).wait_recv()
            forward(phase, s, dx).start()

    def wait_blocks(phase, s):
        keep(phase, s).wait()
        for dx, dy in straight:
            direct(phase, s, dx, dy).wait_recv()
        for dx in range(2):
            forward(phase, s, dx).wait_recv()

    def end_blocks(phase, s):
        for dx, dy in straight:
            direct(phase, s, dx, dy).wait_send()
        for dx in range(2):
            hop(phase, s, dx).wait_send()
            forward(phase, s, dx).wait_send()

    def piece_of(ref, s, index):
        return ref.at[s, pl.ds(pl.multiple_of(index * PIECE, 8), PIECE), :]

    def owner_of(s, f):
        return FIELDS * s + f

    def tail_copy(s, f, distance):
        return remote(
            wave_piece.at[s, f],
            piece_of(recv_tail, s, me),
            tail_send.at[s, f],
            tail_recv.at[s, distance],
            pencil=jnp.int32(owner_of(s, f)),
        )

    def lines(f, tile, block, last):
        first_rows = [pl.ds(p * block + tile * 32 + f * 8, 8) for p in range(PEERS)]
        below = FIELDS * (tile // 3)
        return first_rows + [pl.ds(last + tile % 3 * 8 + below + f, PEERS, stride=block)]

    def spectrum_step(source, target, s, tiles, table, block, last, fields):
        columns = slice(tiles[0] * 128, (tiles[-1] + 1) * 128)
        for f in fields:
            rows = [lines(f, tile, block, last) for tile in tiles]
            loaded = [
                jnp.concatenate([source[s, part, :] for part in parts], axis=0) for parts in rows
            ]
            spectrum = left(wide[512:592, :], jnp.concatenate(loaded, axis=1))
            result = left(wide[592:672, :], spectrum * table[:, columns])
            for i, parts in enumerate(rows):
                for j, part in enumerate(parts):
                    target[s, part, :] = result[j * 8 : j * 8 + 8, i * 128 : (i + 1) * 128]

    def second(s, between):
        for half in range(2):
            fields = range(2 * half, 2 * half + 2)
            spectrum_step(recv, back, s, range(OWN_TILES), kernel_table, BLOCK, LAST, fields)
            if half == 0:
                between()

    def give_copies(s):
        return block_copies(
            (give.at[s], give_fold.at[s]),
            (given.at[odd], given_fold.at[odd]),
            give_send.at[s],
            give_recv.at[odd],
            visitor_group[s],
        )

    def given_copies(source):
        return block_copies(
            (give.at[0], give_fold.at[0]),
            (given.at[source], given_fold.at[source]),
            give_send.at[0],
            give_recv.at[source],
            visitor_group[0],
        )

    def third(s, between):
        def start(t, source):
            def load(slot):
                return take(source, slot * NG)

            def save(part, b, value):
                work[place(part, b, t), :] = value

            finish72_adjoint(load, save)

        def planes(t, carry):
            def source(tile):
                if tile == TAIL_TILE:
                    return field_tail[s, pl.ds(pl.multiple_of(t * 8, 8), 8), :]
                first_row = tile // OWN_TILES * BLOCK + tile % OWN_TILES * 32
                return field[s, pl.ds(pl.multiple_of(first_row + t * 8, 8), 8), :]

            start(t, source)
            return carry

        lax.fori_loop(0, 4, planes, 0)

        def last(tile):
            if tile == TAIL_TILE:
                return field_tail[s, 32:40, :]
            which = tile % OWN_TILES
            first_row = tile // OWN_TILES * BLOCK + LAST + which % 3 * 8
            value = field[s, first_row : first_row + 8, :]
            return pltpu.roll(value, FIELDS, 0) if which > 2 else value

        start(4, last)
        along_z(256)
        between()
        for b in range(9):
            parts = []
            for part in range(8):
                base = (part * 9 + b) * ROWS
                parts.append(work2[base : base + ROWS, :])
            for a, value in enumerate(dft8_adjoint(parts)):


                def store(tile, lanes, piece):
                    rho[tile, :, lanes] = piece

                put(store, point72(a, b) * NG, value)
        weights = []
        for f in range(FIELDS):
            g = 2 * (f % 2) + f // 2
            if s == 0:
                row = jnp.where(
                    even,
                    visit_fold[s, MASKS, FIELDS + g : FIELDS + g + 1, :],
                    visit_fold[s, MASKS, g : g + 1, :],
                )
            else:
                row = jnp.where(
                    even,
                    visit_fold[s, MASKS, g : g + 1, :],
                    own_fold[MASKS, FIELDS + f : FIELDS + f + 1, :],
                )
            weights.append(jnp.broadcast_to(row, (8, 128)))
        last_weight = weights[3]
        for f in range(3):
            last_weight = jnp.where(row_at == f, weights[f], last_weight)

        leaving = give_copies(s)
        for q, (begin, end) in enumerate(QUARTERS):

            def gather(j, carry, q=q, begin=begin):
                tile = begin + j
                phi = [own[tile, rows, :] for rows in first_band]
                chi = [visit[s, tile, rows, :] for rows in first_band]
                value = [rho[tile, field_rows[f], :] * weights[f] for f in range(FIELDS)]
                for a in range(2):
                    stay = value[2 * a] * chi[0] + value[2 * a + 1] * chi[1]
                    if s > 0:
                        stay = stay + total[tile, first_band[a], :]
                    total[tile, first_band[a], :] = stay
                for c in range(2):
                    give[s, tile, first_band[c], :] = value[c] * phi[0] + value[2 + c] * phi[1]
                phi, chi = last_planes(s, j, q)
                value = rho[tile, 32:40, :] * last_weight
                stay, leave = value * chi, value * phi
                stay = stay + pltpu.roll(stay, 7, 0)
                leave = leave + pltpu.roll(leave, 6, 0)
                for band in range(2):
                    row = slice(2 * q + band, 2 * q + band + 1)
                    kept = stay[2 * band : 2 * band + 1]
                    if s > 0:
                        kept = kept + total_fold[j, row, :]
                    total_fold[j, row, :] = kept
                    give_fold[s, j, row, :] = leave[band : band + 1]
                return carry

            lax.fori_loop(0, end - begin, gather, 0, unroll=True)
            leaving[q].start()
        leaving[4].start()

    def tail_back(s, f, j):
        return remote(
            piece_of(back_tail, s, peer(j)),
            field_piece.at[s, f],
            back_tail_send.at[s, j],
            back_tail_recv.at[s, f],
            pencil=peer(j),
        )

    def send_tail(s):
        for f in range(FIELDS):
            owner = owner_of(s, f)

            @pl.when(me == owner)
            def _(f=f, owner=owner):
                recv_tail[s, owner * PIECE : (owner + 1) * PIECE, :] = wave_piece[s, f]

            @pl.when(me != owner)
            def _(f=f, owner=owner):
                tail_copy(s, f, lax.rem(owner - me + PEERS, PEERS)).start()

    def turn_tail(s):
        owned = lax.div(me, FIELDS) == s

        @pl.when(owned)
        def _():
            for j in range(1, PEERS):
                tail_copy(s, 0, j).wait_recv()
            parts = [pl.ds(p * PIECE, 8) for p in range(PEERS)] + [pl.ds(8, PEERS, stride=PIECE)]
            block = jnp.concatenate([recv_tail[s, part, :] for part in parts], axis=0)
            spectrum = left(wide[512:592, :], block) * kernel_tail[...]
            result = left(wide[592:672, :], spectrum)
            for i, part in enumerate(parts):
                back_tail[s, part, :] = result[i * 8 : i * 8 + 8, :]
            mine = lax.rem(me, FIELDS)
            for j in range(1, PEERS):
                tail_back(s, mine, j).start()
            field_piece[s, mine] = back_tail[s, pl.ds(pl.multiple_of(me * PIECE, 8), PIECE), :]

    def end_tail(s):
        for f in range(FIELDS):
            owner = owner_of(s, f)

            @pl.when(me != owner)
            def _(f=f, owner=owner):
                tail_copy(s, f, lax.rem(owner - me + PEERS, PEERS)).wait_send()
                tail_back(s, f, 1).wait_recv()

            field_tail[s, field_rows[f], :] = field_piece[s, f, 0:8, :]
            field_tail[s, 32 + f : 33 + f, :] = field_piece[s, f, 8:9, :]

        @pl.when(lax.div(me, FIELDS) == s)
        def _():
            for j in range(1, PEERS):
                tail_back(s, lax.rem(me, FIELDS), j).wait_send()

    def nothing():
        pass

    def forwards(*which):
        def run():
            for phase, s in which:
                forward_blocks(phase, s)

        return run

    first(0, nothing)
    send_blocks(0, 0)
    send_tail(0)
    first(1, forwards((0, 0)))
    send_blocks(0, 1)
    send_tail(1)
    wait_blocks(0, 0)
    second(0, forwards((0, 1)))
    send_blocks(1, 0)
    turn_tail(0)
    wait_blocks(0, 1)
    second(1, forwards((1, 0)))
    send_blocks(1, 1)
    turn_tail(1)
    wait_blocks(1, 0)
    end_tail(0)
    third(0, forwards((1, 1)))
    wait_blocks(1, 1)
    end_tail(1)
    third(1, nothing)
    for q, (begin, end) in enumerate(QUARTERS):
        for source in range(2):
            given_copies(source)[q].wait_recv()
        for tile in range(begin, end):
            lanes = slice(tile * 128, min(tile * 128 + 128, MERGED))
            for rows, band in zip(first_band, range(2)):
                term = -(total[tile, rows, :] + given[0, tile, rows, :] + given[1, tile, rows, :])
                mixed[tile, pl.ds(band, 8, stride=2), :] = term
            for plane in range(PLANES - 1):
                piece = mixed[tile, 2 * plane : 2 * plane + 2, 0 : lanes.stop - lanes.start]
                out_ref[plane, :, lanes] = piece
    for source in range(2):
        given_copies(source)[4].wait_recv()
    for q, (begin, end) in enumerate(QUARTERS):
        for tile in range(begin, end):
            lanes = slice(tile * 128, min(tile * 128 + 128, MERGED))
            j, rows = tile - begin, slice(2 * q, 2 * q + 2)
            term = total_fold[j, rows, :] + given_fold[0, j, rows, :] + given_fold[1, j, rows, :]
            out_ref[PLANES - 1, :, lanes] = -term[:, 0 : lanes.stop - lanes.start]

    @pl.when(even)
    def _():
        for copy in lower_sends() + lower_relays():
            copy.wait_send()

    @pl.when(jnp.logical_not(even))
    def _():
        for copy in upper_sends():
            copy.wait_send()

    for s in range(2):
        for copy in give_copies(s):
            copy.wait_send()
    for phase in range(2):
        for s in range(2):
            end_blocks(phase, s)


def body(bands, orbitals, pair_mask):
    hbm = pl.BlockSpec(memory_space=pltpu.HBM)
    smem = pl.BlockSpec(memory_space=pltpu.SMEM)
    consts = [jnp.asarray(table) for table in tables()]
    dma = pltpu.SemaphoreType.DMA

    def buffer(*shape):
        return pltpu.VMEM(shape, jnp.float32)

    out = pl.pallas_call(
        functools.partial(kernel, bands),
        out_shape=jax.ShapeDtypeStruct((PLANES, 2, MERGED), jnp.float32),
        in_specs=[smem] + [hbm] * (1 + len(consts)),
        out_specs=pl.BlockSpec(memory_space=pltpu.VMEM),
        scratch_shapes=[
            buffer(PLANES, 2, MERGED),
            pltpu.VMEM(consts[0].shape, jnp.bfloat16),
            buffer(*consts[1].shape),
            buffer(*consts[2].shape),
            buffer(TILES, 16, 128),
            buffer(TILES, 16, 128),
            buffer(FOLD + 1, 8, 128),
            buffer(2, TILES, 16, 128),
            buffer(2, FOLD + 1, 8, 128),
            buffer(TILES, ROWS, 128),
            buffer(NG * ROWS, 128),
            buffer(NG * ROWS, 128),
            buffer(2, PEERS * BLOCK, 128),
            buffer(TAIL_TILE * 8, 128),
            buffer(2, ROWS, 128),
            buffer(2, FIELDS, PIECE, 128),
            buffer(2, PEERS * BLOCK, 128),
            buffer(2, PEERS * PIECE, 128),
            buffer(2, PEERS * BLOCK, 128),
            buffer(2, PEERS * PIECE, 128),
            buffer(2, PEERS * BLOCK, 128),
            buffer(2, ROWS, 128),
            buffer(2, FIELDS, PIECE, 128),
            buffer(2, 2, 2, BLOCK, 128),
            buffer(NG, OWN),
            buffer(NG, 128),
            buffer(TILES, 16, 128),
            buffer(FOLD + 1, 8, 128),
            buffer(2, TILES, 16, 128),
            buffer(2, FOLD + 1, 8, 128),
            buffer(2, TILES, 16, 128),
            buffer(2, FOLD + 1, 8, 128),
            dma((2, 5)),
            dma((2, 5)),
            dma((2, 5)),
            dma((2, 5)),
            dma((2, PEERS)),
            dma((2, PEERS)),
            dma((2, FIELDS)),
            dma((2, PEERS)),
            dma((2, PEERS)),
            dma((2, PEERS)),
            dma((2, PEERS)),
            dma((2, FIELDS)),
            dma((2, 2)),
            dma((2, 2, 2)),
            dma((2, 2, 2)),
            dma((2, 2, 2)),
            dma((4,)),
        ],
        compiler_params=pltpu.CompilerParams(
            collective_id=0, has_side_effects=True, vmem_limit_bytes=64 * 1024 * 1024 - 65536
        ),
    )(pair_mask, orbitals.transpose(1, 0, 2), *consts)
    return out.transpose(1, 0, 2)


def solution(mesh):
    return jax.shard_map(
        functools.partial(body, mesh.shape["band"]),
        mesh=mesh,
        in_specs=(P("band", "pencil", None), P("band", None, None, None)),
        out_specs=P("band", "pencil", None),
        check_vma=False,
    )
```

```python
import functools
import math

import jax
import jax.numpy as jnp
import ml_dtypes
import numpy as np
from jax import lax
from jax.experimental import pallas as pl
from jax.experimental.pallas import tpu as pltpu
from jax.sharding import PartitionSpec as P

MESH = pl.DeviceIdType.MESH
NG = 72
PLANES = 9
PEERS = 8
FIELDS = 4
ROWS = 40
PART = 40
LAST = 24
MERGED = NG * NG
WIDTH = 5248
OWN = 640
TAIL = PEERS * OWN
PIECE = 16
FOLD = 11
MASKS = FOLD
QUARTERS = [(q * FOLD, min((q + 1) * FOLD, 41)) for q in range(4)]
TILES = WIDTH // 128
OWN_TILES = OWN // 128
TAIL_TILE = TILES - 1
coulomb_scale = 20.0
screening = 0.25
HALF = math.sqrt(0.5)


def dft8(x):
    a = [x[j] + x[j + 4] for j in range(4)]
    b = [x[j] - x[j + 4] for j in range(4)]
    e, o = a[0] + a[2], a[1] + a[3]
    u, v = HALF * (b[1] - b[3]), HALF * (b[1] + b[3])
    return [e + o, e - o, b[0] + u, v + b[2], a[0] - a[2], a[1] - a[3], b[0] - u, v - b[2]]


def dft8_adjoint(c):
    p, q = c[0] + c[1], c[0] - c[1]
    a = [p + c[4], q + c[5], p - c[4], q - c[5]]
    d, s = HALF * (c[2] - c[6]), HALF * (c[3] + c[7])
    b = [c[2] + c[6], d + s, c[3] - c[7], s - d]
    return [a[j] + b[j] for j in range(4)] + [a[j] - b[j] for j in range(4)]


def cos9(n):
    return math.cos(2.0 * math.pi * (n % 9) / 9)


def sin9(n):
    return math.sin(2.0 * math.pi * (n % 9) / 9)


def weighted(values, factors):
    total = values[0] * factors[0]
    for value, factor in zip(values[1:], factors[1:]):
        total = total + value * factor
    return total


def dft9(x):
    e = [x[n] + x[9 - n] for n in range(1, 5)]
    o = [x[n] - x[9 - n] for n in range(1, 5)]
    third = e[0] + e[1] + e[3]
    cosines = [x[0] + third + e[2]]
    sines = [None]
    for k in range(1, 5):
        if k == 3:
            cosines.append(x[0] + e[2] - 0.5 * third)
            sines.append(sin9(3) * (o[0] - o[1] + o[3]))
        else:
            cosines.append(x[0] + weighted(e, [cos9(k * n) for n in range(1, 5)]))
            sines.append(weighted(o, [sin9(k * n) for n in range(1, 5)]))
    return cosines, sines


def dft9_adjoint(cosines, sines):
    c, s = cosines, sines
    out = [None] * 9
    out[0] = c[0] + ((c[1] + c[2]) + (c[3] + c[4]))
    for n in range(1, 5):
        if n == 3:
            even = c[0] + c[3] - 0.5 * (c[1] + c[2] + c[4])
            odd = sin9(3) * (s[1] - s[2] + s[4])
        else:
            even = c[0] + weighted(c[1:], [cos9(k * n) for k in range(1, 5)])
            odd = weighted(s[1:], [sin9(k * n) for k in range(1, 5)])
        out[n] = even + odd
        out[9 - n] = even - odd
    return out


def finish72(load, save):
    for part in (0, 1):
        cosines, sines = dft9([load(part, b) for b in range(9)])
        base = part * 9
        save(base, cosines[0])
        for k in range(1, 5):
            save(base + 2 * k - 1, cosines[k])
            save(base + 2 * k, sines[k])
    for k8 in range(3):
        base = 18 + 18 * k8
        cc, cs = dft9([load(2 + 2 * k8, b) for b in range(9)])
        sc, ss = dft9([load(3 + 2 * k8, b) for b in range(9)])
        save(base, cc[0])
        save(base + 1, sc[0])
        for k in range(1, 5):
            at = base + 4 * k - 2
            save(at, cc[k] - ss[k])
            save(at + 1, cc[k] + ss[k])
            save(at + 2, sc[k] + cs[k])
            save(at + 3, sc[k] - cs[k])


def finish72_adjoint(load, save):
    for part in (0, 1):
        base = part * 9
        cosines = [load(base)] + [load(base + 2 * k - 1) for k in range(1, 5)]
        sines = [None] + [load(base + 2 * k) for k in range(1, 5)]
        for b, value in enumerate(dft9_adjoint(cosines, sines)):
            save(part, b, value)
    for k8 in range(3):
        base = 18 + 18 * k8
        cc, sc, cs, ss = [load(base)], [load(base + 1)], [None], [None]
        for k in range(1, 5):
            at = base + 4 * k - 2
            plus, minus, sine_plus, sine_minus = [load(at + i) for i in range(4)]
            cc.append(plus + minus)
            ss.append(minus - plus)
            sc.append(sine_plus + sine_minus)
            cs.append(sine_plus - sine_minus)
        for b, value in enumerate(dft9_adjoint(cc, cs)):
            save(2 + 2 * k8, b, value)
        for b, value in enumerate(dft9_adjoint(sc, ss)):
            save(3 + 2 * k8, b, value)


def point72(a, b):
    return (9 * a + 8 * b) % NG


def split(table):
    high = table.astype(ml_dtypes.bfloat16).astype(np.float64)
    return high, (table - high).astype(ml_dtypes.bfloat16).astype(np.float64)


def from_left(table):
    high, low = split(table)
    wide = np.zeros((80, 256))
    wide[:NG, : 3 * NG] = np.concatenate([high, high, low], axis=1)
    return wide


def from_right(table):
    high, low = split(table)
    return np.block([[high, low], [high, np.zeros_like(low)]])


@functools.cache
def tables():
    at = np.arange(NG)
    basis, freq = [np.full(NG, 1.0)], [0]
    for k in range(1, NG // 2):
        basis += [np.cos(2 * np.pi * k * at / NG), np.sin(2 * np.pi * k * at / NG)]
        freq += [k, k]
    basis.append(np.cos(np.pi * at))
    freq.append(NG // 2)
    basis = np.array(basis)
    basis /= np.sqrt((basis * basis).sum(1, keepdims=True))
    freq = np.array(freq, np.float64)
    eye = np.eye(NG)
    parts = [dft8([eye[point72(a, b)] for a in range(8)]) for b in range(9)]
    slots = [None] * NG
    finish72(lambda part, b: parts[b][part], slots.__setitem__)
    slots = np.array(slots)
    norm = (slots * slots).sum(1)
    spectrum = np.abs(np.fft.fft(slots, axis=1))[:, : NG // 2 + 1]
    freq_y = spectrum.argmax(1).astype(np.float64)
    along_z = np.zeros((128, 128))
    along_z[:NG, :NG] = basis.T
    along_x = basis.reshape(NG, PEERS, PLANES)
    along_x = np.concatenate([along_x[:, :, :8].reshape(NG, -1), along_x[:, :, 8]], axis=1)
    column = np.zeros((8, WIDTH), np.float32)
    column[0, :MERGED] = (freq_y[:, None] ** 2 + freq[None, :] ** 2).reshape(-1)
    column[1, :MERGED] = np.repeat(1.0 / norm, NG)
    freq_x = np.broadcast_to((freq**2)[:, None], (NG, 128)).astype(np.float32)
    wide = np.concatenate(
        [from_right(along_z), from_right(along_z.T), from_left(along_x), from_left(along_x.T)]
    )
    return wide.astype(ml_dtypes.bfloat16), column, freq_x


def take(load, start):
    tile, lane = divmod(start, 128)
    value = load(tile)
    if lane == 0:
        return value
    if lane + NG > 128:
        at = lax.broadcasted_iota(jnp.int32, value.shape, 1)
        value = jnp.where(at >= lane, value, load(tile + 1))
    return pltpu.roll(value, 128 - lane, 1)


def put(store, start, value):
    tile, lane = divmod(start, 128)
    if lane:
        value = pltpu.roll(value, lane, 1)
    end = min(lane + NG, 128)
    store(tile, slice(lane, end), value[:, lane:end])
    if lane + NG > 128:
        store(tile + 1, slice(0, lane + NG - 128), value[:, : lane + NG - 128])


def matmul(a, b):
    return jnp.dot(a, b, preferred_element_type=jnp.float32)


def halves(x):
    high = x.astype(jnp.bfloat16)
    return high, (x - high.astype(jnp.float32)).astype(jnp.bfloat16)


def left(table, x):
    high, low = [part.astype(jnp.float32) for part in halves(x)]
    zeros = jnp.zeros((8, x.shape[1]), jnp.float32)
    operand = jnp.concatenate([high, low, high, zeros], axis=0).astype(jnp.bfloat16)
    return matmul(table[:, 0 : operand.shape[0]], operand)[0:NG]


def kernel(
    bands,
    mask_ref,
    bands_hbm,
    wide_hbm,
    column_hbm,
    freq_hbm,
    out_ref,
    bands_ref,
    wide,
    column_ref,
    freq_ref,
    mixed,
    own,
    own_fold,
    visit,
    visit_fold,
    rho,
    work,
    work2,
    wave,
    wave_fold,
    wave_last,
    wave_tail,
    wave_piece,
    recv,
    recv_fold,
    recv_tail,
    back,
    back_fold,
    back_tail,
    field,
    field_fold,
    field_tail,
    field_piece,
    kernel_table,
    kernel_tail,
    total,
    total_fold,
    give,
    give_fold,
    given,
    given_fold,
    visit_send,
    visit_recv,
    give_send,
    give_recv,
    part_send,
    part_recv,
    fold_send,
    fold_recv,
    tail_send,
    tail_recv,
    back_tail_send,
    back_tail_recv,
    load_sem,
):
    me = lax.axis_index("pencil")
    group = lax.axis_index("band")
    me_x, me_y = lax.div(me, 4), lax.rem(me, 4)

    loads = [
        pltpu.make_async_copy(src, dst, load_sem.at[i])
        for i, (src, dst) in enumerate(
            [
                (bands_hbm, bands_ref),
                (wide_hbm, wide),
                (column_hbm, column_ref),
                (freq_hbm, freq_ref),
            ]
        )
    ]
    for load in loads:
        load.start()

    def peer(j):
        return lax.rem(me + j, PEERS)

    def at(dx, dy):
        return lax.rem(me_x + dx, 2) * 4 + lax.rem(me_y + dy + 4, 4)

    def group_at(j):
        return lax.rem(group + j + bands, bands)

    barrier = pltpu.get_barrier_semaphore()
    for j in range(1, PEERS):
        pl.semaphore_signal(barrier, inc=1, device_id={"pencil": peer(j)}, device_id_type=MESH)
    for j in (-2, -1, 1, 2):
        pl.semaphore_signal(barrier, inc=1, device_id={"band": group_at(j)}, device_id_type=MESH)
    loads[0].wait()
    for tile in range(TILES):
        lanes = slice(tile * 128, min(tile * 128 + 128, MERGED))
        live = slice(0, lanes.stop - lanes.start)
        if tile == TAIL_TILE:
            mixed[tile] = jnp.zeros((16, 128), jnp.float32)
            own_fold[tile % FOLD, 6:8, :] = jnp.zeros((2, 128), jnp.float32)
        for plane in range(PLANES - 1):
            mixed[tile, 2 * plane : 2 * plane + 2, live] = bands_ref[plane, :, lanes]
        for band in range(2):
            own[tile, band * 8 : band * 8 + 8, :] = mixed[tile, pl.ds(band, 8, stride=2), :]
        row = tile // FOLD * 2
        own_fold[tile % FOLD, row : row + 2, live] = bands_ref[PLANES - 1, :, lanes]

    def own_mask(s, f):
        return mask_ref[0, s, f // 2, f % 2].astype(jnp.float32)

    for m in range(2 * FIELDS):
        value = own_mask(m // FIELDS, m % FIELDS)
        own_fold[MASKS, m : m + 1, :] = jnp.zeros((1, 128), jnp.float32) + value
    pl.semaphore_wait(barrier, PEERS - 1 + 4)

    def remote(src, dst, send, recv, **device):
        return pltpu.make_async_remote_copy(
            src_ref=src,
            dst_ref=dst,
            send_sem=send,
            recv_sem=recv,
            device_id=device,
            device_id_type=MESH,
        )

    odd = lax.rem(group, 2)
    even = odd == 0
    visitor_group = (
        jnp.where(even, group_at(2), group_at(1)),
        jnp.where(even, group_at(1), group_at(-2)),
    )

    def parts(main, fold):
        return [
            *(main.at[pl.ds(begin, end - begin)] for begin, end in QUARTERS),
            fold,
        ]

    def block_copies(src, dst, send, recv, to):
        return [
            remote(one, two, send.at[q], recv.at[q], band=to)
            for q, (one, two) in enumerate(zip(parts(*src), parts(*dst)))
        ]

    def visit_at(s):
        return visit.at[s], visit_fold.at[s]

    def visit_copies(s, src, send, to):
        return block_copies(src, visit_at(s), send, visit_recv.at[s], to)

    def lower_sends():
        return visit_copies(0, (own, own_fold), visit_send.at[0], group_at(-2))

    def lower_relays():
        return visit_copies(0, visit_at(0), visit_send.at[1], group_at(1))

    def upper_sends():
        return visit_copies(1, (own, own_fold), visit_send.at[0], group_at(2)) + visit_copies(
            1, (own, own_fold), visit_send.at[1], group_at(-1)
        )

    @pl.when(even)
    def _():
        for copy in lower_sends():
            copy.start()

    @pl.when(jnp.logical_not(even))
    def _():
        for copy in upper_sends():
            copy.start()

    def kernel_columns(start, width):
        squared = column_ref[0:1, pl.ds(start, width)]
        scale = column_ref[1:2, pl.ds(start, width)]
        return coulomb_scale / (freq_ref[:, 0:1] + squared + screening) * scale

    for load in loads[1:]:
        load.wait()
    kernel_table[...] = kernel_columns(pl.multiple_of(me * OWN, 128), OWN)
    kernel_tail[...] = kernel_columns(TAIL, 128)
    wave_tail[...] = jnp.zeros((2, ROWS, 128), jnp.float32)
    for s in range(2):
        for p in range(PEERS):
            back_fold[s, (p + 1) * LAST - 8 : (p + 1) * LAST, :] = jnp.zeros((8, 128), jnp.float32)
            back_tail[s, (p + 1) * PIECE - 8 : (p + 1) * PIECE, :] = jnp.zeros((8, 128), jnp.float32)
        field_tail[s, 32:40, :] = jnp.zeros((8, 128), jnp.float32)
        for f in range(FIELDS):
            wave_piece[s, f, 8:16, :] = jnp.zeros((8, 128), jnp.float32)

    first_band = [slice(band * 8, band * 8 + 8) for band in range(2)]
    field_rows = [slice(f * 8, f * 8 + 8) for f in range(FIELDS)]
    row_at = lax.broadcasted_iota(jnp.int32, (8, 128), 0)
    resident_one = lax.rem(lax.div(row_at, 2), 2) == 1
    visitor_one = lax.rem(row_at, 2) == 1

    def last_planes(s, j, q):
        a = [own_fold[j, 2 * q + band : 2 * q + band + 1, :] for band in range(2)]
        c = [visit_fold[s, j, 2 * q + band : 2 * q + band + 1, :] for band in range(2)]
        wide_a = [jnp.broadcast_to(row, (8, 128)) for row in a]
        wide_c = [jnp.broadcast_to(row, (8, 128)) for row in c]
        return (
            jnp.where(resident_one, wide_a[1], wide_a[0]),
            jnp.where(visitor_one, wide_c[1], wide_c[0]),
        )

    def along_z(start):
        table = wide[start : start + 256, :]

        def step(i, carry):
            rows = pl.ds(pl.multiple_of(i * 720, 720), 720)
            both = matmul(jnp.concatenate(halves(work[rows, :]), axis=1), table)
            work2[rows, :] = both[:, :128] + both[:, 128:]
            return carry

        lax.fori_loop(0, NG * ROWS // 720, step, 0)

    def place(part, b, t):
        return pl.ds(pl.multiple_of((part * 9 + b) * ROWS + t * 8, 8), 8)

    def first(s):
        arriving = visit_copies(s, (own, own_fold), visit_send.at[0], group_at(1))
        arriving[4].wait_recv()
        relays = lower_relays()
        if s == 0:

            @pl.when(even)
            def _():
                relays[4].start()

        for q, (begin, end) in enumerate(QUARTERS):
            arriving[q].wait_recv()
            if s == 0:

                @pl.when(even)
                def _(q=q):
                    relays[q].start()

            def products(j, carry, q=q, begin=begin):
                tile = begin + j
                phi = [own[tile, rows, :] for rows in first_band]
                chi = [visit[s, tile, rows, :] for rows in first_band]
                for f in range(FIELDS):
                    rho[tile, field_rows[f], :] = phi[f // 2] * chi[f % 2]
                phi, chi = last_planes(s, j, q)
                rho[tile, 32:40, :] = phi * chi
                return carry

            lax.fori_loop(0, end - begin, products, 0, unroll=True)
        for b in range(9):
            starts = [point72(a, b) * NG for a in range(8)]
            parts = dft8([take(lambda i: rho[i], at) for at in starts])
            for part in range(8):
                base = (part * 9 + b) * ROWS
                work[base : base + ROWS, :] = parts[part]
        along_z(0)

        def finish(t, target):
            def load(part, b):
                return work2[place(part, b, t), :]

            def save(slot, value):
                put(target, slot * NG, value)

            finish72(load, save)

        def last(tile, lanes, piece):
            if tile == TAIL_TILE:
                wave_tail[s, 32:40, lanes] = piece
            else:
                wave_last[tile * 8 : tile * 8 + 8, lanes] = piece

        finish(4, last)
        upper = lax.broadcasted_iota(jnp.int32, (8, 128), 0) < FIELDS
        for q in range(PEERS):
            for i in range(3):
                tile = (q * OWN_TILES + i) * 8
                piece = wave_last[tile : tile + 8, :]
                if i < 2:
                    piece = jnp.where(upper, piece, wave_last[tile + 24 : tile + 32, :])
                wave_fold[s, q * LAST + i * 8 : q * LAST + i * 8 + 8, :] = piece
        send_fold(0, s)

        def planes(t, carry):
            def target(tile, lanes, piece):
                if tile == TAIL_TILE:
                    wave_tail[s, pl.ds(pl.multiple_of(t * 8, 8), 8), lanes] = piece
                else:
                    wave[s, t, tile * 8 : tile * 8 + 8, lanes] = piece

            finish(t, target)
            send_part(0, s, t)
            return carry

        lax.fori_loop(0, FIELDS, planes, 0)
        for f in range(FIELDS):
            wave_piece[s, f, 0:8, :] = wave_tail[s, field_rows[f], :]
            wave_piece[s, f, 8:9, :] = wave_tail[s, 32 + f : 33 + f, :]

    part_refs = ((wave, recv), (back, field))
    fold_refs = ((wave_fold, recv_fold), (back_fold, field_fold))
    straight = [(1, 2), (0, 2), (1, 1), (1, 3), (0, 1), (0, 3), (1, 0)]

    def rows_of(index, rows):
        return pl.ds(pl.multiple_of(index * rows, 8), rows)

    def send_part(phase, s, f):
        src, dst = part_refs[phase]
        for dx, dy in straight:
            to = at(dx, dy)
            remote(
                src.at[s, f, rows_of(to, PART)],
                dst.at[s, f, rows_of(me, PART)],
                part_send.at[phase, s],
                part_recv.at[phase, s, f],
                pencil=to,
            ).start()
        dst[s, f, rows_of(me, PART), :] = src[s, f, rows_of(me, PART), :]

    def send_fold(phase, s):
        src, dst = fold_refs[phase]
        for dx, dy in straight:
            to = at(dx, dy)
            remote(
                src.at[s, rows_of(to, LAST)],
                dst.at[s, rows_of(me, LAST)],
                fold_send.at[phase, s],
                fold_recv.at[phase, s],
                pencil=to,
            ).start()
        dst[s, rows_of(me, LAST), :] = src[s, rows_of(me, LAST), :]

    def drain(view, sem):
        pltpu.make_async_copy(view, view, sem).wait()

    def wait_part(phase, s, f):
        drain(part_refs[phase][1].at[s, f, pl.ds(0, 7 * PART)], part_recv.at[phase, s, f])

    def wait_fold(phase, s):
        drain(fold_refs[phase][1].at[s, pl.ds(0, 7 * LAST)], fold_recv.at[phase, s])

    def end_blocks(phase, s):
        drain(part_refs[phase][0].at[s, :, pl.ds(0, 7 * PART)], part_send.at[phase, s])
        drain(fold_refs[phase][0].at[s, pl.ds(0, 7 * LAST)], fold_send.at[phase, s])

    def piece_of(ref, s, index):
        return ref.at[s, pl.ds(pl.multiple_of(index * PIECE, 8), PIECE), :]

    def owner_of(s, f):
        return FIELDS * s + f

    def tail_copy(s, f, distance):
        return remote(
            wave_piece.at[s, f],
            piece_of(recv_tail, s, me),
            tail_send.at[s, f],
            tail_recv.at[s, distance],
            pencil=jnp.int32(owner_of(s, f)),
        )

    def second(s):
        wait_fold(0, s)

        def last_rows(f, tile):
            return pl.ds(tile % 3 * 8 + FIELDS * (tile // 3) + f, PEERS, stride=LAST)

        for f in range(FIELDS):
            wait_part(0, s, f)
            columns = []
            for tile in range(OWN_TILES):
                starts = [p * PART + tile * 8 for p in range(PEERS)]
                rows = [recv[s, f, start : start + 8, :] for start in starts]
                rows.append(recv_fold[s, last_rows(f, tile), :])
                columns.append(jnp.concatenate(rows, axis=0))
            spectrum = left(wide[512:592, :], jnp.concatenate(columns, axis=1))
            result = left(wide[592:672, :], spectrum * kernel_table[...])
            for tile in range(OWN_TILES):
                lanes = slice(tile * 128, tile * 128 + 128)
                for p in range(PEERS):
                    start = p * PART + tile * 8
                    back[s, f, start : start + 8, :] = result[p * 8 : p * 8 + 8, lanes]
                back_fold[s, last_rows(f, tile), :] = result[64:72, lanes]
            send_part(1, s, f)
        send_fold(1, s)

    def give_copies(s):
        return block_copies(
            (give.at[s], give_fold.at[s]),
            (given.at[odd], given_fold.at[odd]),
            give_send.at[s],
            give_recv.at[odd],
            visitor_group[s],
        )

    def given_copies(source):
        return block_copies(
            (give.at[0], give_fold.at[0]),
            (given.at[source], given_fold.at[source]),
            give_send.at[0],
            give_recv.at[source],
            visitor_group[0],
        )

    def third(s):
        def start(t, source):
            def load(slot):
                return take(source, slot * NG)

            def save(part, b, value):
                work[place(part, b, t), :] = value

            finish72_adjoint(load, save)

        def planes(t, carry):
            wait_part(1, s, t)

            def source(tile):
                if tile == TAIL_TILE:
                    return field_tail[s, pl.ds(pl.multiple_of(t * 8, 8), 8), :]
                return field[s, t, tile * 8 : tile * 8 + 8, :]

            start(t, source)
            return carry

        lax.fori_loop(0, FIELDS, planes, 0)
        wait_fold(1, s)

        def last(tile):
            if tile == TAIL_TILE:
                return field_tail[s, 32:40, :]
            which = tile % OWN_TILES
            first_row = tile // OWN_TILES * LAST + which % 3 * 8
            value = field_fold[s, first_row : first_row + 8, :]
            return pltpu.roll(value, FIELDS, 0) if which > 2 else value

        start(4, last)
        along_z(256)
        for b in range(9):
            parts = []
            for part in range(8):
                base = (part * 9 + b) * ROWS
                parts.append(work2[base : base + ROWS, :])
            for a, value in enumerate(dft8_adjoint(parts)):


                def store(tile, lanes, piece):
                    rho[tile, :, lanes] = piece

                put(store, point72(a, b) * NG, value)
        weights = []
        for f in range(FIELDS):
            g = 2 * (f % 2) + f // 2
            if s == 0:
                row = jnp.where(
                    even,
                    visit_fold[s, MASKS, FIELDS + g : FIELDS + g + 1, :],
                    visit_fold[s, MASKS, g : g + 1, :],
                )
            else:
                row = jnp.where(
                    even,
                    visit_fold[s, MASKS, g : g + 1, :],
                    own_fold[MASKS, FIELDS + f : FIELDS + f + 1, :],
                )
            weights.append(jnp.broadcast_to(row, (8, 128)))
        last_weight = weights[3]
        for f in range(3):
            last_weight = jnp.where(row_at == f, weights[f], last_weight)

        leaving = give_copies(s)
        for q, (begin, end) in enumerate(QUARTERS):

            def gather(j, carry, q=q, begin=begin):
                tile = begin + j
                phi = [own[tile, rows, :] for rows in first_band]
                chi = [visit[s, tile, rows, :] for rows in first_band]
                value = [rho[tile, field_rows[f], :] * weights[f] for f in range(FIELDS)]
                for a in range(2):
                    stay = value[2 * a] * chi[0] + value[2 * a + 1] * chi[1]
                    if s > 0:
                        stay = stay + total[tile, first_band[a], :]
                    total[tile, first_band[a], :] = stay
                for c in range(2):
                    give[s, tile, first_band[c], :] = value[c] * phi[0] + value[2 + c] * phi[1]
                phi, chi = last_planes(s, j, q)
                value = rho[tile, 32:40, :] * last_weight
                stay, leave = value * chi, value * phi
                stay = stay + pltpu.roll(stay, 7, 0)
                leave = leave + pltpu.roll(leave, 6, 0)
                for band in range(2):
                    row = slice(2 * q + band, 2 * q + band + 1)
                    kept = stay[2 * band : 2 * band + 1]
                    if s > 0:
                        kept = kept + total_fold[j, row, :]
                    total_fold[j, row, :] = kept
                    give_fold[s, j, row, :] = leave[band : band + 1]
                return carry

            lax.fori_loop(0, end - begin, gather, 0, unroll=True)
            leaving[q].start()
        leaving[4].start()

    def tail_back(s, f, j):
        return remote(
            piece_of(back_tail, s, peer(j)),
            field_piece.at[s, f],
            back_tail_send.at[s, j],
            back_tail_recv.at[s, f],
            pencil=peer(j),
        )

    def send_tail(s):
        for f in range(FIELDS):
            owner = owner_of(s, f)

            @pl.when(me == owner)
            def _(f=f, owner=owner):
                recv_tail[s, owner * PIECE : (owner + 1) * PIECE, :] = wave_piece[s, f]

            @pl.when(me != owner)
            def _(f=f, owner=owner):
                tail_copy(s, f, lax.rem(owner - me + PEERS, PEERS)).start()

    def turn_tail(s):
        owned = lax.div(me, FIELDS) == s

        @pl.when(owned)
        def _():
            for j in range(1, PEERS):
                tail_copy(s, 0, j).wait_recv()
            parts = [pl.ds(p * PIECE, 8) for p in range(PEERS)] + [pl.ds(8, PEERS, stride=PIECE)]
            block = jnp.concatenate([recv_tail[s, part, :] for part in parts], axis=0)
            spectrum = left(wide[512:592, :], block) * kernel_tail[...]
            result = left(wide[592:672, :], spectrum)
            for i, part in enumerate(parts):
                back_tail[s, part, :] = result[i * 8 : i * 8 + 8, :]
            mine = lax.rem(me, FIELDS)
            for j in range(1, PEERS):
                tail_back(s, mine, j).start()
            field_piece[s, mine] = back_tail[s, pl.ds(pl.multiple_of(me * PIECE, 8), PIECE), :]

    def end_tail(s):
        for f in range(FIELDS):
            owner = owner_of(s, f)

            @pl.when(me != owner)
            def _(f=f, owner=owner):
                tail_copy(s, f, lax.rem(owner - me + PEERS, PEERS)).wait_send()
                tail_back(s, f, 1).wait_recv()

            field_tail[s, field_rows[f], :] = field_piece[s, f, 0:8, :]
            field_tail[s, 32 + f : 33 + f, :] = field_piece[s, f, 8:9, :]

        @pl.when(lax.div(me, FIELDS) == s)
        def _():
            for j in range(1, PEERS):
                tail_back(s, lax.rem(me, FIELDS), j).wait_send()

    first(0)
    send_tail(0)
    first(1)
    send_tail(1)
    second(0)
    turn_tail(0)
    second(1)
    turn_tail(1)
    end_tail(0)
    third(0)
    end_tail(1)
    third(1)
    for q, (begin, end) in enumerate(QUARTERS):
        for source in range(2):
            given_copies(source)[q].wait_recv()
        for tile in range(begin, end):
            lanes = slice(tile * 128, min(tile * 128 + 128, MERGED))
            for rows, band in zip(first_band, range(2)):
                term = -(total[tile, rows, :] + given[0, tile, rows, :] + given[1, tile, rows, :])
                mixed[tile, pl.ds(band, 8, stride=2), :] = term
            for plane in range(PLANES - 1):
                piece = mixed[tile, 2 * plane : 2 * plane + 2, 0 : lanes.stop - lanes.start]
                out_ref[plane, :, lanes] = piece
    for source in range(2):
        given_copies(source)[4].wait_recv()
    for q, (begin, end) in enumerate(QUARTERS):
        for tile in range(begin, end):
            lanes = slice(tile * 128, min(tile * 128 + 128, MERGED))
            j, rows = tile - begin, slice(2 * q, 2 * q + 2)
            term = total_fold[j, rows, :] + given_fold[0, j, rows, :] + given_fold[1, j, rows, :]
            out_ref[PLANES - 1, :, lanes] = -term[:, 0 : lanes.stop - lanes.start]

    @pl.when(even)
    def _():
        for copy in lower_sends() + lower_relays():
            copy.wait_send()

    @pl.when(jnp.logical_not(even))
    def _():
        for copy in upper_sends():
            copy.wait_send()

    for s in range(2):
        for copy in give_copies(s):
            copy.wait_send()
    for phase in range(2):
        for s in range(2):
            end_blocks(phase, s)


def body(bands, orbitals, pair_mask):
    hbm = pl.BlockSpec(memory_space=pltpu.HBM)
    smem = pl.BlockSpec(memory_space=pltpu.SMEM)
    consts = [jnp.asarray(table) for table in tables()]
    dma = pltpu.SemaphoreType.DMA

    def buffer(*shape):
        return pltpu.VMEM(shape, jnp.float32)

    out = pl.pallas_call(
        functools.partial(kernel, bands),
        out_shape=jax.ShapeDtypeStruct((PLANES, 2, MERGED), jnp.float32),
        in_specs=[smem] + [hbm] * (1 + len(consts)),
        out_specs=pl.BlockSpec(memory_space=pltpu.VMEM),
        scratch_shapes=[
            buffer(PLANES, 2, MERGED),
            pltpu.VMEM(consts[0].shape, jnp.bfloat16),
            buffer(*consts[1].shape),
            buffer(*consts[2].shape),
            buffer(TILES, 16, 128),
            buffer(TILES, 16, 128),
            buffer(FOLD + 1, 8, 128),
            buffer(2, TILES, 16, 128),
            buffer(2, FOLD + 1, 8, 128),
            buffer(TILES, ROWS, 128),
            buffer(NG * ROWS, 128),
            buffer(NG * ROWS, 128),
            buffer(2, FIELDS, PEERS * PART, 128),
            buffer(2, PEERS * LAST, 128),
            buffer(TAIL_TILE * 8, 128),
            buffer(2, ROWS, 128),
            buffer(2, FIELDS, PIECE, 128),
            buffer(2, FIELDS, PEERS * PART, 128),
            buffer(2, PEERS * LAST, 128),
            buffer(2, PEERS * PIECE, 128),
            buffer(2, FIELDS, PEERS * PART, 128),
            buffer(2, PEERS * LAST, 128),
            buffer(2, PEERS * PIECE, 128),
            buffer(2, FIELDS, PEERS * PART, 128),
            buffer(2, PEERS * LAST, 128),
            buffer(2, ROWS, 128),
            buffer(2, FIELDS, PIECE, 128),
            buffer(NG, OWN),
            buffer(NG, 128),
            buffer(TILES, 16, 128),
            buffer(FOLD + 1, 8, 128),
            buffer(2, TILES, 16, 128),
            buffer(2, FOLD + 1, 8, 128),
            buffer(2, TILES, 16, 128),
            buffer(2, FOLD + 1, 8, 128),
            dma((2, 5)),
            dma((2, 5)),
            dma((2, 5)),
            dma((2, 5)),
            dma((2, 2)),
            dma((2, 2, FIELDS)),
            dma((2, 2)),
            dma((2, 2)),
            dma((2, FIELDS)),
            dma((2, PEERS)),
            dma((2, PEERS)),
            dma((2, FIELDS)),
            dma((4,)),
        ],
        compiler_params=pltpu.CompilerParams(
            collective_id=0, has_side_effects=True, vmem_limit_bytes=64 * 1024 * 1024 - 65536
        ),
    )(pair_mask, orbitals.transpose(1, 0, 2), *consts)
    return out.transpose(1, 0, 2)


def solution(mesh):
    return jax.shard_map(
        functools.partial(body, mesh.shape["band"]),
        mesh=mesh,
        in_specs=(P("band", "pencil", None), P("band", None, None, None)),
        out_specs=P("band", "pencil", None),
        check_vma=False,
    )
```

```python
import functools
import math

import jax
import jax.numpy as jnp
import ml_dtypes
import numpy as np
from jax import lax
from jax.experimental import pallas as pl
from jax.experimental.pallas import tpu as pltpu
from jax.sharding import PartitionSpec as P

MESH = pl.DeviceIdType.MESH
NG = 72
PLANES = 9
PEERS = 8
FIELDS = 4
ROWS = 40
PART = 40
LAST = 24
MERGED = NG * NG
WIDTH = 5248
OWN = 640
TAIL = PEERS * OWN
PIECE = 16
FOLD = 11
MASKS = FOLD
QUARTERS = [(q * FOLD, min((q + 1) * FOLD, 41)) for q in range(4)]
TILES = WIDTH // 128
OWN_TILES = OWN // 128
TAIL_TILE = TILES - 1
coulomb_scale = 20.0
screening = 0.25
HALF = math.sqrt(0.5)


def dft8(x):
    a = [x[j] + x[j + 4] for j in range(4)]
    b = [x[j] - x[j + 4] for j in range(4)]
    e, o = a[0] + a[2], a[1] + a[3]
    u, v = HALF * (b[1] - b[3]), HALF * (b[1] + b[3])
    return [e + o, e - o, b[0] + u, v + b[2], a[0] - a[2], a[1] - a[3], b[0] - u, v - b[2]]


def dft8_adjoint(c):
    p, q = c[0] + c[1], c[0] - c[1]
    a = [p + c[4], q + c[5], p - c[4], q - c[5]]
    d, s = HALF * (c[2] - c[6]), HALF * (c[3] + c[7])
    b = [c[2] + c[6], d + s, c[3] - c[7], s - d]
    return [a[j] + b[j] for j in range(4)] + [a[j] - b[j] for j in range(4)]


def cos9(n):
    return math.cos(2.0 * math.pi * (n % 9) / 9)


def sin9(n):
    return math.sin(2.0 * math.pi * (n % 9) / 9)


def weighted(values, factors):
    total = values[0] * factors[0]
    for value, factor in zip(values[1:], factors[1:]):
        total = total + value * factor
    return total


def dft9(x):
    e = [x[n] + x[9 - n] for n in range(1, 5)]
    o = [x[n] - x[9 - n] for n in range(1, 5)]
    third = e[0] + e[1] + e[3]
    cosines = [x[0] + third + e[2]]
    sines = [None]
    for k in range(1, 5):
        if k == 3:
            cosines.append(x[0] + e[2] - 0.5 * third)
            sines.append(sin9(3) * (o[0] - o[1] + o[3]))
        else:
            cosines.append(x[0] + weighted(e, [cos9(k * n) for n in range(1, 5)]))
            sines.append(weighted(o, [sin9(k * n) for n in range(1, 5)]))
    return cosines, sines


def dft9_adjoint(cosines, sines):
    c, s = cosines, sines
    out = [None] * 9
    out[0] = c[0] + ((c[1] + c[2]) + (c[3] + c[4]))
    for n in range(1, 5):
        if n == 3:
            even = c[0] + c[3] - 0.5 * (c[1] + c[2] + c[4])
            odd = sin9(3) * (s[1] - s[2] + s[4])
        else:
            even = c[0] + weighted(c[1:], [cos9(k * n) for k in range(1, 5)])
            odd = weighted(s[1:], [sin9(k * n) for k in range(1, 5)])
        out[n] = even + odd
        out[9 - n] = even - odd
    return out


def finish72(load, save):
    for part in (0, 1):
        cosines, sines = dft9([load(part, b) for b in range(9)])
        base = part * 9
        save(base, cosines[0])
        for k in range(1, 5):
            save(base + 2 * k - 1, cosines[k])
            save(base + 2 * k, sines[k])
    for k8 in range(3):
        base = 18 + 18 * k8
        cc, cs = dft9([load(2 + 2 * k8, b) for b in range(9)])
        sc, ss = dft9([load(3 + 2 * k8, b) for b in range(9)])
        save(base, cc[0])
        save(base + 1, sc[0])
        for k in range(1, 5):
            at = base + 4 * k - 2
            save(at, cc[k] - ss[k])
            save(at + 1, cc[k] + ss[k])
            save(at + 2, sc[k] + cs[k])
            save(at + 3, sc[k] - cs[k])


def finish72_adjoint(load, save):
    for part in (0, 1):
        base = part * 9
        cosines = [load(base)] + [load(base + 2 * k - 1) for k in range(1, 5)]
        sines = [None] + [load(base + 2 * k) for k in range(1, 5)]
        for b, value in enumerate(dft9_adjoint(cosines, sines)):
            save(part, b, value)
    for k8 in range(3):
        base = 18 + 18 * k8
        cc, sc, cs, ss = [load(base)], [load(base + 1)], [None], [None]
        for k in range(1, 5):
            at = base + 4 * k - 2
            plus, minus, sine_plus, sine_minus = [load(at + i) for i in range(4)]
            cc.append(plus + minus)
            ss.append(minus - plus)
            sc.append(sine_plus + sine_minus)
            cs.append(sine_plus - sine_minus)
        for b, value in enumerate(dft9_adjoint(cc, cs)):
            save(2 + 2 * k8, b, value)
        for b, value in enumerate(dft9_adjoint(sc, ss)):
            save(3 + 2 * k8, b, value)


def point72(a, b):
    return (9 * a + 8 * b) % NG


def split(table):
    high = table.astype(ml_dtypes.bfloat16).astype(np.float64)
    return high, (table - high).astype(ml_dtypes.bfloat16).astype(np.float64)


def from_left(table):
    high, low = split(table)
    wide = np.zeros((80, 256))
    wide[:NG, : 3 * NG] = np.concatenate([high, high, low], axis=1)
    return wide


def from_right(table):
    high, low = split(table)
    return np.block([[high, low], [high, np.zeros_like(low)]])


@functools.cache
def tables():
    at = np.arange(NG)
    basis, freq = [np.full(NG, 1.0)], [0]
    for k in range(1, NG // 2):
        basis += [np.cos(2 * np.pi * k * at / NG), np.sin(2 * np.pi * k * at / NG)]
        freq += [k, k]
    basis.append(np.cos(np.pi * at))
    freq.append(NG // 2)
    basis = np.array(basis)
    basis /= np.sqrt((basis * basis).sum(1, keepdims=True))
    freq = np.array(freq, np.float64)
    eye = np.eye(NG)
    parts = [dft8([eye[point72(a, b)] for a in range(8)]) for b in range(9)]
    slots = [None] * NG
    finish72(lambda part, b: parts[b][part], slots.__setitem__)
    slots = np.array(slots)
    norm = (slots * slots).sum(1)
    spectrum = np.abs(np.fft.fft(slots, axis=1))[:, : NG // 2 + 1]
    freq_y = spectrum.argmax(1).astype(np.float64)
    along_z = np.zeros((128, 128))
    along_z[:NG, :NG] = basis.T
    along_x = basis.reshape(NG, PEERS, PLANES)
    along_x = np.concatenate([along_x[:, :, :8].reshape(NG, -1), along_x[:, :, 8]], axis=1)
    column = np.zeros((8, WIDTH), np.float32)
    column[0, :MERGED] = (freq_y[:, None] ** 2 + freq[None, :] ** 2).reshape(-1)
    column[1, :MERGED] = np.repeat(1.0 / norm, NG)
    freq_x = np.broadcast_to((freq**2)[:, None], (NG, 128)).astype(np.float32)
    wide = np.concatenate(
        [from_right(along_z), from_right(along_z.T), from_left(along_x), from_left(along_x.T)]
    )
    return wide.astype(ml_dtypes.bfloat16), column, freq_x


def take(load, start):
    tile, lane = divmod(start, 128)
    value = load(tile)
    if lane == 0:
        return value
    if lane + NG > 128:
        at = lax.broadcasted_iota(jnp.int32, value.shape, 1)
        value = jnp.where(at >= lane, value, load(tile + 1))
    return pltpu.roll(value, 128 - lane, 1)


def put(store, start, value):
    tile, lane = divmod(start, 128)
    if lane:
        value = pltpu.roll(value, lane, 1)
    end = min(lane + NG, 128)
    store(tile, slice(lane, end), value[:, lane:end])
    if lane + NG > 128:
        store(tile + 1, slice(0, lane + NG - 128), value[:, : lane + NG - 128])


def matmul(a, b):
    return jnp.dot(a, b, preferred_element_type=jnp.float32)


def halves(x):
    high = x.astype(jnp.bfloat16)
    return high, (x - high.astype(jnp.float32)).astype(jnp.bfloat16)


def left(table, x):
    high, low = [part.astype(jnp.float32) for part in halves(x)]
    zeros = jnp.zeros((8, x.shape[1]), jnp.float32)
    operand = jnp.concatenate([high, low, high, zeros], axis=0).astype(jnp.bfloat16)
    return matmul(table[:, 0 : operand.shape[0]], operand)[0:NG]


def kernel(
    bands,
    mask_ref,
    bands_hbm,
    wide_hbm,
    column_hbm,
    freq_hbm,
    out_ref,
    bands_ref,
    wide,
    column_ref,
    freq_ref,
    mixed,
    own,
    own_fold,
    visit,
    visit_fold,
    rho,
    work,
    work2,
    wave,
    wave_fold,
    wave_tail,
    wave_piece,
    recv,
    recv_fold,
    recv_tail,
    back,
    back_fold,
    back_tail,
    field,
    field_fold,
    field_tail,
    field_piece,
    kernel_table,
    kernel_tail,
    total,
    total_fold,
    give,
    give_fold,
    given,
    given_fold,
    visit_send,
    visit_recv,
    give_send,
    give_recv,
    part_send,
    part_recv,
    fold_send,
    fold_recv,
    tail_send,
    tail_recv,
    back_tail_send,
    back_tail_recv,
    load_sem,
):
    me = lax.axis_index("pencil")
    group = lax.axis_index("band")
    me_x, me_y = lax.div(me, 4), lax.rem(me, 4)

    loads = [
        pltpu.make_async_copy(src, dst, load_sem.at[i])
        for i, (src, dst) in enumerate(
            [
                (bands_hbm, bands_ref),
                (wide_hbm, wide),
                (column_hbm, column_ref),
                (freq_hbm, freq_ref),
            ]
        )
    ]
    for load in loads:
        load.start()

    def peer(j):
        return lax.rem(me + j, PEERS)

    def at(dx, dy):
        return lax.rem(me_x + dx, 2) * 4 + lax.rem(me_y + dy + 4, 4)

    def group_at(j):
        return lax.rem(group + j + bands, bands)

    barrier = pltpu.get_barrier_semaphore()
    for j in range(1, PEERS):
        pl.semaphore_signal(barrier, inc=1, device_id={"pencil": peer(j)}, device_id_type=MESH)
    for j in (-2, -1, 1, 2):
        pl.semaphore_signal(barrier, inc=1, device_id={"band": group_at(j)}, device_id_type=MESH)
    loads[0].wait()
    def take_tile(tile, j, q, width):
        lanes = pl.ds(tile * 128, width)
        if width == 128:
            lanes = pl.ds(pl.multiple_of(tile * 128, 128), 128)
        live = slice(0, width)
        for plane in range(PLANES - 1):
            mixed[tile, 2 * plane : 2 * plane + 2, live] = bands_ref[plane, :, lanes]
        for band in range(2):
            own[tile, band * 8 : band * 8 + 8, :] = mixed[tile, pl.ds(band, 8, stride=2), :]
        own_fold[j, 2 * q : 2 * q + 2, live] = bands_ref[PLANES - 1, :, lanes]

    def tile_loop(begin, end, step):
        def run(j, carry):
            step(begin + j, j)
            return carry

        lax.fori_loop(0, end - begin, run, 0)

    mixed[TAIL_TILE] = jnp.zeros((16, 128), jnp.float32)
    own_fold[TAIL_TILE % FOLD, 6:8, :] = jnp.zeros((2, 128), jnp.float32)
    for q, (begin, end) in enumerate(QUARTERS):
        tile_loop(begin, min(end, TAIL_TILE), lambda tile, j, q=q: take_tile(tile, j, q, 128))
    take_tile(TAIL_TILE, TAIL_TILE % FOLD, 3, MERGED - TAIL)

    def own_mask(s, f):
        return mask_ref[0, s, f // 2, f % 2].astype(jnp.float32)

    for m in range(2 * FIELDS):
        value = own_mask(m // FIELDS, m % FIELDS)
        own_fold[MASKS, m : m + 1, :] = jnp.zeros((1, 128), jnp.float32) + value
    pl.semaphore_wait(barrier, PEERS - 1 + 4)

    def remote(src, dst, send, recv, **device):
        return pltpu.make_async_remote_copy(
            src_ref=src,
            dst_ref=dst,
            send_sem=send,
            recv_sem=recv,
            device_id=device,
            device_id_type=MESH,
        )

    odd = lax.rem(group, 2)
    even = odd == 0

    def visitor_group(s):
        near = jnp.where(even, group_at(2), group_at(1))
        return jnp.where(s == 0, near, jnp.where(even, group_at(1), group_at(-2)))

    def parts(main, fold):
        return [
            *(main.at[pl.ds(begin, end - begin)] for begin, end in QUARTERS),
            fold,
        ]

    def block_copies(src, dst, send, recv, to):
        return [
            remote(one, two, send.at[q], recv.at[q], band=to)
            for q, (one, two) in enumerate(zip(parts(*src), parts(*dst)))
        ]

    def visit_at(s):
        return visit.at[s], visit_fold.at[s]

    def visit_copies(s, src, send, to):
        return block_copies(src, visit_at(s), send, visit_recv.at[s], to)

    def lower_sends():
        return visit_copies(0, (own, own_fold), visit_send.at[0], group_at(-2))

    def lower_relays():
        return visit_copies(0, visit_at(0), visit_send.at[1], group_at(1))

    def upper_sends():
        return visit_copies(1, (own, own_fold), visit_send.at[0], group_at(2)) + visit_copies(
            1, (own, own_fold), visit_send.at[1], group_at(-1)
        )

    @pl.when(even)
    def _():
        for copy in lower_sends():
            copy.start()

    @pl.when(jnp.logical_not(even))
    def _():
        for copy in upper_sends():
            copy.start()

    def kernel_columns(start, width):
        squared = column_ref[0:1, pl.ds(start, width)]
        scale = column_ref[1:2, pl.ds(start, width)]
        return coulomb_scale / (freq_ref[:, 0:1] + squared + screening) * scale

    for load in loads[1:]:
        load.wait()
    kernel_table[...] = kernel_columns(pl.multiple_of(me * OWN, 128), OWN)
    kernel_tail[...] = kernel_columns(TAIL, 128)
    wave_tail[...] = jnp.zeros((2, ROWS, 128), jnp.float32)
    total_fold[...] = jnp.zeros((FOLD + 1, 8, 128), jnp.float32)

    def clear(tile, carry):
        total[tile] = jnp.zeros((16, 128), jnp.float32)
        return carry

    lax.fori_loop(0, TILES, clear, 0)
    for s in range(2):
        for p in range(PEERS):
            back_fold[s, (p + 1) * LAST - 8 : (p + 1) * LAST, :] = jnp.zeros((8, 128), jnp.float32)
            back_tail[s, (p + 1) * PIECE - 8 : (p + 1) * PIECE, :] = jnp.zeros((8, 128), jnp.float32)
        field_tail[s, 32:40, :] = jnp.zeros((8, 128), jnp.float32)
        for f in range(FIELDS):
            wave_piece[s, f, 8:16, :] = jnp.zeros((8, 128), jnp.float32)

    first_band = [slice(band * 8, band * 8 + 8) for band in range(2)]
    field_rows = [slice(f * 8, f * 8 + 8) for f in range(FIELDS)]
    row_at = lax.broadcasted_iota(jnp.int32, (8, 128), 0)
    resident_one = lax.rem(lax.div(row_at, 2), 2) == 1
    visitor_one = lax.rem(row_at, 2) == 1

    def last_planes(s, j, q):
        a = [own_fold[j, 2 * q + band : 2 * q + band + 1, :] for band in range(2)]
        c = [visit_fold[s, j, 2 * q + band : 2 * q + band + 1, :] for band in range(2)]
        wide_a = [jnp.broadcast_to(row, (8, 128)) for row in a]
        wide_c = [jnp.broadcast_to(row, (8, 128)) for row in c]
        return (
            jnp.where(resident_one, wide_a[1], wide_a[0]),
            jnp.where(visitor_one, wide_c[1], wide_c[0]),
        )

    def along_z(start):
        for i in range(2):
            rows = pl.ds(i * 288, 288)
            both = matmul(jnp.concatenate(halves(work[rows, :]), axis=1), wide[start : start + 256, :])
            work2[rows, :] = both[:, :128] + both[:, 128:]

    def place(part, b):
        return slice((part * 9 + b) * 8, (part * 9 + b) * 8 + 8)

    def row_of(t):
        return pl.ds(pl.multiple_of(t * 8, 8), 8)

    def first(s):
        arriving = visit_copies(s, (own, own_fold), visit_send.at[0], group_at(1))
        relays = lower_relays()
        for q in (4, 0, 1, 2, 3):
            arriving[q].wait_recv()

            @pl.when((s == 0) & even)
            def _(q=q):
                relays[q].start()

        def one_row(i, carry):
            t = lax.rem(i + FIELDS, FIELDS + 1)

            @pl.when(i > 0)
            def _():
                resident, visitor = row_of(lax.div(t, 2)), row_of(lax.rem(t, 2))
                for tile in range(TILES):
                    rho[tile, row_of(t), :] = own[tile, resident, :] * visit[s, tile, visitor, :]

            @pl.when(i == 0)
            def _():
                for q, (begin, end) in enumerate(QUARTERS):

                    def products(tile, j, q=q):
                        phi, chi = last_planes(s, j, q)
                        rho[tile, 32:40, :] = phi * chi

                    tile_loop(begin, end, products)

            for b in range(9):
                starts = [point72(a, b) * NG for a in range(8)]
                values = [take(lambda tile: rho[tile, row_of(t), :], at) for at in starts]
                for part, value in enumerate(dft8(values)):
                    work[place(part, b), :] = value
            along_z(0)

            def load(part, b):
                return work2[place(part, b), :]

            def target(tile, lanes, piece):
                if tile == TAIL_TILE:
                    wave_tail[s, row_of(t), lanes] = piece
                else:
                    wave[s, t, tile * 8 : tile * 8 + 8, lanes] = piece

            def save(slot, value):
                put(target, slot * NG, value)

            finish72(load, save)

            @pl.when(i == 0)
            def _():
                upper = lax.broadcasted_iota(jnp.int32, (8, 128), 0) < FIELDS

                def fold(q, carry):
                    for k in range(3):
                        at_row = pl.multiple_of((q * OWN_TILES + k) * 8, 8)
                        piece = wave[s, FIELDS, pl.ds(at_row, 8), :]
                        if k < 2:
                            below = wave[s, FIELDS, pl.ds(at_row + 24, 8), :]
                            piece = jnp.where(upper, piece, below)
                        to_row = pl.multiple_of(q * LAST + k * 8, 8)
                        wave_fold[s, pl.ds(to_row, 8), :] = piece
                    return carry

                lax.fori_loop(0, PEERS, fold, 0)
                send_fold(0, s)

            @pl.when(i > 0)
            def _():
                send_part(0, s, t)

            return carry

        lax.fori_loop(0, FIELDS + 1, one_row, 0)
        for f in range(FIELDS):
            wave_piece[s, f, 0:8, :] = wave_tail[s, field_rows[f], :]
            wave_piece[s, f, 8:9, :] = wave_tail[s, 32 + f : 33 + f, :]

    part_refs = ((wave, recv), (back, field))
    fold_refs = ((wave_fold, recv_fold), (back_fold, field_fold))
    straight = [(1, 2), (0, 2), (1, 1), (1, 3), (0, 1), (0, 3), (1, 0)]

    def rows_of(index, rows):
        return pl.ds(pl.multiple_of(index * rows, 8), rows)

    def send_part(phase, s, f):
        src, dst = part_refs[phase]
        for dx, dy in straight:
            to = at(dx, dy)
            remote(
                src.at[s, f, rows_of(to, PART)],
                dst.at[s, f, rows_of(me, PART)],
                part_send.at[phase, s],
                part_recv.at[phase, s, f],
                pencil=to,
            ).start()
        dst[s, f, rows_of(me, PART), :] = src[s, f, rows_of(me, PART), :]

    def send_fold(phase, s):
        src, dst = fold_refs[phase]
        for dx, dy in straight:
            to = at(dx, dy)
            remote(
                src.at[s, rows_of(to, LAST)],
                dst.at[s, rows_of(me, LAST)],
                fold_send.at[phase, s],
                fold_recv.at[phase, s],
                pencil=to,
            ).start()
        dst[s, rows_of(me, LAST), :] = src[s, rows_of(me, LAST), :]

    def drain(view, sem):
        pltpu.make_async_copy(view, view, sem).wait()

    def wait_part(phase, s, f):
        drain(part_refs[phase][1].at[s, f, pl.ds(0, 7 * PART)], part_recv.at[phase, s, f])

    def wait_fold(phase, s):
        drain(fold_refs[phase][1].at[s, pl.ds(0, 7 * LAST)], fold_recv.at[phase, s])

    def end_blocks(phase, s):
        parts = part_refs[phase][0].at[s, pl.ds(0, FIELDS), pl.ds(0, 7 * PART)]
        drain(parts, part_send.at[phase, s])
        drain(fold_refs[phase][0].at[s, pl.ds(0, 7 * LAST)], fold_send.at[phase, s])

    def piece_of(ref, s, index):
        return ref.at[s, pl.ds(pl.multiple_of(index * PIECE, 8), PIECE), :]

    def owner_of(s, f):
        return FIELDS * s + f

    def tail_copy(s, f, distance):
        return remote(
            wave_piece.at[s, f],
            piece_of(recv_tail, s, me),
            tail_send.at[s, f],
            tail_recv.at[s, distance],
            pencil=owner_of(s, f),
        )

    def second(s):
        wait_fold(0, s)

        def last_rows(f, tile):
            return pl.ds(tile % 3 * 8 + FIELDS * (tile // 3) + f, PEERS, stride=LAST)

        def one_field(f, carry):
            wait_part(0, s, f)
            columns = []
            for tile in range(OWN_TILES):
                starts = [p * PART + tile * 8 for p in range(PEERS)]
                rows = [recv[s, f, start : start + 8, :] for start in starts]
                rows.append(recv_fold[s, last_rows(f, tile), :])
                columns.append(jnp.concatenate(rows, axis=0))
            spectrum = left(wide[512:592, :], jnp.concatenate(columns, axis=1))
            result = left(wide[592:672, :], spectrum * kernel_table[...])
            for tile in range(OWN_TILES):
                lanes = slice(tile * 128, tile * 128 + 128)
                for p in range(PEERS):
                    start = p * PART + tile * 8
                    back[s, f, start : start + 8, :] = result[p * 8 : p * 8 + 8, lanes]
                back_fold[s, last_rows(f, tile), :] = result[64:72, lanes]
            send_part(1, s, f)
            return carry

        lax.fori_loop(0, FIELDS, one_field, 0)
        send_fold(1, s)

    def give_copies(s):
        return block_copies(
            (give.at[s], give_fold.at[s]),
            (given.at[odd], given_fold.at[odd]),
            give_send.at[s],
            give_recv.at[odd],
            visitor_group(s),
        )

    def given_copies(source):
        return block_copies(
            (give.at[0], give_fold.at[0]),
            (given.at[source], given_fold.at[source]),
            give_send.at[0],
            give_recv.at[source],
            visitor_group(0),
        )

    def third(s):
        def one_row(t, carry):
            @pl.when(t < FIELDS)
            def _():
                wait_part(1, s, t)

            @pl.when(t == FIELDS)
            def _():
                wait_fold(1, s)

                def unfold(q, carry):
                    for k in range(OWN_TILES):
                        from_row = pl.multiple_of(q * LAST + k % 3 * 8, 8)
                        value = field_fold[s, pl.ds(from_row, 8), :]
                        value = pltpu.roll(value, FIELDS, 0) if k > 2 else value
                        to_row = pl.multiple_of((q * OWN_TILES + k) * 8, 8)
                        field[s, FIELDS, pl.ds(to_row, 8), :] = value
                    return carry

                lax.fori_loop(0, PEERS, unfold, 0)

            def source(tile):
                if tile == TAIL_TILE:
                    return field_tail[s, row_of(t), :]
                return field[s, t, tile * 8 : tile * 8 + 8, :]

            def load(slot):
                return take(source, slot * NG)

            def save(part, b, value):
                work[place(part, b), :] = value

            finish72_adjoint(load, save)
            along_z(256)

            def target(tile, lanes, piece):
                rho[tile, row_of(t), lanes] = piece

            for b in range(9):
                values = dft8_adjoint([work2[place(part, b), :] for part in range(8)])
                for a, value in enumerate(values):
                    put(target, point72(a, b) * NG, value)
            return carry

        lax.fori_loop(0, FIELDS + 1, one_row, 0)
        weights = []
        for f in range(FIELDS):
            g = 2 * (f % 2) + f // 2
            above = visit_fold[s, MASKS, FIELDS + g : FIELDS + g + 1, :]
            same = visit_fold[s, MASKS, g : g + 1, :]
            mine = own_fold[MASKS, FIELDS + f : FIELDS + f + 1, :]
            row = jnp.where(s == 0, jnp.where(even, above, same), jnp.where(even, same, mine))
            weights.append(jnp.broadcast_to(row, (8, 128)))
        last_weight = weights[3]
        for f in range(3):
            last_weight = jnp.where(row_at == f, weights[f], last_weight)

        leaving = give_copies(s)
        for q, (begin, end) in enumerate(QUARTERS):

            def gather(tile, j, q=q):
                phi = [own[tile, rows, :] for rows in first_band]
                chi = [visit[s, tile, rows, :] for rows in first_band]
                value = [rho[tile, field_rows[f], :] * weights[f] for f in range(FIELDS)]
                for a in range(2):
                    stay = value[2 * a] * chi[0] + value[2 * a + 1] * chi[1]
                    total[tile, first_band[a], :] += stay
                for c in range(2):
                    give[s, tile, first_band[c], :] = value[c] * phi[0] + value[2 + c] * phi[1]
                phi, chi = last_planes(s, j, q)
                value = rho[tile, 32:40, :] * last_weight
                stay, leave = value * chi, value * phi
                stay = stay + pltpu.roll(stay, 7, 0)
                leave = leave + pltpu.roll(leave, 6, 0)
                for band in range(2):
                    row = slice(2 * q + band, 2 * q + band + 1)
                    total_fold[j, row, :] += stay[2 * band : 2 * band + 1]
                    give_fold[s, j, row, :] = leave[band : band + 1]

            tile_loop(begin, end, gather)
            leaving[q].start()
        leaving[4].start()

    def tail_back(s, f, j):
        return remote(
            piece_of(back_tail, s, peer(j)),
            field_piece.at[s, f],
            back_tail_send.at[s, j],
            back_tail_recv.at[s, f],
            pencil=peer(j),
        )

    def send_tail(s):
        for f in range(FIELDS):
            owner = owner_of(s, f)

            @pl.when(me == owner)
            def _(f=f, owner=owner):
                recv_tail[s, rows_of(owner, PIECE), :] = wave_piece[s, f]

            @pl.when(me != owner)
            def _(f=f, owner=owner):
                tail_copy(s, f, lax.rem(owner - me + PEERS, PEERS)).start()

    def turn_tail(s):
        owned = lax.div(me, FIELDS) == s

        @pl.when(owned)
        def _():
            for j in range(1, PEERS):
                tail_copy(s, 0, j).wait_recv()
            parts = [pl.ds(p * PIECE, 8) for p in range(PEERS)] + [pl.ds(8, PEERS, stride=PIECE)]
            block = jnp.concatenate([recv_tail[s, part, :] for part in parts], axis=0)
            spectrum = left(wide[512:592, :], block) * kernel_tail[...]
            result = left(wide[592:672, :], spectrum)
            for i, part in enumerate(parts):
                back_tail[s, part, :] = result[i * 8 : i * 8 + 8, :]
            mine = lax.rem(me, FIELDS)
            for j in range(1, PEERS):
                tail_back(s, mine, j).start()
            field_piece[s, mine] = back_tail[s, pl.ds(pl.multiple_of(me * PIECE, 8), PIECE), :]

    def end_tail(s):
        for f in range(FIELDS):
            owner = owner_of(s, f)

            @pl.when(me != owner)
            def _(f=f, owner=owner):
                tail_copy(s, f, lax.rem(owner - me + PEERS, PEERS)).wait_send()
                tail_back(s, f, 1).wait_recv()

            field_tail[s, field_rows[f], :] = field_piece[s, f, 0:8, :]
            field_tail[s, 32 + f : 33 + f, :] = field_piece[s, f, 8:9, :]

        @pl.when(lax.div(me, FIELDS) == s)
        def _():
            for j in range(1, PEERS):
                tail_back(s, lax.rem(me, FIELDS), j).wait_send()

    def slots(*stages):
        def run(s, carry):
            for stage in stages:
                stage(s)
            return carry

        lax.fori_loop(0, 2, run, 0)

    slots(first, send_tail)
    slots(second, turn_tail)
    slots(end_tail, third)

    for q, (begin, end) in enumerate(QUARTERS):
        for source in range(2):
            given_copies(source)[q].wait_recv()

        def result(tile, j, width=128):
            lanes = pl.ds(tile * 128, width)
            if width == 128:
                lanes = pl.ds(pl.multiple_of(tile * 128, 128), 128)
            for rows, band in zip(first_band, range(2)):
                term = -(total[tile, rows, :] + given[0, tile, rows, :] + given[1, tile, rows, :])
                mixed[tile, pl.ds(band, 8, stride=2), :] = term
            for plane in range(PLANES - 1):
                piece = mixed[tile, 2 * plane : 2 * plane + 2, 0:width]
                out_ref[plane, :, lanes] = piece

        tile_loop(begin, min(end, TAIL_TILE), result)
        if end > TAIL_TILE:
            result(TAIL_TILE, 0, MERGED - TAIL)
    for source in range(2):
        given_copies(source)[4].wait_recv()
    for q, (begin, end) in enumerate(QUARTERS):

        def last_result(tile, j, q=q, width=128):
            lanes = pl.ds(tile * 128, width)
            if width == 128:
                lanes = pl.ds(pl.multiple_of(tile * 128, 128), 128)
            rows = slice(2 * q, 2 * q + 2)
            term = total_fold[j, rows, :] + given_fold[0, j, rows, :] + given_fold[1, j, rows, :]
            out_ref[PLANES - 1, :, lanes] = -term[:, 0:width]

        tile_loop(begin, min(end, TAIL_TILE), last_result)
        if end > TAIL_TILE:
            last_result(TAIL_TILE, TAIL_TILE - begin, width=MERGED - TAIL)

    @pl.when(even)
    def _():
        for copy in lower_sends() + lower_relays():
            copy.wait_send()

    @pl.when(jnp.logical_not(even))
    def _():
        for copy in upper_sends():
            copy.wait_send()

    for s in range(2):
        for copy in give_copies(s):
            copy.wait_send()
    for phase in range(2):
        for s in range(2):
            end_blocks(phase, s)


def body(bands, orbitals, pair_mask):
    hbm = pl.BlockSpec(memory_space=pltpu.HBM)
    smem = pl.BlockSpec(memory_space=pltpu.SMEM)
    consts = [jnp.asarray(table) for table in tables()]
    dma = pltpu.SemaphoreType.DMA

    def buffer(*shape):
        return pltpu.VMEM(shape, jnp.float32)

    out = pl.pallas_call(
        functools.partial(kernel, bands),
        out_shape=jax.ShapeDtypeStruct((PLANES, 2, MERGED), jnp.float32),
        in_specs=[smem] + [hbm] * (1 + len(consts)),
        out_specs=pl.BlockSpec(memory_space=pltpu.VMEM),
        scratch_shapes=[
            buffer(PLANES, 2, MERGED),
            pltpu.VMEM(consts[0].shape, jnp.bfloat16),
            buffer(*consts[1].shape),
            buffer(*consts[2].shape),
            buffer(TILES, 16, 128),
            buffer(TILES, 16, 128),
            buffer(FOLD + 1, 8, 128),
            buffer(2, TILES, 16, 128),
            buffer(2, FOLD + 1, 8, 128),
            buffer(TILES, ROWS, 128),
            buffer(NG * 8, 128),
            buffer(NG * 8, 128),
            buffer(2, FIELDS + 1, PEERS * PART, 128),
            buffer(2, PEERS * LAST, 128),
            buffer(2, ROWS, 128),
            buffer(2, FIELDS, PIECE, 128),
            buffer(2, FIELDS, PEERS * PART, 128),
            buffer(2, PEERS * LAST, 128),
            buffer(2, PEERS * PIECE, 128),
            buffer(2, FIELDS, PEERS * PART, 128),
            buffer(2, PEERS * LAST, 128),
            buffer(2, PEERS * PIECE, 128),
            buffer(2, FIELDS + 1, PEERS * PART, 128),
            buffer(2, PEERS * LAST, 128),
            buffer(2, ROWS, 128),
            buffer(2, FIELDS, PIECE, 128),
            buffer(NG, OWN),
            buffer(NG, 128),
            buffer(TILES, 16, 128),
            buffer(FOLD + 1, 8, 128),
            buffer(2, TILES, 16, 128),
            buffer(2, FOLD + 1, 8, 128),
            buffer(2, TILES, 16, 128),
            buffer(2, FOLD + 1, 8, 128),
            dma((2, 5)),
            dma((2, 5)),
            dma((2, 5)),
            dma((2, 5)),
            dma((2, 2)),
            dma((2, 2, FIELDS)),
            dma((2, 2)),
            dma((2, 2)),
            dma((2, FIELDS)),
            dma((2, PEERS)),
            dma((2, PEERS)),
            dma((2, FIELDS)),
            dma((4,)),
        ],
        compiler_params=pltpu.CompilerParams(
            collective_id=0, has_side_effects=True, vmem_limit_bytes=64 * 1024 * 1024 - 65536
        ),
    )(pair_mask, orbitals.transpose(1, 0, 2), *consts)
    return out.transpose(1, 0, 2)


def solution(mesh):
    return jax.shard_map(
        functools.partial(body, mesh.shape["band"]),
        mesh=mesh,
        in_specs=(P("band", "pencil", None), P("band", None, None, None)),
        out_specs=P("band", "pencil", None),
        check_vma=False,
    )
```

```python
import functools
import math

import jax
import jax.numpy as jnp
import ml_dtypes
import numpy as np
from jax import lax
from jax.experimental import pallas as pl
from jax.experimental.pallas import tpu as pltpu
from jax.sharding import PartitionSpec as P

MESH = pl.DeviceIdType.MESH
NG = 72
PLANES = 9
PEERS = 8
FIELDS = 4
ROWS = 40
PART = 40
LAST = 24
MERGED = NG * NG
WIDTH = 5248
OWN = 640
TAIL = PEERS * OWN
PIECE = 16
FOLD = 11
MASKS = FOLD
QUARTERS = [(q * FOLD, min((q + 1) * FOLD, 41)) for q in range(4)]
TILES = WIDTH // 128
OWN_TILES = OWN // 128
TAIL_TILE = TILES - 1
coulomb_scale = 20.0
screening = 0.25
HALF = math.sqrt(0.5)


def dft8(x):
    a = [x[j] + x[j + 4] for j in range(4)]
    b = [x[j] - x[j + 4] for j in range(4)]
    e, o = a[0] + a[2], a[1] + a[3]
    u, v = HALF * (b[1] - b[3]), HALF * (b[1] + b[3])
    return [e + o, e - o, b[0] + u, v + b[2], a[0] - a[2], a[1] - a[3], b[0] - u, v - b[2]]


def dft8_adjoint(c):
    p, q = c[0] + c[1], c[0] - c[1]
    a = [p + c[4], q + c[5], p - c[4], q - c[5]]
    d, s = HALF * (c[2] - c[6]), HALF * (c[3] + c[7])
    b = [c[2] + c[6], d + s, c[3] - c[7], s - d]
    return [a[j] + b[j] for j in range(4)] + [a[j] - b[j] for j in range(4)]


def cos9(n):
    return math.cos(2.0 * math.pi * (n % 9) / 9)


def sin9(n):
    return math.sin(2.0 * math.pi * (n % 9) / 9)


def weighted(values, factors):
    total = values[0] * factors[0]
    for value, factor in zip(values[1:], factors[1:]):
        total = total + value * factor
    return total


def dft9(x):
    e = [x[n] + x[9 - n] for n in range(1, 5)]
    o = [x[n] - x[9 - n] for n in range(1, 5)]
    third = e[0] + e[1] + e[3]
    cosines = [x[0] + third + e[2]]
    sines = [None]
    for k in range(1, 5):
        if k == 3:
            cosines.append(x[0] + e[2] - 0.5 * third)
            sines.append(sin9(3) * (o[0] - o[1] + o[3]))
        else:
            cosines.append(x[0] + weighted(e, [cos9(k * n) for n in range(1, 5)]))
            sines.append(weighted(o, [sin9(k * n) for n in range(1, 5)]))
    return cosines, sines


def dft9_adjoint(cosines, sines):
    c, s = cosines, sines
    out = [None] * 9
    out[0] = c[0] + ((c[1] + c[2]) + (c[3] + c[4]))
    for n in range(1, 5):
        if n == 3:
            even = c[0] + c[3] - 0.5 * (c[1] + c[2] + c[4])
            odd = sin9(3) * (s[1] - s[2] + s[4])
        else:
            even = c[0] + weighted(c[1:], [cos9(k * n) for k in range(1, 5)])
            odd = weighted(s[1:], [sin9(k * n) for k in range(1, 5)])
        out[n] = even + odd
        out[9 - n] = even - odd
    return out


def finish72(load, save):
    for part in (0, 1):
        cosines, sines = dft9([load(part, b) for b in range(9)])
        base = part * 9
        save(base, cosines[0])
        for k in range(1, 5):
            save(base + 2 * k - 1, cosines[k])
            save(base + 2 * k, sines[k])
    for k8 in range(3):
        base = 18 + 18 * k8
        cc, cs = dft9([load(2 + 2 * k8, b) for b in range(9)])
        sc, ss = dft9([load(3 + 2 * k8, b) for b in range(9)])
        save(base, cc[0])
        save(base + 1, sc[0])
        for k in range(1, 5):
            at = base + 4 * k - 2
            save(at, cc[k] - ss[k])
            save(at + 1, cc[k] + ss[k])
            save(at + 2, sc[k] + cs[k])
            save(at + 3, sc[k] - cs[k])


def finish72_adjoint(load, save):
    for part in (0, 1):
        base = part * 9
        cosines = [load(base)] + [load(base + 2 * k - 1) for k in range(1, 5)]
        sines = [None] + [load(base + 2 * k) for k in range(1, 5)]
        for b, value in enumerate(dft9_adjoint(cosines, sines)):
            save(part, b, value)
    for k8 in range(3):
        base = 18 + 18 * k8
        cc, sc, cs, ss = [load(base)], [load(base + 1)], [None], [None]
        for k in range(1, 5):
            at = base + 4 * k - 2
            plus, minus, sine_plus, sine_minus = [load(at + i) for i in range(4)]
            cc.append(plus + minus)
            ss.append(minus - plus)
            sc.append(sine_plus + sine_minus)
            cs.append(sine_plus - sine_minus)
        for b, value in enumerate(dft9_adjoint(cc, cs)):
            save(2 + 2 * k8, b, value)
        for b, value in enumerate(dft9_adjoint(sc, ss)):
            save(3 + 2 * k8, b, value)


def point72(a, b):
    return (9 * a + 8 * b) % NG


def split(table):
    high = table.astype(ml_dtypes.bfloat16).astype(np.float64)
    return high, (table - high).astype(ml_dtypes.bfloat16).astype(np.float64)


def from_left(table):
    high, low = split(table)
    wide = np.zeros((80, 256))
    wide[:NG, : 3 * NG] = np.concatenate([high, high, low], axis=1)
    return wide


def from_right(table):
    high, low = split(table)
    return np.block([[high, low], [high, np.zeros_like(low)]])


@functools.cache
def tables():
    at = np.arange(NG)
    basis, freq = [np.full(NG, 1.0)], [0]
    for k in range(1, NG // 2):
        basis += [np.cos(2 * np.pi * k * at / NG), np.sin(2 * np.pi * k * at / NG)]
        freq += [k, k]
    basis.append(np.cos(np.pi * at))
    freq.append(NG // 2)
    basis = np.array(basis)
    basis /= np.sqrt((basis * basis).sum(1, keepdims=True))
    freq = np.array(freq, np.float64)
    eye = np.eye(NG)
    parts = [dft8([eye[point72(a, b)] for a in range(8)]) for b in range(9)]
    slots = [None] * NG
    finish72(lambda part, b: parts[b][part], slots.__setitem__)
    slots = np.array(slots)
    norm = (slots * slots).sum(1)
    spectrum = np.abs(np.fft.fft(slots, axis=1))[:, : NG // 2 + 1]
    freq_y = spectrum.argmax(1).astype(np.float64)
    along_z = np.zeros((128, 128))
    along_z[:NG, :NG] = basis.T
    along_x = basis.reshape(NG, PEERS, PLANES)
    along_x = np.concatenate([along_x[:, :, :8].reshape(NG, -1), along_x[:, :, 8]], axis=1)
    column = np.zeros((8, WIDTH), np.float32)
    column[0, :MERGED] = (freq_y[:, None] ** 2 + freq[None, :] ** 2).reshape(-1)
    column[1, :MERGED] = np.repeat(1.0 / norm, NG)
    freq_x = np.broadcast_to((freq**2)[:, None], (NG, 128)).astype(np.float32)
    wide = np.concatenate(
        [from_right(along_z), from_right(along_z.T), from_left(along_x), from_left(along_x.T)]
    )
    return wide.astype(ml_dtypes.bfloat16), column, freq_x


def take(load, start):
    tile, lane = divmod(start, 128)
    value = load(tile)
    if lane == 0:
        return value
    if lane + NG > 128:
        at = lax.broadcasted_iota(jnp.int32, value.shape, 1)
        value = jnp.where(at >= lane, value, load(tile + 1))
    return pltpu.roll(value, 128 - lane, 1)


def put(store, start, value):
    tile, lane = divmod(start, 128)
    if lane:
        value = pltpu.roll(value, lane, 1)
    end = min(lane + NG, 128)
    store(tile, slice(lane, end), value[:, lane:end])
    if lane + NG > 128:
        store(tile + 1, slice(0, lane + NG - 128), value[:, : lane + NG - 128])


def matmul(a, b):
    return jnp.dot(a, b, preferred_element_type=jnp.float32)


def halves(x):
    high = x.astype(jnp.bfloat16)
    return high, (x - high.astype(jnp.float32)).astype(jnp.bfloat16)


def left(table, x):
    high, low = [part.astype(jnp.float32) for part in halves(x)]
    zeros = jnp.zeros((8, x.shape[1]), jnp.float32)
    operand = jnp.concatenate([high, low, high, zeros], axis=0).astype(jnp.bfloat16)
    return matmul(table[:, 0 : operand.shape[0]], operand)[0:NG]


def kernel(
    bands,
    mask_ref,
    bands_hbm,
    wide_hbm,
    column_hbm,
    freq_hbm,
    out_ref,
    bands_ref,
    wide,
    column_ref,
    freq_ref,
    mixed,
    own,
    own_fold,
    visit,
    visit_fold,
    rho,
    work,
    work2,
    wave,
    wave_fold,
    wave_tail,
    wave_piece,
    recv,
    recv_fold,
    recv_tail,
    back,
    back_fold,
    back_tail,
    field,
    field_fold,
    field_tail,
    field_piece,
    kernel_table,
    kernel_tail,
    total,
    total_fold,
    give,
    give_fold,
    given,
    given_fold,
    visit_send,
    visit_recv,
    give_send,
    give_recv,
    part_send,
    part_recv,
    fold_send,
    fold_recv,
    tail_send,
    tail_recv,
    back_tail_send,
    back_tail_recv,
    load_sem,
):
    me = lax.axis_index("pencil")
    group = lax.axis_index("band")
    me_x, me_y = lax.div(me, 4), lax.rem(me, 4)

    loads = [
        pltpu.make_async_copy(src, dst, load_sem.at[i])
        for i, (src, dst) in enumerate(
            [
                (bands_hbm, bands_ref),
                (wide_hbm, wide),
                (column_hbm, column_ref),
                (freq_hbm, freq_ref),
            ]
        )
    ]
    for load in loads:
        load.start()

    def peer(j):
        return lax.rem(me + j, PEERS)

    def at(dx, dy):
        return lax.rem(me_x + dx, 2) * 4 + lax.rem(me_y + dy + 4, 4)

    def group_at(j):
        return lax.rem(group + j + bands, bands)

    barrier = pltpu.get_barrier_semaphore()
    for j in range(1, PEERS):
        pl.semaphore_signal(barrier, inc=1, device_id={"pencil": peer(j)}, device_id_type=MESH)
    for j in (-2, -1, 1, 2):
        pl.semaphore_signal(barrier, inc=1, device_id={"band": group_at(j)}, device_id_type=MESH)
    loads[0].wait()
    def take_tile(tile, j, q, width):
        lanes = pl.ds(tile * 128, width)
        if width == 128:
            lanes = pl.ds(pl.multiple_of(tile * 128, 128), 128)
        live = slice(0, width)
        for plane in range(PLANES - 1):
            mixed[tile, 2 * plane : 2 * plane + 2, live] = bands_ref[plane, :, lanes]
        for band in range(2):
            own[tile, band * 8 : band * 8 + 8, :] = mixed[tile, pl.ds(band, 8, stride=2), :]
        own_fold[j, 2 * q : 2 * q + 2, live] = bands_ref[PLANES - 1, :, lanes]

    def tile_loop(begin, end, step):
        def run(j, carry):
            step(begin + j, j)
            return carry

        lax.fori_loop(0, end - begin, run, 0)

    mixed[TAIL_TILE] = jnp.zeros((16, 128), jnp.float32)
    own_fold[TAIL_TILE % FOLD, 6:8, :] = jnp.zeros((2, 128), jnp.float32)
    for q, (begin, end) in enumerate(QUARTERS):
        tile_loop(begin, min(end, TAIL_TILE), lambda tile, j, q=q: take_tile(tile, j, q, 128))
    take_tile(TAIL_TILE, TAIL_TILE % FOLD, 3, MERGED - TAIL)

    def own_mask(s, f):
        return mask_ref[0, s, f // 2, f % 2].astype(jnp.float32)

    for m in range(2 * FIELDS):
        value = own_mask(m // FIELDS, m % FIELDS)
        own_fold[MASKS, m : m + 1, :] = jnp.zeros((1, 128), jnp.float32) + value
    pl.semaphore_wait(barrier, PEERS - 1 + 4)

    def remote(src, dst, send, recv, **device):
        return pltpu.make_async_remote_copy(
            src_ref=src,
            dst_ref=dst,
            send_sem=send,
            recv_sem=recv,
            device_id=device,
            device_id_type=MESH,
        )

    odd = lax.rem(group, 2)
    even = odd == 0

    def visitor_group(s):
        near = jnp.where(even, group_at(2), group_at(-1))
        return jnp.where(s == 0, near, jnp.where(even, group_at(1), group_at(-2)))

    def parts(main, fold):
        return [
            *(main.at[pl.ds(begin, end - begin)] for begin, end in QUARTERS),
            fold,
        ]

    def block_copies(src, dst, send, recv, to):
        return [
            remote(one, two, send.at[q], recv.at[q], band=to)
            for q, (one, two) in enumerate(zip(src, dst))
        ]

    def visit_at(s):
        return parts(visit.at[s], visit_fold.at[s])

    own_parts = parts(own, own_fold)

    def give_parts(main, fold):
        return [main.at[0], *parts(main.at[1], fold)]

    def visit_copies(s, src, send, to):
        return block_copies(src, visit_at(s), send, visit_recv.at[s], to)

    def lower_sends():
        return visit_copies(0, own_parts, visit_send.at[0], group_at(-2))

    def lower_relays():
        return visit_copies(0, visit_at(0), visit_send.at[1], group_at(1))

    def upper_sends():
        return visit_copies(1, own_parts, visit_send.at[0], group_at(2)) + visit_copies(
            1, own_parts, visit_send.at[1], group_at(-1)
        )

    @pl.when(even)
    def _():
        for copy in lower_sends():
            copy.start()

    @pl.when(jnp.logical_not(even))
    def _():
        for copy in upper_sends():
            copy.start()

    def kernel_columns(start, width):
        squared = column_ref[0:1, pl.ds(start, width)]
        scale = column_ref[1:2, pl.ds(start, width)]
        return coulomb_scale / (freq_ref[:, 0:1] + squared + screening) * scale

    for load in loads[1:]:
        load.wait()
    kernel_table[...] = kernel_columns(pl.multiple_of(me * OWN, 128), OWN)
    kernel_tail[...] = kernel_columns(TAIL, 128)
    wave_tail[...] = jnp.zeros((2, ROWS, 128), jnp.float32)
    total_fold[...] = jnp.zeros((FOLD + 1, 8, 128), jnp.float32)

    def clear(tile, carry):
        total[tile] = jnp.zeros((16, 128), jnp.float32)
        return carry

    lax.fori_loop(0, TILES, clear, 0)
    for s in range(2):
        for p in range(PEERS):
            back_fold[s, (p + 1) * LAST - 8 : (p + 1) * LAST, :] = jnp.zeros((8, 128), jnp.float32)
            back_tail[s, (p + 1) * PIECE - 8 : (p + 1) * PIECE, :] = jnp.zeros((8, 128), jnp.float32)
        field_tail[s, 32:40, :] = jnp.zeros((8, 128), jnp.float32)
        for f in range(FIELDS):
            wave_piece[s, f, 8:16, :] = jnp.zeros((8, 128), jnp.float32)

    first_band = [slice(band * 8, band * 8 + 8) for band in range(2)]
    field_rows = [slice(f * 8, f * 8 + 8) for f in range(FIELDS)]
    row_at = lax.broadcasted_iota(jnp.int32, (8, 128), 0)
    resident_one = lax.rem(lax.div(row_at, 2), 2) == 1
    visitor_one = lax.rem(row_at, 2) == 1

    def last_planes(s, j, q):
        a = [own_fold[j, 2 * q + band : 2 * q + band + 1, :] for band in range(2)]
        c = [visit_fold[s, j, 2 * q + band : 2 * q + band + 1, :] for band in range(2)]
        wide_a = [jnp.broadcast_to(row, (8, 128)) for row in a]
        wide_c = [jnp.broadcast_to(row, (8, 128)) for row in c]
        return (
            jnp.where(resident_one, wide_a[1], wide_a[0]),
            jnp.where(visitor_one, wide_c[1], wide_c[0]),
        )

    def along_z(start):
        for i in range(2):
            rows = pl.ds(i * 288, 288)
            both = matmul(jnp.concatenate(halves(work[rows, :]), axis=1), wide[start : start + 256, :])
            work2[rows, :] = both[:, :128] + both[:, 128:]

    def place(part, b):
        return slice((part * 9 + b) * 8, (part * 9 + b) * 8 + 8)

    def row_of(t):
        return pl.ds(pl.multiple_of(t * 8, 8), 8)

    def first(s):
        arriving = visit_copies(s, own_parts, visit_send.at[0], group_at(1))
        relays = lower_relays()
        for q in (4, 0, 1, 2, 3):
            arriving[q].wait_recv()

            @pl.when((s == 0) & even)
            def _(q=q):
                relays[q].start()

        def one_row(i, carry):
            t = jnp.where(i == 0, FIELDS, order(jnp.maximum(i - 1, 0)))

            @pl.when(i > 0)
            def _():
                resident, visitor = row_of(lax.div(t, 2)), row_of(lax.rem(t, 2))
                for tile in range(TILES):
                    rho[tile, row_of(t), :] = own[tile, resident, :] * visit[s, tile, visitor, :]

            @pl.when(i == 0)
            def _():
                for q, (begin, end) in enumerate(QUARTERS):

                    def products(tile, j, q=q):
                        phi, chi = last_planes(s, j, q)
                        rho[tile, 32:40, :] = phi * chi

                    tile_loop(begin, end, products)

            for b in range(9):
                starts = [point72(a, b) * NG for a in range(8)]
                values = [take(lambda tile: rho[tile, row_of(t), :], at) for at in starts]
                for part, value in enumerate(dft8(values)):
                    work[place(part, b), :] = value
            along_z(0)

            def load(part, b):
                return work2[place(part, b), :]

            def target(tile, lanes, piece):
                if tile == TAIL_TILE:
                    wave_tail[s, row_of(t), lanes] = piece
                else:
                    wave[s, t, tile * 8 : tile * 8 + 8, lanes] = piece

            def save(slot, value):
                put(target, slot * NG, value)

            finish72(load, save)

            @pl.when(i == 0)
            def _():
                upper = lax.broadcasted_iota(jnp.int32, (8, 128), 0) < FIELDS

                def fold(q, carry):
                    for k in range(3):
                        at_row = pl.multiple_of((q * OWN_TILES + k) * 8, 8)
                        piece = wave[s, FIELDS, pl.ds(at_row, 8), :]
                        if k < 2:
                            below = wave[s, FIELDS, pl.ds(at_row + 24, 8), :]
                            piece = jnp.where(upper, piece, below)
                        to_row = pl.multiple_of(q * LAST + k * 8, 8)
                        wave_fold[s, pl.ds(to_row, 8), :] = piece
                    return carry

                lax.fori_loop(0, PEERS, fold, 0)
                send_fold(0, s)

            @pl.when(i > 0)
            def _():
                send_part(0, s, t)

            return carry

        lax.fori_loop(0, FIELDS + 1, one_row, 0)
        for f in range(FIELDS):
            wave_piece[s, f, 0:8, :] = wave_tail[s, field_rows[f], :]
            wave_piece[s, f, 8:9, :] = wave_tail[s, 32 + f : 33 + f, :]

    part_refs = ((wave, recv), (back, field))
    fold_refs = ((wave_fold, recv_fold), (back_fold, field_fold))
    straight = [(1, 2), (0, 2), (1, 1), (1, 3), (0, 1), (0, 3), (1, 0)]

    def rows_of(index, rows):
        return pl.ds(pl.multiple_of(index * rows, 8), rows)

    def send_part(phase, s, f):
        src, dst = part_refs[phase]
        for dx, dy in straight:
            to = at(dx, dy)
            remote(
                src.at[s, f, rows_of(to, PART)],
                dst.at[s, f, rows_of(me, PART)],
                part_send.at[phase, s],
                part_recv.at[phase, s, f],
                pencil=to,
            ).start()
        dst[s, f, rows_of(me, PART), :] = src[s, f, rows_of(me, PART), :]

    def send_fold(phase, s):
        src, dst = fold_refs[phase]
        for dx, dy in straight:
            to = at(dx, dy)
            remote(
                src.at[s, rows_of(to, LAST)],
                dst.at[s, rows_of(me, LAST)],
                fold_send.at[phase, s],
                fold_recv.at[phase, s],
                pencil=to,
            ).start()
        dst[s, rows_of(me, LAST), :] = src[s, rows_of(me, LAST), :]

    def drain(view, sem):
        pltpu.make_async_copy(view, view, sem).wait()

    def wait_part(phase, s, f):
        drain(part_refs[phase][1].at[s, f, pl.ds(0, 7 * PART)], part_recv.at[phase, s, f])

    def wait_fold(phase, s):
        drain(fold_refs[phase][1].at[s, pl.ds(0, 7 * LAST)], fold_recv.at[phase, s])

    def end_blocks(phase, s):
        parts = part_refs[phase][0].at[s, pl.ds(0, FIELDS), pl.ds(0, 7 * PART)]
        drain(parts, part_send.at[phase, s])
        drain(fold_refs[phase][0].at[s, pl.ds(0, 7 * LAST)], fold_send.at[phase, s])

    def piece_of(ref, s, index):
        return ref.at[s, pl.ds(pl.multiple_of(index * PIECE, 8), PIECE), :]

    def owner_of(s, f):
        return FIELDS * s + f

    def tail_copy(s, f, distance):
        return remote(
            wave_piece.at[s, f],
            piece_of(recv_tail, s, me),
            tail_send.at[s, f],
            tail_recv.at[s, distance],
            pencil=owner_of(s, f),
        )

    def second(s):
        wait_fold(0, s)

        def last_rows(f, tile):
            return pl.ds(tile % 3 * 8 + FIELDS * (tile // 3) + f, PEERS, stride=LAST)

        def one_field(i, carry):
            f = order(i)
            wait_part(0, s, f)
            columns = []
            for tile in range(OWN_TILES):
                starts = [p * PART + tile * 8 for p in range(PEERS)]
                rows = [recv[s, f, start : start + 8, :] for start in starts]
                rows.append(recv_fold[s, last_rows(f, tile), :])
                columns.append(jnp.concatenate(rows, axis=0))
            spectrum = left(wide[512:592, :], jnp.concatenate(columns, axis=1))
            result = left(wide[592:672, :], spectrum * kernel_table[...])
            for tile in range(OWN_TILES):
                lanes = slice(tile * 128, tile * 128 + 128)
                for p in range(PEERS):
                    start = p * PART + tile * 8
                    back[s, f, start : start + 8, :] = result[p * 8 : p * 8 + 8, lanes]
                back_fold[s, last_rows(f, tile), :] = result[64:72, lanes]
            send_part(1, s, f)
            return carry

        lax.fori_loop(0, FIELDS, one_field, 0)
        send_fold(1, s)

    def give_copies(s):
        return block_copies(
            give_parts(give.at[s], give_fold.at[s]),
            give_parts(given.at[odd], given_fold.at[odd]),
            give_send.at[s],
            give_recv.at[odd],
            visitor_group(s),
        )

    def given_copies(source):
        return block_copies(
            give_parts(give.at[0], give_fold.at[0]),
            give_parts(given.at[source], given_fold.at[source]),
            give_send.at[0],
            give_recv.at[source],
            visitor_group(0),
        )

    def join():
        for copy in given_copies(1):
            copy.wait_recv()

        def add(tile, carry):
            for band in range(2):
                give[0, band, tile] += given[1, band, tile]
                given[1, band, tile] = jnp.zeros((8, 128), jnp.float32)
            return carry

        lax.fori_loop(0, TILES, add, 0)
        give_fold[0] = give_fold[0] + given_fold[1]
        given_fold[1] = jnp.zeros((FOLD + 1, 8, 128), jnp.float32)
        for copy in give_copies(0):
            copy.start()

    def order(i):
        return lax.rem(2 * i, FIELDS) + lax.div(i, 2)

    def pair_weights(s):
        weights = []
        for f in range(FIELDS):
            g = 2 * (f % 2) + f // 2
            above = visit_fold[s, MASKS, FIELDS + g : FIELDS + g + 1, :]
            same = visit_fold[s, MASKS, g : g + 1, :]
            mine = own_fold[MASKS, FIELDS + f : FIELDS + f + 1, :]
            row = jnp.where(s == 0, jnp.where(even, above, same), jnp.where(even, same, mine))
            weights.append(jnp.broadcast_to(row, (8, 128)))
        return weights

    def third(s):
        weights = pair_weights(s)
        leaving = give_copies(s)
        held = (s == 0) & even

        def leave(which):
            @pl.when(jnp.logical_not(held))
            def _():
                for part in which:
                    leaving[part].start()

        def gather_band(c, begin, end):
            def gather(tile, j):
                chi = visit[s, tile, first_band[c], :]
                terms = jnp.zeros((8, 128), jnp.float32)
                for a in range(2):
                    value = rho[tile, field_rows[2 * a + c], :] * weights[2 * a + c]
                    total[tile, first_band[a], :] += value * chi
                    terms = terms + value * own[tile, first_band[a], :]
                give[s, c, tile] = terms

            tile_loop(begin, end, gather)

        def one_row(i, carry):
            t = jnp.where(i == FIELDS, FIELDS, order(jnp.minimum(i, FIELDS - 1)))

            @pl.when((s == 1) & even & (i == 2))
            def _():
                join()

            @pl.when(t < FIELDS)
            def _():
                wait_part(1, s, t)

            @pl.when(t == FIELDS)
            def _():
                wait_fold(1, s)

                def unfold(q, carry):
                    for k in range(OWN_TILES):
                        from_row = pl.multiple_of(q * LAST + k % 3 * 8, 8)
                        value = field_fold[s, pl.ds(from_row, 8), :]
                        value = pltpu.roll(value, FIELDS, 0) if k > 2 else value
                        to_row = pl.multiple_of((q * OWN_TILES + k) * 8, 8)
                        field[s, FIELDS, pl.ds(to_row, 8), :] = value
                    return carry

                lax.fori_loop(0, PEERS, unfold, 0)

            def source(tile):
                if tile == TAIL_TILE:
                    return field_tail[s, row_of(t), :]
                return field[s, t, tile * 8 : tile * 8 + 8, :]

            def load(slot):
                return take(source, slot * NG)

            def save(part, b, value):
                work[place(part, b), :] = value

            finish72_adjoint(load, save)
            along_z(256)

            def target(tile, lanes, piece):
                rho[tile, row_of(t), lanes] = piece

            for b in range(9):
                values = dft8_adjoint([work2[place(part, b), :] for part in range(8)])
                for a, value in enumerate(values):
                    put(target, point72(a, b) * NG, value)

            @pl.when(i == 1)
            def _():
                gather_band(0, 0, TILES)
                leave([0])

            return carry

        lax.fori_loop(0, FIELDS + 1, one_row, 0)
        last_weight = weights[3]
        for f in range(3):
            last_weight = jnp.where(row_at == f, weights[f], last_weight)

        for q, (begin, end) in enumerate(QUARTERS):
            gather_band(1, begin, end)
            leave([1 + q])

            def gather_last(tile, j, q=q):
                phi, chi = last_planes(s, j, q)
                value = rho[tile, 32:40, :] * last_weight
                stay, leave = value * chi, value * phi
                stay = stay + pltpu.roll(stay, 7, 0)
                leave = leave + pltpu.roll(leave, 6, 0)
                for band in range(2):
                    row = slice(2 * q + band, 2 * q + band + 1)
                    total_fold[j, row, :] += stay[2 * band : 2 * band + 1]
                    give_fold[s, j, row, :] = leave[band : band + 1]

            tile_loop(begin, end, gather_last)
        leave([5])

    def tail_back(s, f, j):
        return remote(
            piece_of(back_tail, s, peer(j)),
            field_piece.at[s, f],
            back_tail_send.at[s, j],
            back_tail_recv.at[s, f],
            pencil=peer(j),
        )

    def send_tail(s):
        for f in range(FIELDS):
            owner = owner_of(s, f)

            @pl.when(me == owner)
            def _(f=f, owner=owner):
                recv_tail[s, rows_of(owner, PIECE), :] = wave_piece[s, f]

            @pl.when(me != owner)
            def _(f=f, owner=owner):
                tail_copy(s, f, lax.rem(owner - me + PEERS, PEERS)).start()

    def turn_tail(s):
        owned = lax.div(me, FIELDS) == s

        @pl.when(owned)
        def _():
            for j in range(1, PEERS):
                tail_copy(s, 0, j).wait_recv()
            parts = [pl.ds(p * PIECE, 8) for p in range(PEERS)] + [pl.ds(8, PEERS, stride=PIECE)]
            block = jnp.concatenate([recv_tail[s, part, :] for part in parts], axis=0)
            spectrum = left(wide[512:592, :], block) * kernel_tail[...]
            result = left(wide[592:672, :], spectrum)
            for i, part in enumerate(parts):
                back_tail[s, part, :] = result[i * 8 : i * 8 + 8, :]
            mine = lax.rem(me, FIELDS)
            for j in range(1, PEERS):
                tail_back(s, mine, j).start()
            field_piece[s, mine] = back_tail[s, pl.ds(pl.multiple_of(me * PIECE, 8), PIECE), :]

    def end_tail(s):
        for f in range(FIELDS):
            owner = owner_of(s, f)

            @pl.when(me != owner)
            def _(f=f, owner=owner):
                tail_copy(s, f, lax.rem(owner - me + PEERS, PEERS)).wait_send()
                tail_back(s, f, 1).wait_recv()

            field_tail[s, field_rows[f], :] = field_piece[s, f, 0:8, :]
            field_tail[s, 32 + f : 33 + f, :] = field_piece[s, f, 8:9, :]

        @pl.when(lax.div(me, FIELDS) == s)
        def _():
            for j in range(1, PEERS):
                tail_back(s, lax.rem(me, FIELDS), j).wait_send()

    def slots(*stages):
        def run(s, carry):
            for stage in stages:
                stage(s)
            return carry

        lax.fori_loop(0, 2, run, 0)

    slots(first, send_tail)
    slots(second, turn_tail)
    slots(end_tail, third)

    def wait_given(which):
        for part in which:
            given_copies(0)[part].wait_recv()

            @pl.when(jnp.logical_not(even))
            def _(part=part):
                given_copies(1)[part].wait_recv()

    for q, (begin, end) in enumerate(QUARTERS):
        wait_given([0, 1] if q == 0 else [1 + q])

        def result(tile, j, width=128):
            lanes = pl.ds(tile * 128, width)
            if width == 128:
                lanes = pl.ds(pl.multiple_of(tile * 128, 128), 128)
            for rows, band in zip(first_band, range(2)):
                term = -(total[tile, rows, :] + given[0, band, tile] + given[1, band, tile])
                mixed[tile, pl.ds(band, 8, stride=2), :] = term
            for plane in range(PLANES - 1):
                piece = mixed[tile, 2 * plane : 2 * plane + 2, 0:width]
                out_ref[plane, :, lanes] = piece

        tile_loop(begin, min(end, TAIL_TILE), result)
        if end > TAIL_TILE:
            result(TAIL_TILE, 0, MERGED - TAIL)
    wait_given([5])
    for q, (begin, end) in enumerate(QUARTERS):

        def last_result(tile, j, q=q, width=128):
            lanes = pl.ds(tile * 128, width)
            if width == 128:
                lanes = pl.ds(pl.multiple_of(tile * 128, 128), 128)
            rows = slice(2 * q, 2 * q + 2)
            term = total_fold[j, rows, :] + given_fold[0, j, rows, :] + given_fold[1, j, rows, :]
            out_ref[PLANES - 1, :, lanes] = -term[:, 0:width]

        tile_loop(begin, min(end, TAIL_TILE), last_result)
        if end > TAIL_TILE:
            last_result(TAIL_TILE, TAIL_TILE - begin, width=MERGED - TAIL)

    @pl.when(even)
    def _():
        for copy in lower_sends() + lower_relays():
            copy.wait_send()

    @pl.when(jnp.logical_not(even))
    def _():
        for copy in upper_sends():
            copy.wait_send()

    for s in range(2):
        for copy in give_copies(s):
            copy.wait_send()
    for phase in range(2):
        for s in range(2):
            end_blocks(phase, s)


def body(bands, orbitals, pair_mask):
    hbm = pl.BlockSpec(memory_space=pltpu.HBM)
    smem = pl.BlockSpec(memory_space=pltpu.SMEM)
    consts = [jnp.asarray(table) for table in tables()]
    dma = pltpu.SemaphoreType.DMA

    def buffer(*shape):
        return pltpu.VMEM(shape, jnp.float32)

    out = pl.pallas_call(
        functools.partial(kernel, bands),
        out_shape=jax.ShapeDtypeStruct((PLANES, 2, MERGED), jnp.float32),
        in_specs=[smem] + [hbm] * (1 + len(consts)),
        out_specs=pl.BlockSpec(memory_space=pltpu.VMEM),
        scratch_shapes=[
            buffer(PLANES, 2, MERGED),
            pltpu.VMEM(consts[0].shape, jnp.bfloat16),
            buffer(*consts[1].shape),
            buffer(*consts[2].shape),
            buffer(TILES, 16, 128),
            buffer(TILES, 16, 128),
            buffer(FOLD + 1, 8, 128),
            buffer(2, TILES, 16, 128),
            buffer(2, FOLD + 1, 8, 128),
            buffer(TILES, ROWS, 128),
            buffer(NG * 8, 128),
            buffer(NG * 8, 128),
            buffer(2, FIELDS + 1, PEERS * PART, 128),
            buffer(2, PEERS * LAST, 128),
            buffer(2, ROWS, 128),
            buffer(2, FIELDS, PIECE, 128),
            buffer(2, FIELDS, PEERS * PART, 128),
            buffer(2, PEERS * LAST, 128),
            buffer(2, PEERS * PIECE, 128),
            buffer(2, FIELDS, PEERS * PART, 128),
            buffer(2, PEERS * LAST, 128),
            buffer(2, PEERS * PIECE, 128),
            buffer(2, FIELDS + 1, PEERS * PART, 128),
            buffer(2, PEERS * LAST, 128),
            buffer(2, ROWS, 128),
            buffer(2, FIELDS, PIECE, 128),
            buffer(NG, OWN),
            buffer(NG, 128),
            buffer(TILES, 16, 128),
            buffer(FOLD + 1, 8, 128),
            buffer(2, 2, TILES, 8, 128),
            buffer(2, FOLD + 1, 8, 128),
            buffer(2, 2, TILES, 8, 128),
            buffer(2, FOLD + 1, 8, 128),
            dma((2, 5)),
            dma((2, 5)),
            dma((2, 6)),
            dma((2, 6)),
            dma((2, 2)),
            dma((2, 2, FIELDS)),
            dma((2, 2)),
            dma((2, 2)),
            dma((2, FIELDS)),
            dma((2, PEERS)),
            dma((2, PEERS)),
            dma((2, FIELDS)),
            dma((4,)),
        ],
        compiler_params=pltpu.CompilerParams(
            collective_id=0, has_side_effects=True, vmem_limit_bytes=64 * 1024 * 1024 - 65536
        ),
    )(pair_mask, orbitals.transpose(1, 0, 2), *consts)
    return out.transpose(1, 0, 2)


def solution(mesh):
    return jax.shard_map(
        functools.partial(body, mesh.shape["band"]),
        mesh=mesh,
        in_specs=(P("band", "pencil", None), P("band", None, None, None)),
        out_specs=P("band", "pencil", None),
        check_vma=False,
    )
```

```python
import functools
import math

import jax
import jax.numpy as jnp
import ml_dtypes
import numpy as np
from jax import lax
from jax.experimental import pallas as pl
from jax.experimental.pallas import tpu as pltpu
from jax.sharding import PartitionSpec as P

MESH = pl.DeviceIdType.MESH
NG = 72
PLANES = 9
PEERS = 8
FIELDS = 4
ROWS = 40
PART = 40
LAST = 24
MERGED = NG * NG
WIDTH = 5248
OWN = 640
TAIL = PEERS * OWN
PIECE = 16
FOLD = 11
MASKS = FOLD
QUARTERS = [(q * FOLD, min((q + 1) * FOLD, 41)) for q in range(4)]
TILES = WIDTH // 128
OWN_TILES = OWN // 128
TAIL_TILE = TILES - 1
coulomb_scale = 20.0
screening = 0.25
HALF = math.sqrt(0.5)


def dft8(x):
    a = [x[j] + x[j + 4] for j in range(4)]
    b = [x[j] - x[j + 4] for j in range(4)]
    e, o = a[0] + a[2], a[1] + a[3]
    u, v = HALF * (b[1] - b[3]), HALF * (b[1] + b[3])
    return [e + o, e - o, b[0] + u, v + b[2], a[0] - a[2], a[1] - a[3], b[0] - u, v - b[2]]


def dft8_adjoint(c):
    p, q = c[0] + c[1], c[0] - c[1]
    a = [p + c[4], q + c[5], p - c[4], q - c[5]]
    d, s = HALF * (c[2] - c[6]), HALF * (c[3] + c[7])
    b = [c[2] + c[6], d + s, c[3] - c[7], s - d]
    return [a[j] + b[j] for j in range(4)] + [a[j] - b[j] for j in range(4)]


def cos9(n):
    return math.cos(2.0 * math.pi * (n % 9) / 9)


def sin9(n):
    return math.sin(2.0 * math.pi * (n % 9) / 9)


def weighted(values, factors):
    total = values[0] * factors[0]
    for value, factor in zip(values[1:], factors[1:]):
        total = total + value * factor
    return total


def dft9(x):
    e = [x[n] + x[9 - n] for n in range(1, 5)]
    o = [x[n] - x[9 - n] for n in range(1, 5)]
    third = e[0] + e[1] + e[3]
    cosines = [x[0] + third + e[2]]
    sines = [None]
    for k in range(1, 5):
        if k == 3:
            cosines.append(x[0] + e[2] - 0.5 * third)
            sines.append(sin9(3) * (o[0] - o[1] + o[3]))
        else:
            cosines.append(x[0] + weighted(e, [cos9(k * n) for n in range(1, 5)]))
            sines.append(weighted(o, [sin9(k * n) for n in range(1, 5)]))
    return cosines, sines


def dft9_adjoint(cosines, sines):
    c, s = cosines, sines
    out = [None] * 9
    out[0] = c[0] + ((c[1] + c[2]) + (c[3] + c[4]))
    for n in range(1, 5):
        if n == 3:
            even = c[0] + c[3] - 0.5 * (c[1] + c[2] + c[4])
            odd = sin9(3) * (s[1] - s[2] + s[4])
        else:
            even = c[0] + weighted(c[1:], [cos9(k * n) for k in range(1, 5)])
            odd = weighted(s[1:], [sin9(k * n) for k in range(1, 5)])
        out[n] = even + odd
        out[9 - n] = even - odd
    return out


def finish72(load, save):
    for part in (0, 1):
        cosines, sines = dft9([load(part, b) for b in range(9)])
        base = part * 9
        save(base, cosines[0])
        for k in range(1, 5):
            save(base + 2 * k - 1, cosines[k])
            save(base + 2 * k, sines[k])
    for k8 in range(3):
        base = 18 + 18 * k8
        cc, cs = dft9([load(2 + 2 * k8, b) for b in range(9)])
        sc, ss = dft9([load(3 + 2 * k8, b) for b in range(9)])
        save(base, cc[0])
        save(base + 1, sc[0])
        for k in range(1, 5):
            at = base + 4 * k - 2
            save(at, cc[k] - ss[k])
            save(at + 1, cc[k] + ss[k])
            save(at + 2, sc[k] + cs[k])
            save(at + 3, sc[k] - cs[k])


def finish72_adjoint(load, save):
    for part in (0, 1):
        base = part * 9
        cosines = [load(base)] + [load(base + 2 * k - 1) for k in range(1, 5)]
        sines = [None] + [load(base + 2 * k) for k in range(1, 5)]
        for b, value in enumerate(dft9_adjoint(cosines, sines)):
            save(part, b, value)
    for k8 in range(3):
        base = 18 + 18 * k8
        cc, sc, cs, ss = [load(base)], [load(base + 1)], [None], [None]
        for k in range(1, 5):
            at = base + 4 * k - 2
            plus, minus, sine_plus, sine_minus = [load(at + i) for i in range(4)]
            cc.append(plus + minus)
            ss.append(minus - plus)
            sc.append(sine_plus + sine_minus)
            cs.append(sine_plus - sine_minus)
        for b, value in enumerate(dft9_adjoint(cc, cs)):
            save(2 + 2 * k8, b, value)
        for b, value in enumerate(dft9_adjoint(sc, ss)):
            save(3 + 2 * k8, b, value)


def point72(a, b):
    return (9 * a + 8 * b) % NG


def split(table):
    high = table.astype(ml_dtypes.bfloat16).astype(np.float64)
    return high, (table - high).astype(ml_dtypes.bfloat16).astype(np.float64)


def from_left(table):
    high, low = split(table)
    wide = np.zeros((80, 256))
    wide[:NG, : 3 * NG] = np.concatenate([high, high, low], axis=1)
    return wide


def from_right(table):
    high, low = split(table)
    return np.block([[high, low], [high, np.zeros_like(low)]])


@functools.cache
def tables():
    at = np.arange(NG)
    basis, freq = [np.full(NG, 1.0)], [0]
    for k in range(1, NG // 2):
        basis += [np.cos(2 * np.pi * k * at / NG), np.sin(2 * np.pi * k * at / NG)]
        freq += [k, k]
    basis.append(np.cos(np.pi * at))
    freq.append(NG // 2)
    basis = np.array(basis)
    basis /= np.sqrt((basis * basis).sum(1, keepdims=True))
    freq = np.array(freq, np.float64)
    eye = np.eye(NG)
    parts = [dft8([eye[point72(a, b)] for a in range(8)]) for b in range(9)]
    slots = [None] * NG
    finish72(lambda part, b: parts[b][part], slots.__setitem__)
    slots = np.array(slots)
    norm = (slots * slots).sum(1)
    spectrum = np.abs(np.fft.fft(slots, axis=1))[:, : NG // 2 + 1]
    freq_y = spectrum.argmax(1).astype(np.float64)
    along_z = np.zeros((128, 128))
    along_z[:NG, :NG] = basis.T
    along_x = basis.reshape(NG, PEERS, PLANES)
    along_x = np.concatenate([along_x[:, :, :8].reshape(NG, -1), along_x[:, :, 8]], axis=1)
    column = np.zeros((8, WIDTH), np.float32)
    column[0, :MERGED] = (freq_y[:, None] ** 2 + freq[None, :] ** 2).reshape(-1)
    column[1, :MERGED] = np.repeat(1.0 / norm, NG)
    freq_x = np.broadcast_to((freq**2)[:, None], (NG, 128)).astype(np.float32)
    wide = np.concatenate(
        [from_right(along_z), from_right(along_z.T), from_left(along_x), from_left(along_x.T)]
    )
    return wide.astype(ml_dtypes.bfloat16), column, freq_x


def take(load, start):
    tile, lane = divmod(start, 128)
    value = load(tile)
    if lane == 0:
        return value
    if lane + NG > 128:
        at = lax.broadcasted_iota(jnp.int32, value.shape, 1)
        value = jnp.where(at >= lane, value, load(tile + 1))
    return pltpu.roll(value, 128 - lane, 1)


def put(store, start, value):
    tile, lane = divmod(start, 128)
    if lane:
        value = pltpu.roll(value, lane, 1)
    end = min(lane + NG, 128)
    store(tile, slice(lane, end), value[:, lane:end])
    if lane + NG > 128:
        store(tile + 1, slice(0, lane + NG - 128), value[:, : lane + NG - 128])


def matmul(a, b):
    return jnp.dot(a, b, preferred_element_type=jnp.float32)


def halves(x):
    high = x.astype(jnp.bfloat16)
    return high, (x - high.astype(jnp.float32)).astype(jnp.bfloat16)


def left(table, x):
    high, low = [part.astype(jnp.float32) for part in halves(x)]
    zeros = jnp.zeros((8, x.shape[1]), jnp.float32)
    operand = jnp.concatenate([high, low, high, zeros], axis=0).astype(jnp.bfloat16)
    return matmul(table[:, 0 : operand.shape[0]], operand)[0:NG]


def kernel(
    bands,
    mask_ref,
    bands_hbm,
    wide_hbm,
    column_hbm,
    freq_hbm,
    out_ref,
    bands_ref,
    wide,
    column_ref,
    freq_ref,
    mixed,
    own,
    own_fold,
    visit,
    visit_fold,
    rho,
    work,
    work2,
    wave,
    wave_fold,
    wave_tail,
    wave_piece,
    recv,
    recv_fold,
    recv_tail,
    back,
    back_fold,
    back_tail,
    field,
    field_fold,
    field_tail,
    field_piece,
    kernel_table,
    kernel_tail,
    total,
    total_fold,
    base,
    base_fold,
    give,
    give_fold,
    given,
    given_fold,
    visit_send,
    visit_recv,
    give_send,
    give_recv,
    part_send,
    part_recv,
    fold_send,
    fold_recv,
    tail_send,
    tail_recv,
    back_tail_send,
    back_tail_recv,
    load_sem,
):
    me = lax.axis_index("pencil")
    group = lax.axis_index("band")
    me_x, me_y = lax.div(me, 4), lax.rem(me, 4)

    loads = [
        pltpu.make_async_copy(src, dst, load_sem.at[i])
        for i, (src, dst) in enumerate(
            [
                (bands_hbm, bands_ref),
                (wide_hbm, wide),
                (column_hbm, column_ref),
                (freq_hbm, freq_ref),
            ]
        )
    ]
    for load in loads:
        load.start()

    def peer(j):
        return lax.rem(me + j, PEERS)

    def at(dx, dy):
        return lax.rem(me_x + dx, 2) * 4 + lax.rem(me_y + dy + 4, 4)

    def group_at(j):
        return lax.rem(group + j + bands, bands)

    barrier = pltpu.get_barrier_semaphore()
    for j in range(1, PEERS):
        pl.semaphore_signal(barrier, inc=1, device_id={"pencil": peer(j)}, device_id_type=MESH)
    for j in (-2, -1, 1, 2):
        pl.semaphore_signal(barrier, inc=1, device_id={"band": group_at(j)}, device_id_type=MESH)
    loads[0].wait()
    def take_tile(tile, j, q, width):
        lanes = pl.ds(tile * 128, width)
        if width == 128:
            lanes = pl.ds(pl.multiple_of(tile * 128, 128), 128)
        live = slice(0, width)
        for plane in range(PLANES - 1):
            mixed[tile, 2 * plane : 2 * plane + 2, live] = bands_ref[plane, :, lanes]
        for band in range(2):
            own[tile, band * 8 : band * 8 + 8, :] = mixed[tile, pl.ds(band, 8, stride=2), :]
        own_fold[j, 2 * q : 2 * q + 2, live] = bands_ref[PLANES - 1, :, lanes]

    def tile_loop(begin, end, step):
        def run(j, carry):
            step(begin + j, j)
            return carry

        lax.fori_loop(0, end - begin, run, 0)

    mixed[TAIL_TILE] = jnp.zeros((16, 128), jnp.float32)
    own_fold[TAIL_TILE % FOLD, 6:8, :] = jnp.zeros((2, 128), jnp.float32)
    for q, (begin, end) in enumerate(QUARTERS):
        tile_loop(begin, min(end, TAIL_TILE), lambda tile, j, q=q: take_tile(tile, j, q, 128))
    take_tile(TAIL_TILE, TAIL_TILE % FOLD, 3, MERGED - TAIL)

    def own_mask(s, f):
        return mask_ref[0, s, f // 2, f % 2].astype(jnp.float32)

    for m in range(2 * FIELDS):
        value = own_mask(m // FIELDS, m % FIELDS)
        own_fold[MASKS, m : m + 1, :] = jnp.zeros((1, 128), jnp.float32) + value
    pl.semaphore_wait(barrier, PEERS - 1 + 4)

    def remote(src, dst, send, recv, **device):
        return pltpu.make_async_remote_copy(
            src_ref=src,
            dst_ref=dst,
            send_sem=send,
            recv_sem=recv,
            device_id=device,
            device_id_type=MESH,
        )

    even = lax.rem(group, 2) == 0

    def terms_group(s):
        near = jnp.where(even, group_at(1), group_at(-1))
        return jnp.where(s == 0, near, jnp.where(even, group_at(2), group_at(-2)))

    def parts(main, fold):
        return [
            *(main.at[pl.ds(begin, end - begin)] for begin, end in QUARTERS),
            fold,
        ]

    def block_copies(src, dst, send, recv, to):
        return [
            remote(one, two, send.at[q], recv.at[q], band=to)
            for q, (one, two) in enumerate(zip(src, dst))
        ]

    def visit_at(s):
        return parts(visit.at[s], visit_fold.at[s])

    own_parts = parts(own, own_fold)

    def give_parts(main, fold):
        return [main.at[0], *parts(main.at[1], fold)]

    def visit_copies(s, src, send, to):
        return block_copies(src, visit_at(s), send, visit_recv.at[s], to)

    def near_sends():
        return visit_copies(0, own_parts, visit_send.at[0], group_at(-1))

    def far_sends():
        to = jnp.where(even, group_at(-2), group_at(2))
        return visit_copies(1, own_parts, visit_send.at[1], to)

    for copy in near_sends():
        copy.start()

    @pl.when(jnp.logical_not(even))
    def _():
        for copy in far_sends():
            copy.start()

    def kernel_columns(start, width):
        squared = column_ref[0:1, pl.ds(start, width)]
        scale = column_ref[1:2, pl.ds(start, width)]
        return coulomb_scale / (freq_ref[:, 0:1] + squared + screening) * scale

    for load in loads[1:]:
        load.wait()
    kernel_table[...] = kernel_columns(pl.multiple_of(me * OWN, 128), OWN)
    kernel_tail[...] = kernel_columns(TAIL, 128)
    wave_tail[...] = jnp.zeros((2, ROWS, 128), jnp.float32)
    total_fold[...] = jnp.zeros((FOLD + 1, 8, 128), jnp.float32)
    base_fold[...] = jnp.zeros((FOLD + 1, 8, 128), jnp.float32)

    def clear(tile, carry):
        total[tile] = jnp.zeros((16, 128), jnp.float32)
        base[:, tile] = jnp.zeros((2, 8, 128), jnp.float32)
        return carry

    lax.fori_loop(0, TILES, clear, 0)
    for s in range(2):
        for p in range(PEERS):
            back_fold[s, (p + 1) * LAST - 8 : (p + 1) * LAST, :] = jnp.zeros((8, 128), jnp.float32)
            back_tail[s, (p + 1) * PIECE - 8 : (p + 1) * PIECE, :] = jnp.zeros((8, 128), jnp.float32)
        field_tail[s, 32:40, :] = jnp.zeros((8, 128), jnp.float32)
        for f in range(FIELDS):
            wave_piece[s, f, 8:16, :] = jnp.zeros((8, 128), jnp.float32)

    first_band = [slice(band * 8, band * 8 + 8) for band in range(2)]
    field_rows = [slice(f * 8, f * 8 + 8) for f in range(FIELDS)]
    row_at = lax.broadcasted_iota(jnp.int32, (8, 128), 0)
    resident_one = lax.rem(lax.div(row_at, 2), 2) == 1
    visitor_one = lax.rem(row_at, 2) == 1

    def last_planes(s, j, q):
        a = [own_fold[j, 2 * q + band : 2 * q + band + 1, :] for band in range(2)]
        c = [visit_fold[s, j, 2 * q + band : 2 * q + band + 1, :] for band in range(2)]
        wide_a = [jnp.broadcast_to(row, (8, 128)) for row in a]
        wide_c = [jnp.broadcast_to(row, (8, 128)) for row in c]
        return (
            jnp.where(resident_one, wide_a[1], wide_a[0]),
            jnp.where(visitor_one, wide_c[1], wide_c[0]),
        )

    def along_z(start):
        for i in range(2):
            rows = pl.ds(i * 288, 288)
            both = matmul(jnp.concatenate(halves(work[rows, :]), axis=1), wide[start : start + 256, :])
            work2[rows, :] = both[:, :128] + both[:, 128:]

    def place(part, b):
        return slice((part * 9 + b) * 8, (part * 9 + b) * 8 + 8)

    def row_of(t):
        return pl.ds(pl.multiple_of(t * 8, 8), 8)

    def first(s):
        arriving = visit_copies(s, own_parts, visit_send.at[0], group_at(1))
        for q in (4, 0, 1, 2, 3):
            arriving[q].wait_recv()

        def one_row(i, carry):
            t = jnp.where(i == 0, FIELDS, order(jnp.maximum(i - 1, 0)))

            @pl.when((s == 0) & even & (i == 2))
            def _():
                for copy in far_sends():
                    copy.start()

            @pl.when(i > 0)
            def _():
                resident, visitor = row_of(lax.div(t, 2)), row_of(lax.rem(t, 2))
                for tile in range(TILES):
                    rho[tile, row_of(t), :] = own[tile, resident, :] * visit[s, tile, visitor, :]

            @pl.when(i == 0)
            def _():
                for q, (begin, end) in enumerate(QUARTERS):

                    def products(tile, j, q=q):
                        phi, chi = last_planes(s, j, q)
                        rho[tile, 32:40, :] = phi * chi

                    tile_loop(begin, end, products)

            for b in range(9):
                starts = [point72(a, b) * NG for a in range(8)]
                values = [take(lambda tile: rho[tile, row_of(t), :], at) for at in starts]
                for part, value in enumerate(dft8(values)):
                    work[place(part, b), :] = value
            along_z(0)

            def load(part, b):
                return work2[place(part, b), :]

            def target(tile, lanes, piece):
                if tile == TAIL_TILE:
                    wave_tail[s, row_of(t), lanes] = piece
                else:
                    wave[s, t, tile * 8 : tile * 8 + 8, lanes] = piece

            def save(slot, value):
                put(target, slot * NG, value)

            finish72(load, save)

            @pl.when(i == 0)
            def _():
                upper = lax.broadcasted_iota(jnp.int32, (8, 128), 0) < FIELDS

                def fold(q, carry):
                    for k in range(3):
                        at_row = pl.multiple_of((q * OWN_TILES + k) * 8, 8)
                        piece = wave[s, FIELDS, pl.ds(at_row, 8), :]
                        if k < 2:
                            below = wave[s, FIELDS, pl.ds(at_row + 24, 8), :]
                            piece = jnp.where(upper, piece, below)
                        to_row = pl.multiple_of(q * LAST + k * 8, 8)
                        wave_fold[s, pl.ds(to_row, 8), :] = piece
                    return carry

                lax.fori_loop(0, PEERS, fold, 0)
                send_fold(0, s)

            @pl.when(i > 0)
            def _():
                send_part(0, s, t)

            return carry

        lax.fori_loop(0, FIELDS + 1, one_row, 0)
        for f in range(FIELDS):
            wave_piece[s, f, 0:8, :] = wave_tail[s, field_rows[f], :]
            wave_piece[s, f, 8:9, :] = wave_tail[s, 32 + f : 33 + f, :]

    part_refs = ((wave, recv), (back, field))
    fold_refs = ((wave_fold, recv_fold), (back_fold, field_fold))
    straight = [(1, 2), (0, 2), (1, 1), (1, 3), (0, 1), (0, 3), (1, 0)]

    def rows_of(index, rows):
        return pl.ds(pl.multiple_of(index * rows, 8), rows)

    def send_part(phase, s, f):
        src, dst = part_refs[phase]
        for dx, dy in straight:
            to = at(dx, dy)
            remote(
                src.at[s, f, rows_of(to, PART)],
                dst.at[s, f, rows_of(me, PART)],
                part_send.at[phase, s],
                part_recv.at[phase, s, f],
                pencil=to,
            ).start()
        dst[s, f, rows_of(me, PART), :] = src[s, f, rows_of(me, PART), :]

    def send_fold(phase, s):
        src, dst = fold_refs[phase]
        for dx, dy in straight:
            to = at(dx, dy)
            remote(
                src.at[s, rows_of(to, LAST)],
                dst.at[s, rows_of(me, LAST)],
                fold_send.at[phase, s],
                fold_recv.at[phase, s],
                pencil=to,
            ).start()
        dst[s, rows_of(me, LAST), :] = src[s, rows_of(me, LAST), :]

    def drain(view, sem):
        pltpu.make_async_copy(view, view, sem).wait()

    def wait_part(phase, s, f):
        drain(part_refs[phase][1].at[s, f, pl.ds(0, 7 * PART)], part_recv.at[phase, s, f])

    def wait_fold(phase, s):
        drain(fold_refs[phase][1].at[s, pl.ds(0, 7 * LAST)], fold_recv.at[phase, s])

    def end_blocks(phase, s):
        parts = part_refs[phase][0].at[s, pl.ds(0, FIELDS), pl.ds(0, 7 * PART)]
        drain(parts, part_send.at[phase, s])
        drain(fold_refs[phase][0].at[s, pl.ds(0, 7 * LAST)], fold_send.at[phase, s])

    def piece_of(ref, s, index):
        return ref.at[s, pl.ds(pl.multiple_of(index * PIECE, 8), PIECE), :]

    def owner_of(s, f):
        return FIELDS * s + f

    def tail_copy(s, f, distance):
        return remote(
            wave_piece.at[s, f],
            piece_of(recv_tail, s, me),
            tail_send.at[s, f],
            tail_recv.at[s, distance],
            pencil=owner_of(s, f),
        )

    def second(s):
        wait_fold(0, s)

        def last_rows(f, tile):
            return pl.ds(tile % 3 * 8 + FIELDS * (tile // 3) + f, PEERS, stride=LAST)

        def one_field(i, carry):
            f = order(i)
            wait_part(0, s, f)
            columns = []
            for tile in range(OWN_TILES):
                starts = [p * PART + tile * 8 for p in range(PEERS)]
                rows = [recv[s, f, start : start + 8, :] for start in starts]
                rows.append(recv_fold[s, last_rows(f, tile), :])
                columns.append(jnp.concatenate(rows, axis=0))
            spectrum = left(wide[512:592, :], jnp.concatenate(columns, axis=1))
            result = left(wide[592:672, :], spectrum * kernel_table[...])
            for tile in range(OWN_TILES):
                lanes = slice(tile * 128, tile * 128 + 128)
                for p in range(PEERS):
                    start = p * PART + tile * 8
                    back[s, f, start : start + 8, :] = result[p * 8 : p * 8 + 8, lanes]
                back_fold[s, last_rows(f, tile), :] = result[64:72, lanes]
            send_part(1, s, f)
            return carry

        lax.fori_loop(0, FIELDS, one_field, 0)
        send_fold(1, s)

    def give_copies(s):
        return block_copies(
            give_parts(give.at[s], give_fold.at[s]),
            give_parts(given.at[s], given_fold.at[s]),
            give_send.at[s],
            give_recv.at[s],
            terms_group(s),
        )

    def order(i):
        return lax.rem(2 * i, FIELDS) + lax.div(i, 2)

    def pair_weights(s):
        weights = []
        for f in range(FIELDS):
            g = 2 * (f % 2) + f // 2
            above = visit_fold[s, MASKS, FIELDS + g : FIELDS + g + 1, :]
            same = visit_fold[s, MASKS, g : g + 1, :]
            mine = own_fold[MASKS, FIELDS + f : FIELDS + f + 1, :]
            row = jnp.where(s == 0, same, jnp.where(even, above, mine))
            weights.append(jnp.broadcast_to(row, (8, 128)))
        return weights

    def third(s):
        weights = pair_weights(s)
        leaving = give_copies(s)

        def leave(which):
            for part in which:
                leaving[part].start()

        def gather_band(c, begin, end):
            def gather(tile, j):
                chi = visit[s, tile, first_band[c], :]
                terms = base[c, tile]
                for a in range(2):
                    value = rho[tile, field_rows[2 * a + c], :] * weights[2 * a + c]
                    total[tile, first_band[a], :] += value * chi
                    terms = terms + value * own[tile, first_band[a], :]
                give[s, c, tile] = terms

            tile_loop(begin, end, gather)

        def one_row(i, carry):
            t = jnp.where(i == FIELDS, FIELDS, order(jnp.minimum(i, FIELDS - 1)))

            @pl.when(t < FIELDS)
            def _():
                wait_part(1, s, t)

            @pl.when(t == FIELDS)
            def _():
                wait_fold(1, s)

                def unfold(q, carry):
                    for k in range(OWN_TILES):
                        from_row = pl.multiple_of(q * LAST + k % 3 * 8, 8)
                        value = field_fold[s, pl.ds(from_row, 8), :]
                        value = pltpu.roll(value, FIELDS, 0) if k > 2 else value
                        to_row = pl.multiple_of((q * OWN_TILES + k) * 8, 8)
                        field[s, FIELDS, pl.ds(to_row, 8), :] = value
                    return carry

                lax.fori_loop(0, PEERS, unfold, 0)

            def source(tile):
                if tile == TAIL_TILE:
                    return field_tail[s, row_of(t), :]
                return field[s, t, tile * 8 : tile * 8 + 8, :]

            def load(slot):
                return take(source, slot * NG)

            def save(part, b, value):
                work[place(part, b), :] = value

            finish72_adjoint(load, save)
            along_z(256)

            def target(tile, lanes, piece):
                rho[tile, row_of(t), lanes] = piece

            for b in range(9):
                values = dft8_adjoint([work2[place(part, b), :] for part in range(8)])
                for a, value in enumerate(values):
                    put(target, point72(a, b) * NG, value)

            @pl.when((s == 1) & even & (i == 1))
            def _():
                for copy in give_copies(0):
                    copy.wait_recv()

                def join(tile, carry):
                    for band in range(2):
                        base[band, tile] = given[0, band, tile]
                    return carry

                lax.fori_loop(0, TILES, join, 0)
                base_fold[...] = given_fold[0]

            @pl.when(i == 1)
            def _():
                gather_band(0, 0, TILES)
                leave([0])

            return carry

        lax.fori_loop(0, FIELDS + 1, one_row, 0)
        last_weight = weights[3]
        for f in range(3):
            last_weight = jnp.where(row_at == f, weights[f], last_weight)

        for q, (begin, end) in enumerate(QUARTERS):
            gather_band(1, begin, end)
            leave([1 + q])

            def gather_last(tile, j, q=q):
                phi, chi = last_planes(s, j, q)
                value = rho[tile, 32:40, :] * last_weight
                stay, leave = value * chi, value * phi
                stay = stay + pltpu.roll(stay, 7, 0)
                leave = leave + pltpu.roll(leave, 6, 0)
                for band in range(2):
                    row = slice(2 * q + band, 2 * q + band + 1)
                    total_fold[j, row, :] += stay[2 * band : 2 * band + 1]
                    give_fold[s, j, row, :] = leave[band : band + 1] + base_fold[j, row, :]

            tile_loop(begin, end, gather_last)
        leave([5])

    def tail_back(s, f, j):
        return remote(
            piece_of(back_tail, s, peer(j)),
            field_piece.at[s, f],
            back_tail_send.at[s, j],
            back_tail_recv.at[s, f],
            pencil=peer(j),
        )

    def send_tail(s):
        for f in range(FIELDS):
            owner = owner_of(s, f)

            @pl.when(me == owner)
            def _(f=f, owner=owner):
                recv_tail[s, rows_of(owner, PIECE), :] = wave_piece[s, f]

            @pl.when(me != owner)
            def _(f=f, owner=owner):
                tail_copy(s, f, lax.rem(owner - me + PEERS, PEERS)).start()

    def turn_tail(s):
        owned = lax.div(me, FIELDS) == s

        @pl.when(owned)
        def _():
            for j in range(1, PEERS):
                tail_copy(s, 0, j).wait_recv()
            parts = [pl.ds(p * PIECE, 8) for p in range(PEERS)] + [pl.ds(8, PEERS, stride=PIECE)]
            block = jnp.concatenate([recv_tail[s, part, :] for part in parts], axis=0)
            spectrum = left(wide[512:592, :], block) * kernel_tail[...]
            result = left(wide[592:672, :], spectrum)
            for i, part in enumerate(parts):
                back_tail[s, part, :] = result[i * 8 : i * 8 + 8, :]
            mine = lax.rem(me, FIELDS)
            for j in range(1, PEERS):
                tail_back(s, mine, j).start()
            field_piece[s, mine] = back_tail[s, pl.ds(pl.multiple_of(me * PIECE, 8), PIECE), :]

    def end_tail(s):
        for f in range(FIELDS):
            owner = owner_of(s, f)

            @pl.when(me != owner)
            def _(f=f, owner=owner):
                tail_copy(s, f, lax.rem(owner - me + PEERS, PEERS)).wait_send()
                tail_back(s, f, 1).wait_recv()

            field_tail[s, field_rows[f], :] = field_piece[s, f, 0:8, :]
            field_tail[s, 32 + f : 33 + f, :] = field_piece[s, f, 8:9, :]

        @pl.when(lax.div(me, FIELDS) == s)
        def _():
            for j in range(1, PEERS):
                tail_back(s, lax.rem(me, FIELDS), j).wait_send()

    def slots(*stages):
        def run(s, carry):
            for stage in stages:
                stage(s)
            return carry

        lax.fori_loop(0, 2, run, 0)

    slots(first, send_tail)
    slots(second, turn_tail)
    slots(end_tail, third)

    def wait_given(which):
        for part in which:
            give_copies(1)[part].wait_recv()

            @pl.when(jnp.logical_not(even))
            def _(part=part):
                give_copies(0)[part].wait_recv()

    for q, (begin, end) in enumerate(QUARTERS):
        wait_given([0, 1] if q == 0 else [1 + q])

        def result(tile, j, width=128):
            lanes = pl.ds(tile * 128, width)
            if width == 128:
                lanes = pl.ds(pl.multiple_of(tile * 128, 128), 128)
            for rows, band in zip(first_band, range(2)):
                near = jnp.where(even, 0.0, given[0, band, tile])
                term = -(total[tile, rows, :] + near + given[1, band, tile])
                mixed[tile, pl.ds(band, 8, stride=2), :] = term
            for plane in range(PLANES - 1):
                piece = mixed[tile, 2 * plane : 2 * plane + 2, 0:width]
                out_ref[plane, :, lanes] = piece

        tile_loop(begin, min(end, TAIL_TILE), result)
        if end > TAIL_TILE:
            result(TAIL_TILE, 0, MERGED - TAIL)
    wait_given([5])
    for q, (begin, end) in enumerate(QUARTERS):

        def last_result(tile, j, q=q, width=128):
            lanes = pl.ds(tile * 128, width)
            if width == 128:
                lanes = pl.ds(pl.multiple_of(tile * 128, 128), 128)
            rows = slice(2 * q, 2 * q + 2)
            near = jnp.where(even, 0.0, given_fold[0, j, rows, :])
            term = total_fold[j, rows, :] + near + given_fold[1, j, rows, :]
            out_ref[PLANES - 1, :, lanes] = -term[:, 0:width]

        tile_loop(begin, min(end, TAIL_TILE), last_result)
        if end > TAIL_TILE:
            last_result(TAIL_TILE, TAIL_TILE - begin, width=MERGED - TAIL)

    for copy in near_sends() + far_sends():
        copy.wait_send()

    for s in range(2):
        for copy in give_copies(s):
            copy.wait_send()
    for phase in range(2):
        for s in range(2):
            end_blocks(phase, s)


def body(bands, orbitals, pair_mask):
    hbm = pl.BlockSpec(memory_space=pltpu.HBM)
    smem = pl.BlockSpec(memory_space=pltpu.SMEM)
    consts = [jnp.asarray(table) for table in tables()]
    dma = pltpu.SemaphoreType.DMA

    def buffer(*shape):
        return pltpu.VMEM(shape, jnp.float32)

    out = pl.pallas_call(
        functools.partial(kernel, bands),
        out_shape=jax.ShapeDtypeStruct((PLANES, 2, MERGED), jnp.float32),
        in_specs=[smem] + [hbm] * (1 + len(consts)),
        out_specs=pl.BlockSpec(memory_space=pltpu.VMEM),
        scratch_shapes=[
            buffer(PLANES, 2, MERGED),
            pltpu.VMEM(consts[0].shape, jnp.bfloat16),
            buffer(*consts[1].shape),
            buffer(*consts[2].shape),
            buffer(TILES, 16, 128),
            buffer(TILES, 16, 128),
            buffer(FOLD + 1, 8, 128),
            buffer(2, TILES, 16, 128),
            buffer(2, FOLD + 1, 8, 128),
            buffer(TILES, ROWS, 128),
            buffer(NG * 8, 128),
            buffer(NG * 8, 128),
            buffer(2, FIELDS + 1, PEERS * PART, 128),
            buffer(2, PEERS * LAST, 128),
            buffer(2, ROWS, 128),
            buffer(2, FIELDS, PIECE, 128),
            buffer(2, FIELDS, PEERS * PART, 128),
            buffer(2, PEERS * LAST, 128),
            buffer(2, PEERS * PIECE, 128),
            buffer(2, FIELDS, PEERS * PART, 128),
            buffer(2, PEERS * LAST, 128),
            buffer(2, PEERS * PIECE, 128),
            buffer(2, FIELDS + 1, PEERS * PART, 128),
            buffer(2, PEERS * LAST, 128),
            buffer(2, ROWS, 128),
            buffer(2, FIELDS, PIECE, 128),
            buffer(NG, OWN),
            buffer(NG, 128),
            buffer(TILES, 16, 128),
            buffer(FOLD + 1, 8, 128),
            buffer(2, TILES, 8, 128),
            buffer(FOLD + 1, 8, 128),
            buffer(2, 2, TILES, 8, 128),
            buffer(2, FOLD + 1, 8, 128),
            buffer(2, 2, TILES, 8, 128),
            buffer(2, FOLD + 1, 8, 128),
            dma((2, 5)),
            dma((2, 5)),
            dma((2, 6)),
            dma((2, 6)),
            dma((2, 2)),
            dma((2, 2, FIELDS)),
            dma((2, 2)),
            dma((2, 2)),
            dma((2, FIELDS)),
            dma((2, PEERS)),
            dma((2, PEERS)),
            dma((2, FIELDS)),
            dma((4,)),
        ],
        compiler_params=pltpu.CompilerParams(
            collective_id=0, has_side_effects=True, vmem_limit_bytes=64 * 1024 * 1024 - 65536
        ),
    )(pair_mask, orbitals.transpose(1, 0, 2), *consts)
    return out.transpose(1, 0, 2)


def solution(mesh):
    return jax.shard_map(
        functools.partial(body, mesh.shape["band"]),
        mesh=mesh,
        in_specs=(P("band", "pencil", None), P("band", None, None, None)),
        out_specs=P("band", "pencil", None),
        check_vma=False,
    )
```

```python
import functools
import math

import jax
import jax.numpy as jnp
import ml_dtypes
import numpy as np
from jax import lax
from jax.experimental import pallas as pl
from jax.experimental.pallas import tpu as pltpu
from jax.sharding import PartitionSpec as P

MESH = pl.DeviceIdType.MESH
NG = 72
PLANES = 9
PEERS = 8
FIELDS = 4
ROWS = 40
PART = 40
LAST = 24
MERGED = NG * NG
WIDTH = 5248
OWN = 640
TAIL = PEERS * OWN
PIECE = 16
FOLD = 11
MASKS = FOLD
QUARTERS = [(q * FOLD, min((q + 1) * FOLD, 41)) for q in range(4)]
TILES = WIDTH // 128
OWN_TILES = OWN // 128
TAIL_TILE = TILES - 1
coulomb_scale = 20.0
screening = 0.25
HALF = math.sqrt(0.5)


def dft8(x):
    a = [x[j] + x[j + 4] for j in range(4)]
    b = [x[j] - x[j + 4] for j in range(4)]
    e, o = a[0] + a[2], a[1] + a[3]
    u, v = HALF * (b[1] - b[3]), HALF * (b[1] + b[3])
    return [e + o, e - o, b[0] + u, v + b[2], a[0] - a[2], a[1] - a[3], b[0] - u, v - b[2]]


def dft8_adjoint(c):
    p, q = c[0] + c[1], c[0] - c[1]
    a = [p + c[4], q + c[5], p - c[4], q - c[5]]
    d, s = HALF * (c[2] - c[6]), HALF * (c[3] + c[7])
    b = [c[2] + c[6], d + s, c[3] - c[7], s - d]
    return [a[j] + b[j] for j in range(4)] + [a[j] - b[j] for j in range(4)]


def cos9(n):
    return math.cos(2.0 * math.pi * (n % 9) / 9)


def sin9(n):
    return math.sin(2.0 * math.pi * (n % 9) / 9)


def weighted(values, factors):
    total = values[0] * factors[0]
    for value, factor in zip(values[1:], factors[1:]):
        total = total + value * factor
    return total


def dft9(x):
    e = [x[n] + x[9 - n] for n in range(1, 5)]
    o = [x[n] - x[9 - n] for n in range(1, 5)]
    third = e[0] + e[1] + e[3]
    cosines = [x[0] + third + e[2]]
    sines = [None]
    for k in range(1, 5):
        if k == 3:
            cosines.append(x[0] + e[2] - 0.5 * third)
            sines.append(sin9(3) * (o[0] - o[1] + o[3]))
        else:
            cosines.append(x[0] + weighted(e, [cos9(k * n) for n in range(1, 5)]))
            sines.append(weighted(o, [sin9(k * n) for n in range(1, 5)]))
    return cosines, sines


def dft9_adjoint(cosines, sines):
    c, s = cosines, sines
    out = [None] * 9
    out[0] = c[0] + ((c[1] + c[2]) + (c[3] + c[4]))
    for n in range(1, 5):
        if n == 3:
            even = c[0] + c[3] - 0.5 * (c[1] + c[2] + c[4])
            odd = sin9(3) * (s[1] - s[2] + s[4])
        else:
            even = c[0] + weighted(c[1:], [cos9(k * n) for k in range(1, 5)])
            odd = weighted(s[1:], [sin9(k * n) for k in range(1, 5)])
        out[n] = even + odd
        out[9 - n] = even - odd
    return out


def finish72(load, save):
    for part in (0, 1):
        cosines, sines = dft9([load(part, b) for b in range(9)])
        base = part * 9
        save(base, cosines[0])
        for k in range(1, 5):
            save(base + 2 * k - 1, cosines[k])
            save(base + 2 * k, sines[k])
    for k8 in range(3):
        base = 18 + 18 * k8
        cc, cs = dft9([load(2 + 2 * k8, b) for b in range(9)])
        sc, ss = dft9([load(3 + 2 * k8, b) for b in range(9)])
        save(base, cc[0])
        save(base + 1, sc[0])
        for k in range(1, 5):
            at = base + 4 * k - 2
            save(at, cc[k] - ss[k])
            save(at + 1, cc[k] + ss[k])
            save(at + 2, sc[k] + cs[k])
            save(at + 3, sc[k] - cs[k])


def finish72_adjoint(load, save):
    for part in (0, 1):
        base = part * 9
        cosines = [load(base)] + [load(base + 2 * k - 1) for k in range(1, 5)]
        sines = [None] + [load(base + 2 * k) for k in range(1, 5)]
        for b, value in enumerate(dft9_adjoint(cosines, sines)):
            save(part, b, value)
    for k8 in range(3):
        base = 18 + 18 * k8
        cc, sc, cs, ss = [load(base)], [load(base + 1)], [None], [None]
        for k in range(1, 5):
            at = base + 4 * k - 2
            plus, minus, sine_plus, sine_minus = [load(at + i) for i in range(4)]
            cc.append(plus + minus)
            ss.append(minus - plus)
            sc.append(sine_plus + sine_minus)
            cs.append(sine_plus - sine_minus)
        for b, value in enumerate(dft9_adjoint(cc, cs)):
            save(2 + 2 * k8, b, value)
        for b, value in enumerate(dft9_adjoint(sc, ss)):
            save(3 + 2 * k8, b, value)


def point72(a, b):
    return (9 * a + 8 * b) % NG


def split(table):
    high = table.astype(ml_dtypes.bfloat16).astype(np.float64)
    return high, (table - high).astype(ml_dtypes.bfloat16).astype(np.float64)


def from_left(table):
    high, low = split(table)
    wide = np.zeros((80, 256))
    wide[:NG, : 3 * NG] = np.concatenate([high, high, low], axis=1)
    return wide


def from_right(table):
    high, low = split(table)
    return np.block([[high, low], [high, np.zeros_like(low)]])


@functools.cache
def tables():
    at = np.arange(NG)
    basis, freq = [np.full(NG, 1.0)], [0]
    for k in range(1, NG // 2):
        basis += [np.cos(2 * np.pi * k * at / NG), np.sin(2 * np.pi * k * at / NG)]
        freq += [k, k]
    basis.append(np.cos(np.pi * at))
    freq.append(NG // 2)
    basis = np.array(basis)
    basis /= np.sqrt((basis * basis).sum(1, keepdims=True))
    freq = np.array(freq, np.float64)
    eye = np.eye(NG)
    parts = [dft8([eye[point72(a, b)] for a in range(8)]) for b in range(9)]
    slots = [None] * NG
    finish72(lambda part, b: parts[b][part], slots.__setitem__)
    slots = np.array(slots)
    norm = (slots * slots).sum(1)
    spectrum = np.abs(np.fft.fft(slots, axis=1))[:, : NG // 2 + 1]
    freq_y = spectrum.argmax(1).astype(np.float64)
    along_z = np.zeros((128, 128))
    along_z[:NG, :NG] = basis.T
    along_x = basis.reshape(NG, PEERS, PLANES)
    along_x = np.concatenate([along_x[:, :, :8].reshape(NG, -1), along_x[:, :, 8]], axis=1)
    column = np.zeros((8, WIDTH), np.float32)
    column[0, :MERGED] = (freq_y[:, None] ** 2 + freq[None, :] ** 2).reshape(-1)
    column[1, :MERGED] = np.repeat(1.0 / norm, NG)
    freq_x = np.broadcast_to((freq**2)[:, None], (NG, 128)).astype(np.float32)
    wide = np.concatenate(
        [from_right(along_z), from_right(along_z.T), from_left(along_x), from_left(along_x.T)]
    )
    return wide.astype(ml_dtypes.bfloat16), column, freq_x


def take(load, start):
    tile, lane = divmod(start, 128)
    value = load(tile)
    if lane == 0:
        return value
    if lane + NG > 128:
        at = lax.broadcasted_iota(jnp.int32, value.shape, 1)
        value = jnp.where(at >= lane, value, load(tile + 1))
    return pltpu.roll(value, 128 - lane, 1)


def put(store, start, value):
    tile, lane = divmod(start, 128)
    if lane:
        value = pltpu.roll(value, lane, 1)
    end = min(lane + NG, 128)
    store(tile, slice(lane, end), value[:, lane:end])
    if lane + NG > 128:
        store(tile + 1, slice(0, lane + NG - 128), value[:, : lane + NG - 128])


def matmul(a, b):
    return jnp.dot(a, b, preferred_element_type=jnp.float32)


def halves(x):
    high = x.astype(jnp.bfloat16)
    return high, (x - high.astype(jnp.float32)).astype(jnp.bfloat16)


def left(table, x):
    high, low = [part.astype(jnp.float32) for part in halves(x)]
    zeros = jnp.zeros((8, x.shape[1]), jnp.float32)
    operand = jnp.concatenate([high, low, high, zeros], axis=0).astype(jnp.bfloat16)
    return matmul(table[:, 0 : operand.shape[0]], operand)[0:NG]


def kernel(
    bands,
    mask_ref,
    bands_hbm,
    wide_hbm,
    column_hbm,
    freq_hbm,
    out_ref,
    bands_ref,
    wide,
    column_ref,
    freq_ref,
    mixed,
    own,
    own_fold,
    visit,
    visit_fold,
    rho,
    work,
    work2,
    wave,
    wave_fold,
    wave_tail,
    wave_piece,
    recv,
    recv_fold,
    recv_tail,
    back,
    back_fold,
    back_tail,
    field,
    field_fold,
    field_tail,
    field_piece,
    kernel_table,
    kernel_tail,
    total,
    total_fold,
    base,
    base_fold,
    give,
    give_fold,
    given,
    given_fold,
    visit_send,
    visit_recv,
    pass_send,
    give_send,
    give_recv,
    part_send,
    part_recv,
    fold_send,
    fold_recv,
    tail_send,
    tail_recv,
    back_tail_send,
    back_tail_recv,
    load_sem,
):
    me = lax.axis_index("pencil")
    group = lax.axis_index("band")
    me_x, me_y = lax.div(me, 4), lax.rem(me, 4)

    loads = [
        pltpu.make_async_copy(src, dst, load_sem.at[i])
        for i, (src, dst) in enumerate(
            [
                (bands_hbm, bands_ref),
                (wide_hbm, wide),
                (column_hbm, column_ref),
                (freq_hbm, freq_ref),
            ]
        )
    ]
    for load in loads:
        load.start()

    def peer(j):
        return lax.rem(me + j, PEERS)

    def at(dx, dy):
        return lax.rem(me_x + dx, 2) * 4 + lax.rem(me_y + dy + 4, 4)

    def group_at(j):
        return lax.rem(group + j + bands, bands)

    barrier = pltpu.get_barrier_semaphore()
    for j in range(1, PEERS):
        pl.semaphore_signal(barrier, inc=1, device_id={"pencil": peer(j)}, device_id_type=MESH)
    for j in (-2, -1, 1, 2):
        pl.semaphore_signal(barrier, inc=1, device_id={"band": group_at(j)}, device_id_type=MESH)
    loads[0].wait()
    def take_tile(tile, j, q, width):
        lanes = pl.ds(tile * 128, width)
        if width == 128:
            lanes = pl.ds(pl.multiple_of(tile * 128, 128), 128)
        live = slice(0, width)
        for plane in range(PLANES - 1):
            mixed[tile, 2 * plane : 2 * plane + 2, live] = bands_ref[plane, :, lanes]
        for band in range(2):
            own[tile, band * 8 : band * 8 + 8, :] = mixed[tile, pl.ds(band, 8, stride=2), :]
        own_fold[j, 2 * q : 2 * q + 2, live] = bands_ref[PLANES - 1, :, lanes]

    def tile_loop(begin, end, step):
        def run(j, carry):
            step(begin + j, j)
            return carry

        lax.fori_loop(0, end - begin, run, 0)

    mixed[TAIL_TILE] = jnp.zeros((16, 128), jnp.float32)
    own_fold[TAIL_TILE % FOLD, 6:8, :] = jnp.zeros((2, 128), jnp.float32)
    for q, (begin, end) in enumerate(QUARTERS):
        tile_loop(begin, min(end, TAIL_TILE), lambda tile, j, q=q: take_tile(tile, j, q, 128))
    take_tile(TAIL_TILE, TAIL_TILE % FOLD, 3, MERGED - TAIL)

    def own_mask(s, f):
        return mask_ref[0, s, f // 2, f % 2].astype(jnp.float32)

    for m in range(2 * FIELDS):
        value = own_mask(m // FIELDS, m % FIELDS)
        own_fold[MASKS, m : m + 1, :] = jnp.zeros((1, 128), jnp.float32) + value
    pl.semaphore_wait(barrier, PEERS - 1 + 4)

    def remote(src, dst, send, recv, **device):
        return pltpu.make_async_remote_copy(
            src_ref=src,
            dst_ref=dst,
            send_sem=send,
            recv_sem=recv,
            device_id=device,
            device_id_type=MESH,
        )

    even = lax.rem(group, 2) == 0

    def terms_group(s):
        near = jnp.where(even, group_at(1), group_at(-1))
        return jnp.where(s == 0, near, jnp.where(even, group_at(2), group_at(-2)))

    def parts(main, fold):
        return [
            *(main.at[pl.ds(begin, end - begin)] for begin, end in QUARTERS),
            fold,
        ]

    def block_copies(src, dst, send, recv, to):
        return [
            remote(one, two, send.at[q], recv.at[q], band=to)
            for q, (one, two) in enumerate(zip(src, dst))
        ]

    def visit_at(s):
        return parts(visit.at[s], visit_fold.at[s])

    own_parts = parts(own, own_fold)

    def give_parts(main, fold):
        return [main.at[0], *parts(main.at[1], fold)]

    def visit_copies(s, src, send, to):
        return block_copies(src, visit_at(s), send, visit_recv.at[s], to)

    def near_sends():
        return visit_copies(0, own_parts, visit_send.at[0], group_at(-1))

    def far_sends():
        return visit_copies(1, own_parts, visit_send.at[1], group_at(2))

    def passes():
        return visit_copies(1, visit_at(0), pass_send, group_at(-1))

    for copy in near_sends():
        copy.start()

    @pl.when(jnp.logical_not(even))
    def _():
        for copy in far_sends():
            copy.start()

    def kernel_columns(start, width):
        squared = column_ref[0:1, pl.ds(start, width)]
        scale = column_ref[1:2, pl.ds(start, width)]
        return coulomb_scale / (freq_ref[:, 0:1] + squared + screening) * scale

    for load in loads[1:]:
        load.wait()
    kernel_table[...] = kernel_columns(pl.multiple_of(me * OWN, 128), OWN)
    kernel_tail[...] = kernel_columns(TAIL, 128)
    wave_tail[...] = jnp.zeros((2, ROWS, 128), jnp.float32)
    total_fold[...] = jnp.zeros((FOLD + 1, 8, 128), jnp.float32)
    base_fold[...] = jnp.zeros((FOLD + 1, 8, 128), jnp.float32)

    def clear(tile, carry):
        total[tile] = jnp.zeros((16, 128), jnp.float32)
        base[:, tile] = jnp.zeros((2, 8, 128), jnp.float32)
        return carry

    lax.fori_loop(0, TILES, clear, 0)
    for s in range(2):
        for p in range(PEERS):
            back_fold[s, (p + 1) * LAST - 8 : (p + 1) * LAST, :] = jnp.zeros((8, 128), jnp.float32)
            back_tail[s, (p + 1) * PIECE - 8 : (p + 1) * PIECE, :] = jnp.zeros((8, 128), jnp.float32)
        field_tail[s, 32:40, :] = jnp.zeros((8, 128), jnp.float32)
        for f in range(FIELDS):
            wave_piece[s, f, 8:16, :] = jnp.zeros((8, 128), jnp.float32)

    first_band = [slice(band * 8, band * 8 + 8) for band in range(2)]
    field_rows = [slice(f * 8, f * 8 + 8) for f in range(FIELDS)]
    row_at = lax.broadcasted_iota(jnp.int32, (8, 128), 0)
    resident_one = lax.rem(lax.div(row_at, 2), 2) == 1
    visitor_one = lax.rem(row_at, 2) == 1

    def last_planes(s, j, q):
        a = [own_fold[j, 2 * q + band : 2 * q + band + 1, :] for band in range(2)]
        c = [visit_fold[s, j, 2 * q + band : 2 * q + band + 1, :] for band in range(2)]
        wide_a = [jnp.broadcast_to(row, (8, 128)) for row in a]
        wide_c = [jnp.broadcast_to(row, (8, 128)) for row in c]
        return (
            jnp.where(resident_one, wide_a[1], wide_a[0]),
            jnp.where(visitor_one, wide_c[1], wide_c[0]),
        )

    def along_z(start):
        for i in range(2):
            rows = pl.ds(i * 288, 288)
            both = matmul(jnp.concatenate(halves(work[rows, :]), axis=1), wide[start : start + 256, :])
            work2[rows, :] = both[:, :128] + both[:, 128:]

    def place(part, b):
        return slice((part * 9 + b) * 8, (part * 9 + b) * 8 + 8)

    def row_of(t):
        return pl.ds(pl.multiple_of(t * 8, 8), 8)

    def first(s):
        arriving = visit_copies(s, own_parts, visit_send.at[0], group_at(1))
        passing = passes()
        for q in (4, 0, 1, 2, 3):
            arriving[q].wait_recv()

            @pl.when((s == 0) & jnp.logical_not(even))
            def _(q=q):
                passing[q].start()

        def one_row(i, carry):
            t = jnp.where(i == 0, FIELDS, order(jnp.maximum(i - 1, 0)))

            @pl.when(i > 0)
            def _():
                resident, visitor = row_of(lax.div(t, 2)), row_of(lax.rem(t, 2))
                for tile in range(TILES):
                    rho[tile, row_of(t), :] = own[tile, resident, :] * visit[s, tile, visitor, :]

            @pl.when(i == 0)
            def _():
                for q, (begin, end) in enumerate(QUARTERS):

                    def products(tile, j, q=q):
                        phi, chi = last_planes(s, j, q)
                        rho[tile, 32:40, :] = phi * chi

                    tile_loop(begin, end, products)

            for b in range(9):
                starts = [point72(a, b) * NG for a in range(8)]
                values = [take(lambda tile: rho[tile, row_of(t), :], at) for at in starts]
                for part, value in enumerate(dft8(values)):
                    work[place(part, b), :] = value
            along_z(0)

            def load(part, b):
                return work2[place(part, b), :]

            def target(tile, lanes, piece):
                if tile == TAIL_TILE:
                    wave_tail[s, row_of(t), lanes] = piece
                else:
                    wave[s, t, tile * 8 : tile * 8 + 8, lanes] = piece

            def save(slot, value):
                put(target, slot * NG, value)

            finish72(load, save)

            @pl.when(i == 0)
            def _():
                upper = lax.broadcasted_iota(jnp.int32, (8, 128), 0) < FIELDS

                def fold(q, carry):
                    for k in range(3):
                        at_row = pl.multiple_of((q * OWN_TILES + k) * 8, 8)
                        piece = wave[s, FIELDS, pl.ds(at_row, 8), :]
                        if k < 2:
                            below = wave[s, FIELDS, pl.ds(at_row + 24, 8), :]
                            piece = jnp.where(upper, piece, below)
                        to_row = pl.multiple_of(q * LAST + k * 8, 8)
                        wave_fold[s, pl.ds(to_row, 8), :] = piece
                    return carry

                lax.fori_loop(0, PEERS, fold, 0)
                send_fold(0, s)

            @pl.when(i > 0)
            def _():
                send_part(0, s, t)

            return carry

        lax.fori_loop(0, FIELDS + 1, one_row, 0)
        for f in range(FIELDS):
            wave_piece[s, f, 0:8, :] = wave_tail[s, field_rows[f], :]
            wave_piece[s, f, 8:9, :] = wave_tail[s, 32 + f : 33 + f, :]

    part_refs = ((wave, recv), (back, field))
    fold_refs = ((wave_fold, recv_fold), (back_fold, field_fold))
    straight = [(1, 2), (0, 2), (1, 1), (1, 3), (0, 1), (0, 3), (1, 0)]

    def rows_of(index, rows):
        return pl.ds(pl.multiple_of(index * rows, 8), rows)

    def send_part(phase, s, f):
        src, dst = part_refs[phase]
        for dx, dy in straight:
            to = at(dx, dy)
            remote(
                src.at[s, f, rows_of(to, PART)],
                dst.at[s, f, rows_of(me, PART)],
                part_send.at[phase, s],
                part_recv.at[phase, s, f],
                pencil=to,
            ).start()
        dst[s, f, rows_of(me, PART), :] = src[s, f, rows_of(me, PART), :]

    def send_fold(phase, s):
        src, dst = fold_refs[phase]
        for dx, dy in straight:
            to = at(dx, dy)
            remote(
                src.at[s, rows_of(to, LAST)],
                dst.at[s, rows_of(me, LAST)],
                fold_send.at[phase, s],
                fold_recv.at[phase, s],
                pencil=to,
            ).start()
        dst[s, rows_of(me, LAST), :] = src[s, rows_of(me, LAST), :]

    def drain(view, sem):
        pltpu.make_async_copy(view, view, sem).wait()

    def wait_part(phase, s, f):
        drain(part_refs[phase][1].at[s, f, pl.ds(0, 7 * PART)], part_recv.at[phase, s, f])

    def wait_fold(phase, s):
        drain(fold_refs[phase][1].at[s, pl.ds(0, 7 * LAST)], fold_recv.at[phase, s])

    def end_blocks(phase, s):
        parts = part_refs[phase][0].at[s, pl.ds(0, FIELDS), pl.ds(0, 7 * PART)]
        drain(parts, part_send.at[phase, s])
        drain(fold_refs[phase][0].at[s, pl.ds(0, 7 * LAST)], fold_send.at[phase, s])

    def piece_of(ref, s, index):
        return ref.at[s, pl.ds(pl.multiple_of(index * PIECE, 8), PIECE), :]

    def owner_of(s, f):
        return FIELDS * s + f

    def tail_copy(s, f, distance):
        return remote(
            wave_piece.at[s, f],
            piece_of(recv_tail, s, me),
            tail_send.at[s, f],
            tail_recv.at[s, distance],
            pencil=owner_of(s, f),
        )

    def second(s):
        wait_fold(0, s)

        def last_rows(f, tile):
            return pl.ds(tile % 3 * 8 + FIELDS * (tile // 3) + f, PEERS, stride=LAST)

        def one_field(i, carry):
            f = order(i)
            wait_part(0, s, f)
            columns = []
            for tile in range(OWN_TILES):
                starts = [p * PART + tile * 8 for p in range(PEERS)]
                rows = [recv[s, f, start : start + 8, :] for start in starts]
                rows.append(recv_fold[s, last_rows(f, tile), :])
                columns.append(jnp.concatenate(rows, axis=0))
            spectrum = left(wide[512:592, :], jnp.concatenate(columns, axis=1))
            result = left(wide[592:672, :], spectrum * kernel_table[...])
            for tile in range(OWN_TILES):
                lanes = slice(tile * 128, tile * 128 + 128)
                for p in range(PEERS):
                    start = p * PART + tile * 8
                    back[s, f, start : start + 8, :] = result[p * 8 : p * 8 + 8, lanes]
                back_fold[s, last_rows(f, tile), :] = result[64:72, lanes]
            send_part(1, s, f)
            return carry

        lax.fori_loop(0, FIELDS, one_field, 0)
        send_fold(1, s)

    def give_copies(s):
        return block_copies(
            give_parts(give.at[s], give_fold.at[s]),
            give_parts(given.at[s], given_fold.at[s]),
            give_send.at[s],
            give_recv.at[s],
            terms_group(s),
        )

    def order(i):
        return lax.rem(2 * i, FIELDS) + lax.div(i, 2)

    def pair_weights(s):
        weights = []
        for f in range(FIELDS):
            g = 2 * (f % 2) + f // 2
            above = visit_fold[s, MASKS, FIELDS + g : FIELDS + g + 1, :]
            same = visit_fold[s, MASKS, g : g + 1, :]
            mine = own_fold[MASKS, FIELDS + f : FIELDS + f + 1, :]
            row = jnp.where(s == 0, same, jnp.where(even, above, mine))
            weights.append(jnp.broadcast_to(row, (8, 128)))
        return weights

    def third(s):
        weights = pair_weights(s)
        leaving = give_copies(s)

        def leave(which):
            for part in which:
                leaving[part].start()

        def gather_band(c, begin, end):
            def gather(tile, j):
                chi = visit[s, tile, first_band[c], :]
                terms = base[c, tile]
                for a in range(2):
                    value = rho[tile, field_rows[2 * a + c], :] * weights[2 * a + c]
                    total[tile, first_band[a], :] += value * chi
                    terms = terms + value * own[tile, first_band[a], :]
                give[s, c, tile] = terms

            tile_loop(begin, end, gather)

        def one_row(i, carry):
            t = jnp.where(i == FIELDS, FIELDS, order(jnp.minimum(i, FIELDS - 1)))

            @pl.when(t < FIELDS)
            def _():
                wait_part(1, s, t)

            @pl.when(t == FIELDS)
            def _():
                wait_fold(1, s)

                def unfold(q, carry):
                    for k in range(OWN_TILES):
                        from_row = pl.multiple_of(q * LAST + k % 3 * 8, 8)
                        value = field_fold[s, pl.ds(from_row, 8), :]
                        value = pltpu.roll(value, FIELDS, 0) if k > 2 else value
                        to_row = pl.multiple_of((q * OWN_TILES + k) * 8, 8)
                        field[s, FIELDS, pl.ds(to_row, 8), :] = value
                    return carry

                lax.fori_loop(0, PEERS, unfold, 0)

            def source(tile):
                if tile == TAIL_TILE:
                    return field_tail[s, row_of(t), :]
                return field[s, t, tile * 8 : tile * 8 + 8, :]

            def load(slot):
                return take(source, slot * NG)

            def save(part, b, value):
                work[place(part, b), :] = value

            finish72_adjoint(load, save)
            along_z(256)

            def target(tile, lanes, piece):
                rho[tile, row_of(t), lanes] = piece

            for b in range(9):
                values = dft8_adjoint([work2[place(part, b), :] for part in range(8)])
                for a, value in enumerate(values):
                    put(target, point72(a, b) * NG, value)

            @pl.when((s == 1) & even & (i == 1))
            def _():
                for copy in give_copies(0):
                    copy.wait_recv()

                def join(tile, carry):
                    for band in range(2):
                        base[band, tile] = given[0, band, tile]
                    return carry

                lax.fori_loop(0, TILES, join, 0)
                base_fold[...] = given_fold[0]

            @pl.when(i == 1)
            def _():
                gather_band(0, 0, TILES)
                leave([0])

            return carry

        lax.fori_loop(0, FIELDS + 1, one_row, 0)
        last_weight = weights[3]
        for f in range(3):
            last_weight = jnp.where(row_at == f, weights[f], last_weight)

        for q, (begin, end) in enumerate(QUARTERS):
            gather_band(1, begin, end)
            leave([1 + q])

            def gather_last(tile, j, q=q):
                phi, chi = last_planes(s, j, q)
                value = rho[tile, 32:40, :] * last_weight
                stay, leave = value * chi, value * phi
                stay = stay + pltpu.roll(stay, 7, 0)
                leave = leave + pltpu.roll(leave, 6, 0)
                for band in range(2):
                    row = slice(2 * q + band, 2 * q + band + 1)
                    total_fold[j, row, :] += stay[2 * band : 2 * band + 1]
                    give_fold[s, j, row, :] = leave[band : band + 1] + base_fold[j, row, :]

            tile_loop(begin, end, gather_last)
        leave([5])

    def tail_back(s, f, j):
        return remote(
            piece_of(back_tail, s, peer(j)),
            field_piece.at[s, f],
            back_tail_send.at[s, j],
            back_tail_recv.at[s, f],
            pencil=peer(j),
        )

    def send_tail(s):
        for f in range(FIELDS):
            owner = owner_of(s, f)

            @pl.when(me == owner)
            def _(f=f, owner=owner):
                recv_tail[s, rows_of(owner, PIECE), :] = wave_piece[s, f]

            @pl.when(me != owner)
            def _(f=f, owner=owner):
                tail_copy(s, f, lax.rem(owner - me + PEERS, PEERS)).start()

    def turn_tail(s):
        owned = lax.div(me, FIELDS) == s

        @pl.when(owned)
        def _():
            for j in range(1, PEERS):
                tail_copy(s, 0, j).wait_recv()
            parts = [pl.ds(p * PIECE, 8) for p in range(PEERS)] + [pl.ds(8, PEERS, stride=PIECE)]
            block = jnp.concatenate([recv_tail[s, part, :] for part in parts], axis=0)
            spectrum = left(wide[512:592, :], block) * kernel_tail[...]
            result = left(wide[592:672, :], spectrum)
            for i, part in enumerate(parts):
                back_tail[s, part, :] = result[i * 8 : i * 8 + 8, :]
            mine = lax.rem(me, FIELDS)
            for j in range(1, PEERS):
                tail_back(s, mine, j).start()
            field_piece[s, mine] = back_tail[s, pl.ds(pl.multiple_of(me * PIECE, 8), PIECE), :]

    def end_tail(s):
        for f in range(FIELDS):
            owner = owner_of(s, f)

            @pl.when(me != owner)
            def _(f=f, owner=owner):
                tail_copy(s, f, lax.rem(owner - me + PEERS, PEERS)).wait_send()
                tail_back(s, f, 1).wait_recv()

            field_tail[s, field_rows[f], :] = field_piece[s, f, 0:8, :]
            field_tail[s, 32 + f : 33 + f, :] = field_piece[s, f, 8:9, :]

        @pl.when(lax.div(me, FIELDS) == s)
        def _():
            for j in range(1, PEERS):
                tail_back(s, lax.rem(me, FIELDS), j).wait_send()

    def slots(*stages):
        def run(s, carry):
            for stage in stages:
                stage(s)
            return carry

        lax.fori_loop(0, 2, run, 0)

    slots(first, send_tail)
    slots(second, turn_tail)
    slots(end_tail, third)

    def wait_given(which):
        for part in which:
            give_copies(1)[part].wait_recv()

            @pl.when(jnp.logical_not(even))
            def _(part=part):
                give_copies(0)[part].wait_recv()

    for q, (begin, end) in enumerate(QUARTERS):
        wait_given([0, 1] if q == 0 else [1 + q])

        def result(tile, j, width=128):
            lanes = pl.ds(tile * 128, width)
            if width == 128:
                lanes = pl.ds(pl.multiple_of(tile * 128, 128), 128)
            for rows, band in zip(first_band, range(2)):
                near = jnp.where(even, 0.0, given[0, band, tile])
                term = -(total[tile, rows, :] + near + given[1, band, tile])
                mixed[tile, pl.ds(band, 8, stride=2), :] = term
            for plane in range(PLANES - 1):
                piece = mixed[tile, 2 * plane : 2 * plane + 2, 0:width]
                out_ref[plane, :, lanes] = piece

        tile_loop(begin, min(end, TAIL_TILE), result)
        if end > TAIL_TILE:
            result(TAIL_TILE, 0, MERGED - TAIL)
    wait_given([5])
    for q, (begin, end) in enumerate(QUARTERS):

        def last_result(tile, j, q=q, width=128):
            lanes = pl.ds(tile * 128, width)
            if width == 128:
                lanes = pl.ds(pl.multiple_of(tile * 128, 128), 128)
            rows = slice(2 * q, 2 * q + 2)
            near = jnp.where(even, 0.0, given_fold[0, j, rows, :])
            term = total_fold[j, rows, :] + near + given_fold[1, j, rows, :]
            out_ref[PLANES - 1, :, lanes] = -term[:, 0:width]

        tile_loop(begin, min(end, TAIL_TILE), last_result)
        if end > TAIL_TILE:
            last_result(TAIL_TILE, TAIL_TILE - begin, width=MERGED - TAIL)

    for copy in near_sends():
        copy.wait_send()

    @pl.when(jnp.logical_not(even))
    def _():
        for copy in far_sends() + passes():
            copy.wait_send()

    for s in range(2):
        for copy in give_copies(s):
            copy.wait_send()
    for phase in range(2):
        for s in range(2):
            end_blocks(phase, s)


def body(bands, orbitals, pair_mask):
    hbm = pl.BlockSpec(memory_space=pltpu.HBM)
    smem = pl.BlockSpec(memory_space=pltpu.SMEM)
    consts = [jnp.asarray(table) for table in tables()]
    dma = pltpu.SemaphoreType.DMA

    def buffer(*shape):
        return pltpu.VMEM(shape, jnp.float32)

    out = pl.pallas_call(
        functools.partial(kernel, bands),
        out_shape=jax.ShapeDtypeStruct((PLANES, 2, MERGED), jnp.float32),
        in_specs=[smem] + [hbm] * (1 + len(consts)),
        out_specs=pl.BlockSpec(memory_space=pltpu.VMEM),
        scratch_shapes=[
            buffer(PLANES, 2, MERGED),
            pltpu.VMEM(consts[0].shape, jnp.bfloat16),
            buffer(*consts[1].shape),
            buffer(*consts[2].shape),
            buffer(TILES, 16, 128),
            buffer(TILES, 16, 128),
            buffer(FOLD + 1, 8, 128),
            buffer(2, TILES, 16, 128),
            buffer(2, FOLD + 1, 8, 128),
            buffer(TILES, ROWS, 128),
            buffer(NG * 8, 128),
            buffer(NG * 8, 128),
            buffer(2, FIELDS + 1, PEERS * PART, 128),
            buffer(2, PEERS * LAST, 128),
            buffer(2, ROWS, 128),
            buffer(2, FIELDS, PIECE, 128),
            buffer(2, FIELDS, PEERS * PART, 128),
            buffer(2, PEERS * LAST, 128),
            buffer(2, PEERS * PIECE, 128),
            buffer(2, FIELDS, PEERS * PART, 128),
            buffer(2, PEERS * LAST, 128),
            buffer(2, PEERS * PIECE, 128),
            buffer(2, FIELDS + 1, PEERS * PART, 128),
            buffer(2, PEERS * LAST, 128),
            buffer(2, ROWS, 128),
            buffer(2, FIELDS, PIECE, 128),
            buffer(NG, OWN),
            buffer(NG, 128),
            buffer(TILES, 16, 128),
            buffer(FOLD + 1, 8, 128),
            buffer(2, TILES, 8, 128),
            buffer(FOLD + 1, 8, 128),
            buffer(2, 2, TILES, 8, 128),
            buffer(2, FOLD + 1, 8, 128),
            buffer(2, 2, TILES, 8, 128),
            buffer(2, FOLD + 1, 8, 128),
            dma((2, 5)),
            dma((2, 5)),
            dma((5,)),
            dma((2, 6)),
            dma((2, 6)),
            dma((2, 2)),
            dma((2, 2, FIELDS)),
            dma((2, 2)),
            dma((2, 2)),
            dma((2, FIELDS)),
            dma((2, PEERS)),
            dma((2, PEERS)),
            dma((2, FIELDS)),
            dma((4,)),
        ],
        compiler_params=pltpu.CompilerParams(
            collective_id=0, has_side_effects=True, vmem_limit_bytes=64 * 1024 * 1024 - 65536
        ),
    )(pair_mask, orbitals.transpose(1, 0, 2), *consts)
    return out.transpose(1, 0, 2)


def solution(mesh):
    return jax.shard_map(
        functools.partial(body, mesh.shape["band"]),
        mesh=mesh,
        in_specs=(P("band", "pencil", None), P("band", None, None, None)),
        out_specs=P("band", "pencil", None),
        check_vma=False,
    )
```

```python
import functools
import math

import jax
import jax.numpy as jnp
import ml_dtypes
import numpy as np
from jax import lax
from jax.experimental import pallas as pl
from jax.experimental.pallas import tpu as pltpu
from jax.sharding import PartitionSpec as P

MESH = pl.DeviceIdType.MESH
NG = 72
PLANES = 9
PEERS = 8
FIELDS = 4
ROWS = 40
PART = 40
LAST = 24
MERGED = NG * NG
WIDTH = 5248
OWN = 640
TAIL = PEERS * OWN
PIECE = 16
FOLD = 11
MASKS = FOLD
QUARTERS = [(q * FOLD, min((q + 1) * FOLD, 41)) for q in range(4)]
TILES = WIDTH // 128
OWN_TILES = OWN // 128
TAIL_TILE = TILES - 1
coulomb_scale = 20.0
screening = 0.25
HALF = math.sqrt(0.5)


def dft8(x):
    a = [x[j] + x[j + 4] for j in range(4)]
    b = [x[j] - x[j + 4] for j in range(4)]
    e, o = a[0] + a[2], a[1] + a[3]
    u, v = HALF * (b[1] - b[3]), HALF * (b[1] + b[3])
    return [e + o, e - o, b[0] + u, v + b[2], a[0] - a[2], a[1] - a[3], b[0] - u, v - b[2]]


def dft8_adjoint(c):
    p, q = c[0] + c[1], c[0] - c[1]
    a = [p + c[4], q + c[5], p - c[4], q - c[5]]
    d, s = HALF * (c[2] - c[6]), HALF * (c[3] + c[7])
    b = [c[2] + c[6], d + s, c[3] - c[7], s - d]
    return [a[j] + b[j] for j in range(4)] + [a[j] - b[j] for j in range(4)]


def cos9(n):
    return math.cos(2.0 * math.pi * (n % 9) / 9)


def sin9(n):
    return math.sin(2.0 * math.pi * (n % 9) / 9)


def weighted(values, factors):
    total = values[0] * factors[0]
    for value, factor in zip(values[1:], factors[1:]):
        total = total + value * factor
    return total


def dft9(x):
    e = [x[n] + x[9 - n] for n in range(1, 5)]
    o = [x[n] - x[9 - n] for n in range(1, 5)]
    third = e[0] + e[1] + e[3]
    cosines = [x[0] + third + e[2]]
    sines = [None]
    for k in range(1, 5):
        if k == 3:
            cosines.append(x[0] + e[2] - 0.5 * third)
            sines.append(sin9(3) * (o[0] - o[1] + o[3]))
        else:
            cosines.append(x[0] + weighted(e, [cos9(k * n) for n in range(1, 5)]))
            sines.append(weighted(o, [sin9(k * n) for n in range(1, 5)]))
    return cosines, sines


def dft9_adjoint(cosines, sines):
    c, s = cosines, sines
    out = [None] * 9
    out[0] = c[0] + ((c[1] + c[2]) + (c[3] + c[4]))
    for n in range(1, 5):
        if n == 3:
            even = c[0] + c[3] - 0.5 * (c[1] + c[2] + c[4])
            odd = sin9(3) * (s[1] - s[2] + s[4])
        else:
            even = c[0] + weighted(c[1:], [cos9(k * n) for k in range(1, 5)])
            odd = weighted(s[1:], [sin9(k * n) for k in range(1, 5)])
        out[n] = even + odd
        out[9 - n] = even - odd
    return out


def finish72(load, save):
    for part in (0, 1):
        cosines, sines = dft9([load(part, b) for b in range(9)])
        base = part * 9
        save(base, cosines[0])
        for k in range(1, 5):
            save(base + 2 * k - 1, cosines[k])
            save(base + 2 * k, sines[k])
    for k8 in range(3):
        base = 18 + 18 * k8
        cc, cs = dft9([load(2 + 2 * k8, b) for b in range(9)])
        sc, ss = dft9([load(3 + 2 * k8, b) for b in range(9)])
        save(base, cc[0])
        save(base + 1, sc[0])
        for k in range(1, 5):
            at = base + 4 * k - 2
            save(at, cc[k] - ss[k])
            save(at + 1, cc[k] + ss[k])
            save(at + 2, sc[k] + cs[k])
            save(at + 3, sc[k] - cs[k])


def finish72_adjoint(load, save):
    for part in (0, 1):
        base = part * 9
        cosines = [load(base)] + [load(base + 2 * k - 1) for k in range(1, 5)]
        sines = [None] + [load(base + 2 * k) for k in range(1, 5)]
        for b, value in enumerate(dft9_adjoint(cosines, sines)):
            save(part, b, value)
    for k8 in range(3):
        base = 18 + 18 * k8
        cc, sc, cs, ss = [load(base)], [load(base + 1)], [None], [None]
        for k in range(1, 5):
            at = base + 4 * k - 2
            plus, minus, sine_plus, sine_minus = [load(at + i) for i in range(4)]
            cc.append(plus + minus)
            ss.append(minus - plus)
            sc.append(sine_plus + sine_minus)
            cs.append(sine_plus - sine_minus)
        for b, value in enumerate(dft9_adjoint(cc, cs)):
            save(2 + 2 * k8, b, value)
        for b, value in enumerate(dft9_adjoint(sc, ss)):
            save(3 + 2 * k8, b, value)


def point72(a, b):
    return (9 * a + 8 * b) % NG


def split(table):
    high = table.astype(ml_dtypes.bfloat16).astype(np.float64)
    return high, (table - high).astype(ml_dtypes.bfloat16).astype(np.float64)


def from_left(table):
    high, low = split(table)
    wide = np.zeros((80, 256))
    wide[:NG, : 3 * NG] = np.concatenate([high, high, low], axis=1)
    return wide


def from_right(table):
    high, low = split(table)
    return np.block([[high, low], [high, np.zeros_like(low)]])


@functools.cache
def tables():
    at = np.arange(NG)
    basis, freq = [np.full(NG, 1.0)], [0]
    for k in range(1, NG // 2):
        basis += [np.cos(2 * np.pi * k * at / NG), np.sin(2 * np.pi * k * at / NG)]
        freq += [k, k]
    basis.append(np.cos(np.pi * at))
    freq.append(NG // 2)
    basis = np.array(basis)
    basis /= np.sqrt((basis * basis).sum(1, keepdims=True))
    freq = np.array(freq, np.float64)
    eye = np.eye(NG)
    parts = [dft8([eye[point72(a, b)] for a in range(8)]) for b in range(9)]
    slots = [None] * NG
    finish72(lambda part, b: parts[b][part], slots.__setitem__)
    slots = np.array(slots)
    norm = (slots * slots).sum(1)
    spectrum = np.abs(np.fft.fft(slots, axis=1))[:, : NG // 2 + 1]
    freq_y = spectrum.argmax(1).astype(np.float64)
    along_z = np.zeros((128, 128))
    along_z[:NG, :NG] = basis.T
    along_x = basis.reshape(NG, PEERS, PLANES)
    along_x = np.concatenate([along_x[:, :, :8].reshape(NG, -1), along_x[:, :, 8]], axis=1)
    column = np.zeros((8, WIDTH), np.float32)
    column[0, :MERGED] = (freq_y[:, None] ** 2 + freq[None, :] ** 2).reshape(-1)
    column[1, :MERGED] = np.repeat(1.0 / norm, NG)
    freq_x = np.broadcast_to((freq**2)[:, None], (NG, 128)).astype(np.float32)
    wide = np.concatenate(
        [from_right(along_z), from_right(along_z.T), from_left(along_x), from_left(along_x.T)]
    )
    return wide.astype(ml_dtypes.bfloat16), column, freq_x


def take(load, start):
    tile, lane = divmod(start, 128)
    value = load(tile)
    if lane == 0:
        return value
    if lane + NG > 128:
        at = lax.broadcasted_iota(jnp.int32, value.shape, 1)
        value = jnp.where(at >= lane, value, load(tile + 1))
    return pltpu.roll(value, 128 - lane, 1)


def put(store, start, value):
    tile, lane = divmod(start, 128)
    if lane:
        value = pltpu.roll(value, lane, 1)
    end = min(lane + NG, 128)
    store(tile, slice(lane, end), value[:, lane:end])
    if lane + NG > 128:
        store(tile + 1, slice(0, lane + NG - 128), value[:, : lane + NG - 128])


def matmul(a, b):
    return jnp.dot(a, b, preferred_element_type=jnp.float32)


def halves(x):
    high = x.astype(jnp.bfloat16)
    return high, (x - high.astype(jnp.float32)).astype(jnp.bfloat16)


def left(table, x):
    high, low = [part.astype(jnp.float32) for part in halves(x)]
    zeros = jnp.zeros((8, x.shape[1]), jnp.float32)
    operand = jnp.concatenate([high, low, high, zeros], axis=0).astype(jnp.bfloat16)
    return matmul(table[:, 0 : operand.shape[0]], operand)[0:NG]


def kernel(
    bands,
    mask_ref,
    bands_hbm,
    wide_hbm,
    column_hbm,
    freq_hbm,
    out_ref,
    bands_ref,
    wide,
    column_ref,
    freq_ref,
    mixed,
    own,
    own_fold,
    visit,
    visit_fold,
    rho,
    work,
    work2,
    wave,
    wave_fold,
    wave_tail,
    wave_piece,
    recv,
    recv_fold,
    recv_tail,
    back,
    back_fold,
    back_tail,
    field,
    field_fold,
    field_tail,
    field_piece,
    kernel_table,
    kernel_tail,
    total,
    total_fold,
    base,
    base_fold,
    give,
    give_fold,
    given,
    given_fold,
    visit_send,
    visit_recv,
    pass_send,
    give_send,
    give_recv,
    part_send,
    part_recv,
    fold_send,
    fold_recv,
    tail_send,
    tail_recv,
    back_tail_send,
    back_tail_recv,
    load_sem,
):
    me = lax.axis_index("pencil")
    group = lax.axis_index("band")
    me_x, me_y = lax.div(me, 4), lax.rem(me, 4)

    loads = [
        pltpu.make_async_copy(src, dst, load_sem.at[i])
        for i, (src, dst) in enumerate(
            [
                (bands_hbm, bands_ref),
                (wide_hbm, wide),
                (column_hbm, column_ref),
                (freq_hbm, freq_ref),
            ]
        )
    ]
    for load in loads:
        load.start()

    def peer(j):
        return lax.rem(me + j, PEERS)

    def at(dx, dy):
        return lax.rem(me_x + dx, 2) * 4 + lax.rem(me_y + dy + 4, 4)

    def group_at(j):
        return lax.rem(group + j + bands, bands)

    barrier = pltpu.get_barrier_semaphore()
    for j in range(1, PEERS):
        pl.semaphore_signal(barrier, inc=1, device_id={"pencil": peer(j)}, device_id_type=MESH)
    for j in (-2, -1, 1, 2):
        pl.semaphore_signal(barrier, inc=1, device_id={"band": group_at(j)}, device_id_type=MESH)
    def remote(src, dst, send, recv, **device):
        return pltpu.make_async_remote_copy(
            src_ref=src,
            dst_ref=dst,
            send_sem=send,
            recv_sem=recv,
            device_id=device,
            device_id_type=MESH,
        )

    even = lax.rem(group, 2) == 0

    def terms_group(s):
        near = jnp.where(even, group_at(1), group_at(-1))
        return jnp.where(s == 0, near, jnp.where(even, group_at(2), group_at(-2)))

    def parts(main, fold):
        return [
            *(main.at[pl.ds(begin, end - begin)] for begin, end in QUARTERS),
            fold,
        ]

    def block_copies(src, dst, send, recv, to):
        return [
            remote(one, two, send.at[q], recv.at[q], band=to)
            for q, (one, two) in enumerate(zip(src, dst))
        ]

    def visit_at(s):
        return parts(visit.at[s], visit_fold.at[s])

    own_parts = parts(own, own_fold)

    def give_parts(main, fold):
        return [main.at[0], *parts(main.at[1], fold)]

    def visit_copies(s, src, send, to):
        return block_copies(src, visit_at(s), send, visit_recv.at[s], to)

    def near_sends():
        return visit_copies(0, own_parts, visit_send.at[0], group_at(-1))

    def far_sends():
        return visit_copies(1, own_parts, visit_send.at[1], group_at(2))

    def passes():
        return visit_copies(1, visit_at(0), pass_send, group_at(-1))

    loads[0].wait()
    def take_tile(tile, j, q, width):
        lanes = pl.ds(tile * 128, width)
        if width == 128:
            lanes = pl.ds(pl.multiple_of(tile * 128, 128), 128)
        live = slice(0, width)
        for plane in range(PLANES - 1):
            mixed[tile, 2 * plane : 2 * plane + 2, live] = bands_ref[plane, :, lanes]
        for band in range(2):
            own[tile, band * 8 : band * 8 + 8, :] = mixed[tile, pl.ds(band, 8, stride=2), :]
        own_fold[j, 2 * q : 2 * q + 2, live] = bands_ref[PLANES - 1, :, lanes]

    def tile_loop(begin, end, step):
        def run(j, carry):
            step(begin + j, j)
            return carry

        lax.fori_loop(0, end - begin, run, 0, unroll=True)

    mixed[TAIL_TILE] = jnp.zeros((16, 128), jnp.float32)
    own_fold[TAIL_TILE % FOLD, 6:8, :] = jnp.zeros((2, 128), jnp.float32)

    def own_mask(s, f):
        return mask_ref[0, s, f // 2, f % 2].astype(jnp.float32)

    for m in range(2 * FIELDS):
        value = own_mask(m // FIELDS, m % FIELDS)
        own_fold[MASKS, m : m + 1, :] = jnp.zeros((1, 128), jnp.float32) + value
    pl.semaphore_wait(barrier, PEERS - 1 + 4)
    near, far = near_sends(), far_sends()

    def send_own(part):
        near[part].start()

        @pl.when(jnp.logical_not(even))
        def _():
            far[part].start()

    for q, (begin, end) in enumerate(QUARTERS):
        tile_loop(begin, min(end, TAIL_TILE), lambda tile, j, q=q: take_tile(tile, j, q, 128))
        if end > TAIL_TILE:
            take_tile(TAIL_TILE, TAIL_TILE % FOLD, q, MERGED - TAIL)
        send_own(q)
    send_own(4)

    def kernel_columns(start, width):
        squared = column_ref[0:1, pl.ds(start, width)]
        scale = column_ref[1:2, pl.ds(start, width)]
        return coulomb_scale / (freq_ref[:, 0:1] + squared + screening) * scale

    for load in loads[1:]:
        load.wait()
    kernel_table[...] = kernel_columns(pl.multiple_of(me * OWN, 128), OWN)
    kernel_tail[...] = kernel_columns(TAIL, 128)
    wave_tail[...] = jnp.zeros((2, ROWS, 128), jnp.float32)
    total_fold[...] = jnp.zeros((FOLD + 1, 8, 128), jnp.float32)
    base_fold[...] = jnp.zeros((FOLD + 1, 8, 128), jnp.float32)

    def clear(tile, carry):
        total[tile] = jnp.zeros((16, 128), jnp.float32)
        base[:, tile] = jnp.zeros((2, 8, 128), jnp.float32)
        return carry

    lax.fori_loop(0, TILES, clear, 0)
    for s in range(2):
        for p in range(PEERS):
            back_fold[s, (p + 1) * LAST - 8 : (p + 1) * LAST, :] = jnp.zeros((8, 128), jnp.float32)
            back_tail[s, (p + 1) * PIECE - 8 : (p + 1) * PIECE, :] = jnp.zeros((8, 128), jnp.float32)
        field_tail[s, 32:40, :] = jnp.zeros((8, 128), jnp.float32)
        for f in range(FIELDS):
            wave_piece[s, f, 8:16, :] = jnp.zeros((8, 128), jnp.float32)

    first_band = [slice(band * 8, band * 8 + 8) for band in range(2)]
    field_rows = [slice(f * 8, f * 8 + 8) for f in range(FIELDS)]
    row_at = lax.broadcasted_iota(jnp.int32, (8, 128), 0)
    resident_one = lax.rem(lax.div(row_at, 2), 2) == 1
    visitor_one = lax.rem(row_at, 2) == 1

    def last_planes(s, j, q):
        a = [own_fold[j, 2 * q + band : 2 * q + band + 1, :] for band in range(2)]
        c = [visit_fold[s, j, 2 * q + band : 2 * q + band + 1, :] for band in range(2)]
        wide_a = [jnp.broadcast_to(row, (8, 128)) for row in a]
        wide_c = [jnp.broadcast_to(row, (8, 128)) for row in c]
        return (
            jnp.where(resident_one, wide_a[1], wide_a[0]),
            jnp.where(visitor_one, wide_c[1], wide_c[0]),
        )

    def along_z(start):
        for i in range(2):
            rows = pl.ds(i * 288, 288)
            both = matmul(jnp.concatenate(halves(work[rows, :]), axis=1), wide[start : start + 256, :])
            work2[rows, :] = both[:, :128] + both[:, 128:]

    def place(part, b):
        return slice((part * 9 + b) * 8, (part * 9 + b) * 8 + 8)

    def row_of(t):
        return pl.ds(pl.multiple_of(t * 8, 8), 8)

    def first(s):
        arriving = visit_copies(s, own_parts, visit_send.at[0], group_at(1))
        passing = passes()
        for q in range(5):
            arriving[q].wait_recv()

            @pl.when((s == 0) & jnp.logical_not(even))
            def _(q=q):
                passing[q].start()

        def one_row(i, carry):
            t = jnp.where(i == 0, FIELDS, order(jnp.maximum(i - 1, 0)))

            @pl.when(i > 0)
            def _():
                resident, visitor = row_of(lax.div(t, 2)), row_of(lax.rem(t, 2))
                for tile in range(TILES):
                    rho[tile, row_of(t), :] = own[tile, resident, :] * visit[s, tile, visitor, :]

            @pl.when(i == 0)
            def _():
                for q, (begin, end) in enumerate(QUARTERS):

                    def products(tile, j, q=q):
                        phi, chi = last_planes(s, j, q)
                        rho[tile, 32:40, :] = phi * chi

                    tile_loop(begin, end, products)

            for b in range(9):
                starts = [point72(a, b) * NG for a in range(8)]
                values = [take(lambda tile: rho[tile, row_of(t), :], at) for at in starts]
                for part, value in enumerate(dft8(values)):
                    work[place(part, b), :] = value
            along_z(0)

            def load(part, b):
                return work2[place(part, b), :]

            def target(tile, lanes, piece):
                if tile == TAIL_TILE:
                    wave_tail[s, row_of(t), lanes] = piece
                else:
                    wave[s, t, tile * 8 : tile * 8 + 8, lanes] = piece

            def save(slot, value):
                put(target, slot * NG, value)

            finish72(load, save)

            @pl.when(i == 0)
            def _():
                upper = lax.broadcasted_iota(jnp.int32, (8, 128), 0) < FIELDS

                def fold(q, carry):
                    for k in range(3):
                        at_row = pl.multiple_of((q * OWN_TILES + k) * 8, 8)
                        piece = wave[s, FIELDS, pl.ds(at_row, 8), :]
                        if k < 2:
                            below = wave[s, FIELDS, pl.ds(at_row + 24, 8), :]
                            piece = jnp.where(upper, piece, below)
                        to_row = pl.multiple_of(q * LAST + k * 8, 8)
                        wave_fold[s, pl.ds(to_row, 8), :] = piece
                    return carry

                lax.fori_loop(0, PEERS, fold, 0)
                send_fold(0, s)

            @pl.when(i > 0)
            def _():
                send_part(0, s, t)

            return carry

        lax.fori_loop(0, FIELDS + 1, one_row, 0)
        for f in range(FIELDS):
            wave_piece[s, f, 0:8, :] = wave_tail[s, field_rows[f], :]
            wave_piece[s, f, 8:9, :] = wave_tail[s, 32 + f : 33 + f, :]

    part_refs = ((wave, recv), (back, field))
    fold_refs = ((wave_fold, recv_fold), (back_fold, field_fold))
    straight = [(1, 2), (0, 2), (1, 1), (1, 3), (0, 1), (0, 3), (1, 0)]

    def rows_of(index, rows):
        return pl.ds(pl.multiple_of(index * rows, 8), rows)

    def send_part(phase, s, f):
        src, dst = part_refs[phase]
        for dx, dy in straight:
            to = at(dx, dy)
            remote(
                src.at[s, f, rows_of(to, PART)],
                dst.at[s, f, rows_of(me, PART)],
                part_send.at[phase, s],
                part_recv.at[phase, s, f],
                pencil=to,
            ).start()
        dst[s, f, rows_of(me, PART), :] = src[s, f, rows_of(me, PART), :]

    def send_fold(phase, s):
        src, dst = fold_refs[phase]
        for dx, dy in straight:
            to = at(dx, dy)
            remote(
                src.at[s, rows_of(to, LAST)],
                dst.at[s, rows_of(me, LAST)],
                fold_send.at[phase, s],
                fold_recv.at[phase, s],
                pencil=to,
            ).start()
        dst[s, rows_of(me, LAST), :] = src[s, rows_of(me, LAST), :]

    def drain(view, sem):
        pltpu.make_async_copy(view, view, sem).wait()

    def wait_part(phase, s, f):
        drain(part_refs[phase][1].at[s, f, pl.ds(0, 7 * PART)], part_recv.at[phase, s, f])

    def wait_fold(phase, s):
        drain(fold_refs[phase][1].at[s, pl.ds(0, 7 * LAST)], fold_recv.at[phase, s])

    def end_blocks(phase, s):
        parts = part_refs[phase][0].at[s, pl.ds(0, FIELDS), pl.ds(0, 7 * PART)]
        drain(parts, part_send.at[phase, s])
        drain(fold_refs[phase][0].at[s, pl.ds(0, 7 * LAST)], fold_send.at[phase, s])

    def piece_of(ref, s, index):
        return ref.at[s, pl.ds(pl.multiple_of(index * PIECE, 8), PIECE), :]

    def owner_of(s, f):
        return FIELDS * s + f

    def tail_copy(s, f, distance):
        return remote(
            wave_piece.at[s, f],
            piece_of(recv_tail, s, me),
            tail_send.at[s, f],
            tail_recv.at[s, distance],
            pencil=owner_of(s, f),
        )

    def second(s):
        wait_fold(0, s)

        def last_rows(f, tile):
            return pl.ds(tile % 3 * 8 + FIELDS * (tile // 3) + f, PEERS, stride=LAST)

        def one_field(i, carry):
            f = order(i)
            wait_part(0, s, f)
            columns = []
            for tile in range(OWN_TILES):
                starts = [p * PART + tile * 8 for p in range(PEERS)]
                rows = [recv[s, f, start : start + 8, :] for start in starts]
                rows.append(recv_fold[s, last_rows(f, tile), :])
                columns.append(jnp.concatenate(rows, axis=0))
            spectrum = left(wide[512:592, :], jnp.concatenate(columns, axis=1))
            result = left(wide[592:672, :], spectrum * kernel_table[...])
            for tile in range(OWN_TILES):
                lanes = slice(tile * 128, tile * 128 + 128)
                for p in range(PEERS):
                    start = p * PART + tile * 8
                    back[s, f, start : start + 8, :] = result[p * 8 : p * 8 + 8, lanes]
                back_fold[s, last_rows(f, tile), :] = result[64:72, lanes]
            send_part(1, s, f)
            return carry

        lax.fori_loop(0, FIELDS, one_field, 0)
        send_fold(1, s)

    def give_copies(s):
        return block_copies(
            give_parts(give.at[s], give_fold.at[s]),
            give_parts(given.at[s], given_fold.at[s]),
            give_send.at[s],
            give_recv.at[s],
            terms_group(s),
        )

    def order(i):
        return lax.rem(2 * i, FIELDS) + lax.div(i, 2)

    def pair_weights(s):
        weights = []
        for f in range(FIELDS):
            g = 2 * (f % 2) + f // 2
            above = visit_fold[s, MASKS, FIELDS + g : FIELDS + g + 1, :]
            same = visit_fold[s, MASKS, g : g + 1, :]
            mine = own_fold[MASKS, FIELDS + f : FIELDS + f + 1, :]
            row = jnp.where(s == 0, same, jnp.where(even, above, mine))
            weights.append(jnp.broadcast_to(row, (8, 128)))
        return weights

    def third(s):
        weights = pair_weights(s)
        leaving = give_copies(s)

        def leave(which):
            for part in which:
                leaving[part].start()

        def gather_band(c, begin, end):
            def gather(tile, j):
                chi = visit[s, tile, first_band[c], :]
                terms = base[c, tile]
                for a in range(2):
                    value = rho[tile, field_rows[2 * a + c], :] * weights[2 * a + c]
                    total[tile, first_band[a], :] += value * chi
                    terms = terms + value * own[tile, first_band[a], :]
                give[s, c, tile] = terms

            tile_loop(begin, end, gather)

        def one_row(i, carry):
            t = jnp.where(i == FIELDS, FIELDS, order(jnp.minimum(i, FIELDS - 1)))

            @pl.when(t < FIELDS)
            def _():
                wait_part(1, s, t)

            @pl.when(t == FIELDS)
            def _():
                wait_fold(1, s)

                def unfold(q, carry):
                    for k in range(OWN_TILES):
                        from_row = pl.multiple_of(q * LAST + k % 3 * 8, 8)
                        value = field_fold[s, pl.ds(from_row, 8), :]
                        value = pltpu.roll(value, FIELDS, 0) if k > 2 else value
                        to_row = pl.multiple_of((q * OWN_TILES + k) * 8, 8)
                        field[s, FIELDS, pl.ds(to_row, 8), :] = value
                    return carry

                lax.fori_loop(0, PEERS, unfold, 0)

            def source(tile):
                if tile == TAIL_TILE:
                    return field_tail[s, row_of(t), :]
                return field[s, t, tile * 8 : tile * 8 + 8, :]

            def load(slot):
                return take(source, slot * NG)

            def save(part, b, value):
                work[place(part, b), :] = value

            finish72_adjoint(load, save)
            along_z(256)

            def target(tile, lanes, piece):
                rho[tile, row_of(t), lanes] = piece

            for b in range(9):
                values = dft8_adjoint([work2[place(part, b), :] for part in range(8)])
                for a, value in enumerate(values):
                    put(target, point72(a, b) * NG, value)

            @pl.when((s == 1) & even & (i == 1))
            def _():
                for copy in give_copies(0):
                    copy.wait_recv()

                def join(tile, carry):
                    for band in range(2):
                        base[band, tile] = given[0, band, tile]
                    return carry

                lax.fori_loop(0, TILES, join, 0)
                base_fold[...] = given_fold[0]

            @pl.when(i == 1)
            def _():
                gather_band(0, 0, TILES)
                leave([0])

            return carry

        lax.fori_loop(0, FIELDS + 1, one_row, 0)
        last_weight = weights[3]
        for f in range(3):
            last_weight = jnp.where(row_at == f, weights[f], last_weight)

        for q, (begin, end) in enumerate(QUARTERS):
            gather_band(1, begin, end)
            leave([1 + q])

            def gather_last(tile, j, q=q):
                phi, chi = last_planes(s, j, q)
                value = rho[tile, 32:40, :] * last_weight
                stay, leave = value * chi, value * phi
                stay = stay + pltpu.roll(stay, 7, 0)
                leave = leave + pltpu.roll(leave, 6, 0)
                for band in range(2):
                    row = slice(2 * q + band, 2 * q + band + 1)
                    total_fold[j, row, :] += stay[2 * band : 2 * band + 1]
                    give_fold[s, j, row, :] = leave[band : band + 1] + base_fold[j, row, :]

            tile_loop(begin, end, gather_last)
        leave([5])

    def tail_back(s, f, j):
        return remote(
            piece_of(back_tail, s, peer(j)),
            field_piece.at[s, f],
            back_tail_send.at[s, j],
            back_tail_recv.at[s, f],
            pencil=peer(j),
        )

    def send_tail(s):
        for f in range(FIELDS):
            owner = owner_of(s, f)

            @pl.when(me == owner)
            def _(f=f, owner=owner):
                recv_tail[s, rows_of(owner, PIECE), :] = wave_piece[s, f]

            @pl.when(me != owner)
            def _(f=f, owner=owner):
                tail_copy(s, f, lax.rem(owner - me + PEERS, PEERS)).start()

    def turn_tail(s):
        owned = lax.div(me, FIELDS) == s

        @pl.when(owned)
        def _():
            for j in range(1, PEERS):
                tail_copy(s, 0, j).wait_recv()
            parts = [pl.ds(p * PIECE, 8) for p in range(PEERS)] + [pl.ds(8, PEERS, stride=PIECE)]
            block = jnp.concatenate([recv_tail[s, part, :] for part in parts], axis=0)
            spectrum = left(wide[512:592, :], block) * kernel_tail[...]
            result = left(wide[592:672, :], spectrum)
            for i, part in enumerate(parts):
                back_tail[s, part, :] = result[i * 8 : i * 8 + 8, :]
            mine = lax.rem(me, FIELDS)
            for j in range(1, PEERS):
                tail_back(s, mine, j).start()
            field_piece[s, mine] = back_tail[s, pl.ds(pl.multiple_of(me * PIECE, 8), PIECE), :]

    def end_tail(s):
        for f in range(FIELDS):
            owner = owner_of(s, f)

            @pl.when(me != owner)
            def _(f=f, owner=owner):
                tail_copy(s, f, lax.rem(owner - me + PEERS, PEERS)).wait_send()
                tail_back(s, f, 1).wait_recv()

            field_tail[s, field_rows[f], :] = field_piece[s, f, 0:8, :]
            field_tail[s, 32 + f : 33 + f, :] = field_piece[s, f, 8:9, :]

        @pl.when(lax.div(me, FIELDS) == s)
        def _():
            for j in range(1, PEERS):
                tail_back(s, lax.rem(me, FIELDS), j).wait_send()

    def slots(*stages):
        def run(s, carry):
            for stage in stages:
                stage(s)
            return carry

        lax.fori_loop(0, 2, run, 0)

    slots(first, send_tail)
    slots(second, turn_tail)
    slots(end_tail, third)

    def wait_given(which):
        for part in which:
            give_copies(1)[part].wait_recv()

            @pl.when(jnp.logical_not(even))
            def _(part=part):
                give_copies(0)[part].wait_recv()

    for q, (begin, end) in enumerate(QUARTERS):
        wait_given([0, 1] if q == 0 else [1 + q])

        def result(tile, j, width=128):
            lanes = pl.ds(tile * 128, width)
            if width == 128:
                lanes = pl.ds(pl.multiple_of(tile * 128, 128), 128)
            for rows, band in zip(first_band, range(2)):
                near = jnp.where(even, 0.0, given[0, band, tile])
                term = -(total[tile, rows, :] + near + given[1, band, tile])
                mixed[tile, pl.ds(band, 8, stride=2), :] = term
            for plane in range(PLANES - 1):
                piece = mixed[tile, 2 * plane : 2 * plane + 2, 0:width]
                out_ref[plane, :, lanes] = piece

        tile_loop(begin, min(end, TAIL_TILE), result)
        if end > TAIL_TILE:
            result(TAIL_TILE, 0, MERGED - TAIL)
    wait_given([5])
    for q, (begin, end) in enumerate(QUARTERS):

        def last_result(tile, j, q=q, width=128):
            lanes = pl.ds(tile * 128, width)
            if width == 128:
                lanes = pl.ds(pl.multiple_of(tile * 128, 128), 128)
            rows = slice(2 * q, 2 * q + 2)
            near = jnp.where(even, 0.0, given_fold[0, j, rows, :])
            term = total_fold[j, rows, :] + near + given_fold[1, j, rows, :]
            out_ref[PLANES - 1, :, lanes] = -term[:, 0:width]

        tile_loop(begin, min(end, TAIL_TILE), last_result)
        if end > TAIL_TILE:
            last_result(TAIL_TILE, TAIL_TILE - begin, width=MERGED - TAIL)

    for copy in near_sends():
        copy.wait_send()

    @pl.when(jnp.logical_not(even))
    def _():
        for copy in far_sends() + passes():
            copy.wait_send()

    for s in range(2):
        for copy in give_copies(s):
            copy.wait_send()
    for phase in range(2):
        for s in range(2):
            end_blocks(phase, s)


def body(bands, orbitals, pair_mask):
    hbm = pl.BlockSpec(memory_space=pltpu.HBM)
    smem = pl.BlockSpec(memory_space=pltpu.SMEM)
    consts = [jnp.asarray(table) for table in tables()]
    dma = pltpu.SemaphoreType.DMA

    def buffer(*shape):
        return pltpu.VMEM(shape, jnp.float32)

    out = pl.pallas_call(
        functools.partial(kernel, bands),
        out_shape=jax.ShapeDtypeStruct((PLANES, 2, MERGED), jnp.float32),
        in_specs=[smem] + [hbm] * (1 + len(consts)),
        out_specs=pl.BlockSpec(memory_space=pltpu.VMEM),
        scratch_shapes=[
            buffer(PLANES, 2, MERGED),
            pltpu.VMEM(consts[0].shape, jnp.bfloat16),
            buffer(*consts[1].shape),
            buffer(*consts[2].shape),
            buffer(TILES, 16, 128),
            buffer(TILES, 16, 128),
            buffer(FOLD + 1, 8, 128),
            buffer(2, TILES, 16, 128),
            buffer(2, FOLD + 1, 8, 128),
            buffer(TILES, ROWS, 128),
            buffer(NG * 8, 128),
            buffer(NG * 8, 128),
            buffer(2, FIELDS + 1, PEERS * PART, 128),
            buffer(2, PEERS * LAST, 128),
            buffer(2, ROWS, 128),
            buffer(2, FIELDS, PIECE, 128),
            buffer(2, FIELDS, PEERS * PART, 128),
            buffer(2, PEERS * LAST, 128),
            buffer(2, PEERS * PIECE, 128),
            buffer(2, FIELDS, PEERS * PART, 128),
            buffer(2, PEERS * LAST, 128),
            buffer(2, PEERS * PIECE, 128),
            buffer(2, FIELDS + 1, PEERS * PART, 128),
            buffer(2, PEERS * LAST, 128),
            buffer(2, ROWS, 128),
            buffer(2, FIELDS, PIECE, 128),
            buffer(NG, OWN),
            buffer(NG, 128),
            buffer(TILES, 16, 128),
            buffer(FOLD + 1, 8, 128),
            buffer(2, TILES, 8, 128),
            buffer(FOLD + 1, 8, 128),
            buffer(2, 2, TILES, 8, 128),
            buffer(2, FOLD + 1, 8, 128),
            buffer(2, 2, TILES, 8, 128),
            buffer(2, FOLD + 1, 8, 128),
            dma((2, 5)),
            dma((2, 5)),
            dma((5,)),
            dma((2, 6)),
            dma((2, 6)),
            dma((2, 2)),
            dma((2, 2, FIELDS)),
            dma((2, 2)),
            dma((2, 2)),
            dma((2, FIELDS)),
            dma((2, PEERS)),
            dma((2, PEERS)),
            dma((2, FIELDS)),
            dma((4,)),
        ],
        compiler_params=pltpu.CompilerParams(
            collective_id=0, has_side_effects=True, vmem_limit_bytes=64 * 1024 * 1024 - 65536
        ),
    )(pair_mask, orbitals.transpose(1, 0, 2), *consts)
    return out.transpose(1, 0, 2)


def solution(mesh):
    return jax.shard_map(
        functools.partial(body, mesh.shape["band"]),
        mesh=mesh,
        in_specs=(P("band", "pencil", None), P("band", None, None, None)),
        out_specs=P("band", "pencil", None),
        check_vma=False,
    )
```

```python
import functools
import math

import jax
import jax.numpy as jnp
import ml_dtypes
import numpy as np
from jax import lax
from jax.experimental import pallas as pl
from jax.experimental.pallas import tpu as pltpu
from jax.sharding import PartitionSpec as P

MESH = pl.DeviceIdType.MESH
NG = 72
PLANES = 9
PEERS = 8
FIELDS = 4
ROWS = 40
PART = 40
LAST = 24
MERGED = NG * NG
WIDTH = 5248
OWN = 640
TAIL = PEERS * OWN
PIECE = 16
FOLD = 11
MASKS = FOLD
QUARTERS = [(q * FOLD, min((q + 1) * FOLD, 41)) for q in range(4)]
TILES = WIDTH // 128
OWN_TILES = OWN // 128
TAIL_TILE = TILES - 1
coulomb_scale = 20.0
screening = 0.25
HALF = math.sqrt(0.5)


def dft8(x):
    a = [x[j] + x[j + 4] for j in range(4)]
    b = [x[j] - x[j + 4] for j in range(4)]
    e, o = a[0] + a[2], a[1] + a[3]
    u, v = HALF * (b[1] - b[3]), HALF * (b[1] + b[3])
    return [e + o, e - o, b[0] + u, v + b[2], a[0] - a[2], a[1] - a[3], b[0] - u, v - b[2]]


def dft8_adjoint(c):
    p, q = c[0] + c[1], c[0] - c[1]
    a = [p + c[4], q + c[5], p - c[4], q - c[5]]
    d, s = HALF * (c[2] - c[6]), HALF * (c[3] + c[7])
    b = [c[2] + c[6], d + s, c[3] - c[7], s - d]
    return [a[j] + b[j] for j in range(4)] + [a[j] - b[j] for j in range(4)]


def cos9(n):
    return math.cos(2.0 * math.pi * (n % 9) / 9)


def sin9(n):
    return math.sin(2.0 * math.pi * (n % 9) / 9)


def weighted(values, factors):
    total = values[0] * factors[0]
    for value, factor in zip(values[1:], factors[1:]):
        total = total + value * factor
    return total


def dft9(x):
    e = [x[n] + x[9 - n] for n in range(1, 5)]
    o = [x[n] - x[9 - n] for n in range(1, 5)]
    third = e[0] + e[1] + e[3]
    cosines = [x[0] + third + e[2]]
    sines = [None]
    for k in range(1, 5):
        if k == 3:
            cosines.append(x[0] + e[2] - 0.5 * third)
            sines.append(sin9(3) * (o[0] - o[1] + o[3]))
        else:
            cosines.append(x[0] + weighted(e, [cos9(k * n) for n in range(1, 5)]))
            sines.append(weighted(o, [sin9(k * n) for n in range(1, 5)]))
    return cosines, sines


def dft9_adjoint(cosines, sines):
    c, s = cosines, sines
    out = [None] * 9
    out[0] = c[0] + ((c[1] + c[2]) + (c[3] + c[4]))
    for n in range(1, 5):
        if n == 3:
            even = c[0] + c[3] - 0.5 * (c[1] + c[2] + c[4])
            odd = sin9(3) * (s[1] - s[2] + s[4])
        else:
            even = c[0] + weighted(c[1:], [cos9(k * n) for k in range(1, 5)])
            odd = weighted(s[1:], [sin9(k * n) for k in range(1, 5)])
        out[n] = even + odd
        out[9 - n] = even - odd
    return out


def finish72(load, save):
    for part in (0, 1):
        cosines, sines = dft9([load(part, b) for b in range(9)])
        base = part * 9
        save(base, cosines[0])
        for k in range(1, 5):
            save(base + 2 * k - 1, cosines[k])
            save(base + 2 * k, sines[k])
    for k8 in range(3):
        base = 18 + 18 * k8
        cc, cs = dft9([load(2 + 2 * k8, b) for b in range(9)])
        sc, ss = dft9([load(3 + 2 * k8, b) for b in range(9)])
        save(base, cc[0])
        save(base + 1, sc[0])
        for k in range(1, 5):
            at = base + 4 * k - 2
            save(at, cc[k] - ss[k])
            save(at + 1, cc[k] + ss[k])
            save(at + 2, sc[k] + cs[k])
            save(at + 3, sc[k] - cs[k])


def finish72_adjoint(load, save):
    for part in (0, 1):
        base = part * 9
        cosines = [load(base)] + [load(base + 2 * k - 1) for k in range(1, 5)]
        sines = [None] + [load(base + 2 * k) for k in range(1, 5)]
        for b, value in enumerate(dft9_adjoint(cosines, sines)):
            save(part, b, value)
    for k8 in range(3):
        base = 18 + 18 * k8
        cc, sc, cs, ss = [load(base)], [load(base + 1)], [None], [None]
        for k in range(1, 5):
            at = base + 4 * k - 2
            plus, minus, sine_plus, sine_minus = [load(at + i) for i in range(4)]
            cc.append(plus + minus)
            ss.append(minus - plus)
            sc.append(sine_plus + sine_minus)
            cs.append(sine_plus - sine_minus)
        for b, value in enumerate(dft9_adjoint(cc, cs)):
            save(2 + 2 * k8, b, value)
        for b, value in enumerate(dft9_adjoint(sc, ss)):
            save(3 + 2 * k8, b, value)


def point72(a, b):
    return (9 * a + 8 * b) % NG


def split(table):
    high = table.astype(ml_dtypes.bfloat16).astype(np.float64)
    return high, (table - high).astype(ml_dtypes.bfloat16).astype(np.float64)


def from_left(table):
    high, low = split(table)
    wide = np.zeros((80, 256))
    wide[:NG, : 3 * NG] = np.concatenate([high, high, low], axis=1)
    return wide


def from_right(table):
    high, low = split(table)
    return np.block([[high, low], [high, np.zeros_like(low)]])


@functools.cache
def tables():
    at = np.arange(NG)
    basis, freq = [np.full(NG, 1.0)], [0]
    for k in range(1, NG // 2):
        basis += [np.cos(2 * np.pi * k * at / NG), np.sin(2 * np.pi * k * at / NG)]
        freq += [k, k]
    basis.append(np.cos(np.pi * at))
    freq.append(NG // 2)
    basis = np.array(basis)
    basis /= np.sqrt((basis * basis).sum(1, keepdims=True))
    freq = np.array(freq, np.float64)
    eye = np.eye(NG)
    parts = [dft8([eye[point72(a, b)] for a in range(8)]) for b in range(9)]
    slots = [None] * NG
    finish72(lambda part, b: parts[b][part], slots.__setitem__)
    slots = np.array(slots)
    norm = (slots * slots).sum(1)
    spectrum = np.abs(np.fft.fft(slots, axis=1))[:, : NG // 2 + 1]
    freq_y = spectrum.argmax(1).astype(np.float64)
    along_z = np.zeros((128, 128))
    along_z[:NG, :NG] = basis.T
    along_x = basis.reshape(NG, PEERS, PLANES)
    along_x = np.concatenate([along_x[:, :, :8].reshape(NG, -1), along_x[:, :, 8]], axis=1)
    column = np.zeros((8, WIDTH), np.float32)
    column[0, :MERGED] = (freq_y[:, None] ** 2 + freq[None, :] ** 2).reshape(-1)
    column[1, :MERGED] = np.repeat(1.0 / norm, NG)
    freq_x = np.broadcast_to((freq**2)[:, None], (NG, 128)).astype(np.float32)
    wide = np.concatenate(
        [from_right(along_z), from_right(along_z.T), from_left(along_x), from_left(along_x.T)]
    )
    return wide.astype(ml_dtypes.bfloat16), column, freq_x


def take(load, start):
    tile, lane = divmod(start, 128)
    value = load(tile)
    if lane == 0:
        return value
    if lane + NG > 128:
        at = lax.broadcasted_iota(jnp.int32, value.shape, 1)
        value = jnp.where(at >= lane, value, load(tile + 1))
    return pltpu.roll(value, 128 - lane, 1)


def put(store, start, value):
    tile, lane = divmod(start, 128)
    if lane:
        value = pltpu.roll(value, lane, 1)
    end = min(lane + NG, 128)
    store(tile, slice(lane, end), value[:, lane:end])
    if lane + NG > 128:
        store(tile + 1, slice(0, lane + NG - 128), value[:, : lane + NG - 128])


def matmul(a, b):
    return jnp.dot(a, b, preferred_element_type=jnp.float32)


def halves(x):
    high = x.astype(jnp.bfloat16)
    return high, (x - high.astype(jnp.float32)).astype(jnp.bfloat16)


def left(table, x):
    high, low = [part.astype(jnp.float32) for part in halves(x)]
    zeros = jnp.zeros((8, x.shape[1]), jnp.float32)
    operand = jnp.concatenate([high, low, high, zeros], axis=0).astype(jnp.bfloat16)
    return matmul(table[:, 0 : operand.shape[0]], operand)[0:NG]


def kernel(
    bands,
    mask_ref,
    bands_hbm,
    wide_hbm,
    column_hbm,
    freq_hbm,
    out_ref,
    bands_ref,
    wide,
    column_ref,
    freq_ref,
    mixed,
    own,
    own_fold,
    visit,
    visit_fold,
    rho,
    work,
    work2,
    wave,
    wave_fold,
    wave_tail,
    wave_piece,
    recv,
    recv_fold,
    recv_tail,
    back,
    back_fold,
    back_tail,
    field,
    field_fold,
    field_tail,
    field_piece,
    kernel_table,
    kernel_tail,
    total,
    total_fold,
    base,
    base_fold,
    give,
    give_fold,
    given,
    given_fold,
    visit_send,
    visit_recv,
    pass_send,
    give_send,
    give_recv,
    part_send,
    part_recv,
    fold_send,
    fold_recv,
    tail_send,
    tail_recv,
    back_tail_send,
    back_tail_recv,
    load_sem,
):
    me = lax.axis_index("pencil")
    group = lax.axis_index("band")
    me_x, me_y = lax.div(me, 4), lax.rem(me, 4)

    loads = [
        pltpu.make_async_copy(src, dst, load_sem.at[i])
        for i, (src, dst) in enumerate(
            [
                (bands_hbm, bands_ref),
                (wide_hbm, wide),
                (column_hbm, column_ref),
                (freq_hbm, freq_ref),
            ]
        )
    ]
    for load in loads:
        load.start()

    def peer(j):
        return lax.rem(me + j, PEERS)

    def at(dx, dy):
        return lax.rem(me_x + dx, 2) * 4 + lax.rem(me_y + dy + 4, 4)

    def group_at(j):
        return lax.rem(group + j + bands, bands)

    barrier = pltpu.get_barrier_semaphore()
    for j in range(1, PEERS):
        pl.semaphore_signal(barrier, inc=1, device_id={"pencil": peer(j)}, device_id_type=MESH)
    for j in (-2, -1, 1, 2):
        pl.semaphore_signal(barrier, inc=1, device_id={"band": group_at(j)}, device_id_type=MESH)
    def remote(src, dst, send, recv, **device):
        return pltpu.make_async_remote_copy(
            src_ref=src,
            dst_ref=dst,
            send_sem=send,
            recv_sem=recv,
            device_id=device,
            device_id_type=MESH,
        )

    even = lax.rem(group, 2) == 0

    def terms_group(s):
        near = jnp.where(even, group_at(1), group_at(-1))
        return jnp.where(s == 0, near, jnp.where(even, group_at(2), group_at(-2)))

    def parts(main, fold):
        return [
            *(main.at[pl.ds(begin, end - begin)] for begin, end in QUARTERS),
            fold,
        ]

    def block_copies(src, dst, send, recv, to):
        return [
            remote(one, two, send.at[q], recv.at[q], band=to)
            for q, (one, two) in enumerate(zip(src, dst))
        ]

    def visit_at(s):
        return parts(visit.at[s], visit_fold.at[s])

    own_parts = parts(own, own_fold)

    def give_parts(main, fold):
        return [main.at[0], *parts(main.at[1], fold)]

    def visit_copies(s, src, send, to):
        return block_copies(src, visit_at(s), send, visit_recv.at[s], to)

    def near_sends():
        return visit_copies(0, own_parts, visit_send.at[0], group_at(-1))

    def far_sends():
        return visit_copies(1, own_parts, visit_send.at[1], group_at(2))

    def passes():
        return visit_copies(1, visit_at(0), pass_send, group_at(-1))

    loads[0].wait()
    def take_tile(tile, j, q, width):
        lanes = pl.ds(tile * 128, width)
        if width == 128:
            lanes = pl.ds(pl.multiple_of(tile * 128, 128), 128)
        live = slice(0, width)
        for plane in range(PLANES - 1):
            mixed[tile, 2 * plane : 2 * plane + 2, live] = bands_ref[plane, :, lanes]
        for band in range(2):
            own[tile, band * 8 : band * 8 + 8, :] = mixed[tile, pl.ds(band, 8, stride=2), :]
        own_fold[j, 2 * q : 2 * q + 2, live] = bands_ref[PLANES - 1, :, lanes]

    def tile_loop(begin, end, step):
        def run(j, carry):
            step(begin + j, j)
            return carry

        lax.fori_loop(0, end - begin, run, 0, unroll=True)

    mixed[TAIL_TILE] = jnp.zeros((16, 128), jnp.float32)
    own_fold[TAIL_TILE % FOLD, 6:8, :] = jnp.zeros((2, 128), jnp.float32)

    def own_mask(s, f):
        return mask_ref[0, s, f // 2, f % 2].astype(jnp.float32)

    for m in range(2 * FIELDS):
        value = own_mask(m // FIELDS, m % FIELDS)
        own_fold[MASKS, m : m + 1, :] = jnp.zeros((1, 128), jnp.float32) + value
    pl.semaphore_wait(barrier, PEERS - 1 + 4)
    near, far = near_sends(), far_sends()

    def send_own(part):
        near[part].start()

        @pl.when(jnp.logical_not(even))
        def _():
            far[part].start()

    for q, (begin, end) in enumerate(QUARTERS):
        tile_loop(begin, min(end, TAIL_TILE), lambda tile, j, q=q: take_tile(tile, j, q, 128))
        if end > TAIL_TILE:
            take_tile(TAIL_TILE, TAIL_TILE % FOLD, q, MERGED - TAIL)
        send_own(q)
    send_own(4)

    def kernel_columns(start, width):
        squared = column_ref[0:1, pl.ds(start, width)]
        scale = column_ref[1:2, pl.ds(start, width)]
        return coulomb_scale / (freq_ref[:, 0:1] + squared + screening) * scale

    for load in loads[1:]:
        load.wait()
    kernel_table[...] = kernel_columns(pl.multiple_of(me * OWN, 128), OWN)
    kernel_tail[...] = kernel_columns(TAIL, 128)
    wave_tail[...] = jnp.zeros((2, ROWS, 128), jnp.float32)
    total_fold[...] = jnp.zeros((FOLD + 1, 8, 128), jnp.float32)
    base_fold[...] = jnp.zeros((FOLD + 1, 8, 128), jnp.float32)

    def clear(tile, carry):
        total[tile] = jnp.zeros((16, 128), jnp.float32)
        base[:, tile] = jnp.zeros((2, 8, 128), jnp.float32)
        return carry

    lax.fori_loop(0, TILES, clear, 0)
    for s in range(2):
        for p in range(PEERS):
            back_fold[s, (p + 1) * LAST - 8 : (p + 1) * LAST, :] = jnp.zeros((8, 128), jnp.float32)
            back_tail[s, (p + 1) * PIECE - 8 : (p + 1) * PIECE, :] = jnp.zeros((8, 128), jnp.float32)
        field_tail[s, 32:40, :] = jnp.zeros((8, 128), jnp.float32)
        for f in range(FIELDS):
            wave_piece[s, f, 8:16, :] = jnp.zeros((8, 128), jnp.float32)

    first_band = [slice(band * 8, band * 8 + 8) for band in range(2)]
    field_rows = [slice(f * 8, f * 8 + 8) for f in range(FIELDS)]
    row_at = lax.broadcasted_iota(jnp.int32, (8, 128), 0)
    resident_one = lax.rem(lax.div(row_at, 2), 2) == 1
    visitor_one = lax.rem(row_at, 2) == 1

    def last_planes(s, j, q):
        a = [own_fold[j, 2 * q + band : 2 * q + band + 1, :] for band in range(2)]
        c = [visit_fold[s, j, 2 * q + band : 2 * q + band + 1, :] for band in range(2)]
        wide_a = [jnp.broadcast_to(row, (8, 128)) for row in a]
        wide_c = [jnp.broadcast_to(row, (8, 128)) for row in c]
        return (
            jnp.where(resident_one, wide_a[1], wide_a[0]),
            jnp.where(visitor_one, wide_c[1], wide_c[0]),
        )

    def along_z(start):
        both = matmul(jnp.concatenate(halves(work[...]), axis=1), wide[start : start + 256, :])
        work2[...] = both[:, :128] + both[:, 128:]

    def place(part, b):
        return slice((part * 9 + b) * 8, (part * 9 + b) * 8 + 8)

    def row_of(t):
        return pl.ds(pl.multiple_of(t * 8, 8), 8)

    def first(s):
        arriving = visit_copies(s, own_parts, visit_send.at[0], group_at(1))
        passing = passes()
        for q in range(5):
            arriving[q].wait_recv()

            @pl.when((s == 0) & jnp.logical_not(even))
            def _(q=q):
                passing[q].start()

        def one_row(i, carry):
            t = jnp.where(i == 0, FIELDS, order(jnp.maximum(i - 1, 0)))

            @pl.when(i > 0)
            def _():
                resident, visitor = row_of(lax.div(t, 2)), row_of(lax.rem(t, 2))
                for tile in range(TILES):
                    rho[tile, row_of(t), :] = own[tile, resident, :] * visit[s, tile, visitor, :]

            @pl.when(i == 0)
            def _():
                for q, (begin, end) in enumerate(QUARTERS):

                    def products(tile, j, q=q):
                        phi, chi = last_planes(s, j, q)
                        rho[tile, 32:40, :] = phi * chi

                    tile_loop(begin, end, products)

            for b in range(9):
                starts = [point72(a, b) * NG for a in range(8)]
                values = [take(lambda tile: rho[tile, row_of(t), :], at) for at in starts]
                for part, value in enumerate(dft8(values)):
                    work[place(part, b), :] = value
            along_z(0)

            def load(part, b):
                return work2[place(part, b), :]

            def target(tile, lanes, piece):
                if tile == TAIL_TILE:
                    wave_tail[s, row_of(t), lanes] = piece
                else:
                    wave[s, t, tile * 8 : tile * 8 + 8, lanes] = piece

            def save(slot, value):
                put(target, slot * NG, value)

            finish72(load, save)

            @pl.when(i == 0)
            def _():
                upper = lax.broadcasted_iota(jnp.int32, (8, 128), 0) < FIELDS

                def fold(q, carry):
                    for k in range(3):
                        at_row = pl.multiple_of((q * OWN_TILES + k) * 8, 8)
                        piece = wave[s, FIELDS, pl.ds(at_row, 8), :]
                        if k < 2:
                            below = wave[s, FIELDS, pl.ds(at_row + 24, 8), :]
                            piece = jnp.where(upper, piece, below)
                        to_row = pl.multiple_of(q * LAST + k * 8, 8)
                        wave_fold[s, pl.ds(to_row, 8), :] = piece
                    return carry

                lax.fori_loop(0, PEERS, fold, 0)
                send_fold(0, s)

            @pl.when(i > 0)
            def _():
                send_part(0, s, t)

            return carry

        lax.fori_loop(0, FIELDS + 1, one_row, 0)
        for f in range(FIELDS):
            wave_piece[s, f, 0:8, :] = wave_tail[s, field_rows[f], :]
            wave_piece[s, f, 8:9, :] = wave_tail[s, 32 + f : 33 + f, :]

    part_refs = ((wave, recv), (back, field))
    fold_refs = ((wave_fold, recv_fold), (back_fold, field_fold))
    straight = [(1, 2), (0, 2), (1, 1), (1, 3), (0, 1), (0, 3), (1, 0)]

    def rows_of(index, rows):
        return pl.ds(pl.multiple_of(index * rows, 8), rows)

    def send_part(phase, s, f):
        src, dst = part_refs[phase]
        for dx, dy in straight:
            to = at(dx, dy)
            remote(
                src.at[s, f, rows_of(to, PART)],
                dst.at[s, f, rows_of(me, PART)],
                part_send.at[phase, s],
                part_recv.at[phase, s, f],
                pencil=to,
            ).start()
        dst[s, f, rows_of(me, PART), :] = src[s, f, rows_of(me, PART), :]

    def send_fold(phase, s):
        src, dst = fold_refs[phase]
        for dx, dy in straight:
            to = at(dx, dy)
            remote(
                src.at[s, rows_of(to, LAST)],
                dst.at[s, rows_of(me, LAST)],
                fold_send.at[phase, s],
                fold_recv.at[phase, s],
                pencil=to,
            ).start()
        dst[s, rows_of(me, LAST), :] = src[s, rows_of(me, LAST), :]

    def drain(view, sem):
        pltpu.make_async_copy(view, view, sem).wait()

    def wait_part(phase, s, f):
        drain(part_refs[phase][1].at[s, f, pl.ds(0, 7 * PART)], part_recv.at[phase, s, f])

    def wait_fold(phase, s):
        drain(fold_refs[phase][1].at[s, pl.ds(0, 7 * LAST)], fold_recv.at[phase, s])

    def end_blocks(phase, s):
        parts = part_refs[phase][0].at[s, pl.ds(0, FIELDS), pl.ds(0, 7 * PART)]
        drain(parts, part_send.at[phase, s])
        drain(fold_refs[phase][0].at[s, pl.ds(0, 7 * LAST)], fold_send.at[phase, s])

    def piece_of(ref, s, index):
        return ref.at[s, pl.ds(pl.multiple_of(index * PIECE, 8), PIECE), :]

    def owner_of(s, f):
        return FIELDS * s + f

    def tail_copy(s, f, distance):
        return remote(
            wave_piece.at[s, f],
            piece_of(recv_tail, s, me),
            tail_send.at[s, f],
            tail_recv.at[s, distance],
            pencil=owner_of(s, f),
        )

    def second(s):
        wait_fold(0, s)

        def last_rows(f, tile):
            return pl.ds(tile % 3 * 8 + FIELDS * (tile // 3) + f, PEERS, stride=LAST)

        def one_field(i, carry):
            f = order(i)
            wait_part(0, s, f)
            columns = []
            for tile in range(OWN_TILES):
                starts = [p * PART + tile * 8 for p in range(PEERS)]
                rows = [recv[s, f, start : start + 8, :] for start in starts]
                rows.append(recv_fold[s, last_rows(f, tile), :])
                columns.append(jnp.concatenate(rows, axis=0))
            spectrum = left(wide[512:592, :], jnp.concatenate(columns, axis=1))
            result = left(wide[592:672, :], spectrum * kernel_table[...])
            for tile in range(OWN_TILES):
                lanes = slice(tile * 128, tile * 128 + 128)
                for p in range(PEERS):
                    start = p * PART + tile * 8
                    back[s, f, start : start + 8, :] = result[p * 8 : p * 8 + 8, lanes]
                back_fold[s, last_rows(f, tile), :] = result[64:72, lanes]
            send_part(1, s, f)
            return carry

        lax.fori_loop(0, FIELDS, one_field, 0)
        send_fold(1, s)

    def give_copies(s):
        return block_copies(
            give_parts(give.at[s], give_fold.at[s]),
            give_parts(given.at[s], given_fold.at[s]),
            give_send.at[s],
            give_recv.at[s],
            terms_group(s),
        )

    def order(i):
        return lax.rem(2 * i, FIELDS) + lax.div(i, 2)

    def pair_weights(s):
        weights = []
        for f in range(FIELDS):
            g = 2 * (f % 2) + f // 2
            above = visit_fold[s, MASKS, FIELDS + g : FIELDS + g + 1, :]
            same = visit_fold[s, MASKS, g : g + 1, :]
            mine = own_fold[MASKS, FIELDS + f : FIELDS + f + 1, :]
            row = jnp.where(s == 0, same, jnp.where(even, above, mine))
            weights.append(jnp.broadcast_to(row, (8, 128)))
        return weights

    def third(s):
        weights = pair_weights(s)
        leaving = give_copies(s)

        def leave(which):
            for part in which:
                leaving[part].start()

        def gather_band(c, begin, end):
            def gather(tile, j):
                chi = visit[s, tile, first_band[c], :]
                terms = base[c, tile]
                for a in range(2):
                    value = rho[tile, field_rows[2 * a + c], :] * weights[2 * a + c]
                    total[tile, first_band[a], :] += value * chi
                    terms = terms + value * own[tile, first_band[a], :]
                give[s, c, tile] = terms

            tile_loop(begin, end, gather)

        def one_row(i, carry):
            t = jnp.where(i == FIELDS, FIELDS, order(jnp.minimum(i, FIELDS - 1)))

            @pl.when(t < FIELDS)
            def _():
                wait_part(1, s, t)

            @pl.when(t == FIELDS)
            def _():
                wait_fold(1, s)

                def unfold(q, carry):
                    for k in range(OWN_TILES):
                        from_row = pl.multiple_of(q * LAST + k % 3 * 8, 8)
                        value = field_fold[s, pl.ds(from_row, 8), :]
                        value = pltpu.roll(value, FIELDS, 0) if k > 2 else value
                        to_row = pl.multiple_of((q * OWN_TILES + k) * 8, 8)
                        field[s, FIELDS, pl.ds(to_row, 8), :] = value
                    return carry

                lax.fori_loop(0, PEERS, unfold, 0)

            def source(tile):
                if tile == TAIL_TILE:
                    return field_tail[s, row_of(t), :]
                return field[s, t, tile * 8 : tile * 8 + 8, :]

            def load(slot):
                return take(source, slot * NG)

            def save(part, b, value):
                work[place(part, b), :] = value

            finish72_adjoint(load, save)
            along_z(256)

            def target(tile, lanes, piece):
                rho[tile, row_of(t), lanes] = piece

            for b in range(9):
                values = dft8_adjoint([work2[place(part, b), :] for part in range(8)])
                for a, value in enumerate(values):
                    put(target, point72(a, b) * NG, value)

            @pl.when((s == 1) & even & (i == 1))
            def _():
                for copy in give_copies(0):
                    copy.wait_recv()

                def join(tile, carry):
                    for band in range(2):
                        base[band, tile] = given[0, band, tile]
                    return carry

                lax.fori_loop(0, TILES, join, 0)
                base_fold[...] = given_fold[0]

            @pl.when(i == 1)
            def _():
                gather_band(0, 0, TILES)
                leave([0])

            return carry

        lax.fori_loop(0, FIELDS + 1, one_row, 0)
        last_weight = weights[3]
        for f in range(3):
            last_weight = jnp.where(row_at == f, weights[f], last_weight)

        for q, (begin, end) in enumerate(QUARTERS):
            gather_band(1, begin, end)
            leave([1 + q])

            def gather_last(tile, j, q=q):
                phi, chi = last_planes(s, j, q)
                value = rho[tile, 32:40, :] * last_weight
                stay, leave = value * chi, value * phi
                stay = stay + pltpu.roll(stay, 7, 0)
                leave = leave + pltpu.roll(leave, 6, 0)
                for band in range(2):
                    row = slice(2 * q + band, 2 * q + band + 1)
                    total_fold[j, row, :] += stay[2 * band : 2 * band + 1]
                    give_fold[s, j, row, :] = leave[band : band + 1] + base_fold[j, row, :]

            tile_loop(begin, end, gather_last)
        leave([5])

    def tail_back(s, f, j):
        return remote(
            piece_of(back_tail, s, peer(j)),
            field_piece.at[s, f],
            back_tail_send.at[s, j],
            back_tail_recv.at[s, f],
            pencil=peer(j),
        )

    def send_tail(s):
        for f in range(FIELDS):
            owner = owner_of(s, f)

            @pl.when(me == owner)
            def _(f=f, owner=owner):
                recv_tail[s, rows_of(owner, PIECE), :] = wave_piece[s, f]

            @pl.when(me != owner)
            def _(f=f, owner=owner):
                tail_copy(s, f, lax.rem(owner - me + PEERS, PEERS)).start()

    def turn_tail(s):
        owned = lax.div(me, FIELDS) == s

        @pl.when(owned)
        def _():
            for j in range(1, PEERS):
                tail_copy(s, 0, j).wait_recv()
            parts = [pl.ds(p * PIECE, 8) for p in range(PEERS)] + [pl.ds(8, PEERS, stride=PIECE)]
            block = jnp.concatenate([recv_tail[s, part, :] for part in parts], axis=0)
            spectrum = left(wide[512:592, :], block) * kernel_tail[...]
            result = left(wide[592:672, :], spectrum)
            for i, part in enumerate(parts):
                back_tail[s, part, :] = result[i * 8 : i * 8 + 8, :]
            mine = lax.rem(me, FIELDS)
            for j in range(1, PEERS):
                tail_back(s, mine, j).start()
            field_piece[s, mine] = back_tail[s, pl.ds(pl.multiple_of(me * PIECE, 8), PIECE), :]

    def end_tail(s):
        for f in range(FIELDS):
            owner = owner_of(s, f)

            @pl.when(me != owner)
            def _(f=f, owner=owner):
                tail_copy(s, f, lax.rem(owner - me + PEERS, PEERS)).wait_send()
                tail_back(s, f, 1).wait_recv()

            field_tail[s, field_rows[f], :] = field_piece[s, f, 0:8, :]
            field_tail[s, 32 + f : 33 + f, :] = field_piece[s, f, 8:9, :]

        @pl.when(lax.div(me, FIELDS) == s)
        def _():
            for j in range(1, PEERS):
                tail_back(s, lax.rem(me, FIELDS), j).wait_send()

    def slots(*stages):
        def run(s, carry):
            for stage in stages:
                stage(s)
            return carry

        lax.fori_loop(0, 2, run, 0)

    slots(first, send_tail)
    slots(second, turn_tail)
    slots(end_tail, third)

    def wait_given(which):
        for part in which:
            give_copies(1)[part].wait_recv()

            @pl.when(jnp.logical_not(even))
            def _(part=part):
                give_copies(0)[part].wait_recv()

    for q, (begin, end) in enumerate(QUARTERS):
        wait_given([0, 1] if q == 0 else [1 + q])

        def result(tile, j, width=128):
            lanes = pl.ds(tile * 128, width)
            if width == 128:
                lanes = pl.ds(pl.multiple_of(tile * 128, 128), 128)
            for rows, band in zip(first_band, range(2)):
                near = jnp.where(even, 0.0, given[0, band, tile])
                term = -(total[tile, rows, :] + near + given[1, band, tile])
                mixed[tile, pl.ds(band, 8, stride=2), :] = term
            for plane in range(PLANES - 1):
                piece = mixed[tile, 2 * plane : 2 * plane + 2, 0:width]
                out_ref[plane, :, lanes] = piece

        tile_loop(begin, min(end, TAIL_TILE), result)
        if end > TAIL_TILE:
            result(TAIL_TILE, 0, MERGED - TAIL)
    wait_given([5])
    for q, (begin, end) in enumerate(QUARTERS):

        def last_result(tile, j, q=q, width=128):
            lanes = pl.ds(tile * 128, width)
            if width == 128:
                lanes = pl.ds(pl.multiple_of(tile * 128, 128), 128)
            rows = slice(2 * q, 2 * q + 2)
            near = jnp.where(even, 0.0, given_fold[0, j, rows, :])
            term = total_fold[j, rows, :] + near + given_fold[1, j, rows, :]
            out_ref[PLANES - 1, :, lanes] = -term[:, 0:width]

        tile_loop(begin, min(end, TAIL_TILE), last_result)
        if end > TAIL_TILE:
            last_result(TAIL_TILE, TAIL_TILE - begin, width=MERGED - TAIL)

    for copy in near_sends():
        copy.wait_send()

    @pl.when(jnp.logical_not(even))
    def _():
        for copy in far_sends() + passes():
            copy.wait_send()

    for s in range(2):
        for copy in give_copies(s):
            copy.wait_send()
    for phase in range(2):
        for s in range(2):
            end_blocks(phase, s)


def body(bands, orbitals, pair_mask):
    hbm = pl.BlockSpec(memory_space=pltpu.HBM)
    smem = pl.BlockSpec(memory_space=pltpu.SMEM)
    consts = [jnp.asarray(table) for table in tables()]
    dma = pltpu.SemaphoreType.DMA

    def buffer(*shape):
        return pltpu.VMEM(shape, jnp.float32)

    out = pl.pallas_call(
        functools.partial(kernel, bands),
        out_shape=jax.ShapeDtypeStruct((PLANES, 2, MERGED), jnp.float32),
        in_specs=[smem] + [hbm] * (1 + len(consts)),
        out_specs=pl.BlockSpec(memory_space=pltpu.VMEM),
        scratch_shapes=[
            buffer(PLANES, 2, MERGED),
            pltpu.VMEM(consts[0].shape, jnp.bfloat16),
            buffer(*consts[1].shape),
            buffer(*consts[2].shape),
            buffer(TILES, 16, 128),
            buffer(TILES, 16, 128),
            buffer(FOLD + 1, 8, 128),
            buffer(2, TILES, 16, 128),
            buffer(2, FOLD + 1, 8, 128),
            buffer(TILES, ROWS, 128),
            buffer(NG * 8, 128),
            buffer(NG * 8, 128),
            buffer(2, FIELDS + 1, PEERS * PART, 128),
            buffer(2, PEERS * LAST, 128),
            buffer(2, ROWS, 128),
            buffer(2, FIELDS, PIECE, 128),
            buffer(2, FIELDS, PEERS * PART, 128),
            buffer(2, PEERS * LAST, 128),
            buffer(2, PEERS * PIECE, 128),
            buffer(2, FIELDS, PEERS * PART, 128),
            buffer(2, PEERS * LAST, 128),
            buffer(2, PEERS * PIECE, 128),
            buffer(2, FIELDS + 1, PEERS * PART, 128),
            buffer(2, PEERS * LAST, 128),
            buffer(2, ROWS, 128),
            buffer(2, FIELDS, PIECE, 128),
            buffer(NG, OWN),
            buffer(NG, 128),
            buffer(TILES, 16, 128),
            buffer(FOLD + 1, 8, 128),
            buffer(2, TILES, 8, 128),
            buffer(FOLD + 1, 8, 128),
            buffer(2, 2, TILES, 8, 128),
            buffer(2, FOLD + 1, 8, 128),
            buffer(2, 2, TILES, 8, 128),
            buffer(2, FOLD + 1, 8, 128),
            dma((2, 5)),
            dma((2, 5)),
            dma((5,)),
            dma((2, 6)),
            dma((2, 6)),
            dma((2, 2)),
            dma((2, 2, FIELDS)),
            dma((2, 2)),
            dma((2, 2)),
            dma((2, FIELDS)),
            dma((2, PEERS)),
            dma((2, PEERS)),
            dma((2, FIELDS)),
            dma((4,)),
        ],
        compiler_params=pltpu.CompilerParams(
            collective_id=0, has_side_effects=True, vmem_limit_bytes=64 * 1024 * 1024 - 65536
        ),
    )(pair_mask, orbitals.transpose(1, 0, 2), *consts)
    return out.transpose(1, 0, 2)


def solution(mesh):
    return jax.shard_map(
        functools.partial(body, mesh.shape["band"]),
        mesh=mesh,
        in_specs=(P("band", "pencil", None), P("band", None, None, None)),
        out_specs=P("band", "pencil", None),
        check_vma=False,
    )
```

```python
import functools
import math

import jax
import jax.numpy as jnp
import ml_dtypes
import numpy as np
from jax import lax
from jax.experimental import pallas as pl
from jax.experimental.pallas import tpu as pltpu
from jax.sharding import PartitionSpec as P

MESH = pl.DeviceIdType.MESH
NG = 72
PLANES = 9
PEERS = 8
FIELDS = 4
ROWS = 40
PART = 40
LAST = 24
MERGED = NG * NG
WIDTH = 5248
OWN = 640
TAIL = PEERS * OWN
PIECE = 16
FOLD = 11
MASKS = FOLD
QUARTERS = [(q * FOLD, min((q + 1) * FOLD, 41)) for q in range(4)]
TILES = WIDTH // 128
OWN_TILES = OWN // 128
TAIL_TILE = TILES - 1
coulomb_scale = 20.0
screening = 0.25
HALF = math.sqrt(0.5)


def dft8(x):
    a = [x[j] + x[j + 4] for j in range(4)]
    b = [x[j] - x[j + 4] for j in range(4)]
    e, o = a[0] + a[2], a[1] + a[3]
    u, v = HALF * (b[1] - b[3]), HALF * (b[1] + b[3])
    return [e + o, e - o, b[0] + u, v + b[2], a[0] - a[2], a[1] - a[3], b[0] - u, v - b[2]]


def dft8_adjoint(c):
    p, q = c[0] + c[1], c[0] - c[1]
    a = [p + c[4], q + c[5], p - c[4], q - c[5]]
    d, s = HALF * (c[2] - c[6]), HALF * (c[3] + c[7])
    b = [c[2] + c[6], d + s, c[3] - c[7], s - d]
    return [a[j] + b[j] for j in range(4)] + [a[j] - b[j] for j in range(4)]


def cos9(n):
    return math.cos(2.0 * math.pi * (n % 9) / 9)


def sin9(n):
    return math.sin(2.0 * math.pi * (n % 9) / 9)


def weighted(values, factors):
    total = values[0] * factors[0]
    for value, factor in zip(values[1:], factors[1:]):
        total = total + value * factor
    return total


def dft9(x):
    e = [x[n] + x[9 - n] for n in range(1, 5)]
    o = [x[n] - x[9 - n] for n in range(1, 5)]
    third = e[0] + e[1] + e[3]
    cosines = [x[0] + third + e[2]]
    sines = [None]
    for k in range(1, 5):
        if k == 3:
            cosines.append(x[0] + e[2] - 0.5 * third)
            sines.append(sin9(3) * (o[0] - o[1] + o[3]))
        else:
            cosines.append(x[0] + weighted(e, [cos9(k * n) for n in range(1, 5)]))
            sines.append(weighted(o, [sin9(k * n) for n in range(1, 5)]))
    return cosines, sines


def dft9_adjoint(cosines, sines):
    c, s = cosines, sines
    out = [None] * 9
    out[0] = c[0] + ((c[1] + c[2]) + (c[3] + c[4]))
    for n in range(1, 5):
        if n == 3:
            even = c[0] + c[3] - 0.5 * (c[1] + c[2] + c[4])
            odd = sin9(3) * (s[1] - s[2] + s[4])
        else:
            even = c[0] + weighted(c[1:], [cos9(k * n) for k in range(1, 5)])
            odd = weighted(s[1:], [sin9(k * n) for k in range(1, 5)])
        out[n] = even + odd
        out[9 - n] = even - odd
    return out


def finish72(load, save):
    for part in (0, 1):
        cosines, sines = dft9([load(part, b) for b in range(9)])
        base = part * 9
        save(base, cosines[0])
        for k in range(1, 5):
            save(base + 2 * k - 1, cosines[k])
            save(base + 2 * k, sines[k])
    for k8 in range(3):
        base = 18 + 18 * k8
        cc, cs = dft9([load(2 + 2 * k8, b) for b in range(9)])
        sc, ss = dft9([load(3 + 2 * k8, b) for b in range(9)])
        save(base, cc[0])
        save(base + 1, sc[0])
        for k in range(1, 5):
            at = base + 4 * k - 2
            save(at, cc[k] - ss[k])
            save(at + 1, cc[k] + ss[k])
            save(at + 2, sc[k] + cs[k])
            save(at + 3, sc[k] - cs[k])


def finish72_adjoint(load, save):
    for part in (0, 1):
        base = part * 9
        cosines = [load(base)] + [load(base + 2 * k - 1) for k in range(1, 5)]
        sines = [None] + [load(base + 2 * k) for k in range(1, 5)]
        for b, value in enumerate(dft9_adjoint(cosines, sines)):
            save(part, b, value)
    for k8 in range(3):
        base = 18 + 18 * k8
        cc, sc, cs, ss = [load(base)], [load(base + 1)], [None], [None]
        for k in range(1, 5):
            at = base + 4 * k - 2
            plus, minus, sine_plus, sine_minus = [load(at + i) for i in range(4)]
            cc.append(plus + minus)
            ss.append(minus - plus)
            sc.append(sine_plus + sine_minus)
            cs.append(sine_plus - sine_minus)
        for b, value in enumerate(dft9_adjoint(cc, cs)):
            save(2 + 2 * k8, b, value)
        for b, value in enumerate(dft9_adjoint(sc, ss)):
            save(3 + 2 * k8, b, value)


def point72(a, b):
    return (9 * a + 8 * b) % NG


def split(table):
    high = table.astype(ml_dtypes.bfloat16).astype(np.float64)
    return high, (table - high).astype(ml_dtypes.bfloat16).astype(np.float64)


def from_left(table):
    high, low = split(table)
    wide = np.zeros((80, 256))
    wide[:NG, : 3 * NG] = np.concatenate([high, high, low], axis=1)
    return wide


def from_right(table):
    high, low = split(table)
    return np.block([[high, low], [high, np.zeros_like(low)]])


@functools.cache
def tables():
    at = np.arange(NG)
    basis, freq = [np.full(NG, 1.0)], [0]
    for k in range(1, NG // 2):
        basis += [np.cos(2 * np.pi * k * at / NG), np.sin(2 * np.pi * k * at / NG)]
        freq += [k, k]
    basis.append(np.cos(np.pi * at))
    freq.append(NG // 2)
    basis = np.array(basis)
    basis /= np.sqrt((basis * basis).sum(1, keepdims=True))
    freq = np.array(freq, np.float64)
    eye = np.eye(NG)
    parts = [dft8([eye[point72(a, b)] for a in range(8)]) for b in range(9)]
    slots = [None] * NG
    finish72(lambda part, b: parts[b][part], slots.__setitem__)
    slots = np.array(slots)
    norm = (slots * slots).sum(1)
    spectrum = np.abs(np.fft.fft(slots, axis=1))[:, : NG // 2 + 1]
    freq_y = spectrum.argmax(1).astype(np.float64)
    along_z = np.zeros((128, 128))
    along_z[:NG, :NG] = basis.T
    along_x = basis.reshape(NG, PEERS, PLANES)
    along_x = np.concatenate([along_x[:, :, :8].reshape(NG, -1), along_x[:, :, 8]], axis=1)
    column = np.zeros((8, WIDTH), np.float32)
    column[0, :MERGED] = (freq_y[:, None] ** 2 + freq[None, :] ** 2).reshape(-1)
    column[1, :MERGED] = np.repeat(1.0 / norm, NG)
    freq_x = np.broadcast_to((freq**2)[:, None], (NG, 128)).astype(np.float32)
    wide = np.concatenate(
        [from_right(along_z), from_right(along_z.T), from_left(along_x), from_left(along_x.T)]
    )
    return wide.astype(ml_dtypes.bfloat16), column, freq_x


def take(load, start):
    tile, lane = divmod(start, 128)
    value = load(tile)
    if lane == 0:
        return value
    if lane + NG > 128:
        at = lax.broadcasted_iota(jnp.int32, value.shape, 1)
        value = jnp.where(at >= lane, value, load(tile + 1))
    return pltpu.roll(value, 128 - lane, 1)


def put(store, start, value):
    tile, lane = divmod(start, 128)
    if lane:
        value = pltpu.roll(value, lane, 1)
    end = min(lane + NG, 128)
    store(tile, slice(lane, end), value[:, lane:end])
    if lane + NG > 128:
        store(tile + 1, slice(0, lane + NG - 128), value[:, : lane + NG - 128])


def matmul(a, b):
    return jnp.dot(a, b, preferred_element_type=jnp.float32)


def halves(x):
    high = x.astype(jnp.bfloat16)
    return high, (x - high.astype(jnp.float32)).astype(jnp.bfloat16)


def left(table, x):
    high, low = [part.astype(jnp.float32) for part in halves(x)]
    zeros = jnp.zeros((8, x.shape[1]), jnp.float32)
    operand = jnp.concatenate([high, low, high, zeros], axis=0).astype(jnp.bfloat16)
    return matmul(table[:, 0 : operand.shape[0]], operand)[0:NG]


def kernel(
    bands,
    mask_ref,
    bands_hbm,
    wide_hbm,
    column_hbm,
    freq_hbm,
    out_ref,
    bands_ref,
    wide,
    column_ref,
    freq_ref,
    mixed,
    own,
    own_fold,
    visit,
    visit_fold,
    rho,
    work,
    work2,
    wave,
    wave_fold,
    wave_tail,
    wave_piece,
    recv,
    recv_fold,
    recv_tail,
    back,
    back_fold,
    back_tail,
    field,
    field_fold,
    field_tail,
    field_piece,
    kernel_table,
    kernel_tail,
    total,
    total_fold,
    base,
    base_fold,
    give,
    give_fold,
    given,
    given_fold,
    visit_send,
    visit_recv,
    pass_send,
    give_send,
    give_recv,
    part_send,
    part_recv,
    fold_send,
    fold_recv,
    tail_send,
    tail_recv,
    back_tail_send,
    back_tail_recv,
    load_sem,
):
    me = lax.axis_index("pencil")
    group = lax.axis_index("band")
    me_x, me_y = lax.div(me, 4), lax.rem(me, 4)

    loads = [
        pltpu.make_async_copy(src, dst, load_sem.at[i])
        for i, (src, dst) in enumerate(
            [
                (bands_hbm, bands_ref),
                (wide_hbm, wide),
                (column_hbm, column_ref),
                (freq_hbm, freq_ref),
            ]
        )
    ]
    for load in loads:
        load.start()

    def peer(j):
        return lax.rem(me + j, PEERS)

    def at(dx, dy):
        return lax.rem(me_x + dx, 2) * 4 + lax.rem(me_y + dy + 4, 4)

    def group_at(j):
        return lax.rem(group + j + bands, bands)

    barrier = pltpu.get_barrier_semaphore()
    for j in range(1, PEERS):
        pl.semaphore_signal(barrier, inc=1, device_id={"pencil": peer(j)}, device_id_type=MESH)
    for j in (-2, -1, 1, 2):
        pl.semaphore_signal(barrier, inc=1, device_id={"band": group_at(j)}, device_id_type=MESH)
    def remote(src, dst, send, recv, **device):
        return pltpu.make_async_remote_copy(
            src_ref=src,
            dst_ref=dst,
            send_sem=send,
            recv_sem=recv,
            device_id=device,
            device_id_type=MESH,
        )

    even = lax.rem(group, 2) == 0

    def terms_group(s):
        near = jnp.where(even, group_at(1), group_at(-1))
        return jnp.where(s == 0, near, jnp.where(even, group_at(2), group_at(-2)))

    def parts(main, fold):
        return [
            *(main.at[pl.ds(begin, end - begin)] for begin, end in QUARTERS),
            fold,
        ]

    def block_copies(src, dst, send, recv, to):
        return [
            remote(one, two, send.at[q], recv.at[q], band=to)
            for q, (one, two) in enumerate(zip(src, dst))
        ]

    def visit_at(s):
        return parts(visit.at[s], visit_fold.at[s])

    own_parts = parts(own, own_fold)

    def give_parts(main, fold):
        return [main.at[0], *parts(main.at[1], fold)]

    def visit_copies(s, src, send, to):
        return block_copies(src, visit_at(s), send, visit_recv.at[s], to)

    def near_sends():
        return visit_copies(0, own_parts, visit_send.at[0], group_at(-1))

    def far_sends():
        return visit_copies(1, own_parts, visit_send.at[1], group_at(2))

    def passes():
        return visit_copies(1, visit_at(0), pass_send, group_at(-1))

    loads[0].wait()
    def take_tile(tile, j, q, width):
        lanes = pl.ds(tile * 128, width)
        if width == 128:
            lanes = pl.ds(pl.multiple_of(tile * 128, 128), 128)
        live = slice(0, width)
        for plane in range(PLANES - 1):
            mixed[tile, 2 * plane : 2 * plane + 2, live] = bands_ref[plane, :, lanes]
        for band in range(2):
            own[tile, band * 8 : band * 8 + 8, :] = mixed[tile, pl.ds(band, 8, stride=2), :]
        own_fold[j, 2 * q : 2 * q + 2, live] = bands_ref[PLANES - 1, :, lanes]

    def tile_loop(begin, end, step):
        def run(j, carry):
            step(begin + j, j)
            return carry

        lax.fori_loop(0, end - begin, run, 0, unroll=True)

    mixed[TAIL_TILE] = jnp.zeros((16, 128), jnp.float32)
    own_fold[TAIL_TILE % FOLD, 6:8, :] = jnp.zeros((2, 128), jnp.float32)

    def own_mask(s, f):
        return mask_ref[0, s, f // 2, f % 2].astype(jnp.float32)

    for m in range(2 * FIELDS):
        value = own_mask(m // FIELDS, m % FIELDS)
        own_fold[MASKS, m : m + 1, :] = jnp.zeros((1, 128), jnp.float32) + value
    pl.semaphore_wait(barrier, PEERS - 1 + 4)
    near, far = near_sends(), far_sends()

    def send_own(part):
        near[part].start()

        @pl.when(jnp.logical_not(even))
        def _():
            far[part].start()

    for q, (begin, end) in enumerate(QUARTERS):
        tile_loop(begin, min(end, TAIL_TILE), lambda tile, j, q=q: take_tile(tile, j, q, 128))
        if end > TAIL_TILE:
            take_tile(TAIL_TILE, TAIL_TILE % FOLD, q, MERGED - TAIL)
        send_own(q)
    send_own(4)

    def kernel_columns(start, width):
        squared = column_ref[0:1, pl.ds(start, width)]
        scale = column_ref[1:2, pl.ds(start, width)]
        return coulomb_scale / (freq_ref[:, 0:1] + squared + screening) * scale

    for load in loads[1:]:
        load.wait()
    kernel_table[...] = kernel_columns(pl.multiple_of(me * OWN, 128), OWN)
    kernel_tail[...] = kernel_columns(TAIL, 128)
    wave_tail[...] = jnp.zeros((2, ROWS, 128), jnp.float32)
    total_fold[...] = jnp.zeros((FOLD + 1, 8, 128), jnp.float32)
    base_fold[...] = jnp.zeros((FOLD + 1, 8, 128), jnp.float32)

    def clear(tile, carry):
        total[tile] = jnp.zeros((16, 128), jnp.float32)
        base[:, tile] = jnp.zeros((2, 8, 128), jnp.float32)
        return carry

    lax.fori_loop(0, TILES, clear, 0)
    for s in range(2):
        for p in range(PEERS):
            back_fold[s, (p + 1) * LAST - 8 : (p + 1) * LAST, :] = jnp.zeros((8, 128), jnp.float32)
            back_tail[s, (p + 1) * PIECE - 8 : (p + 1) * PIECE, :] = jnp.zeros((8, 128), jnp.float32)
        field_tail[s, 32:40, :] = jnp.zeros((8, 128), jnp.float32)
        for f in range(FIELDS):
            wave_piece[s, f, 8:16, :] = jnp.zeros((8, 128), jnp.float32)

    first_band = [slice(band * 8, band * 8 + 8) for band in range(2)]
    field_rows = [slice(f * 8, f * 8 + 8) for f in range(FIELDS)]
    row_at = lax.broadcasted_iota(jnp.int32, (8, 128), 0)
    resident_one = lax.rem(lax.div(row_at, 2), 2) == 1
    visitor_one = lax.rem(row_at, 2) == 1

    def last_planes(s, j, q):
        a = [own_fold[j, 2 * q + band : 2 * q + band + 1, :] for band in range(2)]
        c = [visit_fold[s, j, 2 * q + band : 2 * q + band + 1, :] for band in range(2)]
        wide_a = [jnp.broadcast_to(row, (8, 128)) for row in a]
        wide_c = [jnp.broadcast_to(row, (8, 128)) for row in c]
        return (
            jnp.where(resident_one, wide_a[1], wide_a[0]),
            jnp.where(visitor_one, wide_c[1], wide_c[0]),
        )

    def along_z(start):
        both = matmul(jnp.concatenate(halves(work[...]), axis=1), wide[start : start + 256, :])
        work2[...] = both[:, :128] + both[:, 128:]

    def place(part, b):
        return slice((part * 9 + b) * 8, (part * 9 + b) * 8 + 8)

    def row_of(t):
        return pl.ds(pl.multiple_of(t * 8, 8), 8)

    def first(s):
        arriving = visit_copies(s, own_parts, visit_send.at[0], group_at(1))
        passing = passes()
        for q in range(5):
            arriving[q].wait_recv()

            @pl.when((s == 0) & jnp.logical_not(even))
            def _(q=q):
                passing[q].start()

        def one_row(i, carry):
            t = jnp.where(i == 0, FIELDS, order(jnp.maximum(i - 1, 0)))

            @pl.when(i > 0)
            def _():
                resident, visitor = row_of(lax.div(t, 2)), row_of(lax.rem(t, 2))
                for tile in range(TILES):
                    rho[tile, row_of(t), :] = own[tile, resident, :] * visit[s, tile, visitor, :]

            @pl.when(i == 0)
            def _():
                for q, (begin, end) in enumerate(QUARTERS):

                    def products(tile, j, q=q):
                        phi, chi = last_planes(s, j, q)
                        rho[tile, 32:40, :] = phi * chi

                    tile_loop(begin, end, products)

            for b in range(9):
                starts = [point72(a, b) * NG for a in range(8)]
                values = [take(lambda tile: rho[tile, row_of(t), :], at) for at in starts]
                for part, value in enumerate(dft8(values)):
                    work[place(part, b), :] = value
            along_z(0)

            def load(part, b):
                return work2[place(part, b), :]

            def target(tile, lanes, piece):
                if tile == TAIL_TILE:
                    wave_tail[s, row_of(t), lanes] = piece
                else:
                    wave[s, t, tile * 8 : tile * 8 + 8, lanes] = piece

            def save(slot, value):
                put(target, slot * NG, value)

            finish72(load, save)

            @pl.when(i == 0)
            def _():
                upper = lax.broadcasted_iota(jnp.int32, (8, 128), 0) < FIELDS

                def fold(q, carry):
                    for k in range(3):
                        at_row = pl.multiple_of((q * OWN_TILES + k) * 8, 8)
                        piece = wave[s, FIELDS, pl.ds(at_row, 8), :]
                        if k < 2:
                            below = wave[s, FIELDS, pl.ds(at_row + 24, 8), :]
                            piece = jnp.where(upper, piece, below)
                        to_row = pl.multiple_of(q * LAST + k * 8, 8)
                        wave_fold[s, pl.ds(to_row, 8), :] = piece
                    return carry

                lax.fori_loop(0, PEERS, fold, 0)
                send_fold(0, s)

            @pl.when(i > 0)
            def _():
                send_part(0, s, t)

            return carry

        lax.fori_loop(0, FIELDS + 1, one_row, 0)
        for f in range(FIELDS):
            wave_piece[s, f, 0:8, :] = wave_tail[s, field_rows[f], :]
            wave_piece[s, f, 8:9, :] = wave_tail[s, 32 + f : 33 + f, :]

    part_refs = ((wave, recv), (back, field))
    fold_refs = ((wave_fold, recv_fold), (back_fold, field_fold))
    straight = [(1, 2), (0, 2), (1, 1), (1, 3), (0, 1), (0, 3), (1, 0)]

    def rows_of(index, rows):
        return pl.ds(pl.multiple_of(index * rows, 8), rows)

    def send_part(phase, s, f):
        src, dst = part_refs[phase]
        for dx, dy in straight:
            to = at(dx, dy)
            remote(
                src.at[s, f, rows_of(to, PART)],
                dst.at[s, f, rows_of(me, PART)],
                part_send.at[phase, s],
                part_recv.at[phase, s, f],
                pencil=to,
            ).start()
        dst[s, f, rows_of(me, PART), :] = src[s, f, rows_of(me, PART), :]

    def send_fold(phase, s):
        src, dst = fold_refs[phase]
        for dx, dy in straight:
            to = at(dx, dy)
            remote(
                src.at[s, rows_of(to, LAST)],
                dst.at[s, rows_of(me, LAST)],
                fold_send.at[phase, s],
                fold_recv.at[phase, s],
                pencil=to,
            ).start()
        dst[s, rows_of(me, LAST), :] = src[s, rows_of(me, LAST), :]

    def drain(view, sem):
        pltpu.make_async_copy(view, view, sem).wait()

    def wait_part(phase, s, f):
        drain(part_refs[phase][1].at[s, f, pl.ds(0, 7 * PART)], part_recv.at[phase, s, f])

    def wait_fold(phase, s):
        drain(fold_refs[phase][1].at[s, pl.ds(0, 7 * LAST)], fold_recv.at[phase, s])

    def end_blocks(phase, s):
        parts = part_refs[phase][0].at[s, pl.ds(0, FIELDS), pl.ds(0, 7 * PART)]
        drain(parts, part_send.at[phase, s])
        drain(fold_refs[phase][0].at[s, pl.ds(0, 7 * LAST)], fold_send.at[phase, s])

    def piece_of(ref, s, index):
        return ref.at[s, pl.ds(pl.multiple_of(index * PIECE, 8), PIECE), :]

    def owner_of(s, f):
        return FIELDS * s + f

    def tail_copy(s, f, distance):
        return remote(
            wave_piece.at[s, f],
            piece_of(recv_tail, s, me),
            tail_send.at[s, f],
            tail_recv.at[s, distance],
            pencil=owner_of(s, f),
        )

    def second(s):
        wait_fold(0, s)

        def last_rows(f, tile):
            return pl.ds(tile % 3 * 8 + FIELDS * (tile // 3) + f, PEERS, stride=LAST)

        def one_field(i, carry):
            f = order(i)
            wait_part(0, s, f)
            columns = []
            for tile in range(OWN_TILES):
                starts = [p * PART + tile * 8 for p in range(PEERS)]
                rows = [recv[s, f, start : start + 8, :] for start in starts]
                rows.append(recv_fold[s, last_rows(f, tile), :])
                columns.append(jnp.concatenate(rows, axis=0))
            spectrum = left(wide[512:592, :], jnp.concatenate(columns, axis=1))
            result = left(wide[592:672, :], spectrum * kernel_table[...])
            for tile in range(OWN_TILES):
                lanes = slice(tile * 128, tile * 128 + 128)
                for p in range(PEERS):
                    start = p * PART + tile * 8
                    back[s, f, start : start + 8, :] = result[p * 8 : p * 8 + 8, lanes]
                back_fold[s, last_rows(f, tile), :] = result[64:72, lanes]
            send_part(1, s, f)
            return carry

        lax.fori_loop(0, FIELDS, one_field, 0)
        send_fold(1, s)

    def give_copies(s):
        return block_copies(
            give_parts(give.at[s], give_fold.at[s]),
            give_parts(given.at[s], given_fold.at[s]),
            give_send.at[s],
            give_recv.at[s],
            terms_group(s),
        )

    def order(i):
        return lax.rem(2 * i, FIELDS) + lax.div(i, 2)

    def pair_weights(s):
        weights = []
        for f in range(FIELDS):
            g = 2 * (f % 2) + f // 2
            above = visit_fold[s, MASKS, FIELDS + g : FIELDS + g + 1, :]
            same = visit_fold[s, MASKS, g : g + 1, :]
            mine = own_fold[MASKS, FIELDS + f : FIELDS + f + 1, :]
            row = jnp.where(s == 0, same, jnp.where(even, above, mine))
            weights.append(jnp.broadcast_to(row, (8, 128)))
        return weights

    def third(s):
        weights = pair_weights(s)
        leaving = give_copies(s)

        def leave(which):
            for part in which:
                leaving[part].start()

        def gather_band(c, begin, end):
            def gather(tile, j):
                chi = visit[s, tile, first_band[c], :]
                terms = base[c, tile]
                for a in range(2):
                    value = rho[tile, field_rows[2 * a + c], :] * weights[2 * a + c]
                    total[tile, first_band[a], :] += value * chi
                    terms = terms + value * own[tile, first_band[a], :]
                give[s, c, tile] = terms

            tile_loop(begin, end, gather)

        def one_row(i, carry):
            t = jnp.where(i == FIELDS, FIELDS, order(jnp.minimum(i, FIELDS - 1)))

            @pl.when(t < FIELDS)
            def _():
                wait_part(1, s, t)

            @pl.when(t == FIELDS)
            def _():
                wait_fold(1, s)

                def unfold(q, carry):
                    for k in range(OWN_TILES):
                        from_row = pl.multiple_of(q * LAST + k % 3 * 8, 8)
                        value = field_fold[s, pl.ds(from_row, 8), :]
                        value = pltpu.roll(value, FIELDS, 0) if k > 2 else value
                        to_row = pl.multiple_of((q * OWN_TILES + k) * 8, 8)
                        field[s, FIELDS, pl.ds(to_row, 8), :] = value
                    return carry

                lax.fori_loop(0, PEERS, unfold, 0)

            def source(tile):
                if tile == TAIL_TILE:
                    return field_tail[s, row_of(t), :]
                return field[s, t, tile * 8 : tile * 8 + 8, :]

            def load(slot):
                return take(source, slot * NG)

            def save(part, b, value):
                work[place(part, b), :] = value

            finish72_adjoint(load, save)
            along_z(256)

            def target(tile, lanes, piece):
                rho[tile, row_of(t), lanes] = piece

            for b in range(9):
                values = dft8_adjoint([work2[place(part, b), :] for part in range(8)])
                for a, value in enumerate(values):
                    put(target, point72(a, b) * NG, value)

            @pl.when((s == 1) & even & (i == 1))
            def _():
                for copy in give_copies(0):
                    copy.wait_recv()

                def join(tile, carry):
                    for band in range(2):
                        base[band, tile] = given[0, band, tile]
                    return carry

                lax.fori_loop(0, TILES, join, 0)
                base_fold[...] = given_fold[0]

            @pl.when(i == 1)
            def _():
                gather_band(0, 0, TILES)
                leave([0])

            @pl.when(i == 3)
            def _():
                for q, (begin, end) in enumerate(QUARTERS):
                    gather_band(1, begin, end)
                    leave([1 + q])

            return carry

        lax.fori_loop(0, FIELDS + 1, one_row, 0)
        last_weight = weights[3]
        for f in range(3):
            last_weight = jnp.where(row_at == f, weights[f], last_weight)

        for q, (begin, end) in enumerate(QUARTERS):

            def gather_last(tile, j, q=q):
                phi, chi = last_planes(s, j, q)
                value = rho[tile, 32:40, :] * last_weight
                stay, leave = value * chi, value * phi
                stay = stay + pltpu.roll(stay, 7, 0)
                leave = leave + pltpu.roll(leave, 6, 0)
                for band in range(2):
                    row = slice(2 * q + band, 2 * q + band + 1)
                    total_fold[j, row, :] += stay[2 * band : 2 * band + 1]
                    give_fold[s, j, row, :] = leave[band : band + 1] + base_fold[j, row, :]

            tile_loop(begin, end, gather_last)
        leave([5])

    def tail_back(s, f, j):
        return remote(
            piece_of(back_tail, s, peer(j)),
            field_piece.at[s, f],
            back_tail_send.at[s, j],
            back_tail_recv.at[s, f],
            pencil=peer(j),
        )

    def send_tail(s):
        for f in range(FIELDS):
            owner = owner_of(s, f)

            @pl.when(me == owner)
            def _(f=f, owner=owner):
                recv_tail[s, rows_of(owner, PIECE), :] = wave_piece[s, f]

            @pl.when(me != owner)
            def _(f=f, owner=owner):
                tail_copy(s, f, lax.rem(owner - me + PEERS, PEERS)).start()

    def turn_tail(s):
        owned = lax.div(me, FIELDS) == s

        @pl.when(owned)
        def _():
            for j in range(1, PEERS):
                tail_copy(s, 0, j).wait_recv()
            parts = [pl.ds(p * PIECE, 8) for p in range(PEERS)] + [pl.ds(8, PEERS, stride=PIECE)]
            block = jnp.concatenate([recv_tail[s, part, :] for part in parts], axis=0)
            spectrum = left(wide[512:592, :], block) * kernel_tail[...]
            result = left(wide[592:672, :], spectrum)
            for i, part in enumerate(parts):
                back_tail[s, part, :] = result[i * 8 : i * 8 + 8, :]
            mine = lax.rem(me, FIELDS)
            for j in range(1, PEERS):
                tail_back(s, mine, j).start()
            field_piece[s, mine] = back_tail[s, pl.ds(pl.multiple_of(me * PIECE, 8), PIECE), :]

    def end_tail(s):
        for f in range(FIELDS):
            owner = owner_of(s, f)

            @pl.when(me != owner)
            def _(f=f, owner=owner):
                tail_copy(s, f, lax.rem(owner - me + PEERS, PEERS)).wait_send()
                tail_back(s, f, 1).wait_recv()

            field_tail[s, field_rows[f], :] = field_piece[s, f, 0:8, :]
            field_tail[s, 32 + f : 33 + f, :] = field_piece[s, f, 8:9, :]

        @pl.when(lax.div(me, FIELDS) == s)
        def _():
            for j in range(1, PEERS):
                tail_back(s, lax.rem(me, FIELDS), j).wait_send()

    def slots(*stages):
        def run(s, carry):
            for stage in stages:
                stage(s)
            return carry

        lax.fori_loop(0, 2, run, 0)

    slots(first, send_tail)
    slots(second, turn_tail)
    slots(end_tail, third)

    def wait_given(which):
        for part in which:
            give_copies(1)[part].wait_recv()

            @pl.when(jnp.logical_not(even))
            def _(part=part):
                give_copies(0)[part].wait_recv()

    for q, (begin, end) in enumerate(QUARTERS):
        wait_given([0, 1] if q == 0 else [1 + q])

        def result(tile, j, width=128):
            lanes = pl.ds(tile * 128, width)
            if width == 128:
                lanes = pl.ds(pl.multiple_of(tile * 128, 128), 128)
            for rows, band in zip(first_band, range(2)):
                near = jnp.where(even, 0.0, given[0, band, tile])
                term = -(total[tile, rows, :] + near + given[1, band, tile])
                mixed[tile, pl.ds(band, 8, stride=2), :] = term
            for plane in range(PLANES - 1):
                piece = mixed[tile, 2 * plane : 2 * plane + 2, 0:width]
                out_ref[plane, :, lanes] = piece

        tile_loop(begin, min(end, TAIL_TILE), result)
        if end > TAIL_TILE:
            result(TAIL_TILE, 0, MERGED - TAIL)
    wait_given([5])
    for q, (begin, end) in enumerate(QUARTERS):

        def last_result(tile, j, q=q, width=128):
            lanes = pl.ds(tile * 128, width)
            if width == 128:
                lanes = pl.ds(pl.multiple_of(tile * 128, 128), 128)
            rows = slice(2 * q, 2 * q + 2)
            near = jnp.where(even, 0.0, given_fold[0, j, rows, :])
            term = total_fold[j, rows, :] + near + given_fold[1, j, rows, :]
            out_ref[PLANES - 1, :, lanes] = -term[:, 0:width]

        tile_loop(begin, min(end, TAIL_TILE), last_result)
        if end > TAIL_TILE:
            last_result(TAIL_TILE, TAIL_TILE - begin, width=MERGED - TAIL)

    for copy in near_sends():
        copy.wait_send()

    @pl.when(jnp.logical_not(even))
    def _():
        for copy in far_sends() + passes():
            copy.wait_send()

    for s in range(2):
        for copy in give_copies(s):
            copy.wait_send()
    for phase in range(2):
        for s in range(2):
            end_blocks(phase, s)


def body(bands, orbitals, pair_mask):
    hbm = pl.BlockSpec(memory_space=pltpu.HBM)
    smem = pl.BlockSpec(memory_space=pltpu.SMEM)
    consts = [jnp.asarray(table) for table in tables()]
    dma = pltpu.SemaphoreType.DMA

    def buffer(*shape):
        return pltpu.VMEM(shape, jnp.float32)

    out = pl.pallas_call(
        functools.partial(kernel, bands),
        out_shape=jax.ShapeDtypeStruct((PLANES, 2, MERGED), jnp.float32),
        in_specs=[smem] + [hbm] * (1 + len(consts)),
        out_specs=pl.BlockSpec(memory_space=pltpu.VMEM),
        scratch_shapes=[
            buffer(PLANES, 2, MERGED),
            pltpu.VMEM(consts[0].shape, jnp.bfloat16),
            buffer(*consts[1].shape),
            buffer(*consts[2].shape),
            buffer(TILES, 16, 128),
            buffer(TILES, 16, 128),
            buffer(FOLD + 1, 8, 128),
            buffer(2, TILES, 16, 128),
            buffer(2, FOLD + 1, 8, 128),
            buffer(TILES, ROWS, 128),
            buffer(NG * 8, 128),
            buffer(NG * 8, 128),
            buffer(2, FIELDS + 1, PEERS * PART, 128),
            buffer(2, PEERS * LAST, 128),
            buffer(2, ROWS, 128),
            buffer(2, FIELDS, PIECE, 128),
            buffer(2, FIELDS, PEERS * PART, 128),
            buffer(2, PEERS * LAST, 128),
            buffer(2, PEERS * PIECE, 128),
            buffer(2, FIELDS, PEERS * PART, 128),
            buffer(2, PEERS * LAST, 128),
            buffer(2, PEERS * PIECE, 128),
            buffer(2, FIELDS + 1, PEERS * PART, 128),
            buffer(2, PEERS * LAST, 128),
            buffer(2, ROWS, 128),
            buffer(2, FIELDS, PIECE, 128),
            buffer(NG, OWN),
            buffer(NG, 128),
            buffer(TILES, 16, 128),
            buffer(FOLD + 1, 8, 128),
            buffer(2, TILES, 8, 128),
            buffer(FOLD + 1, 8, 128),
            buffer(2, 2, TILES, 8, 128),
            buffer(2, FOLD + 1, 8, 128),
            buffer(2, 2, TILES, 8, 128),
            buffer(2, FOLD + 1, 8, 128),
            dma((2, 5)),
            dma((2, 5)),
            dma((5,)),
            dma((2, 6)),
            dma((2, 6)),
            dma((2, 2)),
            dma((2, 2, FIELDS)),
            dma((2, 2)),
            dma((2, 2)),
            dma((2, FIELDS)),
            dma((2, PEERS)),
            dma((2, PEERS)),
            dma((2, FIELDS)),
            dma((4,)),
        ],
        compiler_params=pltpu.CompilerParams(
            collective_id=0, has_side_effects=True, vmem_limit_bytes=64 * 1024 * 1024 - 65536
        ),
    )(pair_mask, orbitals.transpose(1, 0, 2), *consts)
    return out.transpose(1, 0, 2)


def solution(mesh):
    return jax.shard_map(
        functools.partial(body, mesh.shape["band"]),
        mesh=mesh,
        in_specs=(P("band", "pencil", None), P("band", None, None, None)),
        out_specs=P("band", "pencil", None),
        check_vma=False,
    )
```

```python
import functools
import math

import jax
import jax.numpy as jnp
import ml_dtypes
import numpy as np
from jax import lax
from jax.experimental import pallas as pl
from jax.experimental.pallas import tpu as pltpu
from jax.sharding import PartitionSpec as P

MESH = pl.DeviceIdType.MESH
NG = 72
PLANES = 9
PEERS = 8
FIELDS = 4
ROWS = 40
PART = 40
LAST = 24
MERGED = NG * NG
WIDTH = 5248
OWN = 640
TAIL = PEERS * OWN
PIECE = 16
FOLD = 11
MASKS = FOLD
QUARTERS = [(q * FOLD, min((q + 1) * FOLD, 41)) for q in range(4)]
TILES = WIDTH // 128
OWN_TILES = OWN // 128
TAIL_TILE = TILES - 1
coulomb_scale = 20.0
screening = 0.25
HALF = math.sqrt(0.5)


def dft8(x):
    a = [x[j] + x[j + 4] for j in range(4)]
    b = [x[j] - x[j + 4] for j in range(4)]
    e, o = a[0] + a[2], a[1] + a[3]
    u, v = HALF * (b[1] - b[3]), HALF * (b[1] + b[3])
    return [e + o, e - o, b[0] + u, v + b[2], a[0] - a[2], a[1] - a[3], b[0] - u, v - b[2]]


def dft8_adjoint(c):
    p, q = c[0] + c[1], c[0] - c[1]
    a = [p + c[4], q + c[5], p - c[4], q - c[5]]
    d, s = HALF * (c[2] - c[6]), HALF * (c[3] + c[7])
    b = [c[2] + c[6], d + s, c[3] - c[7], s - d]
    return [a[j] + b[j] for j in range(4)] + [a[j] - b[j] for j in range(4)]


def cos9(n):
    return math.cos(2.0 * math.pi * (n % 9) / 9)


def sin9(n):
    return math.sin(2.0 * math.pi * (n % 9) / 9)


def weighted(values, factors):
    total = values[0] * factors[0]
    for value, factor in zip(values[1:], factors[1:]):
        total = total + value * factor
    return total


def dft9(x):
    e = [x[n] + x[9 - n] for n in range(1, 5)]
    o = [x[n] - x[9 - n] for n in range(1, 5)]
    third = e[0] + e[1] + e[3]
    cosines = [x[0] + third + e[2]]
    sines = [None]
    for k in range(1, 5):
        if k == 3:
            cosines.append(x[0] + e[2] - 0.5 * third)
            sines.append(sin9(3) * (o[0] - o[1] + o[3]))
        else:
            cosines.append(x[0] + weighted(e, [cos9(k * n) for n in range(1, 5)]))
            sines.append(weighted(o, [sin9(k * n) for n in range(1, 5)]))
    return cosines, sines


def dft9_adjoint(cosines, sines):
    c, s = cosines, sines
    out = [None] * 9
    out[0] = c[0] + ((c[1] + c[2]) + (c[3] + c[4]))
    for n in range(1, 5):
        if n == 3:
            even = c[0] + c[3] - 0.5 * (c[1] + c[2] + c[4])
            odd = sin9(3) * (s[1] - s[2] + s[4])
        else:
            even = c[0] + weighted(c[1:], [cos9(k * n) for k in range(1, 5)])
            odd = weighted(s[1:], [sin9(k * n) for k in range(1, 5)])
        out[n] = even + odd
        out[9 - n] = even - odd
    return out


def finish72(load, save):
    for part in (0, 1):
        cosines, sines = dft9([load(part, b) for b in range(9)])
        base = part * 9
        save(base, cosines[0])
        for k in range(1, 5):
            save(base + 2 * k - 1, cosines[k])
            save(base + 2 * k, sines[k])
    for k8 in range(3):
        base = 18 + 18 * k8
        cc, cs = dft9([load(2 + 2 * k8, b) for b in range(9)])
        sc, ss = dft9([load(3 + 2 * k8, b) for b in range(9)])
        save(base, cc[0])
        save(base + 1, sc[0])
        for k in range(1, 5):
            at = base + 4 * k - 2
            save(at, cc[k] - ss[k])
            save(at + 1, cc[k] + ss[k])
            save(at + 2, sc[k] + cs[k])
            save(at + 3, sc[k] - cs[k])


def finish72_adjoint(load, save):
    for part in (0, 1):
        base = part * 9
        cosines = [load(base)] + [load(base + 2 * k - 1) for k in range(1, 5)]
        sines = [None] + [load(base + 2 * k) for k in range(1, 5)]
        for b, value in enumerate(dft9_adjoint(cosines, sines)):
            save(part, b, value)
    for k8 in range(3):
        base = 18 + 18 * k8
        cc, sc, cs, ss = [load(base)], [load(base + 1)], [None], [None]
        for k in range(1, 5):
            at = base + 4 * k - 2
            plus, minus, sine_plus, sine_minus = [load(at + i) for i in range(4)]
            cc.append(plus + minus)
            ss.append(minus - plus)
            sc.append(sine_plus + sine_minus)
            cs.append(sine_plus - sine_minus)
        for b, value in enumerate(dft9_adjoint(cc, cs)):
            save(2 + 2 * k8, b, value)
        for b, value in enumerate(dft9_adjoint(sc, ss)):
            save(3 + 2 * k8, b, value)


def point72(a, b):
    return (9 * a + 8 * b) % NG


def split(table):
    high = table.astype(ml_dtypes.bfloat16).astype(np.float64)
    return high, (table - high).astype(ml_dtypes.bfloat16).astype(np.float64)


def from_left(table):
    high, low = split(table)
    wide = np.zeros((80, 256))
    wide[:NG, : 3 * NG] = np.concatenate([high, high, low], axis=1)
    return wide


def from_right(table):
    high, low = split(table)
    return np.block([[high, low], [high, np.zeros_like(low)]])


@functools.cache
def tables():
    at = np.arange(NG)
    basis, freq = [np.full(NG, 1.0)], [0]
    for k in range(1, NG // 2):
        basis += [np.cos(2 * np.pi * k * at / NG), np.sin(2 * np.pi * k * at / NG)]
        freq += [k, k]
    basis.append(np.cos(np.pi * at))
    freq.append(NG // 2)
    basis = np.array(basis)
    basis /= np.sqrt((basis * basis).sum(1, keepdims=True))
    freq = np.array(freq, np.float64)
    eye = np.eye(NG)
    parts = [dft8([eye[point72(a, b)] for a in range(8)]) for b in range(9)]
    slots = [None] * NG
    finish72(lambda part, b: parts[b][part], slots.__setitem__)
    slots = np.array(slots)
    norm = (slots * slots).sum(1)
    spectrum = np.abs(np.fft.fft(slots, axis=1))[:, : NG // 2 + 1]
    freq_y = spectrum.argmax(1).astype(np.float64)
    along_z = np.zeros((128, 128))
    along_z[:NG, :NG] = basis.T
    along_x = basis.reshape(NG, PEERS, PLANES)
    along_x = np.concatenate([along_x[:, :, :8].reshape(NG, -1), along_x[:, :, 8]], axis=1)
    column = np.zeros((8, WIDTH), np.float32)
    column[0, :MERGED] = (freq_y[:, None] ** 2 + freq[None, :] ** 2).reshape(-1)
    column[1, :MERGED] = np.repeat(1.0 / norm, NG)
    freq_x = np.broadcast_to((freq**2)[:, None], (NG, 128)).astype(np.float32)
    wide = np.concatenate(
        [from_right(along_z), from_right(along_z.T), from_left(along_x), from_left(along_x.T)]
    )
    return wide.astype(ml_dtypes.bfloat16), column, freq_x


def take(load, start):
    tile, lane = divmod(start, 128)
    value = load(tile)
    if lane == 0:
        return value
    if lane + NG > 128:
        at = lax.broadcasted_iota(jnp.int32, value.shape, 1)
        value = jnp.where(at >= lane, value, load(tile + 1))
    return pltpu.roll(value, 128 - lane, 1)


def put(store, start, value):
    tile, lane = divmod(start, 128)
    if lane:
        value = pltpu.roll(value, lane, 1)
    end = min(lane + NG, 128)
    store(tile, slice(lane, end), value[:, lane:end])
    if lane + NG > 128:
        store(tile + 1, slice(0, lane + NG - 128), value[:, : lane + NG - 128])


def matmul(a, b):
    return jnp.dot(a, b, preferred_element_type=jnp.float32)


def halves(x):
    high = x.astype(jnp.bfloat16)
    return high, (x - high.astype(jnp.float32)).astype(jnp.bfloat16)


def left(table, x):
    high, low = [part.astype(jnp.float32) for part in halves(x)]
    zeros = jnp.zeros((8, x.shape[1]), jnp.float32)
    operand = jnp.concatenate([high, low, high, zeros], axis=0).astype(jnp.bfloat16)
    return matmul(table[:, 0 : operand.shape[0]], operand)[0:NG]


def kernel(
    bands,
    mask_ref,
    bands_hbm,
    wide_hbm,
    column_hbm,
    freq_hbm,
    out_ref,
    bands_ref,
    wide,
    column_ref,
    freq_ref,
    mixed,
    own,
    own_fold,
    visit,
    visit_fold,
    rho,
    work,
    work2,
    wave,
    wave_fold,
    wave_tail,
    wave_piece,
    recv,
    recv_fold,
    recv_tail,
    back,
    back_fold,
    back_tail,
    field,
    field_fold,
    field_tail,
    field_piece,
    kernel_table,
    kernel_tail,
    total,
    total_fold,
    base,
    base_fold,
    give,
    give_fold,
    given,
    given_fold,
    visit_send,
    visit_recv,
    pass_send,
    give_send,
    give_recv,
    part_send,
    part_recv,
    fold_send,
    fold_recv,
    tail_send,
    tail_recv,
    back_tail_send,
    back_tail_recv,
    load_sem,
):
    me = lax.axis_index("pencil")
    group = lax.axis_index("band")
    me_x, me_y = lax.div(me, 4), lax.rem(me, 4)

    loads = [
        pltpu.make_async_copy(src, dst, load_sem.at[i])
        for i, (src, dst) in enumerate(
            [
                (bands_hbm, bands_ref),
                (wide_hbm, wide),
                (column_hbm, column_ref),
                (freq_hbm, freq_ref),
            ]
        )
    ]
    for load in loads:
        load.start()

    def peer(j):
        return lax.rem(me + j, PEERS)

    def at(dx, dy):
        return lax.rem(me_x + dx, 2) * 4 + lax.rem(me_y + dy + 4, 4)

    def group_at(j):
        return lax.rem(group + j + bands, bands)

    barrier = pltpu.get_barrier_semaphore()
    for j in range(1, PEERS):
        pl.semaphore_signal(barrier, inc=1, device_id={"pencil": peer(j)}, device_id_type=MESH)
    for j in (-2, -1, 1, 2):
        pl.semaphore_signal(barrier, inc=1, device_id={"band": group_at(j)}, device_id_type=MESH)
    def remote(src, dst, send, recv, **device):
        return pltpu.make_async_remote_copy(
            src_ref=src,
            dst_ref=dst,
            send_sem=send,
            recv_sem=recv,
            device_id=device,
            device_id_type=MESH,
        )

    even = lax.rem(group, 2) == 0

    def terms_group(s):
        near = jnp.where(even, group_at(1), group_at(-1))
        return jnp.where(s == 0, near, jnp.where(even, group_at(2), group_at(-2)))

    def parts(main, fold):
        return [
            *(main.at[pl.ds(begin, end - begin)] for begin, end in QUARTERS),
            fold,
        ]

    def block_copies(src, dst, send, recv, to):
        return [
            remote(one, two, send.at[q], recv.at[q], band=to)
            for q, (one, two) in enumerate(zip(src, dst))
        ]

    def block_parts(main, fold):
        first = [main.at[pl.ds(begin, end - begin), pl.ds(0, 8)] for begin, end in QUARTERS]
        return [*first, fold, main.at[:, pl.ds(8, 8)]]

    def visit_at(s):
        return block_parts(visit.at[s], visit_fold.at[s])

    own_parts = block_parts(own, own_fold)

    def give_parts(main, fold):
        return [main.at[0], *parts(main.at[1], fold)]

    def visit_copies(s, src, send, to):
        return block_copies(src, visit_at(s), send, visit_recv.at[s], to)

    def near_sends():
        return visit_copies(0, own_parts, visit_send.at[0], group_at(-1))

    def far_sends():
        return visit_copies(1, own_parts, visit_send.at[1], group_at(2))

    def passes():
        return visit_copies(1, visit_at(0), pass_send, group_at(-1))

    loads[0].wait()
    def take_tile(tile, j, q, width):
        lanes = pl.ds(tile * 128, width)
        if width == 128:
            lanes = pl.ds(pl.multiple_of(tile * 128, 128), 128)
        live = slice(0, width)
        for plane in range(PLANES - 1):
            mixed[tile, 2 * plane : 2 * plane + 2, live] = bands_ref[plane, :, lanes]
        for band in range(2):
            own[tile, band * 8 : band * 8 + 8, :] = mixed[tile, pl.ds(band, 8, stride=2), :]
        own_fold[j, 2 * q : 2 * q + 2, live] = bands_ref[PLANES - 1, :, lanes]

    def tile_loop(begin, end, step):
        def run(j, carry):
            step(begin + j, j)
            return carry

        lax.fori_loop(0, end - begin, run, 0, unroll=True)

    mixed[TAIL_TILE] = jnp.zeros((16, 128), jnp.float32)
    own_fold[TAIL_TILE % FOLD, 6:8, :] = jnp.zeros((2, 128), jnp.float32)

    def own_mask(s, f):
        return mask_ref[0, s, f // 2, f % 2].astype(jnp.float32)

    for m in range(2 * FIELDS):
        value = own_mask(m // FIELDS, m % FIELDS)
        own_fold[MASKS, m : m + 1, :] = jnp.zeros((1, 128), jnp.float32) + value
    pl.semaphore_wait(barrier, PEERS - 1 + 4)
    near, far = near_sends(), far_sends()

    def send_own(part):
        near[part].start()

        @pl.when(jnp.logical_not(even))
        def _():
            far[part].start()

    for q, (begin, end) in enumerate(QUARTERS):
        tile_loop(begin, min(end, TAIL_TILE), lambda tile, j, q=q: take_tile(tile, j, q, 128))
        if end > TAIL_TILE:
            take_tile(TAIL_TILE, TAIL_TILE % FOLD, q, MERGED - TAIL)
        send_own(q)
    send_own(4)
    send_own(5)

    def kernel_columns(start, width):
        squared = column_ref[0:1, pl.ds(start, width)]
        scale = column_ref[1:2, pl.ds(start, width)]
        return coulomb_scale / (freq_ref[:, 0:1] + squared + screening) * scale

    for load in loads[1:]:
        load.wait()
    kernel_table[...] = kernel_columns(pl.multiple_of(me * OWN, 128), OWN)
    kernel_tail[...] = kernel_columns(TAIL, 128)
    wave_tail[...] = jnp.zeros((2, ROWS, 128), jnp.float32)
    total_fold[...] = jnp.zeros((FOLD + 1, 8, 128), jnp.float32)
    base_fold[...] = jnp.zeros((FOLD + 1, 8, 128), jnp.float32)

    def clear(tile, carry):
        total[tile] = jnp.zeros((16, 128), jnp.float32)
        base[:, tile] = jnp.zeros((2, 8, 128), jnp.float32)
        return carry

    lax.fori_loop(0, TILES, clear, 0)
    for s in range(2):
        for p in range(PEERS):
            back_fold[s, (p + 1) * LAST - 8 : (p + 1) * LAST, :] = jnp.zeros((8, 128), jnp.float32)
            back_tail[s, (p + 1) * PIECE - 8 : (p + 1) * PIECE, :] = jnp.zeros((8, 128), jnp.float32)
        field_tail[s, 32:40, :] = jnp.zeros((8, 128), jnp.float32)
        for f in range(FIELDS):
            wave_piece[s, f, 8:16, :] = jnp.zeros((8, 128), jnp.float32)

    first_band = [slice(band * 8, band * 8 + 8) for band in range(2)]
    field_rows = [slice(f * 8, f * 8 + 8) for f in range(FIELDS)]
    row_at = lax.broadcasted_iota(jnp.int32, (8, 128), 0)
    resident_one = lax.rem(lax.div(row_at, 2), 2) == 1
    visitor_one = lax.rem(row_at, 2) == 1

    def last_planes(s, j, q):
        a = [own_fold[j, 2 * q + band : 2 * q + band + 1, :] for band in range(2)]
        c = [visit_fold[s, j, 2 * q + band : 2 * q + band + 1, :] for band in range(2)]
        wide_a = [jnp.broadcast_to(row, (8, 128)) for row in a]
        wide_c = [jnp.broadcast_to(row, (8, 128)) for row in c]
        return (
            jnp.where(resident_one, wide_a[1], wide_a[0]),
            jnp.where(visitor_one, wide_c[1], wide_c[0]),
        )

    def along_z(start):
        both = matmul(jnp.concatenate(halves(work[...]), axis=1), wide[start : start + 256, :])
        work2[...] = both[:, :128] + both[:, 128:]

    def place(part, b):
        return slice((part * 9 + b) * 8, (part * 9 + b) * 8 + 8)

    def row_of(t):
        return pl.ds(pl.multiple_of(t * 8, 8), 8)

    def first(s):
        arriving = visit_copies(s, own_parts, visit_send.at[0], group_at(1))
        passing = passes()

        def arrive(part):
            arriving[part].wait_recv()

            @pl.when((s == 0) & jnp.logical_not(even))
            def _():
                passing[part].start()

        for part in range(5):
            arrive(part)

        def one_row(i, carry):
            t = jnp.where(i == 0, FIELDS, order(jnp.maximum(i - 1, 0)))

            @pl.when(i == 3)
            def _():
                arrive(5)

            @pl.when(i > 0)
            def _():
                resident, visitor = row_of(lax.div(t, 2)), row_of(lax.rem(t, 2))
                for tile in range(TILES):
                    rho[tile, row_of(t), :] = own[tile, resident, :] * visit[s, tile, visitor, :]

            @pl.when(i == 0)
            def _():
                for q, (begin, end) in enumerate(QUARTERS):

                    def products(tile, j, q=q):
                        phi, chi = last_planes(s, j, q)
                        rho[tile, 32:40, :] = phi * chi

                    tile_loop(begin, end, products)

            for b in range(9):
                starts = [point72(a, b) * NG for a in range(8)]
                values = [take(lambda tile: rho[tile, row_of(t), :], at) for at in starts]
                for part, value in enumerate(dft8(values)):
                    work[place(part, b), :] = value
            along_z(0)

            def load(part, b):
                return work2[place(part, b), :]

            def target(tile, lanes, piece):
                if tile == TAIL_TILE:
                    wave_tail[s, row_of(t), lanes] = piece
                else:
                    wave[s, t, tile * 8 : tile * 8 + 8, lanes] = piece

            def save(slot, value):
                put(target, slot * NG, value)

            finish72(load, save)

            @pl.when(i == 0)
            def _():
                upper = lax.broadcasted_iota(jnp.int32, (8, 128), 0) < FIELDS

                def fold(q, carry):
                    for k in range(3):
                        at_row = pl.multiple_of((q * OWN_TILES + k) * 8, 8)
                        piece = wave[s, FIELDS, pl.ds(at_row, 8), :]
                        if k < 2:
                            below = wave[s, FIELDS, pl.ds(at_row + 24, 8), :]
                            piece = jnp.where(upper, piece, below)
                        to_row = pl.multiple_of(q * LAST + k * 8, 8)
                        wave_fold[s, pl.ds(to_row, 8), :] = piece
                    return carry

                lax.fori_loop(0, PEERS, fold, 0)
                send_fold(0, s)

            @pl.when(i > 0)
            def _():
                send_part(0, s, t)

            return carry

        lax.fori_loop(0, FIELDS + 1, one_row, 0)
        for f in range(FIELDS):
            wave_piece[s, f, 0:8, :] = wave_tail[s, field_rows[f], :]
            wave_piece[s, f, 8:9, :] = wave_tail[s, 32 + f : 33 + f, :]

    part_refs = ((wave, recv), (back, field))
    fold_refs = ((wave_fold, recv_fold), (back_fold, field_fold))
    straight = [(1, 2), (0, 2), (1, 1), (1, 3), (0, 1), (0, 3), (1, 0)]

    def rows_of(index, rows):
        return pl.ds(pl.multiple_of(index * rows, 8), rows)

    def send_part(phase, s, f):
        src, dst = part_refs[phase]
        for dx, dy in straight:
            to = at(dx, dy)
            remote(
                src.at[s, f, rows_of(to, PART)],
                dst.at[s, f, rows_of(me, PART)],
                part_send.at[phase, s],
                part_recv.at[phase, s, f],
                pencil=to,
            ).start()
        dst[s, f, rows_of(me, PART), :] = src[s, f, rows_of(me, PART), :]

    def send_fold(phase, s):
        src, dst = fold_refs[phase]
        for dx, dy in straight:
            to = at(dx, dy)
            remote(
                src.at[s, rows_of(to, LAST)],
                dst.at[s, rows_of(me, LAST)],
                fold_send.at[phase, s],
                fold_recv.at[phase, s],
                pencil=to,
            ).start()
        dst[s, rows_of(me, LAST), :] = src[s, rows_of(me, LAST), :]

    def drain(view, sem):
        pltpu.make_async_copy(view, view, sem).wait()

    def wait_part(phase, s, f):
        drain(part_refs[phase][1].at[s, f, pl.ds(0, 7 * PART)], part_recv.at[phase, s, f])

    def wait_fold(phase, s):
        drain(fold_refs[phase][1].at[s, pl.ds(0, 7 * LAST)], fold_recv.at[phase, s])

    def end_blocks(phase, s):
        parts = part_refs[phase][0].at[s, pl.ds(0, FIELDS), pl.ds(0, 7 * PART)]
        drain(parts, part_send.at[phase, s])
        drain(fold_refs[phase][0].at[s, pl.ds(0, 7 * LAST)], fold_send.at[phase, s])

    def piece_of(ref, s, index):
        return ref.at[s, pl.ds(pl.multiple_of(index * PIECE, 8), PIECE), :]

    def owner_of(s, f):
        return FIELDS * s + f

    def tail_copy(s, f, distance):
        return remote(
            wave_piece.at[s, f],
            piece_of(recv_tail, s, me),
            tail_send.at[s, f],
            tail_recv.at[s, distance],
            pencil=owner_of(s, f),
        )

    def second(s):
        wait_fold(0, s)

        def last_rows(f, tile):
            return pl.ds(tile % 3 * 8 + FIELDS * (tile // 3) + f, PEERS, stride=LAST)

        def one_field(i, carry):
            f = order(i)
            wait_part(0, s, f)
            columns = []
            for tile in range(OWN_TILES):
                starts = [p * PART + tile * 8 for p in range(PEERS)]
                rows = [recv[s, f, start : start + 8, :] for start in starts]
                rows.append(recv_fold[s, last_rows(f, tile), :])
                columns.append(jnp.concatenate(rows, axis=0))
            spectrum = left(wide[512:592, :], jnp.concatenate(columns, axis=1))
            result = left(wide[592:672, :], spectrum * kernel_table[...])
            for tile in range(OWN_TILES):
                lanes = slice(tile * 128, tile * 128 + 128)
                for p in range(PEERS):
                    start = p * PART + tile * 8
                    back[s, f, start : start + 8, :] = result[p * 8 : p * 8 + 8, lanes]
                back_fold[s, last_rows(f, tile), :] = result[64:72, lanes]
            send_part(1, s, f)
            return carry

        lax.fori_loop(0, FIELDS, one_field, 0)
        send_fold(1, s)

    def give_copies(s):
        return block_copies(
            give_parts(give.at[s], give_fold.at[s]),
            give_parts(given.at[s], given_fold.at[s]),
            give_send.at[s],
            give_recv.at[s],
            terms_group(s),
        )

    def order(i):
        return lax.rem(2 * i, FIELDS) + lax.div(i, 2)

    def pair_weights(s):
        weights = []
        for f in range(FIELDS):
            g = 2 * (f % 2) + f // 2
            above = visit_fold[s, MASKS, FIELDS + g : FIELDS + g + 1, :]
            same = visit_fold[s, MASKS, g : g + 1, :]
            mine = own_fold[MASKS, FIELDS + f : FIELDS + f + 1, :]
            row = jnp.where(s == 0, same, jnp.where(even, above, mine))
            weights.append(jnp.broadcast_to(row, (8, 128)))
        return weights

    def third(s):
        weights = pair_weights(s)
        leaving = give_copies(s)

        def leave(which):
            for part in which:
                leaving[part].start()

        def gather_band(c, begin, end):
            def gather(tile, j):
                chi = visit[s, tile, first_band[c], :]
                terms = base[c, tile]
                for a in range(2):
                    value = rho[tile, field_rows[2 * a + c], :] * weights[2 * a + c]
                    total[tile, first_band[a], :] += value * chi
                    terms = terms + value * own[tile, first_band[a], :]
                give[s, c, tile] = terms

            tile_loop(begin, end, gather)

        def one_row(i, carry):
            t = jnp.where(i == FIELDS, FIELDS, order(jnp.minimum(i, FIELDS - 1)))

            @pl.when(t < FIELDS)
            def _():
                wait_part(1, s, t)

            @pl.when(t == FIELDS)
            def _():
                wait_fold(1, s)

                def unfold(q, carry):
                    for k in range(OWN_TILES):
                        from_row = pl.multiple_of(q * LAST + k % 3 * 8, 8)
                        value = field_fold[s, pl.ds(from_row, 8), :]
                        value = pltpu.roll(value, FIELDS, 0) if k > 2 else value
                        to_row = pl.multiple_of((q * OWN_TILES + k) * 8, 8)
                        field[s, FIELDS, pl.ds(to_row, 8), :] = value
                    return carry

                lax.fori_loop(0, PEERS, unfold, 0)

            def source(tile):
                if tile == TAIL_TILE:
                    return field_tail[s, row_of(t), :]
                return field[s, t, tile * 8 : tile * 8 + 8, :]

            def load(slot):
                return take(source, slot * NG)

            def save(part, b, value):
                work[place(part, b), :] = value

            finish72_adjoint(load, save)
            along_z(256)

            def target(tile, lanes, piece):
                rho[tile, row_of(t), lanes] = piece

            for b in range(9):
                values = dft8_adjoint([work2[place(part, b), :] for part in range(8)])
                for a, value in enumerate(values):
                    put(target, point72(a, b) * NG, value)

            @pl.when((s == 1) & even & (i == 1))
            def _():
                for copy in give_copies(0):
                    copy.wait_recv()

                def join(tile, carry):
                    for band in range(2):
                        base[band, tile] = given[0, band, tile]
                    return carry

                lax.fori_loop(0, TILES, join, 0)
                base_fold[...] = given_fold[0]

            @pl.when(i == 1)
            def _():
                gather_band(0, 0, TILES)
                leave([0])

            @pl.when(i == 3)
            def _():
                for q, (begin, end) in enumerate(QUARTERS):
                    gather_band(1, begin, end)
                    leave([1 + q])

            return carry

        lax.fori_loop(0, FIELDS + 1, one_row, 0)
        last_weight = weights[3]
        for f in range(3):
            last_weight = jnp.where(row_at == f, weights[f], last_weight)

        for q, (begin, end) in enumerate(QUARTERS):

            def gather_last(tile, j, q=q):
                phi, chi = last_planes(s, j, q)
                value = rho[tile, 32:40, :] * last_weight
                stay, leave = value * chi, value * phi
                stay = stay + pltpu.roll(stay, 7, 0)
                leave = leave + pltpu.roll(leave, 6, 0)
                for band in range(2):
                    row = slice(2 * q + band, 2 * q + band + 1)
                    total_fold[j, row, :] += stay[2 * band : 2 * band + 1]
                    give_fold[s, j, row, :] = leave[band : band + 1] + base_fold[j, row, :]

            tile_loop(begin, end, gather_last)
        leave([5])

    def tail_back(s, f, j):
        return remote(
            piece_of(back_tail, s, peer(j)),
            field_piece.at[s, f],
            back_tail_send.at[s, j],
            back_tail_recv.at[s, f],
            pencil=peer(j),
        )

    def send_tail(s):
        for f in range(FIELDS):
            owner = owner_of(s, f)

            @pl.when(me == owner)
            def _(f=f, owner=owner):
                recv_tail[s, rows_of(owner, PIECE), :] = wave_piece[s, f]

            @pl.when(me != owner)
            def _(f=f, owner=owner):
                tail_copy(s, f, lax.rem(owner - me + PEERS, PEERS)).start()

    def turn_tail(s):
        owned = lax.div(me, FIELDS) == s

        @pl.when(owned)
        def _():
            for j in range(1, PEERS):
                tail_copy(s, 0, j).wait_recv()
            parts = [pl.ds(p * PIECE, 8) for p in range(PEERS)] + [pl.ds(8, PEERS, stride=PIECE)]
            block = jnp.concatenate([recv_tail[s, part, :] for part in parts], axis=0)
            spectrum = left(wide[512:592, :], block) * kernel_tail[...]
            result = left(wide[592:672, :], spectrum)
            for i, part in enumerate(parts):
                back_tail[s, part, :] = result[i * 8 : i * 8 + 8, :]
            mine = lax.rem(me, FIELDS)
            for j in range(1, PEERS):
                tail_back(s, mine, j).start()
            field_piece[s, mine] = back_tail[s, pl.ds(pl.multiple_of(me * PIECE, 8), PIECE), :]

    def end_tail(s):
        for f in range(FIELDS):
            owner = owner_of(s, f)

            @pl.when(me != owner)
            def _(f=f, owner=owner):
                tail_copy(s, f, lax.rem(owner - me + PEERS, PEERS)).wait_send()
                tail_back(s, f, 1).wait_recv()

            field_tail[s, field_rows[f], :] = field_piece[s, f, 0:8, :]
            field_tail[s, 32 + f : 33 + f, :] = field_piece[s, f, 8:9, :]

        @pl.when(lax.div(me, FIELDS) == s)
        def _():
            for j in range(1, PEERS):
                tail_back(s, lax.rem(me, FIELDS), j).wait_send()

    def slots(*stages):
        def run(s, carry):
            for stage in stages:
                stage(s)
            return carry

        lax.fori_loop(0, 2, run, 0)

    slots(first, send_tail)
    slots(second, turn_tail)
    slots(end_tail, third)

    def wait_given(which):
        for part in which:
            give_copies(1)[part].wait_recv()

            @pl.when(jnp.logical_not(even))
            def _(part=part):
                give_copies(0)[part].wait_recv()

    for q, (begin, end) in enumerate(QUARTERS):
        wait_given([0, 1] if q == 0 else [1 + q])

        def result(tile, j, width=128):
            lanes = pl.ds(tile * 128, width)
            if width == 128:
                lanes = pl.ds(pl.multiple_of(tile * 128, 128), 128)
            for rows, band in zip(first_band, range(2)):
                near = jnp.where(even, 0.0, given[0, band, tile])
                term = -(total[tile, rows, :] + near + given[1, band, tile])
                mixed[tile, pl.ds(band, 8, stride=2), :] = term
            for plane in range(PLANES - 1):
                piece = mixed[tile, 2 * plane : 2 * plane + 2, 0:width]
                out_ref[plane, :, lanes] = piece

        tile_loop(begin, min(end, TAIL_TILE), result)
        if end > TAIL_TILE:
            result(TAIL_TILE, 0, MERGED - TAIL)
    wait_given([5])
    for q, (begin, end) in enumerate(QUARTERS):

        def last_result(tile, j, q=q, width=128):
            lanes = pl.ds(tile * 128, width)
            if width == 128:
                lanes = pl.ds(pl.multiple_of(tile * 128, 128), 128)
            rows = slice(2 * q, 2 * q + 2)
            near = jnp.where(even, 0.0, given_fold[0, j, rows, :])
            term = total_fold[j, rows, :] + near + given_fold[1, j, rows, :]
            out_ref[PLANES - 1, :, lanes] = -term[:, 0:width]

        tile_loop(begin, min(end, TAIL_TILE), last_result)
        if end > TAIL_TILE:
            last_result(TAIL_TILE, TAIL_TILE - begin, width=MERGED - TAIL)

    for copy in near_sends():
        copy.wait_send()

    @pl.when(jnp.logical_not(even))
    def _():
        for copy in far_sends() + passes():
            copy.wait_send()

    for s in range(2):
        for copy in give_copies(s):
            copy.wait_send()
    for phase in range(2):
        for s in range(2):
            end_blocks(phase, s)


def body(bands, orbitals, pair_mask):
    hbm = pl.BlockSpec(memory_space=pltpu.HBM)
    smem = pl.BlockSpec(memory_space=pltpu.SMEM)
    consts = [jnp.asarray(table) for table in tables()]
    dma = pltpu.SemaphoreType.DMA

    def buffer(*shape):
        return pltpu.VMEM(shape, jnp.float32)

    out = pl.pallas_call(
        functools.partial(kernel, bands),
        out_shape=jax.ShapeDtypeStruct((PLANES, 2, MERGED), jnp.float32),
        in_specs=[smem] + [hbm] * (1 + len(consts)),
        out_specs=pl.BlockSpec(memory_space=pltpu.VMEM),
        scratch_shapes=[
            buffer(PLANES, 2, MERGED),
            pltpu.VMEM(consts[0].shape, jnp.bfloat16),
            buffer(*consts[1].shape),
            buffer(*consts[2].shape),
            buffer(TILES, 16, 128),
            buffer(TILES, 16, 128),
            buffer(FOLD + 1, 8, 128),
            buffer(2, TILES, 16, 128),
            buffer(2, FOLD + 1, 8, 128),
            buffer(TILES, ROWS, 128),
            buffer(NG * 8, 128),
            buffer(NG * 8, 128),
            buffer(2, FIELDS + 1, PEERS * PART, 128),
            buffer(2, PEERS * LAST, 128),
            buffer(2, ROWS, 128),
            buffer(2, FIELDS, PIECE, 128),
            buffer(2, FIELDS, PEERS * PART, 128),
            buffer(2, PEERS * LAST, 128),
            buffer(2, PEERS * PIECE, 128),
            buffer(2, FIELDS, PEERS * PART, 128),
            buffer(2, PEERS * LAST, 128),
            buffer(2, PEERS * PIECE, 128),
            buffer(2, FIELDS + 1, PEERS * PART, 128),
            buffer(2, PEERS * LAST, 128),
            buffer(2, ROWS, 128),
            buffer(2, FIELDS, PIECE, 128),
            buffer(NG, OWN),
            buffer(NG, 128),
            buffer(TILES, 16, 128),
            buffer(FOLD + 1, 8, 128),
            buffer(2, TILES, 8, 128),
            buffer(FOLD + 1, 8, 128),
            buffer(2, 2, TILES, 8, 128),
            buffer(2, FOLD + 1, 8, 128),
            buffer(2, 2, TILES, 8, 128),
            buffer(2, FOLD + 1, 8, 128),
            dma((2, 6)),
            dma((2, 6)),
            dma((6,)),
            dma((2, 6)),
            dma((2, 6)),
            dma((2, 2)),
            dma((2, 2, FIELDS)),
            dma((2, 2)),
            dma((2, 2)),
            dma((2, FIELDS)),
            dma((2, PEERS)),
            dma((2, PEERS)),
            dma((2, FIELDS)),
            dma((4,)),
        ],
        compiler_params=pltpu.CompilerParams(
            collective_id=0, has_side_effects=True, vmem_limit_bytes=64 * 1024 * 1024 - 65536
        ),
    )(pair_mask, orbitals.transpose(1, 0, 2), *consts)
    return out.transpose(1, 0, 2)


def solution(mesh):
    return jax.shard_map(
        functools.partial(body, mesh.shape["band"]),
        mesh=mesh,
        in_specs=(P("band", "pencil", None), P("band", None, None, None)),
        out_specs=P("band", "pencil", None),
        check_vma=False,
    )
```

```python
import functools
import math

import jax
import jax.numpy as jnp
import ml_dtypes
import numpy as np
from jax import lax
from jax.experimental import pallas as pl
from jax.experimental.pallas import tpu as pltpu
from jax.sharding import PartitionSpec as P

MESH = pl.DeviceIdType.MESH
NG = 72
PLANES = 9
PEERS = 8
FIELDS = 4
ROWS = 40
PART = 40
LAST = 24
MERGED = NG * NG
WIDTH = 5248
OWN = 640
TAIL = PEERS * OWN
PIECE = 16
FOLD = 11
MASKS = FOLD
QUARTERS = [(q * FOLD, min((q + 1) * FOLD, 41)) for q in range(4)]
TILES = WIDTH // 128
OWN_TILES = OWN // 128
TAIL_TILE = TILES - 1
coulomb_scale = 20.0
screening = 0.25
HALF = math.sqrt(0.5)


def dft8(x):
    a = [x[j] + x[j + 4] for j in range(4)]
    b = [x[j] - x[j + 4] for j in range(4)]
    e, o = a[0] + a[2], a[1] + a[3]
    u, v = HALF * (b[1] - b[3]), HALF * (b[1] + b[3])
    return [e + o, e - o, b[0] + u, v + b[2], a[0] - a[2], a[1] - a[3], b[0] - u, v - b[2]]


def dft8_adjoint(c):
    p, q = c[0] + c[1], c[0] - c[1]
    a = [p + c[4], q + c[5], p - c[4], q - c[5]]
    d, s = HALF * (c[2] - c[6]), HALF * (c[3] + c[7])
    b = [c[2] + c[6], d + s, c[3] - c[7], s - d]
    return [a[j] + b[j] for j in range(4)] + [a[j] - b[j] for j in range(4)]


def cos9(n):
    return math.cos(2.0 * math.pi * (n % 9) / 9)


def sin9(n):
    return math.sin(2.0 * math.pi * (n % 9) / 9)


def weighted(values, factors):
    total = values[0] * factors[0]
    for value, factor in zip(values[1:], factors[1:]):
        total = total + value * factor
    return total


def dft9(x):
    e = [x[n] + x[9 - n] for n in range(1, 5)]
    o = [x[n] - x[9 - n] for n in range(1, 5)]
    third = e[0] + e[1] + e[3]
    cosines = [x[0] + third + e[2]]
    sines = [None]
    for k in range(1, 5):
        if k == 3:
            cosines.append(x[0] + e[2] - 0.5 * third)
            sines.append(sin9(3) * (o[0] - o[1] + o[3]))
        else:
            cosines.append(x[0] + weighted(e, [cos9(k * n) for n in range(1, 5)]))
            sines.append(weighted(o, [sin9(k * n) for n in range(1, 5)]))
    return cosines, sines


def dft9_adjoint(cosines, sines):
    c, s = cosines, sines
    out = [None] * 9
    out[0] = c[0] + ((c[1] + c[2]) + (c[3] + c[4]))
    for n in range(1, 5):
        if n == 3:
            even = c[0] + c[3] - 0.5 * (c[1] + c[2] + c[4])
            odd = sin9(3) * (s[1] - s[2] + s[4])
        else:
            even = c[0] + weighted(c[1:], [cos9(k * n) for k in range(1, 5)])
            odd = weighted(s[1:], [sin9(k * n) for k in range(1, 5)])
        out[n] = even + odd
        out[9 - n] = even - odd
    return out


def finish72(load, save):
    for part in (0, 1):
        cosines, sines = dft9([load(part, b) for b in range(9)])
        base = part * 9
        save(base, cosines[0])
        for k in range(1, 5):
            save(base + 2 * k - 1, cosines[k])
            save(base + 2 * k, sines[k])
    for k8 in range(3):
        base = 18 + 18 * k8
        cc, cs = dft9([load(2 + 2 * k8, b) for b in range(9)])
        sc, ss = dft9([load(3 + 2 * k8, b) for b in range(9)])
        save(base, cc[0])
        save(base + 1, sc[0])
        for k in range(1, 5):
            at = base + 4 * k - 2
            save(at, cc[k] - ss[k])
            save(at + 1, cc[k] + ss[k])
            save(at + 2, sc[k] + cs[k])
            save(at + 3, sc[k] - cs[k])


def finish72_adjoint(load, save):
    for part in (0, 1):
        base = part * 9
        cosines = [load(base)] + [load(base + 2 * k - 1) for k in range(1, 5)]
        sines = [None] + [load(base + 2 * k) for k in range(1, 5)]
        for b, value in enumerate(dft9_adjoint(cosines, sines)):
            save(part, b, value)
    for k8 in range(3):
        base = 18 + 18 * k8
        cc, sc, cs, ss = [load(base)], [load(base + 1)], [None], [None]
        for k in range(1, 5):
            at = base + 4 * k - 2
            plus, minus, sine_plus, sine_minus = [load(at + i) for i in range(4)]
            cc.append(plus + minus)
            ss.append(minus - plus)
            sc.append(sine_plus + sine_minus)
            cs.append(sine_plus - sine_minus)
        for b, value in enumerate(dft9_adjoint(cc, cs)):
            save(2 + 2 * k8, b, value)
        for b, value in enumerate(dft9_adjoint(sc, ss)):
            save(3 + 2 * k8, b, value)


def point72(a, b):
    return (9 * a + 8 * b) % NG


def split(table):
    high = table.astype(ml_dtypes.bfloat16).astype(np.float64)
    return high, (table - high).astype(ml_dtypes.bfloat16).astype(np.float64)


def from_left(table):
    high, low = split(table)
    wide = np.zeros((80, 256))
    wide[:NG, : 3 * NG] = np.concatenate([high, high, low], axis=1)
    return wide


def from_right(table):
    high, low = split(table)
    return np.block([[high, low], [high, np.zeros_like(low)]])


@functools.cache
def tables():
    at = np.arange(NG)
    basis, freq = [np.full(NG, 1.0)], [0]
    for k in range(1, NG // 2):
        basis += [np.cos(2 * np.pi * k * at / NG), np.sin(2 * np.pi * k * at / NG)]
        freq += [k, k]
    basis.append(np.cos(np.pi * at))
    freq.append(NG // 2)
    basis = np.array(basis)
    basis /= np.sqrt((basis * basis).sum(1, keepdims=True))
    freq = np.array(freq, np.float64)
    eye = np.eye(NG)
    parts = [dft8([eye[point72(a, b)] for a in range(8)]) for b in range(9)]
    slots = [None] * NG
    finish72(lambda part, b: parts[b][part], slots.__setitem__)
    slots = np.array(slots)
    norm = (slots * slots).sum(1)
    spectrum = np.abs(np.fft.fft(slots, axis=1))[:, : NG // 2 + 1]
    freq_y = spectrum.argmax(1).astype(np.float64)
    along_z = np.zeros((128, 128))
    along_z[:NG, :NG] = basis.T
    along_x = basis.reshape(NG, PEERS, PLANES)
    along_x = np.concatenate([along_x[:, :, :8].reshape(NG, -1), along_x[:, :, 8]], axis=1)
    column = np.zeros((8, WIDTH), np.float32)
    column[0, :MERGED] = (freq_y[:, None] ** 2 + freq[None, :] ** 2).reshape(-1)
    column[1, :MERGED] = np.repeat(1.0 / norm, NG)
    freq_x = np.broadcast_to((freq**2)[:, None], (NG, 128)).astype(np.float32)
    wide = np.concatenate(
        [from_right(along_z), from_right(along_z.T), from_left(along_x), from_left(along_x.T)]
    )
    return wide.astype(ml_dtypes.bfloat16), column, freq_x


def take(load, start):
    tile, lane = divmod(start, 128)
    value = load(tile)
    if lane == 0:
        return value
    if lane + NG > 128:
        at = lax.broadcasted_iota(jnp.int32, value.shape, 1)
        value = jnp.where(at >= lane, value, load(tile + 1))
    return pltpu.roll(value, 128 - lane, 1)


def put(store, start, value):
    tile, lane = divmod(start, 128)
    if lane:
        value = pltpu.roll(value, lane, 1)
    end = min(lane + NG, 128)
    store(tile, slice(lane, end), value[:, lane:end])
    if lane + NG > 128:
        store(tile + 1, slice(0, lane + NG - 128), value[:, : lane + NG - 128])


def matmul(a, b):
    return jnp.dot(a, b, preferred_element_type=jnp.float32)


def halves(x):
    high = x.astype(jnp.bfloat16)
    return high, (x - high.astype(jnp.float32)).astype(jnp.bfloat16)


def left(table, x):
    high, low = [part.astype(jnp.float32) for part in halves(x)]
    zeros = jnp.zeros((8, x.shape[1]), jnp.float32)
    operand = jnp.concatenate([high, low, high, zeros], axis=0).astype(jnp.bfloat16)
    return matmul(table[:, 0 : operand.shape[0]], operand)[0:NG]


def kernel(
    bands,
    mask_ref,
    bands_hbm,
    wide_hbm,
    column_hbm,
    freq_hbm,
    out_ref,
    bands_ref,
    wide,
    column_ref,
    freq_ref,
    mixed,
    own,
    own_fold,
    visit,
    visit_fold,
    rho,
    work,
    work2,
    wave,
    wave_fold,
    wave_tail,
    wave_piece,
    recv,
    recv_fold,
    recv_tail,
    back,
    back_fold,
    back_tail,
    field,
    field_fold,
    field_tail,
    field_piece,
    kernel_table,
    kernel_tail,
    total,
    total_fold,
    base,
    base_fold,
    give,
    give_fold,
    given,
    given_fold,
    visit_send,
    visit_recv,
    pass_send,
    give_send,
    give_recv,
    part_send,
    part_recv,
    fold_send,
    fold_recv,
    tail_send,
    tail_recv,
    back_tail_send,
    back_tail_recv,
    load_sem,
):
    me = lax.axis_index("pencil")
    group = lax.axis_index("band")
    me_x, me_y = lax.div(me, 4), lax.rem(me, 4)

    loads = [
        pltpu.make_async_copy(src, dst, load_sem.at[i])
        for i, (src, dst) in enumerate(
            [
                (bands_hbm, bands_ref),
                (wide_hbm, wide),
                (column_hbm, column_ref),
                (freq_hbm, freq_ref),
            ]
        )
    ]
    for load in loads:
        load.start()

    def peer(j):
        return lax.rem(me + j, PEERS)

    def at(dx, dy):
        return lax.rem(me_x + dx, 2) * 4 + lax.rem(me_y + dy + 4, 4)

    def group_at(j):
        return lax.rem(group + j + bands, bands)

    barrier = pltpu.get_barrier_semaphore()
    for j in range(1, PEERS):
        pl.semaphore_signal(barrier, inc=1, device_id={"pencil": peer(j)}, device_id_type=MESH)
    for j in (-2, -1, 1, 2):
        pl.semaphore_signal(barrier, inc=1, device_id={"band": group_at(j)}, device_id_type=MESH)
    def remote(src, dst, send, recv, **device):
        return pltpu.make_async_remote_copy(
            src_ref=src,
            dst_ref=dst,
            send_sem=send,
            recv_sem=recv,
            device_id=device,
            device_id_type=MESH,
        )

    even = lax.rem(group, 2) == 0

    def terms_group(s):
        near = jnp.where(even, group_at(1), group_at(-1))
        return jnp.where(s == 0, near, jnp.where(even, group_at(2), group_at(-2)))

    def parts(main, fold):
        return [
            *(main.at[pl.ds(begin, end - begin)] for begin, end in QUARTERS),
            fold,
        ]

    def block_copies(src, dst, send, recv, to):
        return [
            remote(one, two, send.at[q], recv.at[q], band=to)
            for q, (one, two) in enumerate(zip(src, dst))
        ]

    def block_parts(main, fold):
        first = [main.at[pl.ds(begin, end - begin), pl.ds(0, 8)] for begin, end in QUARTERS]
        return [*first, fold, main.at[:, pl.ds(8, 8)]]

    def visit_at(s):
        return block_parts(visit.at[s], visit_fold.at[s])

    own_parts = block_parts(own, own_fold)

    def give_parts(main, fold):
        return [main.at[0], *parts(main.at[1], fold)]

    def visit_copies(s, src, send, to):
        return block_copies(src, visit_at(s), send, visit_recv.at[s], to)

    def near_sends():
        return visit_copies(0, own_parts, visit_send.at[0], group_at(-1))

    def far_sends():
        return visit_copies(1, own_parts, visit_send.at[1], group_at(2))

    def passes():
        return visit_copies(1, visit_at(0), pass_send, group_at(-1))

    loads[0].wait()
    def take_tile(tile, j, q, width):
        lanes = pl.ds(tile * 128, width)
        if width == 128:
            lanes = pl.ds(pl.multiple_of(tile * 128, 128), 128)
        live = slice(0, width)
        for plane in range(PLANES - 1):
            mixed[tile, 2 * plane : 2 * plane + 2, live] = bands_ref[plane, :, lanes]
        for band in range(2):
            own[tile, band * 8 : band * 8 + 8, :] = mixed[tile, pl.ds(band, 8, stride=2), :]
        own_fold[j, 2 * q : 2 * q + 2, live] = bands_ref[PLANES - 1, :, lanes]

    def tile_loop(begin, end, step):
        def run(j, carry):
            step(begin + j, j)
            return carry

        lax.fori_loop(0, end - begin, run, 0, unroll=True)

    mixed[TAIL_TILE] = jnp.zeros((16, 128), jnp.float32)
    own_fold[TAIL_TILE % FOLD, 6:8, :] = jnp.zeros((2, 128), jnp.float32)

    def own_mask(s, f):
        return mask_ref[0, s, f // 2, f % 2].astype(jnp.float32)

    for m in range(2 * FIELDS):
        value = own_mask(m // FIELDS, m % FIELDS)
        own_fold[MASKS, m : m + 1, :] = jnp.zeros((1, 128), jnp.float32) + value
    pl.semaphore_wait(barrier, PEERS - 1 + 4)
    near, far = near_sends(), far_sends()

    def send_own(part):
        near[part].start()

        @pl.when(jnp.logical_not(even))
        def _():
            far[part].start()

    for q, (begin, end) in enumerate(QUARTERS):
        tile_loop(begin, min(end, TAIL_TILE), lambda tile, j, q=q: take_tile(tile, j, q, 128))
        if end > TAIL_TILE:
            take_tile(TAIL_TILE, TAIL_TILE % FOLD, q, MERGED - TAIL)
        send_own(q)
    send_own(4)
    send_own(5)

    def kernel_columns(start, width):
        squared = column_ref[0:1, pl.ds(start, width)]
        scale = column_ref[1:2, pl.ds(start, width)]
        return coulomb_scale / (freq_ref[:, 0:1] + squared + screening) * scale

    for load in loads[1:]:
        load.wait()
    kernel_table[...] = kernel_columns(pl.multiple_of(me * OWN, 128), OWN)
    kernel_tail[...] = kernel_columns(TAIL, 128)
    wave_tail[...] = jnp.zeros((2, ROWS, 128), jnp.float32)
    total_fold[...] = jnp.zeros((FOLD + 1, 8, 128), jnp.float32)
    base_fold[...] = jnp.zeros((FOLD + 1, 8, 128), jnp.float32)

    def clear(tile, carry):
        total[tile] = jnp.zeros((16, 128), jnp.float32)
        base[:, tile] = jnp.zeros((2, 8, 128), jnp.float32)
        return carry

    lax.fori_loop(0, TILES, clear, 0)
    for s in range(2):
        for p in range(PEERS):
            back_fold[s, (p + 1) * LAST - 8 : (p + 1) * LAST, :] = jnp.zeros((8, 128), jnp.float32)
            back_tail[s, (p + 1) * PIECE - 8 : (p + 1) * PIECE, :] = jnp.zeros((8, 128), jnp.float32)
        field_tail[s, 32:40, :] = jnp.zeros((8, 128), jnp.float32)
        for f in range(FIELDS):
            wave_piece[s, f, 8:16, :] = jnp.zeros((8, 128), jnp.float32)

    first_band = [slice(band * 8, band * 8 + 8) for band in range(2)]
    field_rows = [slice(f * 8, f * 8 + 8) for f in range(FIELDS)]
    row_at = lax.broadcasted_iota(jnp.int32, (8, 128), 0)
    resident_one = lax.rem(lax.div(row_at, 2), 2) == 1
    visitor_one = lax.rem(row_at, 2) == 1

    def last_planes(s, j, q):
        a = [own_fold[j, 2 * q + band : 2 * q + band + 1, :] for band in range(2)]
        c = [visit_fold[s, j, 2 * q + band : 2 * q + band + 1, :] for band in range(2)]
        wide_a = [jnp.broadcast_to(row, (8, 128)) for row in a]
        wide_c = [jnp.broadcast_to(row, (8, 128)) for row in c]
        return (
            jnp.where(resident_one, wide_a[1], wide_a[0]),
            jnp.where(visitor_one, wide_c[1], wide_c[0]),
        )

    def along_z(start):
        both = matmul(jnp.concatenate(halves(work[...]), axis=1), wide[start : start + 256, :])
        work2[...] = both[:, :128] + both[:, 128:]

    def place(part, b):
        return slice((part * 9 + b) * 8, (part * 9 + b) * 8 + 8)

    def row_of(t):
        return pl.ds(pl.multiple_of(t * 8, 8), 8)

    def first(s):
        arriving = visit_copies(s, own_parts, visit_send.at[0], group_at(1))
        passing = passes()

        def arrive(part):
            arriving[part].wait_recv()

            @pl.when((s == 0) & jnp.logical_not(even))
            def _():
                passing[part].start()

        for part in range(5):
            arrive(part)

        def one_row(i, carry):
            t = jnp.where(i == 0, FIELDS, order(jnp.maximum(i - 1, 0)))

            @pl.when(i == 3)
            def _():
                arrive(5)

            @pl.when(i > 0)
            def _():
                resident, visitor = row_of(lax.div(t, 2)), row_of(lax.rem(t, 2))
                for tile in range(TILES):
                    rho[tile, row_of(t), :] = own[tile, resident, :] * visit[s, tile, visitor, :]

            @pl.when(i == 0)
            def _():
                for q, (begin, end) in enumerate(QUARTERS):

                    def products(tile, j, q=q):
                        phi, chi = last_planes(s, j, q)
                        rho[tile, 32:40, :] = phi * chi

                    tile_loop(begin, end, products)

            for b in range(9):
                starts = [point72(a, b) * NG for a in range(8)]
                values = [take(lambda tile: rho[tile, row_of(t), :], at) for at in starts]
                for part, value in enumerate(dft8(values)):
                    work[place(part, b), :] = value
            along_z(0)

            def load(part, b):
                return work2[place(part, b), :]

            def target(tile, lanes, piece):
                if tile == TAIL_TILE:
                    wave_tail[s, row_of(t), lanes] = piece
                else:
                    wave[s, t, tile * 8 : tile * 8 + 8, lanes] = piece

            def save(slot, value):
                put(target, slot * NG, value)

            finish72(load, save)

            @pl.when(i == 0)
            def _():
                upper = lax.broadcasted_iota(jnp.int32, (8, 128), 0) < FIELDS

                def fold(q, carry):
                    for k in range(3):
                        at_row = pl.multiple_of((q * OWN_TILES + k) * 8, 8)
                        piece = wave[s, FIELDS, pl.ds(at_row, 8), :]
                        if k < 2:
                            below = wave[s, FIELDS, pl.ds(at_row + 24, 8), :]
                            piece = jnp.where(upper, piece, below)
                        to_row = pl.multiple_of(q * LAST + k * 8, 8)
                        wave_fold[s, pl.ds(to_row, 8), :] = piece
                    return carry

                lax.fori_loop(0, PEERS, fold, 0)
                send_fold(0, s)

            @pl.when(i > 0)
            def _():
                send_part(0, s, t)

            return carry

        lax.fori_loop(0, FIELDS + 1, one_row, 0)
        for f in range(FIELDS):
            wave_piece[s, f, 0:8, :] = wave_tail[s, field_rows[f], :]
            wave_piece[s, f, 8:9, :] = wave_tail[s, 32 + f : 33 + f, :]

    part_refs = ((wave, recv), (back, field))
    fold_refs = ((wave_fold, recv_fold), (back_fold, field_fold))
    straight = [(1, 2), (0, 2), (1, 1), (1, 3), (0, 1), (0, 3), (1, 0)]

    def rows_of(index, rows):
        return pl.ds(pl.multiple_of(index * rows, 8), rows)

    def send_part(phase, s, f):
        src, dst = part_refs[phase]
        for dx, dy in straight:
            to = at(dx, dy)
            remote(
                src.at[s, f, rows_of(to, PART)],
                dst.at[s, f, rows_of(me, PART)],
                part_send.at[phase, s],
                part_recv.at[phase, s, f],
                pencil=to,
            ).start()
        dst[s, f, rows_of(me, PART), :] = src[s, f, rows_of(me, PART), :]

    def send_fold(phase, s):
        src, dst = fold_refs[phase]
        for dx, dy in straight:
            to = at(dx, dy)
            remote(
                src.at[s, rows_of(to, LAST)],
                dst.at[s, rows_of(me, LAST)],
                fold_send.at[phase, s],
                fold_recv.at[phase, s],
                pencil=to,
            ).start()
        dst[s, rows_of(me, LAST), :] = src[s, rows_of(me, LAST), :]

    def drain(view, sem):
        pltpu.make_async_copy(view, view, sem).wait()

    def wait_part(phase, s, f):
        drain(part_refs[phase][1].at[s, f, pl.ds(0, 7 * PART)], part_recv.at[phase, s, f])

    def wait_fold(phase, s):
        drain(fold_refs[phase][1].at[s, pl.ds(0, 7 * LAST)], fold_recv.at[phase, s])

    def end_blocks(phase, s):
        parts = part_refs[phase][0].at[s, pl.ds(0, FIELDS), pl.ds(0, 7 * PART)]
        drain(parts, part_send.at[phase, s])
        drain(fold_refs[phase][0].at[s, pl.ds(0, 7 * LAST)], fold_send.at[phase, s])

    def piece_of(ref, s, index):
        return ref.at[s, pl.ds(pl.multiple_of(index * PIECE, 8), PIECE), :]

    def owner_of(s, f):
        return FIELDS * s + f

    def tail_copy(s, f, distance):
        return remote(
            wave_piece.at[s, f],
            piece_of(recv_tail, s, me),
            tail_send.at[s, f],
            tail_recv.at[s, distance],
            pencil=owner_of(s, f),
        )

    def second(s):
        wait_fold(0, s)

        def last_rows(f, tile):
            return pl.ds(tile % 3 * 8 + FIELDS * (tile // 3) + f, PEERS, stride=LAST)

        def one_field(i, carry):
            f = order(i)
            wait_part(0, s, f)
            columns = []
            for tile in range(OWN_TILES):
                starts = [p * PART + tile * 8 for p in range(PEERS)]
                rows = [recv[s, f, start : start + 8, :] for start in starts]
                rows.append(recv_fold[s, last_rows(f, tile), :])
                columns.append(jnp.concatenate(rows, axis=0))
            spectrum = left(wide[512:592, :], jnp.concatenate(columns, axis=1))
            result = left(wide[592:672, :], spectrum * kernel_table[...])
            for tile in range(OWN_TILES):
                lanes = slice(tile * 128, tile * 128 + 128)
                for p in range(PEERS):
                    start = p * PART + tile * 8
                    back[s, f, start : start + 8, :] = result[p * 8 : p * 8 + 8, lanes]
                back_fold[s, last_rows(f, tile), :] = result[64:72, lanes]
            send_part(1, s, f)
            return carry

        lax.fori_loop(0, FIELDS, one_field, 0)
        send_fold(1, s)

    def give_copies(s):
        return block_copies(
            give_parts(give.at[s], give_fold.at[s]),
            give_parts(given.at[s], given_fold.at[s]),
            give_send.at[s],
            give_recv.at[s],
            terms_group(s),
        )

    def order(i):
        return lax.rem(2 * i, FIELDS) + lax.div(i, 2)

    def pair_weights(s):
        weights = []
        for f in range(FIELDS):
            g = 2 * (f % 2) + f // 2
            above = visit_fold[s, MASKS, FIELDS + g : FIELDS + g + 1, :]
            same = visit_fold[s, MASKS, g : g + 1, :]
            mine = own_fold[MASKS, FIELDS + f : FIELDS + f + 1, :]
            row = jnp.where(s == 0, same, jnp.where(even, above, mine))
            weights.append(jnp.broadcast_to(row, (8, 128)))
        return weights

    def third(s):
        weights = pair_weights(s)
        leaving = give_copies(s)

        def leave(which):
            for part in which:
                leaving[part].start()

        def gather_band(c, begin, end):
            def gather(tile, j):
                chi = visit[s, tile, first_band[c], :]
                terms = base[c, tile]
                for a in range(2):
                    value = rho[tile, field_rows[2 * a + c], :] * weights[2 * a + c]
                    total[tile, first_band[a], :] += value * chi
                    terms = terms + value * own[tile, first_band[a], :]
                give[s, c, tile] = terms

            tile_loop(begin, end, gather)

        def one_row(i, carry):
            t = jnp.where(i == FIELDS, FIELDS, order(jnp.minimum(i, FIELDS - 1)))

            @pl.when(t < FIELDS)
            def _():
                wait_part(1, s, t)

            @pl.when(t == FIELDS)
            def _():
                wait_fold(1, s)

                def unfold(q, carry):
                    for k in range(OWN_TILES):
                        from_row = pl.multiple_of(q * LAST + k % 3 * 8, 8)
                        value = field_fold[s, pl.ds(from_row, 8), :]
                        value = pltpu.roll(value, FIELDS, 0) if k > 2 else value
                        to_row = pl.multiple_of((q * OWN_TILES + k) * 8, 8)
                        field[s, FIELDS, pl.ds(to_row, 8), :] = value
                    return carry

                lax.fori_loop(0, PEERS, unfold, 0)

            def source(tile):
                if tile == TAIL_TILE:
                    return field_tail[s, row_of(t), :]
                return field[s, t, tile * 8 : tile * 8 + 8, :]

            def load(slot):
                return take(source, slot * NG)

            def save(part, b, value):
                work[place(part, b), :] = value

            finish72_adjoint(load, save)
            along_z(256)

            def target(tile, lanes, piece):
                rho[tile, row_of(t), lanes] = piece

            for b in range(9):
                values = dft8_adjoint([work2[place(part, b), :] for part in range(8)])
                for a, value in enumerate(values):
                    put(target, point72(a, b) * NG, value)

            def join(band, which):
                @pl.when((s == 1) & even)
                def _():
                    for part in which:
                        give_copies(0)[part].wait_recv()
                    base[band] = given[0, band]

            @pl.when(i == 1)
            def _():
                join(0, [0])
                gather_band(0, 0, TILES)
                leave([0])

            @pl.when(i == 3)
            def _():
                join(1, [1, 2, 3, 4])
                for q, (begin, end) in enumerate(QUARTERS):
                    gather_band(1, begin, end)
                    leave([1 + q])

            return carry

        lax.fori_loop(0, FIELDS + 1, one_row, 0)

        @pl.when((s == 1) & even)
        def _():
            give_copies(0)[5].wait_recv()
            base_fold[...] = given_fold[0]

        last_weight = weights[3]
        for f in range(3):
            last_weight = jnp.where(row_at == f, weights[f], last_weight)

        for q, (begin, end) in enumerate(QUARTERS):

            def gather_last(tile, j, q=q):
                phi, chi = last_planes(s, j, q)
                value = rho[tile, 32:40, :] * last_weight
                stay, leave = value * chi, value * phi
                stay = stay + pltpu.roll(stay, 7, 0)
                leave = leave + pltpu.roll(leave, 6, 0)
                for band in range(2):
                    row = slice(2 * q + band, 2 * q + band + 1)
                    total_fold[j, row, :] += stay[2 * band : 2 * band + 1]
                    give_fold[s, j, row, :] = leave[band : band + 1] + base_fold[j, row, :]

            tile_loop(begin, end, gather_last)
        leave([5])

    def tail_back(s, f, j):
        return remote(
            piece_of(back_tail, s, peer(j)),
            field_piece.at[s, f],
            back_tail_send.at[s, j],
            back_tail_recv.at[s, f],
            pencil=peer(j),
        )

    def send_tail(s):
        for f in range(FIELDS):
            owner = owner_of(s, f)

            @pl.when(me == owner)
            def _(f=f, owner=owner):
                recv_tail[s, rows_of(owner, PIECE), :] = wave_piece[s, f]

            @pl.when(me != owner)
            def _(f=f, owner=owner):
                tail_copy(s, f, lax.rem(owner - me + PEERS, PEERS)).start()

    def turn_tail(s):
        owned = lax.div(me, FIELDS) == s

        @pl.when(owned)
        def _():
            for j in range(1, PEERS):
                tail_copy(s, 0, j).wait_recv()
            parts = [pl.ds(p * PIECE, 8) for p in range(PEERS)] + [pl.ds(8, PEERS, stride=PIECE)]
            block = jnp.concatenate([recv_tail[s, part, :] for part in parts], axis=0)
            spectrum = left(wide[512:592, :], block) * kernel_tail[...]
            result = left(wide[592:672, :], spectrum)
            for i, part in enumerate(parts):
                back_tail[s, part, :] = result[i * 8 : i * 8 + 8, :]
            mine = lax.rem(me, FIELDS)
            for j in range(1, PEERS):
                tail_back(s, mine, j).start()
            field_piece[s, mine] = back_tail[s, pl.ds(pl.multiple_of(me * PIECE, 8), PIECE), :]

    def end_tail(s):
        for f in range(FIELDS):
            owner = owner_of(s, f)

            @pl.when(me != owner)
            def _(f=f, owner=owner):
                tail_copy(s, f, lax.rem(owner - me + PEERS, PEERS)).wait_send()
                tail_back(s, f, 1).wait_recv()

            field_tail[s, field_rows[f], :] = field_piece[s, f, 0:8, :]
            field_tail[s, 32 + f : 33 + f, :] = field_piece[s, f, 8:9, :]

        @pl.when(lax.div(me, FIELDS) == s)
        def _():
            for j in range(1, PEERS):
                tail_back(s, lax.rem(me, FIELDS), j).wait_send()

    def slots(*stages):
        def run(s, carry):
            for stage in stages:
                stage(s)
            return carry

        lax.fori_loop(0, 2, run, 0)

    slots(first, send_tail)
    slots(second, turn_tail)
    slots(end_tail, third)

    def wait_given(which):
        for part in which:
            give_copies(1)[part].wait_recv()

            @pl.when(jnp.logical_not(even))
            def _(part=part):
                give_copies(0)[part].wait_recv()

    for q, (begin, end) in enumerate(QUARTERS):
        wait_given([0, 1] if q == 0 else [1 + q])

        def result(tile, j, width=128):
            lanes = pl.ds(tile * 128, width)
            if width == 128:
                lanes = pl.ds(pl.multiple_of(tile * 128, 128), 128)
            for rows, band in zip(first_band, range(2)):
                near = jnp.where(even, 0.0, given[0, band, tile])
                term = -(total[tile, rows, :] + near + given[1, band, tile])
                mixed[tile, pl.ds(band, 8, stride=2), :] = term
            for plane in range(PLANES - 1):
                piece = mixed[tile, 2 * plane : 2 * plane + 2, 0:width]
                out_ref[plane, :, lanes] = piece

        tile_loop(begin, min(end, TAIL_TILE), result)
        if end > TAIL_TILE:
            result(TAIL_TILE, 0, MERGED - TAIL)
    wait_given([5])
    for q, (begin, end) in enumerate(QUARTERS):

        def last_result(tile, j, q=q, width=128):
            lanes = pl.ds(tile * 128, width)
            if width == 128:
                lanes = pl.ds(pl.multiple_of(tile * 128, 128), 128)
            rows = slice(2 * q, 2 * q + 2)
            near = jnp.where(even, 0.0, given_fold[0, j, rows, :])
            term = total_fold[j, rows, :] + near + given_fold[1, j, rows, :]
            out_ref[PLANES - 1, :, lanes] = -term[:, 0:width]

        tile_loop(begin, min(end, TAIL_TILE), last_result)
        if end > TAIL_TILE:
            last_result(TAIL_TILE, TAIL_TILE - begin, width=MERGED - TAIL)

    for copy in near_sends():
        copy.wait_send()

    @pl.when(jnp.logical_not(even))
    def _():
        for copy in far_sends() + passes():
            copy.wait_send()

    for s in range(2):
        for copy in give_copies(s):
            copy.wait_send()
    for phase in range(2):
        for s in range(2):
            end_blocks(phase, s)


def body(bands, orbitals, pair_mask):
    hbm = pl.BlockSpec(memory_space=pltpu.HBM)
    smem = pl.BlockSpec(memory_space=pltpu.SMEM)
    consts = [jnp.asarray(table) for table in tables()]
    dma = pltpu.SemaphoreType.DMA

    def buffer(*shape):
        return pltpu.VMEM(shape, jnp.float32)

    out = pl.pallas_call(
        functools.partial(kernel, bands),
        out_shape=jax.ShapeDtypeStruct((PLANES, 2, MERGED), jnp.float32),
        in_specs=[smem] + [hbm] * (1 + len(consts)),
        out_specs=pl.BlockSpec(memory_space=pltpu.VMEM),
        scratch_shapes=[
            buffer(PLANES, 2, MERGED),
            pltpu.VMEM(consts[0].shape, jnp.bfloat16),
            buffer(*consts[1].shape),
            buffer(*consts[2].shape),
            buffer(TILES, 16, 128),
            buffer(TILES, 16, 128),
            buffer(FOLD + 1, 8, 128),
            buffer(2, TILES, 16, 128),
            buffer(2, FOLD + 1, 8, 128),
            buffer(TILES, ROWS, 128),
            buffer(NG * 8, 128),
            buffer(NG * 8, 128),
            buffer(2, FIELDS + 1, PEERS * PART, 128),
            buffer(2, PEERS * LAST, 128),
            buffer(2, ROWS, 128),
            buffer(2, FIELDS, PIECE, 128),
            buffer(2, FIELDS, PEERS * PART, 128),
            buffer(2, PEERS * LAST, 128),
            buffer(2, PEERS * PIECE, 128),
            buffer(2, FIELDS, PEERS * PART, 128),
            buffer(2, PEERS * LAST, 128),
            buffer(2, PEERS * PIECE, 128),
            buffer(2, FIELDS + 1, PEERS * PART, 128),
            buffer(2, PEERS * LAST, 128),
            buffer(2, ROWS, 128),
            buffer(2, FIELDS, PIECE, 128),
            buffer(NG, OWN),
            buffer(NG, 128),
            buffer(TILES, 16, 128),
            buffer(FOLD + 1, 8, 128),
            buffer(2, TILES, 8, 128),
            buffer(FOLD + 1, 8, 128),
            buffer(2, 2, TILES, 8, 128),
            buffer(2, FOLD + 1, 8, 128),
            buffer(2, 2, TILES, 8, 128),
            buffer(2, FOLD + 1, 8, 128),
            dma((2, 6)),
            dma((2, 6)),
            dma((6,)),
            dma((2, 6)),
            dma((2, 6)),
            dma((2, 2)),
            dma((2, 2, FIELDS)),
            dma((2, 2)),
            dma((2, 2)),
            dma((2, FIELDS)),
            dma((2, PEERS)),
            dma((2, PEERS)),
            dma((2, FIELDS)),
            dma((4,)),
        ],
        compiler_params=pltpu.CompilerParams(
            collective_id=0, has_side_effects=True, vmem_limit_bytes=64 * 1024 * 1024 - 65536
        ),
    )(pair_mask, orbitals.transpose(1, 0, 2), *consts)
    return out.transpose(1, 0, 2)


def solution(mesh):
    return jax.shard_map(
        functools.partial(body, mesh.shape["band"]),
        mesh=mesh,
        in_specs=(P("band", "pencil", None), P("band", None, None, None)),
        out_specs=P("band", "pencil", None),
        check_vma=False,
    )
```

```python
import functools
import math

import jax
import jax.numpy as jnp
import ml_dtypes
import numpy as np
from jax import lax
from jax.experimental import pallas as pl
from jax.experimental.pallas import tpu as pltpu
from jax.sharding import PartitionSpec as P

MESH = pl.DeviceIdType.MESH
NG = 72
PLANES = 9
PEERS = 8
FIELDS = 4
ROWS = 40
PART = 40
LAST = 24
MERGED = NG * NG
WIDTH = 5248
OWN = 640
TAIL = PEERS * OWN
PIECE = 16
FOLD = 11
MASKS = FOLD
QUARTERS = [(q * FOLD, min((q + 1) * FOLD, 41)) for q in range(4)]
TILES = WIDTH // 128
OWN_TILES = OWN // 128
TAIL_TILE = TILES - 1
coulomb_scale = 20.0
screening = 0.25
HALF = math.sqrt(0.5)


def dft8(x):
    a = [x[j] + x[j + 4] for j in range(4)]
    b = [x[j] - x[j + 4] for j in range(4)]
    e, o = a[0] + a[2], a[1] + a[3]
    u, v = HALF * (b[1] - b[3]), HALF * (b[1] + b[3])
    return [e + o, e - o, b[0] + u, v + b[2], a[0] - a[2], a[1] - a[3], b[0] - u, v - b[2]]


def dft8_adjoint(c):
    p, q = c[0] + c[1], c[0] - c[1]
    a = [p + c[4], q + c[5], p - c[4], q - c[5]]
    d, s = HALF * (c[2] - c[6]), HALF * (c[3] + c[7])
    b = [c[2] + c[6], d + s, c[3] - c[7], s - d]
    return [a[j] + b[j] for j in range(4)] + [a[j] - b[j] for j in range(4)]


def cos9(n):
    return math.cos(2.0 * math.pi * (n % 9) / 9)


def sin9(n):
    return math.sin(2.0 * math.pi * (n % 9) / 9)


def weighted(values, factors):
    total = values[0] * factors[0]
    for value, factor in zip(values[1:], factors[1:]):
        total = total + value * factor
    return total


def dft9(x):
    e = [x[n] + x[9 - n] for n in range(1, 5)]
    o = [x[n] - x[9 - n] for n in range(1, 5)]
    third = e[0] + e[1] + e[3]
    cosines = [x[0] + third + e[2]]
    sines = [None]
    for k in range(1, 5):
        if k == 3:
            cosines.append(x[0] + e[2] - 0.5 * third)
            sines.append(sin9(3) * (o[0] - o[1] + o[3]))
        else:
            cosines.append(x[0] + weighted(e, [cos9(k * n) for n in range(1, 5)]))
            sines.append(weighted(o, [sin9(k * n) for n in range(1, 5)]))
    return cosines, sines


def dft9_adjoint(cosines, sines):
    c, s = cosines, sines
    out = [None] * 9
    out[0] = c[0] + ((c[1] + c[2]) + (c[3] + c[4]))
    for n in range(1, 5):
        if n == 3:
            even = c[0] + c[3] - 0.5 * (c[1] + c[2] + c[4])
            odd = sin9(3) * (s[1] - s[2] + s[4])
        else:
            even = c[0] + weighted(c[1:], [cos9(k * n) for k in range(1, 5)])
            odd = weighted(s[1:], [sin9(k * n) for k in range(1, 5)])
        out[n] = even + odd
        out[9 - n] = even - odd
    return out


def finish72(load, save):
    for part in (0, 1):
        cosines, sines = dft9([load(part, b) for b in range(9)])
        base = part * 9
        save(base, cosines[0])
        for k in range(1, 5):
            save(base + 2 * k - 1, cosines[k])
            save(base + 2 * k, sines[k])
    for k8 in range(3):
        base = 18 + 18 * k8
        cc, cs = dft9([load(2 + 2 * k8, b) for b in range(9)])
        sc, ss = dft9([load(3 + 2 * k8, b) for b in range(9)])
        save(base, cc[0])
        save(base + 1, sc[0])
        for k in range(1, 5):
            at = base + 4 * k - 2
            save(at, cc[k] - ss[k])
            save(at + 1, cc[k] + ss[k])
            save(at + 2, sc[k] + cs[k])
            save(at + 3, sc[k] - cs[k])


def finish72_adjoint(load, save):
    for part in (0, 1):
        base = part * 9
        cosines = [load(base)] + [load(base + 2 * k - 1) for k in range(1, 5)]
        sines = [None] + [load(base + 2 * k) for k in range(1, 5)]
        for b, value in enumerate(dft9_adjoint(cosines, sines)):
            save(part, b, value)
    for k8 in range(3):
        base = 18 + 18 * k8
        cc, sc, cs, ss = [load(base)], [load(base + 1)], [None], [None]
        for k in range(1, 5):
            at = base + 4 * k - 2
            plus, minus, sine_plus, sine_minus = [load(at + i) for i in range(4)]
            cc.append(plus + minus)
            ss.append(minus - plus)
            sc.append(sine_plus + sine_minus)
            cs.append(sine_plus - sine_minus)
        for b, value in enumerate(dft9_adjoint(cc, cs)):
            save(2 + 2 * k8, b, value)
        for b, value in enumerate(dft9_adjoint(sc, ss)):
            save(3 + 2 * k8, b, value)


def point72(a, b):
    return (9 * a + 8 * b) % NG


def split(table):
    high = table.astype(ml_dtypes.bfloat16).astype(np.float64)
    return high, (table - high).astype(ml_dtypes.bfloat16).astype(np.float64)


def from_left(table):
    high, low = split(table)
    wide = np.zeros((80, 256))
    wide[:NG, : 3 * NG] = np.concatenate([high, high, low], axis=1)
    return wide


def from_right(table):
    high, low = split(table)
    return np.block([[high, low], [high, np.zeros_like(low)]])


@functools.cache
def tables():
    at = np.arange(NG)
    basis, freq = [np.full(NG, 1.0)], [0]
    for k in range(1, NG // 2):
        basis += [np.cos(2 * np.pi * k * at / NG), np.sin(2 * np.pi * k * at / NG)]
        freq += [k, k]
    basis.append(np.cos(np.pi * at))
    freq.append(NG // 2)
    basis = np.array(basis)
    basis /= np.sqrt((basis * basis).sum(1, keepdims=True))
    freq = np.array(freq, np.float64)
    eye = np.eye(NG)
    parts = [dft8([eye[point72(a, b)] for a in range(8)]) for b in range(9)]
    slots = [None] * NG
    finish72(lambda part, b: parts[b][part], slots.__setitem__)
    slots = np.array(slots)
    norm = (slots * slots).sum(1)
    spectrum = np.abs(np.fft.fft(slots, axis=1))[:, : NG // 2 + 1]
    freq_y = spectrum.argmax(1).astype(np.float64)
    along_z = np.zeros((128, 128))
    along_z[:NG, :NG] = basis.T
    along_x = basis.reshape(NG, PEERS, PLANES)
    along_x = np.concatenate([along_x[:, :, :8].reshape(NG, -1), along_x[:, :, 8]], axis=1)
    column = np.zeros((8, WIDTH), np.float32)
    column[0, :MERGED] = (freq_y[:, None] ** 2 + freq[None, :] ** 2).reshape(-1)
    column[1, :MERGED] = np.repeat(1.0 / norm, NG)
    freq_x = np.broadcast_to((freq**2)[:, None], (NG, 128)).astype(np.float32)
    wide = np.concatenate(
        [from_right(along_z), from_right(along_z.T), from_left(along_x), from_left(along_x.T)]
    )
    return wide.astype(ml_dtypes.bfloat16), column, freq_x


def take(load, start):
    tile, lane = divmod(start, 128)
    value = load(tile)
    if lane == 0:
        return value
    if lane + NG > 128:
        at = lax.broadcasted_iota(jnp.int32, value.shape, 1)
        value = jnp.where(at >= lane, value, load(tile + 1))
    return pltpu.roll(value, 128 - lane, 1)


def put(store, start, value):
    tile, lane = divmod(start, 128)
    if lane:
        value = pltpu.roll(value, lane, 1)
    end = min(lane + NG, 128)
    store(tile, slice(lane, end), value[:, lane:end])
    if lane + NG > 128:
        store(tile + 1, slice(0, lane + NG - 128), value[:, : lane + NG - 128])


def matmul(a, b):
    return jnp.dot(a, b, preferred_element_type=jnp.float32)


def halves(x):
    high = x.astype(jnp.bfloat16)
    return high, (x - high.astype(jnp.float32)).astype(jnp.bfloat16)


def left(table, x):
    high, low = [part.astype(jnp.float32) for part in halves(x)]
    zeros = jnp.zeros((8, x.shape[1]), jnp.float32)
    operand = jnp.concatenate([high, low, high, zeros], axis=0).astype(jnp.bfloat16)
    return matmul(table[:, 0 : operand.shape[0]], operand)[0:NG]


def kernel(
    bands,
    mask_ref,
    bands_hbm,
    wide_hbm,
    column_hbm,
    freq_hbm,
    out_ref,
    bands_ref,
    wide,
    column_ref,
    freq_ref,
    mixed,
    own,
    own_fold,
    visit,
    visit_fold,
    rho,
    work,
    work2,
    wave,
    wave_fold,
    wave_tail,
    wave_piece,
    recv,
    recv_fold,
    recv_tail,
    back,
    back_fold,
    back_tail,
    field,
    field_fold,
    field_tail,
    field_piece,
    kernel_table,
    kernel_tail,
    total,
    total_fold,
    base,
    base_fold,
    give,
    give_fold,
    given,
    given_fold,
    visit_send,
    visit_recv,
    pass_send,
    give_send,
    give_recv,
    part_send,
    part_recv,
    fold_send,
    fold_recv,
    tail_send,
    tail_recv,
    back_tail_send,
    back_tail_recv,
    load_sem,
):
    me = lax.axis_index("pencil")
    group = lax.axis_index("band")
    me_x, me_y = lax.div(me, 4), lax.rem(me, 4)

    loads = [
        pltpu.make_async_copy(src, dst, load_sem.at[i])
        for i, (src, dst) in enumerate(
            [
                (bands_hbm, bands_ref),
                (wide_hbm, wide),
                (column_hbm, column_ref),
                (freq_hbm, freq_ref),
            ]
        )
    ]
    for load in loads:
        load.start()

    def peer(j):
        return lax.rem(me + j, PEERS)

    def at(dx, dy):
        return lax.rem(me_x + dx, 2) * 4 + lax.rem(me_y + dy + 4, 4)

    def group_at(j):
        return lax.rem(group + j + bands, bands)

    barrier = pltpu.get_barrier_semaphore()
    for j in range(1, PEERS):
        pl.semaphore_signal(barrier, inc=1, device_id={"pencil": peer(j)}, device_id_type=MESH)
    for j in (-2, -1, 1, 2):
        pl.semaphore_signal(barrier, inc=1, device_id={"band": group_at(j)}, device_id_type=MESH)
    def remote(src, dst, send, recv, **device):
        return pltpu.make_async_remote_copy(
            src_ref=src,
            dst_ref=dst,
            send_sem=send,
            recv_sem=recv,
            device_id=device,
            device_id_type=MESH,
        )

    even = lax.rem(group, 2) == 0

    def terms_group(s):
        near = jnp.where(even, group_at(1), group_at(-1))
        return jnp.where(s == 0, near, jnp.where(even, group_at(2), group_at(-2)))

    def parts(main, fold):
        return [
            *(main.at[pl.ds(begin, end - begin)] for begin, end in QUARTERS),
            fold,
        ]

    def block_copies(src, dst, send, recv, to):
        return [
            remote(one, two, send.at[q], recv.at[q], band=to)
            for q, (one, two) in enumerate(zip(src, dst))
        ]

    def visit_at(s):
        return parts(visit.at[s], visit_fold.at[s])

    own_parts = parts(own, own_fold)

    def give_parts(main, fold):
        return [main.at[0], *parts(main.at[1], fold)]

    def visit_copies(s, src, send, to):
        return block_copies(src, visit_at(s), send, visit_recv.at[s], to)

    def near_sends():
        return visit_copies(0, own_parts, visit_send.at[0], group_at(-1))

    def far_sends():
        return visit_copies(1, own_parts, visit_send.at[1], group_at(2))

    def passes():
        return visit_copies(1, visit_at(0), pass_send, group_at(-1))

    loads[0].wait()
    def take_tile(tile, j, q, width):
        lanes = pl.ds(tile * 128, width)
        if width == 128:
            lanes = pl.ds(pl.multiple_of(tile * 128, 128), 128)
        live = slice(0, width)
        for plane in range(PLANES - 1):
            mixed[tile, 2 * plane : 2 * plane + 2, live] = bands_ref[plane, :, lanes]
        for band in range(2):
            own[tile, band * 8 : band * 8 + 8, :] = mixed[tile, pl.ds(band, 8, stride=2), :]
        own_fold[j, 2 * q : 2 * q + 2, live] = bands_ref[PLANES - 1, :, lanes]

    def tile_loop(begin, end, step):
        def run(j, carry):
            step(begin + j, j)
            return carry

        lax.fori_loop(0, end - begin, run, 0, unroll=True)

    mixed[TAIL_TILE] = jnp.zeros((16, 128), jnp.float32)
    own_fold[TAIL_TILE % FOLD, 6:8, :] = jnp.zeros((2, 128), jnp.float32)

    def own_mask(s, f):
        return mask_ref[0, s, f // 2, f % 2].astype(jnp.float32)

    for m in range(2 * FIELDS):
        value = own_mask(m // FIELDS, m % FIELDS)
        own_fold[MASKS, m : m + 1, :] = jnp.zeros((1, 128), jnp.float32) + value
    pl.semaphore_wait(barrier, PEERS - 1 + 4)
    near, far = near_sends(), far_sends()

    def send_own(part):
        near[part].start()

        @pl.when(jnp.logical_not(even))
        def _():
            far[part].start()

    for q, (begin, end) in enumerate(QUARTERS):
        tile_loop(begin, min(end, TAIL_TILE), lambda tile, j, q=q: take_tile(tile, j, q, 128))
        if end > TAIL_TILE:
            take_tile(TAIL_TILE, TAIL_TILE % FOLD, q, MERGED - TAIL)
        send_own(q)
    send_own(4)

    def kernel_columns(start, width):
        squared = column_ref[0:1, pl.ds(start, width)]
        scale = column_ref[1:2, pl.ds(start, width)]
        return coulomb_scale / (freq_ref[:, 0:1] + squared + screening) * scale

    for load in loads[1:]:
        load.wait()
    kernel_table[...] = kernel_columns(pl.multiple_of(me * OWN, 128), OWN)
    kernel_tail[...] = kernel_columns(TAIL, 128)
    wave_tail[...] = jnp.zeros((2, ROWS, 128), jnp.float32)
    total_fold[...] = jnp.zeros((FOLD + 1, 8, 128), jnp.float32)
    base_fold[...] = jnp.zeros((FOLD + 1, 8, 128), jnp.float32)

    def clear(tile, carry):
        total[tile] = jnp.zeros((16, 128), jnp.float32)
        base[:, tile] = jnp.zeros((2, 8, 128), jnp.float32)
        return carry

    lax.fori_loop(0, TILES, clear, 0)
    for s in range(2):
        for p in range(PEERS):
            back_fold[s, (p + 1) * LAST - 8 : (p + 1) * LAST, :] = jnp.zeros((8, 128), jnp.float32)
            back_tail[s, (p + 1) * PIECE - 8 : (p + 1) * PIECE, :] = jnp.zeros((8, 128), jnp.float32)
        field_tail[s, 32:40, :] = jnp.zeros((8, 128), jnp.float32)
        for f in range(FIELDS):
            wave_piece[s, f, 8:16, :] = jnp.zeros((8, 128), jnp.float32)

    first_band = [slice(band * 8, band * 8 + 8) for band in range(2)]
    field_rows = [slice(f * 8, f * 8 + 8) for f in range(FIELDS)]
    row_at = lax.broadcasted_iota(jnp.int32, (8, 128), 0)
    resident_one = lax.rem(lax.div(row_at, 2), 2) == 1
    visitor_one = lax.rem(row_at, 2) == 1

    def last_planes(s, j, q):
        a = [own_fold[j, 2 * q + band : 2 * q + band + 1, :] for band in range(2)]
        c = [visit_fold[s, j, 2 * q + band : 2 * q + band + 1, :] for band in range(2)]
        wide_a = [jnp.broadcast_to(row, (8, 128)) for row in a]
        wide_c = [jnp.broadcast_to(row, (8, 128)) for row in c]
        return (
            jnp.where(resident_one, wide_a[1], wide_a[0]),
            jnp.where(visitor_one, wide_c[1], wide_c[0]),
        )

    def along_z(start):
        both = matmul(jnp.concatenate(halves(work[...]), axis=1), wide[start : start + 256, :])
        work2[...] = both[:, :128] + both[:, 128:]

    def place(part, b):
        return slice((part * 9 + b) * 8, (part * 9 + b) * 8 + 8)

    def row_of(t):
        return pl.ds(pl.multiple_of(t * 8, 8), 8)

    def first(s):
        arriving = visit_copies(s, own_parts, visit_send.at[0], group_at(1))
        passing = passes()
        for q in range(5):
            arriving[q].wait_recv()

            @pl.when((s == 0) & jnp.logical_not(even))
            def _(q=q):
                passing[q].start()

        def one_row(i, carry):
            t = jnp.where(i == 0, FIELDS, order(jnp.maximum(i - 1, 0)))

            @pl.when(i > 0)
            def _():
                resident, visitor = row_of(lax.div(t, 2)), row_of(lax.rem(t, 2))
                for tile in range(TILES):
                    rho[tile, row_of(t), :] = own[tile, resident, :] * visit[s, tile, visitor, :]

            @pl.when(i == 0)
            def _():
                for q, (begin, end) in enumerate(QUARTERS):

                    def products(tile, j, q=q):
                        phi, chi = last_planes(s, j, q)
                        rho[tile, 32:40, :] = phi * chi

                    tile_loop(begin, end, products)

            for b in range(9):
                starts = [point72(a, b) * NG for a in range(8)]
                values = [take(lambda tile: rho[tile, row_of(t), :], at) for at in starts]
                for part, value in enumerate(dft8(values)):
                    work[place(part, b), :] = value
            along_z(0)

            def load(part, b):
                return work2[place(part, b), :]

            def target(tile, lanes, piece):
                if tile == TAIL_TILE:
                    wave_tail[s, row_of(t), lanes] = piece
                else:
                    wave[s, t, tile * 8 : tile * 8 + 8, lanes] = piece

            def save(slot, value):
                put(target, slot * NG, value)

            finish72(load, save)

            @pl.when(i == 0)
            def _():
                upper = lax.broadcasted_iota(jnp.int32, (8, 128), 0) < FIELDS

                def fold(q, carry):
                    for k in range(3):
                        at_row = pl.multiple_of((q * OWN_TILES + k) * 8, 8)
                        piece = wave[s, FIELDS, pl.ds(at_row, 8), :]
                        if k < 2:
                            below = wave[s, FIELDS, pl.ds(at_row + 24, 8), :]
                            piece = jnp.where(upper, piece, below)
                        to_row = pl.multiple_of(q * LAST + k * 8, 8)
                        wave_fold[s, pl.ds(to_row, 8), :] = piece
                    return carry

                lax.fori_loop(0, PEERS, fold, 0)
                send_fold(0, s)

            @pl.when(i > 0)
            def _():
                send_part(0, s, t)

            return carry

        lax.fori_loop(0, FIELDS + 1, one_row, 0)
        for f in range(FIELDS):
            wave_piece[s, f, 0:8, :] = wave_tail[s, field_rows[f], :]
            wave_piece[s, f, 8:9, :] = wave_tail[s, 32 + f : 33 + f, :]

    part_refs = ((wave, recv), (back, field))
    fold_refs = ((wave_fold, recv_fold), (back_fold, field_fold))
    straight = [(1, 2), (0, 2), (1, 1), (1, 3), (0, 1), (0, 3), (1, 0)]

    def rows_of(index, rows):
        return pl.ds(pl.multiple_of(index * rows, 8), rows)

    def send_part(phase, s, f):
        src, dst = part_refs[phase]
        for dx, dy in straight:
            to = at(dx, dy)
            remote(
                src.at[s, f, rows_of(to, PART)],
                dst.at[s, f, rows_of(me, PART)],
                part_send.at[phase, s],
                part_recv.at[phase, s, f],
                pencil=to,
            ).start()
        dst[s, f, rows_of(me, PART), :] = src[s, f, rows_of(me, PART), :]

    def send_fold(phase, s):
        src, dst = fold_refs[phase]
        for dx, dy in straight:
            to = at(dx, dy)
            remote(
                src.at[s, rows_of(to, LAST)],
                dst.at[s, rows_of(me, LAST)],
                fold_send.at[phase, s],
                fold_recv.at[phase, s],
                pencil=to,
            ).start()
        dst[s, rows_of(me, LAST), :] = src[s, rows_of(me, LAST), :]

    def drain(view, sem):
        pltpu.make_async_copy(view, view, sem).wait()

    def wait_part(phase, s, f):
        drain(part_refs[phase][1].at[s, f, pl.ds(0, 7 * PART)], part_recv.at[phase, s, f])

    def wait_fold(phase, s):
        drain(fold_refs[phase][1].at[s, pl.ds(0, 7 * LAST)], fold_recv.at[phase, s])

    def end_blocks(phase, s):
        parts = part_refs[phase][0].at[s, pl.ds(0, FIELDS), pl.ds(0, 7 * PART)]
        drain(parts, part_send.at[phase, s])
        drain(fold_refs[phase][0].at[s, pl.ds(0, 7 * LAST)], fold_send.at[phase, s])

    def piece_of(ref, s, index):
        return ref.at[s, pl.ds(pl.multiple_of(index * PIECE, 8), PIECE), :]

    def owner_of(s, f):
        return FIELDS * s + f

    def tail_copy(s, f, distance):
        return remote(
            wave_piece.at[s, f],
            piece_of(recv_tail, s, me),
            tail_send.at[s, f],
            tail_recv.at[s, distance],
            pencil=owner_of(s, f),
        )

    def second(s):
        wait_fold(0, s)

        def last_rows(f, tile):
            return pl.ds(tile % 3 * 8 + FIELDS * (tile // 3) + f, PEERS, stride=LAST)

        def one_field(i, carry):
            f = order(i)
            wait_part(0, s, f)
            columns = []
            for tile in range(OWN_TILES):
                starts = [p * PART + tile * 8 for p in range(PEERS)]
                rows = [recv[s, f, start : start + 8, :] for start in starts]
                rows.append(recv_fold[s, last_rows(f, tile), :])
                columns.append(jnp.concatenate(rows, axis=0))
            spectrum = left(wide[512:592, :], jnp.concatenate(columns, axis=1))
            result = left(wide[592:672, :], spectrum * kernel_table[...])
            for tile in range(OWN_TILES):
                lanes = slice(tile * 128, tile * 128 + 128)
                for p in range(PEERS):
                    start = p * PART + tile * 8
                    back[s, f, start : start + 8, :] = result[p * 8 : p * 8 + 8, lanes]
                back_fold[s, last_rows(f, tile), :] = result[64:72, lanes]
            send_part(1, s, f)
            return carry

        lax.fori_loop(0, FIELDS, one_field, 0)
        send_fold(1, s)

    def give_copies(s):
        return block_copies(
            give_parts(give.at[s], give_fold.at[s]),
            give_parts(given.at[s], given_fold.at[s]),
            give_send.at[s],
            give_recv.at[s],
            terms_group(s),
        )

    def order(i):
        return lax.rem(2 * i, FIELDS) + lax.div(i, 2)

    def pair_weights(s):
        weights = []
        for f in range(FIELDS):
            g = 2 * (f % 2) + f // 2
            above = visit_fold[s, MASKS, FIELDS + g : FIELDS + g + 1, :]
            same = visit_fold[s, MASKS, g : g + 1, :]
            mine = own_fold[MASKS, FIELDS + f : FIELDS + f + 1, :]
            row = jnp.where(s == 0, same, jnp.where(even, above, mine))
            weights.append(jnp.broadcast_to(row, (8, 128)))
        return weights

    def third(s):
        weights = pair_weights(s)
        leaving = give_copies(s)

        def leave(which):
            for part in which:
                leaving[part].start()

        def gather_band(c, begin, end):
            def gather(tile, j):
                chi = visit[s, tile, first_band[c], :]
                terms = base[c, tile]
                for a in range(2):
                    value = rho[tile, field_rows[2 * a + c], :] * weights[2 * a + c]
                    total[tile, first_band[a], :] += value * chi
                    terms = terms + value * own[tile, first_band[a], :]
                give[s, c, tile] = terms

            tile_loop(begin, end, gather)

        def one_row(i, carry):
            t = jnp.where(i == FIELDS, FIELDS, order(jnp.minimum(i, FIELDS - 1)))

            @pl.when(t < FIELDS)
            def _():
                wait_part(1, s, t)

            @pl.when(t == FIELDS)
            def _():
                wait_fold(1, s)

                def unfold(q, carry):
                    for k in range(OWN_TILES):
                        from_row = pl.multiple_of(q * LAST + k % 3 * 8, 8)
                        value = field_fold[s, pl.ds(from_row, 8), :]
                        value = pltpu.roll(value, FIELDS, 0) if k > 2 else value
                        to_row = pl.multiple_of((q * OWN_TILES + k) * 8, 8)
                        field[s, FIELDS, pl.ds(to_row, 8), :] = value
                    return carry

                lax.fori_loop(0, PEERS, unfold, 0)

            def source(tile):
                if tile == TAIL_TILE:
                    return field_tail[s, row_of(t), :]
                return field[s, t, tile * 8 : tile * 8 + 8, :]

            def load(slot):
                return take(source, slot * NG)

            def save(part, b, value):
                work[place(part, b), :] = value

            finish72_adjoint(load, save)
            along_z(256)

            def target(tile, lanes, piece):
                rho[tile, row_of(t), lanes] = piece

            for b in range(9):
                values = dft8_adjoint([work2[place(part, b), :] for part in range(8)])
                for a, value in enumerate(values):
                    put(target, point72(a, b) * NG, value)

            def join(band, which):
                @pl.when((s == 1) & even)
                def _():
                    for part in which:
                        give_copies(0)[part].wait_recv()
                    base[band] = given[0, band]

            @pl.when(i == 1)
            def _():
                join(0, [0])
                gather_band(0, 0, TILES)
                leave([0])

            @pl.when(i == 3)
            def _():
                join(1, [1, 2, 3, 4])
                for q, (begin, end) in enumerate(QUARTERS):
                    gather_band(1, begin, end)
                    leave([1 + q])

            return carry

        lax.fori_loop(0, FIELDS + 1, one_row, 0)

        @pl.when((s == 1) & even)
        def _():
            give_copies(0)[5].wait_recv()
            base_fold[...] = given_fold[0]

        last_weight = weights[3]
        for f in range(3):
            last_weight = jnp.where(row_at == f, weights[f], last_weight)

        for q, (begin, end) in enumerate(QUARTERS):

            def gather_last(tile, j, q=q):
                phi, chi = last_planes(s, j, q)
                value = rho[tile, 32:40, :] * last_weight
                stay, leave = value * chi, value * phi
                stay = stay + pltpu.roll(stay, 7, 0)
                leave = leave + pltpu.roll(leave, 6, 0)
                for band in range(2):
                    row = slice(2 * q + band, 2 * q + band + 1)
                    total_fold[j, row, :] += stay[2 * band : 2 * band + 1]
                    give_fold[s, j, row, :] = leave[band : band + 1] + base_fold[j, row, :]

            tile_loop(begin, end, gather_last)
        leave([5])

    def tail_back(s, f, j):
        return remote(
            piece_of(back_tail, s, peer(j)),
            field_piece.at[s, f],
            back_tail_send.at[s, j],
            back_tail_recv.at[s, f],
            pencil=peer(j),
        )

    def send_tail(s):
        for f in range(FIELDS):
            owner = owner_of(s, f)

            @pl.when(me == owner)
            def _(f=f, owner=owner):
                recv_tail[s, rows_of(owner, PIECE), :] = wave_piece[s, f]

            @pl.when(me != owner)
            def _(f=f, owner=owner):
                tail_copy(s, f, lax.rem(owner - me + PEERS, PEERS)).start()

    def turn_tail(s):
        owned = lax.div(me, FIELDS) == s

        @pl.when(owned)
        def _():
            for j in range(1, PEERS):
                tail_copy(s, 0, j).wait_recv()
            parts = [pl.ds(p * PIECE, 8) for p in range(PEERS)] + [pl.ds(8, PEERS, stride=PIECE)]
            block = jnp.concatenate([recv_tail[s, part, :] for part in parts], axis=0)
            spectrum = left(wide[512:592, :], block) * kernel_tail[...]
            result = left(wide[592:672, :], spectrum)
            for i, part in enumerate(parts):
                back_tail[s, part, :] = result[i * 8 : i * 8 + 8, :]
            mine = lax.rem(me, FIELDS)
            for j in range(1, PEERS):
                tail_back(s, mine, j).start()
            field_piece[s, mine] = back_tail[s, pl.ds(pl.multiple_of(me * PIECE, 8), PIECE), :]

    def end_tail(s):
        for f in range(FIELDS):
            owner = owner_of(s, f)

            @pl.when(me != owner)
            def _(f=f, owner=owner):
                tail_copy(s, f, lax.rem(owner - me + PEERS, PEERS)).wait_send()
                tail_back(s, f, 1).wait_recv()

            field_tail[s, field_rows[f], :] = field_piece[s, f, 0:8, :]
            field_tail[s, 32 + f : 33 + f, :] = field_piece[s, f, 8:9, :]

        @pl.when(lax.div(me, FIELDS) == s)
        def _():
            for j in range(1, PEERS):
                tail_back(s, lax.rem(me, FIELDS), j).wait_send()

    def slots(*stages):
        def run(s, carry):
            for stage in stages:
                stage(s)
            return carry

        lax.fori_loop(0, 2, run, 0)

    slots(first, send_tail)
    slots(second, turn_tail)
    slots(end_tail, third)

    def wait_given(which):
        for part in which:
            give_copies(1)[part].wait_recv()

            @pl.when(jnp.logical_not(even))
            def _(part=part):
                give_copies(0)[part].wait_recv()

    for q, (begin, end) in enumerate(QUARTERS):
        wait_given([0, 1] if q == 0 else [1 + q])

        def result(tile, j, width=128):
            lanes = pl.ds(tile * 128, width)
            if width == 128:
                lanes = pl.ds(pl.multiple_of(tile * 128, 128), 128)
            for rows, band in zip(first_band, range(2)):
                near = jnp.where(even, 0.0, given[0, band, tile])
                term = -(total[tile, rows, :] + near + given[1, band, tile])
                mixed[tile, pl.ds(band, 8, stride=2), :] = term
            for plane in range(PLANES - 1):
                piece = mixed[tile, 2 * plane : 2 * plane + 2, 0:width]
                out_ref[plane, :, lanes] = piece

        tile_loop(begin, min(end, TAIL_TILE), result)
        if end > TAIL_TILE:
            result(TAIL_TILE, 0, MERGED - TAIL)
    wait_given([5])
    for q, (begin, end) in enumerate(QUARTERS):

        def last_result(tile, j, q=q, width=128):
            lanes = pl.ds(tile * 128, width)
            if width == 128:
                lanes = pl.ds(pl.multiple_of(tile * 128, 128), 128)
            rows = slice(2 * q, 2 * q + 2)
            near = jnp.where(even, 0.0, given_fold[0, j, rows, :])
            term = total_fold[j, rows, :] + near + given_fold[1, j, rows, :]
            out_ref[PLANES - 1, :, lanes] = -term[:, 0:width]

        tile_loop(begin, min(end, TAIL_TILE), last_result)
        if end > TAIL_TILE:
            last_result(TAIL_TILE, TAIL_TILE - begin, width=MERGED - TAIL)

    for copy in near_sends():
        copy.wait_send()

    @pl.when(jnp.logical_not(even))
    def _():
        for copy in far_sends() + passes():
            copy.wait_send()

    for s in range(2):
        for copy in give_copies(s):
            copy.wait_send()
    for phase in range(2):
        for s in range(2):
            end_blocks(phase, s)


def body(bands, orbitals, pair_mask):
    hbm = pl.BlockSpec(memory_space=pltpu.HBM)
    smem = pl.BlockSpec(memory_space=pltpu.SMEM)
    consts = [jnp.asarray(table) for table in tables()]
    dma = pltpu.SemaphoreType.DMA

    def buffer(*shape):
        return pltpu.VMEM(shape, jnp.float32)

    out = pl.pallas_call(
        functools.partial(kernel, bands),
        out_shape=jax.ShapeDtypeStruct((PLANES, 2, MERGED), jnp.float32),
        in_specs=[smem] + [hbm] * (1 + len(consts)),
        out_specs=pl.BlockSpec(memory_space=pltpu.VMEM),
        scratch_shapes=[
            buffer(PLANES, 2, MERGED),
            pltpu.VMEM(consts[0].shape, jnp.bfloat16),
            buffer(*consts[1].shape),
            buffer(*consts[2].shape),
            buffer(TILES, 16, 128),
            buffer(TILES, 16, 128),
            buffer(FOLD + 1, 8, 128),
            buffer(2, TILES, 16, 128),
            buffer(2, FOLD + 1, 8, 128),
            buffer(TILES, ROWS, 128),
            buffer(NG * 8, 128),
            buffer(NG * 8, 128),
            buffer(2, FIELDS + 1, PEERS * PART, 128),
            buffer(2, PEERS * LAST, 128),
            buffer(2, ROWS, 128),
            buffer(2, FIELDS, PIECE, 128),
            buffer(2, FIELDS, PEERS * PART, 128),
            buffer(2, PEERS * LAST, 128),
            buffer(2, PEERS * PIECE, 128),
            buffer(2, FIELDS, PEERS * PART, 128),
            buffer(2, PEERS * LAST, 128),
            buffer(2, PEERS * PIECE, 128),
            buffer(2, FIELDS + 1, PEERS * PART, 128),
            buffer(2, PEERS * LAST, 128),
            buffer(2, ROWS, 128),
            buffer(2, FIELDS, PIECE, 128),
            buffer(NG, OWN),
            buffer(NG, 128),
            buffer(TILES, 16, 128),
            buffer(FOLD + 1, 8, 128),
            buffer(2, TILES, 8, 128),
            buffer(FOLD + 1, 8, 128),
            buffer(2, 2, TILES, 8, 128),
            buffer(2, FOLD + 1, 8, 128),
            buffer(2, 2, TILES, 8, 128),
            buffer(2, FOLD + 1, 8, 128),
            dma((2, 5)),
            dma((2, 5)),
            dma((5,)),
            dma((2, 6)),
            dma((2, 6)),
            dma((2, 2)),
            dma((2, 2, FIELDS)),
            dma((2, 2)),
            dma((2, 2)),
            dma((2, FIELDS)),
            dma((2, PEERS)),
            dma((2, PEERS)),
            dma((2, FIELDS)),
            dma((4,)),
        ],
        compiler_params=pltpu.CompilerParams(
            collective_id=0, has_side_effects=True, vmem_limit_bytes=64 * 1024 * 1024 - 65536
        ),
    )(pair_mask, orbitals.transpose(1, 0, 2), *consts)
    return out.transpose(1, 0, 2)


def solution(mesh):
    return jax.shard_map(
        functools.partial(body, mesh.shape["band"]),
        mesh=mesh,
        in_specs=(P("band", "pencil", None), P("band", None, None, None)),
        out_specs=P("band", "pencil", None),
        check_vma=False,
    )
```
